128 devices in a mesh: gx: 8 (over x, y_lo), gy: 16 (over y_hi, z, core).
Axes of the slice: x: 4, y: 4 (y_hi: 2, y_lo: 2; y = y_hi * 2 + y_lo), z: 4, core: 2. Of those that a mesh axis runs over, the one named last changes fastest.
Arguments:
- right_side: float32 [70, 192, 2048], P(None, 'gx', 'gy'), may hold values from -6 to 6
- helm_coef: float32 [70, 192, 2048], P(None, 'gx', 'gy'), may hold values from 0.5 to 4
- vert_coef: float32 [71], replicated, may hold values from 1 to 10
- block_inverse: float32 [4, 5, 14, 14], replicated, may hold values from -0.1 to 0.45, as said below
- edge_flip: int32 [8, 16, 4], P('gx', 'gy'), may hold values 0 or 1
Outputs:
- correction: float32 [70, 192, 2048], P(None, 'gx', 'gy')
The draws below stay inside these ranges and needn't reach their ends.
Inputs may be any that keep to these rules, and one draw needn't show every extreme that they name: `block_inverse`: each block's diagonal entries are positive and larger than the off-diagonal ones.
All inputs are finite; a program needn't handle non-finite values. No bound on the sum of `edge_flip` on one device may be relied on, other than what follows from the above.
Results may differ from the reference program's by a relative error of at most 0.0001.
Values sent between devices are 32-bit elements; how exact they have to be, the bound alone decides.
No kernel may reach another device: no remote copies, remote signals or barrier semaphores. Data moves between devices by JAX's collectives and lax.ppermute only.
A program may use at most 128 MiB of HBM per device.

```python
import math
import jax
import jax.numpy as jnp
from jax import lax

NZ = 70
BLK = 14
NBLK = 5
LEVELS = 4
NX = 192
NY = 2048
N_GX = 8
N_GY = 16


def draw_block_inverse(key, part):
    key = jax.random.fold_in(key, 7)
    first, second = jax.random.split(key)
    diag = jax.random.uniform(first, (LEVELS, NBLK, BLK), jnp.float32, 0.25, 0.45)
    off = jnp.clip(0.02 * jax.random.normal(second, (LEVELS, NBLK, BLK, BLK), jnp.float32), -0.09, 0.09)
    eye = jnp.eye(BLK, dtype=jnp.float32)
    return off * (1.0 - eye) + diag[..., None] * eye


def with_ends(entries, own_key, least, high):
    spot = [jax.random.randint(jax.random.fold_in(own_key, axis), (), 0, length) for axis, length in enumerate(entries.shape)]
    longest = entries.shape.index(max(entries.shape))
    neighbour = spot[:longest] + [(spot[longest] + 1) % entries.shape[longest]] + spot[longest + 1:]
    return entries.at[tuple(spot)].set(least).at[tuple(neighbour)].set(high)


def block_levels(key, extent, shards, least, top_value):
    level = 1.0
    for dim, shards_of in shards:
        steps = jax.random.uniform(jax.random.fold_in(jax.random.fold_in(key, 6), dim), (shards_of,), jnp.float32, least / len(shards), top_value / len(shards))
        level = level * jnp.repeat(jnp.exp(steps), extent[dim] // shards_of).reshape((-1,) + (1,) * (len(extent) - 1 - dim))
    return level


def scatter_about(stream_key, extent, spread, most, cuts=(), kind=jnp.bfloat16):
    result = jax.random.normal(stream_key, extent, jnp.float32) * spread
    if len(cuts) > 0:
        result = block_levels(stream_key, extent, cuts, -0.22, 0.18) * result
    return jnp.clip(result, min=-most, max=most).astype(kind)


def setup_inputs(seed: int = 0) -> dict:
    splits = jax.random.split(jax.random.key(seed), 6)
    right_side = scatter_about(splits[0], (NZ, NX, NY), 1.0, 6.0, ((1, 8), (2, 16)), jnp.float32)
    helm_coef = jnp.clip(jnp.exp(math.log(4.0) - 2.0794415 * jax.random.uniform(splits[1], (NZ, NX, NY), jnp.float32) ** block_levels(splits[1], (NZ, NX, NY), ((1, 8), (2, 16)), -0.2, 0.2)), 0.5, 4.0)
    vert_coef = jnp.clip(jnp.exp(jax.random.uniform(splits[2], (NZ + 1,), jnp.float32, math.log(1.0), math.log(10.0))), 1.0, 10.0)
    block_inverse = draw_block_inverse(jax.random.fold_in(splits[5], 71), 0)
    edge_flip = with_ends((jax.random.randint(splits[4], (N_GX, N_GY, 4), 0, 2) < 1).astype(jnp.int32), jax.random.fold_in(splits[4], 1), 0, 1)
    return {"right_side": right_side, "helm_coef": helm_coef, "vert_coef": vert_coef, "block_inverse": block_inverse, "edge_flip": edge_flip}


def vertical(field, vert_coef):
    zero = jnp.zeros_like(field[:1])
    above = jnp.concatenate([field[1:], zero], axis=0)
    below = jnp.concatenate([zero, field[:-1]], axis=0)
    couple = vert_coef[:, None, None]
    return couple[1:] * (field - above) + couple[:-1] * (field - below)


def operate(field, coef, vert_coef, edge_flip):
    depth, rows, cols = field.shape
    tile_x = rows // N_GX
    tile_y = cols // N_GY
    tiles = field.reshape(depth, N_GX, tile_x, N_GY, tile_y)
    flips = edge_flip > 0
    low_x = jnp.roll(tiles[:, :, tile_x - 1], 1, axis=1)
    low_x = jnp.where(flips[None, :, :, 0, None], low_x[..., ::-1], low_x)
    high_x = jnp.roll(tiles[:, :, 0], -1, axis=1)
    high_x = jnp.where(flips[None, :, :, 1, None], high_x[..., ::-1], high_x)
    low_y = jnp.roll(tiles[..., tile_y - 1], 1, axis=3)
    low_y = jnp.where(flips[None, :, None, :, 2], low_y[:, :, ::-1, :], low_y)
    high_y = jnp.roll(tiles[..., 0], -1, axis=3)
    high_y = jnp.where(flips[None, :, None, :, 3], high_y[:, :, ::-1, :], high_y)
    minus_x = jnp.concatenate([low_x[:, :, None], tiles[:, :, :-1]], axis=2)
    plus_x = jnp.concatenate([tiles[:, :, 1:], high_x[:, :, None]], axis=2)
    minus_y = jnp.concatenate([low_y[..., None], tiles[..., :-1]], axis=4)
    plus_y = jnp.concatenate([tiles[..., 1:], high_y[..., None]], axis=4)
    beside = (minus_x + plus_x + minus_y + plus_y).reshape(depth, rows, cols)
    return (coef * field + 4.0 * field - beside + vertical(field, vert_coef)) * 0.0625


def apply_blocks(inverse, resid):
    shape = resid.shape
    blocks = resid.reshape(inverse.shape[0], BLK, -1)
    out = jnp.einsum("kab,kbn->kan", inverse, blocks, precision=lax.Precision.HIGHEST)
    return out.reshape(shape)


def restrict(field):
    depth, rows, cols = field.shape
    return field.reshape(depth, rows // 2, 2, cols // 2, 2).mean(axis=(2, 4))


def prolong(field):
    return jnp.repeat(jnp.repeat(field, 2, axis=1), 2, axis=2)


def cycle(level, source, coef, vert_coef, block_inverse, edge_flip):
    inverse = block_inverse[level]
    field = apply_blocks(inverse, source)
    if level == LEVELS - 1:
        for sweep in range(3):
            field = field + apply_blocks(inverse, source - operate(field, coef, vert_coef, edge_flip))
        return field
    field = field + apply_blocks(inverse, source - operate(field, coef, vert_coef, edge_flip))
    resid = source - operate(field, coef, vert_coef, edge_flip)
    coarse = cycle(level + 1, restrict(resid), restrict(coef), vert_coef, block_inverse, edge_flip)
    field = field + prolong(coarse)
    for sweep in range(2):
        field = field + apply_blocks(inverse, source - operate(field, coef, vert_coef, edge_flip))
    return field


def reference(right_side, helm_coef, vert_coef, block_inverse, edge_flip):
    return cycle(0, right_side, helm_coef, vert_coef, block_inverse, edge_flip)
```

```python
import jax
import jax.numpy as jnp
from jax import lax
from jax.experimental import pallas as pl
from jax.experimental.pallas import tpu as pltpu
from jax.sharding import PartitionSpec as P

BLK = 14
NBLK = 5
NZ = 70
Z = 72
LANES = 128
F32 = jnp.float32
BF16 = jnp.bfloat16

GEOM = ((24, 1, 128), (6, 2, 64), (6, 1, 32), (3, 1, 16))


def lane_ids(shape):
    return lax.broadcasted_iota(jnp.int32, shape, len(shape) - 1)


def zl():
    return lane_ids((Z, LANES))


def roll(x, shift):
    shift = shift % x.shape[-1]
    return x if shift == 0 else pltpu.roll(x, shift, axis=1)


def col(x, k):
    return jnp.broadcast_to(x[:, k : k + 1], (Z, LANES))


def iota2(n, m):
    return lax.broadcasted_iota(jnp.int32, (n, m), 0), lax.broadcasted_iota(jnp.int32, (n, m), 1)


def lane_dot(x, mat):
    hi = x.astype(BF16).astype(F32)
    both = jnp.concatenate([hi, x - hi], axis=1).astype(BF16)
    twice = jnp.concatenate([mat, mat], axis=0).astype(BF16)
    return jnp.dot(both, twice, preferred_element_type=F32)


def block_dot(winv, x):
    hi = x.astype(BF16).astype(F32)
    parts = jnp.concatenate([hi, hi, x - hi], axis=0).astype(BF16)
    return jnp.dot(winv, parts, preferred_element_type=F32)


def reverse_matrix(width, blocks=(0,)):
    a, b = iota2(LANES, LANES)
    out = jnp.zeros((LANES, LANES), F32)
    for base in blocks:
        inside = (b >= base) & (b < base + width)
        out = jnp.where(inside & (a == 2 * base + width - 1 - b), 1.0, out)
    return out


def flag_row(flags, k):
    return jnp.broadcast_to(flags[k : k + 1, :], (Z, LANES))


class Coef:
    def __init__(self, ref):
        self.mid = jnp.broadcast_to(ref[:, 0:1], (Z, LANES))
        self.up = jnp.broadcast_to(ref[:, 1:2], (Z, LANES))
        self.down = jnp.broadcast_to(ref[:, 2:3], (Z, LANES))


def residual(co, f, c, v, beside):
    above = pltpu.roll(v, Z - 1, axis=0)
    below = pltpu.roll(v, 1, axis=0)
    return f - (c * 0.0625 + co.mid) * v + beside * 0.0625 + co.up * above + co.down * below


def row_of(geom, v, row):
    m_rows, _, ty = geom
    q, m = divmod(row, m_rows)
    return roll(v[m], -q * ty)


def corners(geom, v):
    m_rows, groups, ty = geom
    lane = zl()
    last = v[m_rows - 1]
    base = (groups - 1) * ty
    out = jnp.where(lane == 0, col(v[0], 0), 0.0)
    out = jnp.where(lane == 1, col(v[0], ty - 1), out)
    out = jnp.where(lane == 2, col(last, base), out)
    return jnp.where(lane == 3, col(last, base + ty - 1), out)


def place_col(geom, v, y, offset, out):
    m_rows, groups, ty = geom
    lane = zl()
    for m in range(m_rows):
        row = v[m]
        for q in range(groups):
            out = jnp.where(lane == offset + q * m_rows + m, col(row, q * ty + y), out)
    return out


def pack(geom, parts):
    ty = geom[2]
    per = LANES // ty
    out = []
    for first in range(0, len(parts), per):
        lane = zl()
        acc = parts[first]
        for k, part in enumerate(parts[first + 1 : first + per], 1):
            acc = jnp.where(lane < k * ty, acc, roll(part, k * ty))
        out.append(acc)
    return out


def packed(geom, count):
    per = LANES // geom[2]
    return -(-count // per)


def part_of(geom, ref, k):
    ty = geom[2]
    per = LANES // ty
    return roll(ref[(k // per) * Z : (k // per + 1) * Z, :], -(k % per) * ty)


def put_x(geom, v, c, up, down, flags=None):
    m_rows, groups, _ = geom
    tx = m_rows * groups
    extra = corners(geom, v)
    for ref, edge, second in ((up, tx - 1, tx - 2), (down, 0, 1)):
        parts = [row_of(geom, v, edge), row_of(geom, v, second)]
        if c is not None:
            parts.append(row_of(geom, c, edge))
        parts.append(extra)
        whole = pack(geom, parts)
        for k, part in enumerate(whole):
            ref[k * Z : (k + 1) * Z, :] = part
        if flags is not None:
            ref[len(whole) * Z : len(whole) * Z + 8, :] = flags


def put_y(geom, v, c, up, down):
    ty = geom[2]
    for ref, edge, second in ((up, ty - 1, ty - 2), (down, 0, 1)):
        out = place_col(geom, v, edge, 0, jnp.zeros((Z, LANES), F32))
        out = place_col(geom, v, second, 32, out)
        if c is not None:
            out = place_col(geom, c, edge, 64, out)
        ref[0:Z, :] = out


def merge_y(lo_extra, hi_extra, flags, up, down):
    lane = zl()
    f0, f1 = flag_row(flags, 0) > 0.5, flag_row(flags, 1) > 0.5

    def fill(part, values):
        for k, value in enumerate(values):
            part = jnp.where(lane == 96 + k, value, part)
        return part

    lo = [col(lo_extra, k) for k in range(4)]
    hi = [col(hi_extra, k) for k in range(4)]
    up_new = fill(up, [lo[3], lo[1], hi[1], hi[3], jnp.where(f0, lo[2], lo[3]), jnp.where(f1, hi[0], hi[1])])
    down_new = fill(down, [lo[2], lo[0], hi[0], hi[2], jnp.where(f0, lo[3], lo[2]), jnp.where(f1, hi[1], hi[0])])
    return up_new, down_new


class Halo:
    def __init__(self, lo, lo2, hi, hi2, dn, un):
        self.lo, self.lo2, self.hi, self.hi2, self.dn, self.un = lo, lo2, hi, hi2, dn, un

    def sides(self):
        return jnp.where(zl() < 64, self.dn, roll(self.un, 64))

    def seconds(self):
        return jnp.where(zl() < 64, roll(self.dn, -32), roll(self.un, 32))


class Flags:
    def __init__(self, own, lo, hi, dn, un):
        self.own, self.lo, self.hi, self.dn, self.un = own, lo, hi, dn, un


def turn_row(geom, row, flag):
    return jnp.where(flag > 0.5, lane_dot(row, reverse_matrix(geom[2])), row)


def turn_sides(geom, sides, flag_dn, flag_un):
    tx = geom[0] * geom[1]
    flag = jnp.where(zl() < 64, flag_dn, flag_un)
    return jnp.where(flag > 0.5, lane_dot(sides, reverse_matrix(tx, (0, 64))), sides)


def frame(geom, fl, lo, hi, sides):
    return (
        turn_row(geom, lo, flag_row(fl.own, 0)),
        turn_row(geom, hi, flag_row(fl.own, 1)),
        turn_sides(geom, sides, flag_row(fl.own, 2), flag_row(fl.own, 3)),
    )


def relax_edges(geom, winv, co, v, halo, fl, f_lo, c_lo, f_hi, c_hi, f_sides, c_sides):
    m_rows, groups, ty = geom
    tx = m_rows * groups
    lane = zl()
    dn, un = halo.dn, halo.un

    def beside_row(edge, second, mine, low, high):
        left = jnp.where(lane == 0, low, roll(edge, 1))
        right = jnp.where(lane == ty - 1, high, roll(edge, -1))
        return second + mine + left + right

    def choose(flags, k, first, other):
        return jnp.where(flag_row(flags, k) > 0.5, other, first)

    b_lo = beside_row(
        halo.lo,
        halo.lo2,
        turn_row(geom, row_of(geom, v, 0), flag_row(fl.lo, 1)),
        choose(fl.lo, 2, col(dn, 96), col(dn, 97)),
        choose(fl.lo, 3, col(un, 96), col(un, 97)),
    )
    b_hi = beside_row(
        halo.hi,
        halo.hi2,
        turn_row(geom, row_of(geom, v, tx - 1), flag_row(fl.hi, 0)),
        choose(fl.hi, 2, col(dn, 98), col(dn, 99)),
        choose(fl.hi, 3, col(un, 98), col(un, 99)),
    )
    edge = halo.sides()
    mine = place_col(geom, v, 0, 0, jnp.zeros((Z, LANES), F32))
    mine = place_col(geom, v, ty - 1, 64, mine)
    mine = turn_sides(geom, mine, flag_row(fl.dn, 3), flag_row(fl.un, 2))
    below = jnp.where(lane == 0, col(dn, 100), roll(edge, 1))
    below = jnp.where(lane == 64, col(un, 100), below)
    above = jnp.where(lane == tx - 1, col(dn, 101), roll(edge, -1))
    above = jnp.where(lane == 64 + tx - 1, col(un, 101), above)
    b_sides = halo.seconds() + mine + below + above
    r_lo = residual(co, f_lo, c_lo, halo.lo, b_lo)
    r_hi = residual(co, f_hi, c_hi, halo.hi, b_hi)
    r_sides = residual(co, f_sides, c_sides, edge, b_sides)
    d = block_dot(winv, jnp.concatenate([r_lo, r_hi, r_sides], axis=1))
    return halo.lo + d[:, :LANES], halo.hi + d[:, LANES : 2 * LANES], edge + d[:, 2 * LANES :]


def tile_residual(geom, co, v, f, c, lo, hi, sides, m):
    m_rows, groups, ty = geom
    lane = zl()
    here = v[m]
    if m > 0:
        low_x = v[m - 1]
    else:
        low_x = lo if groups == 1 else jnp.where(lane < ty, lo, roll(v[m_rows - 1], ty))
    if m < m_rows - 1:
        high_x = v[m + 1]
    elif groups == 1:
        high_x = hi
    else:
        high_x = jnp.where(lane < (groups - 1) * ty, roll(v[0], -ty), roll(hi, (groups - 1) * ty))
    low_y, high_y = roll(here, 1), roll(here, -1)
    for q in range(groups):
        row = q * m_rows + m
        low_y = jnp.where(lane == q * ty, col(sides, row), low_y)
        high_y = jnp.where(lane == q * ty + ty - 1, col(sides, 64 + row), high_y)
    return residual(co, f[m], c[m], here, low_x + high_x + low_y + high_y)


def relax_tile(geom, winv, co, v, f, c, edges, store):
    lo, hi, sides = edges
    for m in range(0, geom[0], 2):
        rows = [k for k in (m, m + 1) if k < geom[0]]
        r = [tile_residual(geom, co, v, f, c, lo, hi, sides, k) for k in rows]
        d = block_dot(winv, r[0] if len(r) == 1 else jnp.concatenate(r, axis=1))
        for i, k in enumerate(rows):
            store(k, v[k] + d[:, i * LANES : (i + 1) * LANES])


def start_tile(geom, winv, f, store):
    for m in range(0, geom[0], 2):
        rows = [k for k in (m, m + 1) if k < geom[0]]
        parts = [f[k] for k in rows]
        d = block_dot(winv, parts[0] if len(parts) == 1 else jnp.concatenate(parts, axis=1))
        for i, k in enumerate(rows):
            store(k, d[:, i * LANES : (i + 1) * LANES])


def restrict(fine, coarse, v, out):
    m_rows, _, ty = fine
    cm, cq, cty = coarse
    a, b = iota2(LANES, LANES)
    for mc in range(cm):
        acc = None
        for qc in range(cq):
            q, m = divmod(2 * (qc * cm + mc), m_rows)
            inside = (b >= qc * cty) & (b < (qc + 1) * cty) & (a // 2 == b - qc * cty + q * (ty // 2))
            term = lane_dot(v[m] + v[m + 1], jnp.where(inside, 0.25, 0.0))
            acc = term if acc is None else acc + term
        out[mc] = acc


def prolong_add(fine, coarse, e, v, out):
    m_rows, groups, ty = fine
    cm, _, cty = coarse
    a, b = iota2(LANES, LANES)
    for m in range(0, m_rows, 2):
        acc = None
        for q in range(groups):
            qc, mc = divmod((q * m_rows + m) // 2, cm)
            inside = (b >= q * ty) & (b < (q + 1) * ty) & (a - qc * cty == (b - q * ty) // 2)
            term = lane_dot(e[mc], jnp.where(inside, 1.0, 0.0))
            acc = term if acc is None else acc + term
        out[m] = v[m] + acc
        out[m + 1] = v[m + 1] + acc


class Setter:
    def __init__(self, ref):
        self.ref = ref

    def __call__(self, m, value):
        self.ref[m] = value


def messages(geom, xlo, xhi, ydn, yun, winv):
    n = packed(geom, 4)
    raw = [part_of(geom, xlo, 0), part_of(geom, xlo, 1), part_of(geom, xhi, 0), part_of(geom, xhi, 1), ydn[0:Z, :], yun[0:Z, :]]
    d = block_dot(winv, jnp.concatenate(raw, axis=1))
    halo = Halo(*[d[:, k * LANES : (k + 1) * LANES] for k in range(6)])
    return halo, n


def own_data(geom, xlo, xhi, ydn, yun):
    lane = zl()
    dn, un = ydn[0:Z, :], yun[0:Z, :]
    f_sides = jnp.where(lane < 64, dn, roll(un, 64))
    c_sides = jnp.where(lane < 64, roll(dn, -64), un)
    return (
        part_of(geom, xlo, 0),
        part_of(geom, xlo, 2),
        part_of(geom, xhi, 0),
        part_of(geom, xhi, 2),
        f_sides,
        c_sides,
    )


def flags_of(geom, own, xlo, xhi, ydn, yun):
    n = packed(geom, 4)
    return Flags(own[...], xlo[n * Z : n * Z + 8, :], xhi[n * Z : n * Z + 8, :], ydn[Z : Z + 8, :], yun[Z : Z + 8, :])


def load_top(src, dst):
    for x in range(24):
        dst[x, 0:NZ, :] = src[pl.ds(x, NZ, stride=24), :]
        dst[x, NZ:Z, :] = jnp.zeros((Z - NZ, LANES), F32)


VMEM = pl.BlockSpec(memory_space=pltpu.VMEM)


def call(kernel, outs, args, scratch=(), name=None):
    return pl.pallas_call(
        kernel,
        out_shape=[jax.ShapeDtypeStruct(s, F32) for s in outs],
        in_specs=[VMEM] * len(args),
        out_specs=[VMEM] * len(outs),
        scratch_shapes=[pltpu.VMEM(s, F32) for s in scratch],
        compiler_params=pltpu.CompilerParams(vmem_limit_bytes=48 * 1024 * 1024),
        name=name,
    )(*args)


def tile_shape(level):
    return (GEOM[level][0], Z, LANES)


def x_shape(level, count, flags):
    return (packed(GEOM[level], count) * Z + (8 if flags else 0), LANES)


Y_FULL = (Z + 8, LANES)


def open_kernel(f_in, c_in, flags, f, c, up, down, yup, ydown):
    load_top(f_in, f)
    load_top(c_in, c)
    put_x(GEOM[0], f, c, up, down, flags[...])
    put_y(GEOM[0], f, c, yup, ydown)
    yup[Z : Z + 8, :] = flags[...]
    ydown[Z : Z + 8, :] = flags[...]


def merge_kernel(level, count):
    geom = GEOM[level]

    def kernel(xlo, xhi, flags, yup, ydown, up, down):
        lo, hi = part_of(geom, xlo, count - 1), part_of(geom, xhi, count - 1)
        up[...] = yup[...]
        down[...] = ydown[...]
        a, b = merge_y(lo, hi, flags, yup[0:Z, :], ydown[0:Z, :])
        up[0:Z, :] = a
        down[0:Z, :] = b

    return kernel


def pre_kernel(level):
    geom, coarse = GEOM[level], GEOM[level + 1]

    def kernel(f, c, w, vz, own, xlo, xhi, ydn, yun, v_out, f_next, c_next, up, down, yup, ydown, one, res):
        winv = w[...].astype(BF16)
        co = Coef(vz)
        fl = flags_of(geom, own, xlo, xhi, ydn, yun)
        start_tile(geom, winv, f, Setter(one))
        halo, _ = messages(geom, xlo, xhi, ydn, yun, winv)
        lo2, hi2, sides2 = relax_edges(geom, winv, co, one, halo, fl, *own_data(geom, xlo, xhi, ydn, yun))
        relax_tile(geom, winv, co, one, f, c, frame(geom, fl, halo.lo, halo.hi, halo.sides()), Setter(v_out))
        lo, hi, sides = frame(geom, fl, lo2, hi2, sides2)
        for m in range(geom[0]):
            res[m] = tile_residual(geom, co, v_out, f, c, lo, hi, sides, m)
        restrict(geom, coarse, res, f_next)
        restrict(geom, coarse, c, c_next)
        put_x(coarse, f_next, c_next, up, down, own[...])
        put_y(coarse, f_next, c_next, yup, ydown)
        yup[Z : Z + 8, :] = own[...]
        ydown[Z : Z + 8, :] = own[...]

    return kernel


def bottom_kernel(f, c, w, vz, own, xlo, xhi, ydn, yun, v_out, up, down, yup, ydown, one):
    geom = GEOM[3]
    winv = w[...].astype(BF16)
    co = Coef(vz)
    fl = flags_of(geom, own, xlo, xhi, ydn, yun)
    start_tile(geom, winv, f, Setter(v_out))
    halo, _ = messages(geom, xlo, xhi, ydn, yun, winv)
    lo2, hi2, sides2 = relax_edges(geom, winv, co, v_out, halo, fl, *own_data(geom, xlo, xhi, ydn, yun))
    relax_tile(geom, winv, co, v_out, f, c, frame(geom, fl, halo.lo, halo.hi, halo.sides()), Setter(one))
    relax_tile(geom, winv, co, one, f, c, frame(geom, fl, lo2, hi2, sides2), Setter(v_out))
    put_x(geom, v_out, None, up, down)
    put_y(geom, v_out, None, yup, ydown)


def last_kernel(f, c, w, vz, own, xlo, xhi, ydn, yun, v, fine_v, g, up, down, yup, ydown, e):
    geom, fine = GEOM[3], GEOM[2]
    winv = w[...].astype(BF16)
    co = Coef(vz)
    fl = Flags(own[...], None, None, None, None)
    sides = jnp.where(zl() < 64, ydn[...], roll(yun[...], 64))
    edges = frame(geom, fl, part_of(geom, xlo, 0), part_of(geom, xhi, 0), sides)
    relax_tile(geom, winv, co, v, f, c, edges, Setter(e))
    prolong_add(fine, geom, e, fine_v, g)
    put_x(fine, g, None, up, down)
    put_y(fine, g, None, yup, ydown)


def post_kernel(level):
    geom = GEOM[level]

    def sweeps(f, c, w, vz, own, xlo, xhi, ydn, yun, g, glo, ghi, gdn, gun, one, store):
        winv = w[...].astype(BF16)
        co = Coef(vz)
        fl = flags_of(geom, own, xlo, xhi, ydn, yun)
        halo = Halo(
            part_of(geom, glo, 0), part_of(geom, glo, 1), part_of(geom, ghi, 0), part_of(geom, ghi, 1), gdn[...], gun[...]
        )
        lo2, hi2, sides2 = relax_edges(geom, winv, co, g, halo, fl, *own_data(geom, xlo, xhi, ydn, yun))
        relax_tile(geom, winv, co, g, f, c, frame(geom, fl, halo.lo, halo.hi, halo.sides()), Setter(one))
        relax_tile(geom, winv, co, one, f, c, frame(geom, fl, lo2, hi2, sides2), store)

    if level == 0:

        def kernel(f, c, w, vz, own, xlo, xhi, ydn, yun, g, glo, ghi, gdn, gun, out, one):
            def store(x, value):
                out[pl.ds(x, NZ, stride=24), :] = value[0:NZ, :]

            sweeps(f, c, w, vz, own, xlo, xhi, ydn, yun, g, glo, ghi, gdn, gun, one, store)

        return kernel

    fine = GEOM[level - 1]

    def kernel(f, c, w, vz, own, xlo, xhi, ydn, yun, g, glo, ghi, gdn, gun, fine_v, g_out, up, down, yup, ydown, one, e):
        sweeps(f, c, w, vz, own, xlo, xhi, ydn, yun, g, glo, ghi, gdn, gun, one, Setter(e))
        prolong_add(fine, geom, e, fine_v, g_out)
        put_x(fine, g_out, None, up, down)
        put_y(fine, g_out, None, yup, ydown)

    return kernel


def both_ways(up, down, axis):
    n = lax.axis_size(axis)
    fwd = [(i, (i + 1) % n) for i in range(n)]
    back = [((i + 1) % n, i) for i in range(n)]
    return lax.ppermute(up, axis, fwd), lax.ppermute(down, axis, back)


def block_matrices(block_inverse):
    levels = block_inverse.shape[0]
    whole = jnp.zeros((levels, Z, Z), F32)
    for k in range(NBLK):
        lo, hi = k * BLK, Z - (k + 1) * BLK
        whole = whole + jnp.pad(block_inverse[:, k], ((0, 0), (lo, hi), (lo, hi)))
    high = lax.reduce_precision(whole, 8, 7)
    low = lax.reduce_precision(whole - high, 8, 7)
    return jnp.concatenate([high, low, high], axis=2)


def vertical_columns(vert_coef):
    zero = jnp.zeros((1,), F32)
    up = jnp.concatenate([vert_coef[1:], zero, zero])
    down = jnp.concatenate([vert_coef[:-1], zero, zero])
    cols = jnp.stack([4.0 + up + down, up, down], axis=1) * 0.0625
    return jnp.pad(cols, ((0, 0), (0, LANES - 3)))


def on_device(right_side, helm_coef, vert_coef, block_inverse, edge_flip):
    own = jnp.pad(jnp.broadcast_to(edge_flip.reshape(4, 1).astype(F32), (4, LANES)), ((0, 4), (0, 0)))
    vz = vertical_columns(vert_coef)
    w = block_matrices(block_inverse)
    f_in = right_side.reshape(NZ * 24, LANES)
    c_in = helm_coef.reshape(NZ * 24, LANES)

    def exchange(level, count, up, down, yup, ydown):
        xlo, xhi = both_ways(up, down, "gx")
        shape = yup.shape
        yup, ydown = call(merge_kernel(level, count), [shape, shape], [xlo, xhi, own, yup, ydown], name=f"merge{level}")
        ydn, yun = both_ways(yup, ydown, "gy")
        return xlo, xhi, ydn, yun

    xs = x_shape(0, 4, True)
    f, c, *msg = call(
        open_kernel, [tile_shape(0)] * 2 + [xs, xs, Y_FULL, Y_FULL], [f_in, c_in, own], name="open"
    )
    saved = []
    for level in range(3):
        got = exchange(level, 4, *msg)
        xs = x_shape(level + 1, 4, True)
        t = tile_shape(level)
        nxt = tile_shape(level + 1)
        v, f_next, c_next, *msg = call(
            pre_kernel(level),
            [t, nxt, nxt, xs, xs, Y_FULL, Y_FULL],
            [f, c, w[level], vz, own, *got],
            [t, t],
            name=f"pre{level}",
        )
        saved.append((f, c, got, v))
        f, c = f_next, c_next
    got = exchange(3, 4, *msg)
    t = tile_shape(3)
    xs, ys = x_shape(3, 3, False), (Z, LANES)
    v, up, down, yup, ydown = call(
        bottom_kernel, [t, xs, xs, ys, ys], [f, c, w[3], vz, own, *got], [t], name="bottom"
    )
    xlo, xhi = both_ways(up, down, "gx")
    ydn, yun = both_ways(yup, ydown, "gy")
    t2 = tile_shape(2)
    xs = x_shape(2, 3, False)
    g, *msg = call(
        last_kernel,
        [t2, xs, xs, ys, ys],
        [f, c, w[3], vz, own, xlo, xhi, ydn, yun, v, saved[2][3]],
        [t],
        name="last",
    )
    for level in (2, 1, 0):
        f, c, got, _ = saved[level]
        ggot = exchange(level, 3, *msg)
        t = tile_shape(level)
        args = [f, c, w[level], vz, own, *got, g, *ggot]
        if level == 0:
            (out,) = call(post_kernel(0), [(NZ * 24, LANES)], args, [t], name="post0")
            return out.reshape(NZ, 24, LANES)
        xs = x_shape(level - 1, 3, False)
        g, *msg = call(
            post_kernel(level),
            [tile_shape(level - 1), xs, xs, ys, ys],
            args + [saved[level - 1][3]],
            [t, t],
            name=f"post{level}",
        )


def solution(mesh):
    placed = (P(None, "gx", "gy"), P(None, "gx", "gy"), P(), P(), P("gx", "gy", None))
    return jax.shard_map(
        on_device, mesh=mesh, in_specs=placed, out_specs=P(None, "gx", "gy"), check_vma=False
    )
```

```python
import jax
import jax.numpy as jnp
from jax import lax
from jax.experimental import pallas as pl
from jax.experimental.pallas import tpu as pltpu
from jax.sharding import PartitionSpec as P

BLK = 14
NBLK = 5
NZ = 70
Z = 72
LANES = 128
F32 = jnp.float32
BF16 = jnp.bfloat16

GEOM = ((24, 1, 128), (6, 2, 64), (6, 1, 32), (3, 1, 16))


def lane_ids(shape):
    return lax.broadcasted_iota(jnp.int32, shape, len(shape) - 1)


def zl():
    return lane_ids((Z, LANES))


def roll(x, shift):
    shift = shift % x.shape[-1]
    return x if shift == 0 else pltpu.roll(x, shift, axis=1)


def col(x, k):
    return jnp.broadcast_to(x[:, k : k + 1], (Z, LANES))


def iota2(n, m):
    return lax.broadcasted_iota(jnp.int32, (n, m), 0), lax.broadcasted_iota(jnp.int32, (n, m), 1)


def lane_dot(x, mat):
    hi = x.astype(BF16).astype(F32)
    both = jnp.concatenate([hi, x - hi], axis=1).astype(BF16)
    twice = jnp.concatenate([mat, mat], axis=0).astype(BF16)
    return jnp.dot(both, twice, preferred_element_type=F32)


def block_dot(winv, x):
    hi = x.astype(BF16).astype(F32)
    parts = jnp.concatenate([hi, hi, x - hi], axis=0).astype(BF16)
    return jnp.dot(winv, parts, preferred_element_type=F32)


def reverse_matrix(width):
    a, b = iota2(LANES, LANES)
    return jnp.where((b < width) & (a == width - 1 - b), 1.0, 0.0)


def flag_row(flags, k):
    return jnp.broadcast_to(flags[k : k + 1, :], (Z, LANES))


class Coef:
    def __init__(self, ref, width=LANES):
        self.mid = jnp.broadcast_to(ref[:, 0:1], (Z, width))
        self.up = jnp.broadcast_to(ref[:, 1:2], (Z, width))
        self.down = jnp.broadcast_to(ref[:, 2:3], (Z, width))


def residual(co, f, c, v, beside):
    above = pltpu.roll(v, Z - 1, axis=0)
    below = pltpu.roll(v, 1, axis=0)
    return f - (c * 0.0625 + co.mid) * v + beside * 0.0625 + co.up * above + co.down * below


def row_of(geom, v, row):
    m_rows, _, ty = geom
    q, m = divmod(row, m_rows)
    return roll(v[m], -q * ty)


def corners(geom, v):
    m_rows, groups, ty = geom
    lane = zl()
    last = v[m_rows - 1]
    base = (groups - 1) * ty
    out = jnp.where(lane == 0, col(v[0], 0), 0.0)
    out = jnp.where(lane == 1, col(v[0], ty - 1), out)
    out = jnp.where(lane == 2, col(last, base), out)
    return jnp.where(lane == 3, col(last, base + ty - 1), out)


def whole_rows(geom):
    return geom[1] == 1 and geom[2] == LANES


def tile_rows(geom):
    m_rows, groups, ty = geom
    return [(q * m_rows + m, m, q * ty) for m in range(m_rows) for q in range(groups)]


def own_columns(geom, v):
    ty = geom[2]
    lane = zl()
    out = jnp.zeros((Z, LANES), F32)
    for r, m, base in tile_rows(geom):
        row = v[m]
        first = roll(row, 2 * r + 1 - base)
        out = jnp.where(lane == 2 * r + 1, first, out)
        last = first if whole_rows(geom) else roll(row, 2 * r - (base + ty - 1))
        out = jnp.where(lane == 2 * r, last, out)
    return out


def pack(geom, parts):
    ty = geom[2]
    per = LANES // ty
    out = []
    for first in range(0, len(parts), per):
        lane = zl()
        acc = parts[first]
        for k, part in enumerate(parts[first + 1 : first + per], 1):
            acc = jnp.where(lane < k * ty, acc, roll(part, k * ty))
        out.append(acc)
    return out


def packed(geom, count):
    per = LANES // geom[2]
    return -(-count // per)


def part_of(geom, ref, k):
    ty = geom[2]
    per = LANES // ty
    return roll(ref[(k // per) * Z : (k // per + 1) * Z, :], -(k % per) * ty)


def put_x(geom, v, c, up, down, flags=None):
    m_rows, groups, _ = geom
    tx = m_rows * groups
    extra = corners(geom, v)
    for ref, edge, second in ((up, tx - 1, tx - 2), (down, 0, 1)):
        parts = [row_of(geom, v, edge), row_of(geom, v, second)]
        if c is not None:
            parts.append(row_of(geom, c, edge))
        parts.append(extra)
        whole = pack(geom, parts)
        for k, part in enumerate(whole):
            ref[k * Z : (k + 1) * Z, :] = part
        if flags is not None:
            ref[len(whole) * Z : len(whole) * Z + 8, :] = flags


def put_y(geom, v, c, up, down):
    ty = geom[2]
    lane = zl()
    out_up = jnp.zeros((Z, LANES), F32)
    out_down = out_up
    for r, m, base in tile_rows(geom):
        row = v[m]
        mine = lane // 2 == r
        last = roll(row, 2 * r + 1 - (base + ty - 1))
        first = roll(row, 2 * r - base)
        out_up = jnp.where(mine, last, out_up)
        out_down = jnp.where(mine, first, out_down)
        if c is not None:
            row = c[m]
            out_up = jnp.where(lane == 65 + 2 * r, roll(row, 65 + 2 * r - (base + ty - 1)), out_up)
            out_down = jnp.where(lane == 64 + 2 * r, roll(row, 64 + 2 * r - base), out_down)
    up[0:Z, :] = out_up
    down[0:Z, :] = out_down


def merge_y(lo_extra, hi_extra, flags, up, down):
    lane = zl()
    f0, f1 = flag_row(flags, 0) > 0.5, flag_row(flags, 1) > 0.5

    def fill(part, values):
        for k, value in enumerate(values):
            part = jnp.where(lane == 112 + k, value, part)
        return part

    lo = [col(lo_extra, k) for k in range(4)]
    hi = [col(hi_extra, k) for k in range(4)]
    up_new = fill(up, [lo[3], lo[1], hi[1], hi[3], jnp.where(f0, lo[2], lo[3]), jnp.where(f1, hi[0], hi[1])])
    down_new = fill(down, [lo[2], lo[0], hi[0], hi[2], jnp.where(f0, lo[3], lo[2]), jnp.where(f1, hi[1], hi[0])])
    return up_new, down_new


def odd_lanes():
    return zl() % 2 == 1


class Halo:
    def __init__(self, lo, lo2, hi, hi2, dn, un):
        self.lo, self.lo2, self.hi, self.hi2, self.dn, self.un = lo, lo2, hi, hi2, dn, un

    def sides(self):
        return jnp.where(odd_lanes(), self.dn, self.un)

    def seconds(self):
        return jnp.where(odd_lanes(), roll(self.dn, 1), roll(self.un, -1))


class Flags:
    def __init__(self, own, lo, hi, dn, un):
        self.own, self.lo, self.hi, self.dn, self.un = own, lo, hi, dn, un


def turn_row(geom, row, flag):
    return jnp.where(flag > 0.5, lane_dot(row, reverse_matrix(geom[2])), row)


def turn_sides(geom, sides, flag_dn, flag_un):
    tx = geom[0] * geom[1]
    flag = jnp.where(odd_lanes(), flag_dn, flag_un)
    a, b = iota2(LANES, LANES)
    mat = jnp.where((b < 2 * tx) & (a == 2 * (tx - 1 - b // 2) + b % 2), 1.0, 0.0)
    return jnp.where(flag > 0.5, lane_dot(sides, mat), sides)


def frame(geom, fl, lo, hi, sides):
    return (
        turn_row(geom, lo, flag_row(fl.own, 0)),
        turn_row(geom, hi, flag_row(fl.own, 1)),
        turn_sides(geom, sides, flag_row(fl.own, 2), flag_row(fl.own, 3)),
    )


def relax_edges(geom, winv, co, v, halo, fl, f_lo, c_lo, f_hi, c_hi, f_sides, c_sides):
    m_rows, groups, ty = geom
    tx = m_rows * groups
    lane = zl()
    dn, un = halo.dn, halo.un

    def beside_row(edge, second, mine, low, high):
        left = jnp.where(lane == 0, low, roll(edge, 1))
        right = jnp.where(lane == ty - 1, high, roll(edge, -1))
        return second + mine + left + right

    def choose(flags, k, first, other):
        return jnp.where(flag_row(flags, k) > 0.5, other, first)

    b_lo = beside_row(
        halo.lo,
        halo.lo2,
        turn_row(geom, row_of(geom, v, 0), flag_row(fl.lo, 1)),
        choose(fl.lo, 2, col(dn, 112), col(dn, 113)),
        choose(fl.lo, 3, col(un, 112), col(un, 113)),
    )
    b_hi = beside_row(
        halo.hi,
        halo.hi2,
        turn_row(geom, row_of(geom, v, tx - 1), flag_row(fl.hi, 0)),
        choose(fl.hi, 2, col(dn, 114), col(dn, 115)),
        choose(fl.hi, 3, col(un, 114), col(un, 115)),
    )
    edge = halo.sides()
    mine = turn_sides(geom, own_columns(geom, v), flag_row(fl.dn, 3), flag_row(fl.un, 2))
    below = jnp.where(lane == 1, col(dn, 116), jnp.where(lane == 0, col(un, 116), roll(edge, 2)))
    last = 2 * (tx - 1)
    above = jnp.where(lane == last + 1, col(dn, 117), jnp.where(lane == last, col(un, 117), roll(edge, -2)))
    b_sides = halo.seconds() + mine + below + above
    r_lo = residual(co, f_lo, c_lo, halo.lo, b_lo)
    r_hi = residual(co, f_hi, c_hi, halo.hi, b_hi)
    r_sides = residual(co, f_sides, c_sides, edge, b_sides)
    d = block_dot(winv, jnp.concatenate([r_lo, r_hi, r_sides], axis=1))
    return halo.lo + d[:, :LANES], halo.hi + d[:, LANES : 2 * LANES], edge + d[:, 2 * LANES :]


def tile_residual(geom, co, v, f, c, lo, hi, sides, m):
    m_rows, groups, ty = geom
    lane = zl()
    here = v[m]
    if m > 0:
        low_x = v[m - 1]
    else:
        low_x = lo if groups == 1 else jnp.where(lane < ty, lo, roll(v[m_rows - 1], ty))
    if m < m_rows - 1:
        high_x = v[m + 1]
    elif groups == 1:
        high_x = hi
    else:
        high_x = jnp.where(lane < (groups - 1) * ty, roll(v[0], -ty), roll(hi, (groups - 1) * ty))
    low_y, high_y = roll(here, 1), roll(here, -1)
    for q in range(groups):
        row = q * m_rows + m
        low = roll(sides, q * ty - 2 * row - 1)
        high = low if whole_rows(geom) else roll(sides, q * ty + ty - 1 - 2 * row)
        low_y = jnp.where(lane == q * ty, low, low_y)
        high_y = jnp.where(lane == q * ty + ty - 1, high, high_y)
    return residual(co, f[m], c[m], here, low_x + high_x + low_y + high_y)


def relax_tile(geom, winv, co, v, f, c, edges, store):
    lo, hi, sides = edges
    for m in range(0, geom[0], 2):
        rows = [k for k in (m, m + 1) if k < geom[0]]
        r = [tile_residual(geom, co, v, f, c, lo, hi, sides, k) for k in rows]
        d = block_dot(winv, r[0] if len(r) == 1 else jnp.concatenate(r, axis=1))
        for i, k in enumerate(rows):
            store(k, v[k] + d[:, i * LANES : (i + 1) * LANES])


def start_tile(geom, winv, f, store):
    for m in range(0, geom[0], 2):
        rows = [k for k in (m, m + 1) if k < geom[0]]
        parts = [f[k] for k in rows]
        d = block_dot(winv, parts[0] if len(parts) == 1 else jnp.concatenate(parts, axis=1))
        for i, k in enumerate(rows):
            store(k, d[:, i * LANES : (i + 1) * LANES])


def restrict(fine, coarse, v, out):
    m_rows, _, ty = fine
    cm, cq, cty = coarse
    a, b = iota2(LANES, LANES)
    for mc in range(cm):
        acc = None
        for qc in range(cq):
            q, m = divmod(2 * (qc * cm + mc), m_rows)
            inside = (b >= qc * cty) & (b < (qc + 1) * cty) & (a // 2 == b - qc * cty + q * (ty // 2))
            term = lane_dot(v[m] + v[m + 1], jnp.where(inside, 0.25, 0.0))
            acc = term if acc is None else acc + term
        out[mc] = acc


def prolong_add(fine, coarse, e, v, out):
    m_rows, groups, ty = fine
    cm, _, cty = coarse
    a, b = iota2(LANES, LANES)
    for m in range(0, m_rows, 2):
        acc = None
        for q in range(groups):
            qc, mc = divmod((q * m_rows + m) // 2, cm)
            inside = (b >= q * ty) & (b < (q + 1) * ty) & (a - qc * cty == (b - q * ty) // 2)
            term = lane_dot(e[mc], jnp.where(inside, 1.0, 0.0))
            acc = term if acc is None else acc + term
        out[m] = v[m] + acc
        out[m + 1] = v[m + 1] + acc


class Setter:
    def __init__(self, ref):
        self.ref = ref

    def __call__(self, m, value):
        self.ref[m] = value


def messages(geom, xlo, xhi, ydn, yun, winv):
    n = packed(geom, 4)
    raw = [part_of(geom, xlo, 0), part_of(geom, xlo, 1), part_of(geom, xhi, 0), part_of(geom, xhi, 1), ydn[0:Z, :], yun[0:Z, :]]
    d = block_dot(winv, jnp.concatenate(raw, axis=1))
    halo = Halo(*[d[:, k * LANES : (k + 1) * LANES] for k in range(6)])
    return halo, n


def own_data(geom, xlo, xhi, ydn, yun):
    dn, un = ydn[0:Z, :], yun[0:Z, :]
    f_sides = jnp.where(odd_lanes(), dn, un)
    c_sides = roll(f_sides, -64)
    return (
        part_of(geom, xlo, 0),
        part_of(geom, xlo, 2),
        part_of(geom, xhi, 0),
        part_of(geom, xhi, 2),
        f_sides,
        c_sides,
    )


def flags_of(geom, own, xlo, xhi, ydn, yun):
    n = packed(geom, 4)
    return Flags(own[...], xlo[n * Z : n * Z + 8, :], xhi[n * Z : n * Z + 8, :], ydn[Z : Z + 8, :], yun[Z : Z + 8, :])


def load_top(src, dst):
    for x in range(24):
        dst[x, 0:NZ, :] = src[pl.ds(x, NZ, stride=24), :]
        dst[x, NZ:Z, :] = jnp.zeros((Z - NZ, LANES), F32)


STRIPS = {2: (6, 32, 256), 3: (3, 16, 128)}


def in_tile(strip):
    _, ty, width = strip
    return lane_ids((Z, width)) % ty


def group_dot(x, mat):
    parts = [lane_dot(x[:, k : k + LANES], mat) for k in range(0, x.shape[1], LANES)]
    return parts[0] if len(parts) == 1 else jnp.concatenate(parts, axis=1)


def turn_groups(strip, x, flags, k, count):
    _, ty, width = strip
    a, b = iota2(LANES, LANES)
    mat = jnp.where((a // ty == b // ty) & (b % ty < count) & (a % ty == count - 1 - b % ty), 1.0, 0.0)
    flag = jnp.broadcast_to(flags[k : k + 1, :], (Z, width))
    return jnp.where(flag > 0.5, group_dot(x, mat), x)


def strip_ends(strip, v, flags):
    m_rows, ty, _ = strip
    low = turn_groups(strip, roll(v[m_rows - 1], ty), flags, 0, ty)
    high = turn_groups(strip, roll(v[0], -ty), flags, 1, ty)
    return low, high


def strip_column(strip, v, y, offset, out):
    lt = in_tile(strip)
    for m in range(strip[0]):
        out = jnp.where(lt == offset + m, roll(v[m], offset + m - y), out)
    return out


def strip_message(strip, v, c, ends, up, down):
    m_rows, ty, width = strip
    lt = in_tile(strip)
    for ref, edge, second in ((up, ty - 1, ty - 2), (down, 0, 1)):
        out = strip_column(strip, v, edge, 0, jnp.zeros((Z, width), F32))
        out = strip_column(strip, v, second, m_rows, out)
        if c is not None:
            out = strip_column(strip, c, edge, 2 * m_rows, out)
        for k, end in enumerate(ends):
            out = jnp.where(lt == 3 * m_rows + k, roll(end, 3 * m_rows + k - edge), out)
        ref[0:Z, :] = out


def strip_edges(strip, winv, co, v, sides):
    m_rows, _, width = strip
    lt = in_tile(strip)
    r = []
    for x, raw, flags, k, y in sides:
        mine = strip_column(strip, v, y, 0, jnp.zeros((Z, width), F32))
        mine = turn_groups(strip, mine, flags, k, m_rows)
        low = jnp.where(lt == 0, roll(x, -3 * m_rows), roll(x, 1))
        high = jnp.where(lt == m_rows - 1, roll(x, -2 * m_rows - 2), roll(x, -1))
        r.append(residual(co, raw, roll(raw, -2 * m_rows), x, roll(x, -m_rows) + mine + low + high))
    d = block_dot(winv, jnp.concatenate(r, axis=1))
    return [side[0] + d[:, k * width : (k + 1) * width] for k, side in enumerate(sides)]


def strip_frame(strip, flags, low, high):
    return turn_groups(strip, low, flags, 2, strip[0]), turn_groups(strip, high, flags, 3, strip[0])


def strip_residual(strip, co, v, f, c, ends, sides, m):
    m_rows, ty, _ = strip
    lt = in_tile(strip)
    low_x = v[m - 1] if m > 0 else ends[0]
    high_x = v[m + 1] if m < m_rows - 1 else ends[1]
    low_y = jnp.where(lt == 0, roll(sides[0], -m), roll(v[m], 1))
    high_y = jnp.where(lt == ty - 1, roll(sides[1], ty - 1 - m), roll(v[m], -1))
    return residual(co, f[m], c[m], v[m], low_x + high_x + low_y + high_y)


def strip_relax(strip, winv, co, v, f, c, flags, sides, store):
    ends = strip_ends(strip, v, flags)
    for m in range(strip[0]):
        r = strip_residual(strip, co, v, f, c, ends, sides, m)
        store(m, v[m] + block_dot(winv, r))


def strip_restrict(v, out):
    a, b = iota2(LANES, LANES)
    for m in range(3):
        both = v[2 * m] + v[2 * m + 1]
        out[m] = lane_dot(both[:, :LANES], jnp.where(a // 2 == b, 0.25, 0.0)) + lane_dot(
            both[:, LANES:], jnp.where(a // 2 == b - 64, 0.25, 0.0)
        )


def open_strip_kernel(chunks, f, c, flags, up, down):
    strip = STRIPS[2]
    group = lane_ids((Z, LANES)) // 32
    for m in range(6):
        for ref, k in ((f, m), (c, 6 + m)):
            part = (k // 4) * Z
            halves = []
            for h in range(2):
                acc = None
                for g in range(4):
                    x = roll(chunks[4 * h + g, part : part + Z, :], (g - k % 4) * 32)
                    acc = x if acc is None else jnp.where(group == g, x, acc)
                halves.append(acc)
            ref[m] = jnp.concatenate(halves, axis=1)
    group = lane_ids((8, LANES)) // 32
    for h in range(2):
        acc = None
        for g in range(4):
            x = chunks[4 * h + g, 3 * Z : 3 * Z + 8, :]
            acc = x if acc is None else jnp.where(group == g, x, acc)
        flags[:, h * LANES : (h + 1) * LANES] = acc
    strip_message(strip, f, c, strip_ends(strip, f, flags), up, down)
    up[Z : Z + 8, :] = flags[...]
    down[Z : Z + 8, :] = flags[...]


def strip_sides(values, raws, dn, un, ty):
    return (
        (values[0], raws[0], dn[Z : Z + 8, :], 3, 0),
        (values[1], raws[1], un[Z : Z + 8, :], 2, ty - 1),
    )


def pre_strip_kernel(f, c, w, vz, flags, dn, un, v_out, f_next, c_next, fl_next, up, down, one, res):
    strip = STRIPS[2]
    width = strip[2]
    winv = w[...].astype(BF16)
    co = Coef(vz, width)
    for m in range(6):
        one[m] = block_dot(winv, f[m])
    raws = [dn[0:Z, :], un[0:Z, :]]
    values = [block_dot(winv, x) for x in raws]
    edges = strip_edges(strip, winv, co, one, strip_sides(values, raws, dn, un, strip[1]))
    strip_relax(strip, winv, co, one, f, c, flags, strip_frame(strip, flags, *values), Setter(v_out))
    ends = strip_ends(strip, v_out, flags)
    sides = strip_frame(strip, flags, *edges)
    for m in range(6):
        res[m] = strip_residual(strip, co, v_out, f, c, ends, sides, m)
    strip_restrict(res, f_next)
    strip_restrict(c, c_next)
    a, b = iota2(LANES, LANES)
    fl_next[...] = lane_dot(flags[:, :LANES], jnp.where((b < 64) & (a == (b // 16) * 32), 1.0, 0.0)) + lane_dot(
        flags[:, LANES:], jnp.where((b >= 64) & (a == (b // 16 - 4) * 32), 1.0, 0.0)
    )
    small = STRIPS[3]
    strip_message(small, f_next, c_next, strip_ends(small, f_next, fl_next), up, down)
    up[Z : Z + 8, :] = fl_next[...]
    down[Z : Z + 8, :] = fl_next[...]


def bottom_strip_kernel(f, c, w, vz, flags, dn, un, v_out, up, down, one):
    strip = STRIPS[3]
    winv = w[...].astype(BF16)
    co = Coef(vz)
    for m in range(3):
        v_out[m] = block_dot(winv, f[m])
    raws = [dn[0:Z, :], un[0:Z, :]]
    values = [block_dot(winv, x) for x in raws]
    edges = strip_edges(strip, winv, co, v_out, strip_sides(values, raws, dn, un, strip[1]))
    strip_relax(strip, winv, co, v_out, f, c, flags, strip_frame(strip, flags, *values), Setter(one))
    strip_relax(strip, winv, co, one, f, c, flags, strip_frame(strip, flags, *edges), Setter(v_out))
    strip_message(strip, v_out, None, (), up, down)


def last_strip_kernel(f, c, w, vz, flags, dn, un, v, fine_v, fine_flags, g, up, down, e):
    strip, fine = STRIPS[3], STRIPS[2]
    winv = w[...].astype(BF16)
    strip_relax(strip, winv, Coef(vz), v, f, c, flags, strip_frame(strip, flags, dn[...], un[...]), Setter(e))
    a, b = iota2(LANES, LANES)
    for m in range(3):
        add = jnp.concatenate([lane_dot(e[m], jnp.where(a == 64 * h + b // 2, 1.0, 0.0)) for h in range(2)], axis=1)
        g[2 * m] = fine_v[2 * m] + add
        g[2 * m + 1] = fine_v[2 * m + 1] + add
    strip_message(fine, g, None, strip_ends(fine, g, fine_flags), up, down)


def post_strip_kernel(
    f, c, w, vz, flags, dn, un, g, gdn, gun, fine_v, xlo, xhi, own, g_out, lo_out, hi_out, up, down, one, e, tile, yup, ydown
):
    strip = STRIPS[2]
    fine, geom = GEOM[1], GEOM[2]
    winv = w[...].astype(BF16)
    co = Coef(vz, strip[2])
    raws = [dn[0:Z, :], un[0:Z, :]]
    values = [gdn[...], gun[...]]
    edges = strip_edges(strip, winv, co, g, strip_sides(values, raws, dn, un, strip[1]))
    strip_relax(strip, winv, co, g, f, c, flags, strip_frame(strip, flags, *values), Setter(one))
    strip_relax(strip, winv, co, one, f, c, flags, strip_frame(strip, flags, *edges), Setter(e))

    place = lax.axis_index("gx")

    def tile_row(m, step):
        t = lax.rem(place + (step + 8), 8)
        return pltpu.roll(e[m], lax.rem(8 - t, 8) * 32, axis=1)[:, :LANES]

    for m in range(6):
        tile[m] = tile_row(m, 0)
    prolong_add(fine, geom, tile, fine_v, g_out)
    a, b = iota2(LANES, LANES)
    spread = jnp.where((b < 64) & (a == b // 2), 1.0, 0.0)
    lane = zl()
    extras = []
    for ref, out, step, near in ((xlo, lo_out, -1, 5), (xhi, hi_out, 1, 0)):
        first, last = tile_row(0, step), tile_row(5, step)
        add = lane_dot(last if near else first, spread)
        extra = part_of(fine, ref, 2)
        for k, value in enumerate((col(first, 0), col(first, 31), col(last, 0), col(last, 31))):
            extra = extra + jnp.where(lane == k, value, 0.0)
        extras.append(extra)
        for k, part in enumerate(pack(fine, [part_of(fine, ref, 0) + add, part_of(fine, ref, 1) + add, extra])):
            out[k * Z : (k + 1) * Z, :] = part
    put_y(fine, g_out, None, yup, ydown)
    up[...], down[...] = merge_y(*extras, own, yup[...], ydown[...])


def strip_ring(up, down):
    nx, ny = lax.axis_size("gx"), lax.axis_size("gy")

    def pairs(step):
        out = []
        for i in range(nx):
            for j in range(ny):
                to = (j + step) % ny
                other = i ^ 1 if (2 * j // ny) != (2 * to // ny) else i
                out.append((i * ny + j, other * ny + to))
        return out

    both = ("gx", "gy")
    return lax.ppermute(up, both, pairs(1)), lax.ppermute(down, both, pairs(-1))


LIMIT = 14 * 1024 * 1024
VMEM = pl.BlockSpec(memory_space=pltpu.VMEM)


def call(kernel, outs, args, scratch=(), name=None):
    return pl.pallas_call(
        kernel,
        out_shape=[jax.ShapeDtypeStruct(s, F32) for s in outs],
        in_specs=[VMEM] * len(args),
        out_specs=[VMEM] * len(outs),
        scratch_shapes=[pltpu.VMEM(s, F32) for s in scratch],
        compiler_params=pltpu.CompilerParams(vmem_limit_bytes=LIMIT),
        name=name,
    )(*args)


def tile_shape(level):
    return (GEOM[level][0], Z, LANES)


def x_shape(level, count, flags):
    return (packed(GEOM[level], count) * Z + (8 if flags else 0), LANES)


Y_FULL = (Z + 8, LANES)


PARTS = 5


def open_kernel(f_in, c_in, vert_in, flip_in, f, c, up, down, own, vz, f_raw, c_raw, vert, flip, sems, small):
    rows = NZ * 24 // PARTS
    copies = []
    for k in range(PARTS):
        for i, (src, dst) in enumerate(((f_in, f_raw), (c_in, c_raw))):
            part = pl.ds(k * rows, rows)
            copies.append(pltpu.make_async_copy(src.at[part, :], dst.at[part, :], sems.at[i, k]))
    few = [pltpu.make_async_copy(vert_in, vert, small.at[0]), pltpu.make_async_copy(flip_in, flip, small.at[1])]
    for copy in few + copies:
        copy.start()
    for copy in few:
        copy.wait()
    a, b = iota2(8, 4)
    flags = jnp.broadcast_to(flip[...].astype(F32), (8, 4))
    flags = jnp.broadcast_to(jnp.sum(jnp.where(a == b, flags, 0.0), axis=1, keepdims=True), (8, LANES))
    own[...] = flags
    a, b = iota2(Z, NZ + 1)
    coef = jnp.broadcast_to(vert[...], (Z, NZ + 1))
    high = jnp.sum(jnp.where((b == a + 1) & (a < NZ), coef, 0.0), axis=1, keepdims=True)
    low = jnp.sum(jnp.where((b == a) & (a < NZ), coef, 0.0), axis=1, keepdims=True)
    columns = [jnp.broadcast_to(x * 0.0625, (Z, LANES)) for x in (4.0 + high + low, high, low)]
    lane = zl()
    vz[...] = jnp.where(lane == 0, columns[0], jnp.where(lane == 1, columns[1], columns[2]))
    for copy in copies:
        copy.wait()
    load_top(f_raw, f)
    load_top(c_raw, c)
    put_x(GEOM[0], f, c, up, down, flags)


def block_matrix(inv):
    width = 3 * Z
    a, b = iota2(BLK, width)
    b = b % Z
    spread = jnp.where((b % BLK == a) & (b < NZ), 1.0, 0.0).astype(BF16)
    whole = jnp.zeros((NZ, width), F32)
    left = inv
    for _ in range(3):
        part = left.astype(BF16)
        whole = whole + jnp.dot(part, spread, preferred_element_type=F32)
        left = left - part.astype(F32)
    a, b = iota2(NZ, width)
    whole = jnp.where(a // BLK == (b % Z) // BLK, whole, 0.0)
    high = whole.astype(BF16).astype(F32)
    return jnp.where((b >= Z) & (b < 2 * Z), whole - high, high)


def side_kernel(f, c, inv, own, w0, w1, w2, w3, one, c_next, c_tile, yup, ydown):
    put_y(GEOM[0], f, c, yup, ydown)
    yup[Z : Z + 8, :] = own[...]
    ydown[Z : Z + 8, :] = own[...]
    for level, w in enumerate((w0, w1, w2, w3)):
        w[0:NZ, :] = block_matrix(inv[level])
        w[NZ:Z, :] = jnp.zeros((Z - NZ, 3 * Z), F32)
    start_tile(GEOM[0], w0[...].astype(BF16), f, Setter(one))
    restrict(GEOM[0], GEOM[1], c, c_next)
    restrict(GEOM[1], GEOM[2], c_next, c_tile)


def merge_kernel(level, count):
    geom = GEOM[level]

    def kernel(xlo, xhi, flags, yup, ydown, up, down):
        lo, hi = part_of(geom, xlo, count - 1), part_of(geom, xhi, count - 1)
        up[...] = yup[...]
        down[...] = ydown[...]
        a, b = merge_y(lo, hi, flags, yup[0:Z, :], ydown[0:Z, :])
        up[0:Z, :] = a
        down[0:Z, :] = b

    return kernel


def pre_tile(level, f, c, w, vz, own, xlo, xhi, ydn, yun, one, v_out, res):
    geom = GEOM[level]
    winv = w[...].astype(BF16)
    co = Coef(vz)
    fl = flags_of(geom, own, xlo, xhi, ydn, yun)
    halo, _ = messages(geom, xlo, xhi, ydn, yun, winv)
    lo2, hi2, sides2 = relax_edges(geom, winv, co, one, halo, fl, *own_data(geom, xlo, xhi, ydn, yun))
    relax_tile(geom, winv, co, one, f, c, frame(geom, fl, halo.lo, halo.hi, halo.sides()), Setter(v_out))
    lo, hi, sides = frame(geom, fl, lo2, hi2, sides2)
    for m in range(geom[0]):
        res[m] = tile_residual(geom, co, v_out, f, c, lo, hi, sides, m)


def pre0_kernel(f, c, w, vz, own, xlo, xhi, ydn, yun, one, c_next, v_out, f_next, up, down, yup, ydown, res):
    pre_tile(0, f, c, w, vz, own, xlo, xhi, ydn, yun, one, v_out, res)
    coarse = GEOM[1]
    restrict(GEOM[0], coarse, res, f_next)
    put_x(coarse, f_next, c_next, up, down, own[...])
    put_y(coarse, f_next, c_next, yup, ydown)
    yup[Z : Z + 8, :] = own[...]
    ydown[Z : Z + 8, :] = own[...]


def pre1_kernel(f, c, w, vz, own, xlo, xhi, ydn, yun, c_tile, v_out, up, down, chunks, one, res, f_next):
    start_tile(GEOM[1], w[...].astype(BF16), f, Setter(one))
    pre_tile(1, f, c, w, vz, own, xlo, xhi, ydn, yun, one, v_out, res)
    restrict(GEOM[1], GEOM[2], res, f_next)
    put_x(GEOM[1], v_out, None, up, down)
    whole = pack(GEOM[2], [f_next[m] for m in range(6)] + [c_tile[m] for m in range(6)])
    for t in range(8):
        for k, part in enumerate(whole):
            chunks[t, k * Z : (k + 1) * Z, :] = part
        chunks[t, 3 * Z : 3 * Z + 8, :] = own[...]


def post_kernel(level):
    geom = GEOM[level]

    def sweeps(f, c, w, vz, own, xlo, xhi, ydn, yun, g, glo, ghi, gdn, gun, one, store):
        winv = w[...].astype(BF16)
        co = Coef(vz)
        fl = flags_of(geom, own, xlo, xhi, ydn, yun)
        halo = Halo(
            part_of(geom, glo, 0), part_of(geom, glo, 1), part_of(geom, ghi, 0), part_of(geom, ghi, 1), gdn[...], gun[...]
        )
        lo2, hi2, sides2 = relax_edges(geom, winv, co, g, halo, fl, *own_data(geom, xlo, xhi, ydn, yun))
        relax_tile(geom, winv, co, g, f, c, frame(geom, fl, halo.lo, halo.hi, halo.sides()), Setter(one))
        relax_tile(geom, winv, co, one, f, c, frame(geom, fl, lo2, hi2, sides2), store)

    if level == 0:

        def kernel(f, c, w, vz, own, xlo, xhi, ydn, yun, g, glo, ghi, gdn, gun, out, one):
            def store(x, value):
                out[pl.ds(x, NZ, stride=24), :] = value[0:NZ, :]

            sweeps(f, c, w, vz, own, xlo, xhi, ydn, yun, g, glo, ghi, gdn, gun, one, store)

        return kernel

    fine = GEOM[level - 1]

    def kernel(f, c, w, vz, own, xlo, xhi, ydn, yun, g, glo, ghi, gdn, gun, fine_v, g_out, up, down, yup, ydown, one, e):
        sweeps(f, c, w, vz, own, xlo, xhi, ydn, yun, g, glo, ghi, gdn, gun, one, Setter(e))
        prolong_add(fine, geom, e, fine_v, g_out)
        put_x(fine, g_out, None, up, down)
        put_y(fine, g_out, None, yup, ydown)

    return kernel


def both_ways(up, down, axis):
    n = lax.axis_size(axis)
    fwd = [(i, (i + 1) % n) for i in range(n)]
    back = [((i + 1) % n, i) for i in range(n)]
    return lax.ppermute(up, axis, fwd), lax.ppermute(down, axis, back)


def on_device(right_side, helm_coef, vert_coef, block_inverse, edge_flip):
    inv = block_inverse.reshape(4, NZ, BLK)
    f_in = right_side.reshape(NZ * 24, LANES)
    c_in = helm_coef.reshape(NZ * 24, LANES)
    vert = vert_coef.reshape(1, NZ + 1)
    flip = edge_flip.reshape(1, 4)

    ys = (Z, LANES)
    t0, t1, t2 = tile_shape(0), tile_shape(1), tile_shape(2)
    xs = x_shape(0, 4, True)
    f, c, up, down, own, vz = pl.pallas_call(
        open_kernel,
        out_shape=[jax.ShapeDtypeStruct(x, F32) for x in (t0, t0, xs, xs, (8, LANES), ys)],
        in_specs=[pl.BlockSpec(memory_space=pl.ANY)] * 4,
        out_specs=[VMEM] * 6,
        scratch_shapes=[pltpu.VMEM((NZ * 24, LANES), F32)] * 2
        + [pltpu.VMEM((1, NZ + 1), F32), pltpu.VMEM((1, 4), jnp.int32)]
        + [pltpu.SemaphoreType.DMA((2, PARTS)), pltpu.SemaphoreType.DMA((2,))],
        compiler_params=pltpu.CompilerParams(vmem_limit_bytes=58 * 1024 * 1024),
        name="open",
    )(f_in, c_in, vert, flip)
    xlo, xhi = both_ways(up, down, "gx")
    ws = (Z, 3 * Z)
    *w, one, c1, c_tile, yup, ydown = call(
        side_kernel, [ws] * 4 + [t0, t1, t2, Y_FULL, Y_FULL], [f, c, inv, own], name="side"
    )

    def to_sides(level, count, xlo, xhi, yup, ydown):
        shape = yup.shape
        yup, ydown = call(merge_kernel(level, count), [shape, shape], [xlo, xhi, own, yup, ydown], name=f"merge{level}")
        return both_ways(yup, ydown, "gy")

    got0 = (xlo, xhi, *to_sides(0, 4, xlo, xhi, yup, ydown))
    xs = x_shape(1, 4, True)
    v0, f1, up, down, yup, ydown = call(
        pre0_kernel, [t0, t1, xs, xs, Y_FULL, Y_FULL], [f, c, w[0], vz, own, *got0, one, c1], [t0], name="pre0"
    )
    xlo, xhi = both_ways(up, down, "gx")
    got1 = (xlo, xhi, *to_sides(1, 4, xlo, xhi, yup, ydown))
    xs = x_shape(1, 3, False)
    v1, up, down, chunks = call(
        pre1_kernel, [t1, xs, xs, (8, 3 * Z + 8, LANES)], [f1, c1, w[1], vz, own, *got1, c_tile], [t1, t1, t2], name="pre1"
    )
    v1_lo, v1_hi = both_ways(up, down, "gx")
    chunks = lax.all_to_all(chunks, "gx", 0, 0)
    s2, s3 = (6, Z, 256), (3, Z, 128)
    m2, m3 = (Z, 256), (Z, 128)
    full2, full3 = (Z + 8, 256), (Z + 8, 128)
    f2, c2, fl2, up, down = call(open_strip_kernel, [s2, s2, (8, 256), full2, full2], [chunks], name="open2")
    side2 = strip_ring(up, down)
    v2, f3, c3, fl3, up, down = call(
        pre_strip_kernel, [s2, s3, s3, (8, 128), full3, full3], [f2, c2, w[2], vz, fl2, *side2], [s2, s2], name="pre2"
    )
    side3 = strip_ring(up, down)
    v3, up, down = call(bottom_strip_kernel, [s3, m3, m3], [f3, c3, w[3], vz, fl3, *side3], [s3], name="bottom")
    side = strip_ring(up, down)
    g2, up, down = call(
        last_strip_kernel, [s2, m2, m2], [f3, c3, w[3], vz, fl3, *side, v3, v2, fl2], [s3], name="last"
    )
    side = strip_ring(up, down)
    g1, lo, hi, up, down = call(
        post_strip_kernel,
        [t1, xs, xs, ys, ys],
        [f2, c2, w[2], vz, fl2, *side2, g2, *side, v1, v1_lo, v1_hi, own],
        [s2, s2, t2, ys, ys],
        name="post2",
    )
    side = both_ways(up, down, "gy")
    xs = x_shape(0, 3, False)
    g0, up, down, yup, ydown = call(
        post_kernel(1),
        [t0, xs, xs, ys, ys],
        [f1, c1, w[1], vz, own, *got1, g1, lo, hi, *side, v0],
        [t1, t1],
        name="post1",
    )
    xlo, xhi = both_ways(up, down, "gx")
    got = (xlo, xhi, *to_sides(0, 3, xlo, xhi, yup, ydown))
    (out,) = call(
        post_kernel(0), [(NZ * 24, LANES)], [f, c, w[0], vz, own, *got0, g0, *got], [t0], name="post0"
    )
    return out.reshape(NZ, 24, LANES)


def solution(mesh):
    placed = (P(None, "gx", "gy"), P(None, "gx", "gy"), P(), P(), P("gx", "gy", None))
    return jax.shard_map(
        on_device, mesh=mesh, in_specs=placed, out_specs=P(None, "gx", "gy"), check_vma=False
    )
```

```python
import jax
import jax.numpy as jnp
from jax import lax
from jax.experimental import pallas as pl
from jax.experimental.pallas import tpu as pltpu
from jax.sharding import PartitionSpec as P

BLK = 14
NBLK = 5
NZ = 70
Z = 72
LANES = 128
F32 = jnp.float32
BF16 = jnp.bfloat16

GEOM = ((24, 1, 128), (6, 2, 64), (6, 1, 32), (3, 1, 16))


def lane_ids(shape):
    return lax.broadcasted_iota(jnp.int32, shape, len(shape) - 1)


def zl():
    return lane_ids((Z, LANES))


def roll(x, shift):
    shift = shift % x.shape[-1]
    return x if shift == 0 else pltpu.roll(x, shift, axis=1)


def col(x, k):
    return jnp.broadcast_to(x[:, k : k + 1], (Z, LANES))


def iota2(n, m):
    return lax.broadcasted_iota(jnp.int32, (n, m), 0), lax.broadcasted_iota(jnp.int32, (n, m), 1)


def lane_dot(x, mat):
    hi = x.astype(BF16).astype(F32)
    both = jnp.concatenate([hi, x - hi], axis=1).astype(BF16)
    twice = jnp.concatenate([mat, mat], axis=0).astype(BF16)
    return jnp.dot(both, twice, preferred_element_type=F32)


def block_dot(winv, x):
    hi = x.astype(BF16).astype(F32)
    parts = jnp.concatenate([hi, hi, x - hi], axis=0).astype(BF16)
    return jnp.dot(winv, parts, preferred_element_type=F32)


def reverse_matrix(width):
    a, b = iota2(LANES, LANES)
    return jnp.where((b < width) & (a == width - 1 - b), 1.0, 0.0)


def flag_row(flags, k):
    return jnp.broadcast_to(flags[k : k + 1, :], (Z, LANES))


class Coef:
    def __init__(self, ref, width=LANES):
        self.mid = jnp.broadcast_to(ref[:, 0:1], (Z, width))
        self.up = jnp.broadcast_to(ref[:, 1:2], (Z, width))
        self.down = jnp.broadcast_to(ref[:, 2:3], (Z, width))


def residual(co, f, c, v, beside):
    above = pltpu.roll(v, Z - 1, axis=0)
    below = pltpu.roll(v, 1, axis=0)
    return f - (c * 0.0625 + co.mid) * v + beside * 0.0625 + co.up * above + co.down * below


def row_of(geom, v, row):
    m_rows, _, ty = geom
    q, m = divmod(row, m_rows)
    return roll(v[m], -q * ty)


def corners(geom, v):
    m_rows, groups, ty = geom
    last = v[m_rows - 1]
    base = (groups - 1) * ty
    return corner_rows([col(v[0], 0), col(v[0], ty - 1), col(last, base), col(last, base + ty - 1)])


def corner_rows(columns):
    lane = zl()
    out = jnp.zeros((Z, LANES), F32)
    for k, column in enumerate(columns):
        out = jnp.where(lane == 4 + k, column, out)
    return jnp.concatenate([out, jnp.zeros((LANES - Z, LANES), F32)], axis=0).T[0:8, :]


def corner_columns(rows):
    out = jnp.concatenate([rows, jnp.zeros((LANES - 8, LANES), F32)], axis=0).T[0:Z, :]
    return [col(out, 4 + k) for k in range(4)]


def whole_rows(geom):
    return geom[1] == 1 and geom[2] == LANES


def tile_rows(geom):
    m_rows, groups, ty = geom
    return [(q * m_rows + m, m, q * ty) for m in range(m_rows) for q in range(groups)]


def own_columns(geom, v):
    ty = geom[2]
    lane = zl()
    out = jnp.zeros((Z, LANES), F32)
    for r, m, base in tile_rows(geom):
        row = v[m]
        first = roll(row, 2 * r + 1 - base)
        out = jnp.where(lane == 2 * r + 1, first, out)
        last = first if whole_rows(geom) else roll(row, 2 * r - (base + ty - 1))
        out = jnp.where(lane == 2 * r, last, out)
    return out


def pack(geom, parts):
    ty = geom[2]
    per = LANES // ty
    out = []
    for first in range(0, len(parts), per):
        lane = zl()
        acc = parts[first]
        for k, part in enumerate(parts[first + 1 : first + per], 1):
            acc = jnp.where(lane < k * ty, acc, roll(part, k * ty))
        out.append(acc)
    return out


def packed(geom, count):
    per = LANES // geom[2]
    return -(-count // per)


def part_of(geom, ref, k):
    ty = geom[2]
    per = LANES // ty
    return roll(ref[(k // per) * Z : (k // per + 1) * Z, :], -(k % per) * ty)


def put_x(geom, v, c, up, down, flags=None):
    m_rows, groups, _ = geom
    tx = m_rows * groups
    tail = corners(geom, v)
    if flags is not None:
        tail = tail + flags
    for ref, edge, second in ((up, tx - 1, tx - 2), (down, 0, 1)):
        parts = [row_of(geom, v, edge), row_of(geom, v, second)]
        if c is not None:
            parts.append(row_of(geom, c, edge))
        put_parts(geom, parts, tail, ref)


def put_parts(geom, parts, tail, ref):
    whole = pack(geom, parts)
    for k, part in enumerate(whole):
        ref[k * Z : (k + 1) * Z, :] = part
    ref[len(whole) * Z : len(whole) * Z + 8, :] = tail


def tail_of(geom, ref, count):
    n = packed(geom, count) * Z
    return ref[n : n + 8, :]


def put_y(geom, v, c, up, down):
    ty = geom[2]
    lane = zl()
    out_up = jnp.zeros((Z, LANES), F32)
    out_down = out_up
    for r, m, base in tile_rows(geom):
        row = v[m]
        mine = lane // 2 == r
        last = roll(row, 2 * r + 1 - (base + ty - 1))
        first = roll(row, 2 * r - base)
        out_up = jnp.where(mine, last, out_up)
        out_down = jnp.where(mine, first, out_down)
        if c is not None:
            row = c[m]
            out_up = jnp.where(lane == 65 + 2 * r, roll(row, 65 + 2 * r - (base + ty - 1)), out_up)
            out_down = jnp.where(lane == 64 + 2 * r, roll(row, 64 + 2 * r - base), out_down)
    up[0:Z, :] = out_up
    down[0:Z, :] = out_down


def merge_y(lo, hi, flags, up, down):
    lane = zl()
    f0, f1 = flag_row(flags, 0) > 0.5, flag_row(flags, 1) > 0.5

    def fill(part, values):
        for k, value in enumerate(values):
            part = jnp.where(lane == 112 + k, value, part)
        return part

    up_new = fill(up, [lo[3], lo[1], hi[1], hi[3], jnp.where(f0, lo[2], lo[3]), jnp.where(f1, hi[0], hi[1])])
    down_new = fill(down, [lo[2], lo[0], hi[0], hi[2], jnp.where(f0, lo[3], lo[2]), jnp.where(f1, hi[1], hi[0])])
    return up_new, down_new


def odd_lanes():
    return zl() % 2 == 1


class Halo:
    def __init__(self, lo, lo2, hi, hi2, dn, un):
        self.lo, self.lo2, self.hi, self.hi2, self.dn, self.un = lo, lo2, hi, hi2, dn, un

    def sides(self):
        return jnp.where(odd_lanes(), self.dn, self.un)

    def seconds(self):
        return jnp.where(odd_lanes(), roll(self.dn, 1), roll(self.un, -1))


class Flags:
    def __init__(self, own, lo, hi, dn, un):
        self.own, self.lo, self.hi, self.dn, self.un = own, lo, hi, dn, un


def turn_row(geom, row, flag):
    return jnp.where(flag > 0.5, lane_dot(row, reverse_matrix(geom[2])), row)


def turn_sides(geom, sides, flag_dn, flag_un):
    tx = geom[0] * geom[1]
    flag = jnp.where(odd_lanes(), flag_dn, flag_un)
    a, b = iota2(LANES, LANES)
    mat = jnp.where((b < 2 * tx) & (a == 2 * (tx - 1 - b // 2) + b % 2), 1.0, 0.0)
    return jnp.where(flag > 0.5, lane_dot(sides, mat), sides)


def frame(geom, fl, lo, hi, sides):
    return (
        turn_row(geom, lo, flag_row(fl.own, 0)),
        turn_row(geom, hi, flag_row(fl.own, 1)),
        turn_sides(geom, sides, flag_row(fl.own, 2), flag_row(fl.own, 3)),
    )


def relax_edges(geom, winv, co, v, halo, fl, f_lo, c_lo, f_hi, c_hi, f_sides, c_sides):
    m_rows, groups, ty = geom
    tx = m_rows * groups
    lane = zl()
    dn, un = halo.dn, halo.un

    def beside_row(edge, second, mine, low, high):
        left = jnp.where(lane == 0, low, roll(edge, 1))
        right = jnp.where(lane == ty - 1, high, roll(edge, -1))
        return second + mine + left + right

    def choose(flags, k, first, other):
        return jnp.where(flag_row(flags, k) > 0.5, other, first)

    b_lo = beside_row(
        halo.lo,
        halo.lo2,
        turn_row(geom, row_of(geom, v, 0), flag_row(fl.lo, 1)),
        choose(fl.lo, 2, col(dn, 112), col(dn, 113)),
        choose(fl.lo, 3, col(un, 112), col(un, 113)),
    )
    b_hi = beside_row(
        halo.hi,
        halo.hi2,
        turn_row(geom, row_of(geom, v, tx - 1), flag_row(fl.hi, 0)),
        choose(fl.hi, 2, col(dn, 114), col(dn, 115)),
        choose(fl.hi, 3, col(un, 114), col(un, 115)),
    )
    edge = halo.sides()
    mine = turn_sides(geom, own_columns(geom, v), flag_row(fl.dn, 3), flag_row(fl.un, 2))
    below = jnp.where(lane == 1, col(dn, 116), jnp.where(lane == 0, col(un, 116), roll(edge, 2)))
    last = 2 * (tx - 1)
    above = jnp.where(lane == last + 1, col(dn, 117), jnp.where(lane == last, col(un, 117), roll(edge, -2)))
    b_sides = halo.seconds() + mine + below + above
    r_lo = residual(co, f_lo, c_lo, halo.lo, b_lo)
    r_hi = residual(co, f_hi, c_hi, halo.hi, b_hi)
    r_sides = residual(co, f_sides, c_sides, edge, b_sides)
    d = block_dot(winv, jnp.concatenate([r_lo, r_hi, r_sides], axis=1))
    return halo.lo + d[:, :LANES], halo.hi + d[:, LANES : 2 * LANES], edge + d[:, 2 * LANES :]


def tile_residual(geom, co, v, f, c, lo, hi, sides, m):
    m_rows, groups, ty = geom
    lane = zl()
    here = v[m]
    if lo is None:
        lo = hi = jnp.zeros((Z, LANES), F32)
    if m > 0:
        low_x = v[m - 1]
    else:
        low_x = lo if groups == 1 else jnp.where(lane < ty, lo, roll(v[m_rows - 1], ty))
    if m < m_rows - 1:
        high_x = v[m + 1]
    elif groups == 1:
        high_x = hi
    else:
        high_x = jnp.where(lane < (groups - 1) * ty, roll(v[0], -ty), roll(hi, (groups - 1) * ty))
    low_y, high_y = roll(here, 1), roll(here, -1)
    if sides is None:
        low_y = jnp.where(lane % ty == 0, 0.0, low_y)
        high_y = jnp.where(lane % ty == ty - 1, 0.0, high_y)
        return residual(co, f[m], c[m], here, low_x + high_x + low_y + high_y)
    for q in range(groups):
        row = q * m_rows + m
        low = roll(sides, q * ty - 2 * row - 1)
        high = low if whole_rows(geom) else roll(sides, q * ty + ty - 1 - 2 * row)
        low_y = jnp.where(lane == q * ty, low, low_y)
        high_y = jnp.where(lane == q * ty + ty - 1, high, high_y)
    return residual(co, f[m], c[m], here, low_x + high_x + low_y + high_y)


def relax_tile(geom, winv, co, v, f, c, edges, store):
    lo, hi, sides = edges
    for m in range(0, geom[0], 2):
        rows = [k for k in (m, m + 1) if k < geom[0]]
        r = [tile_residual(geom, co, v, f, c, lo, hi, sides, k) for k in rows]
        d = block_dot(winv, r[0] if len(r) == 1 else jnp.concatenate(r, axis=1))
        for i, k in enumerate(rows):
            store(k, v[k] + d[:, i * LANES : (i + 1) * LANES])


ALONE = (None, None, None)


def add_edges(geom, winv, part, edges, store):
    m_rows, groups, ty = geom
    lane = zl()
    d = block_dot(winv, jnp.concatenate(edges, axis=1) * 0.0625)
    low, high, sides = [d[:, k * LANES : (k + 1) * LANES] for k in range(3)]
    if ty < LANES:
        low = jnp.where(lane < ty, low, 0.0)
        high = jnp.where(lane < ty, high, 0.0)
    for m in range(m_rows):
        x = part[m]
        if m == 0:
            x = x + low
        if m == m_rows - 1:
            x = x + roll(high, (groups - 1) * ty)
        for q in range(groups):
            row = q * m_rows + m
            first = roll(sides, q * ty - 2 * row - 1)
            last = first if whole_rows(geom) else roll(sides, q * ty + ty - 1 - 2 * row)
            x = x + jnp.where(lane == q * ty, first, jnp.where(lane == q * ty + ty - 1, last, 0.0))
        store(m, x)


def start_tile(geom, winv, f, store):
    for m in range(0, geom[0], 2):
        rows = [k for k in (m, m + 1) if k < geom[0]]
        parts = [f[k] for k in rows]
        d = block_dot(winv, parts[0] if len(parts) == 1 else jnp.concatenate(parts, axis=1))
        for i, k in enumerate(rows):
            store(k, d[:, i * LANES : (i + 1) * LANES])


def restrict(fine, coarse, v, out):
    m_rows, _, ty = fine
    cm, cq, cty = coarse
    a, b = iota2(LANES, LANES)
    for mc in range(cm):
        acc = None
        for qc in range(cq):
            q, m = divmod(2 * (qc * cm + mc), m_rows)
            inside = (b >= qc * cty) & (b < (qc + 1) * cty) & (a // 2 == b - qc * cty + q * (ty // 2))
            term = lane_dot(v[m] + v[m + 1], jnp.where(inside, 0.25, 0.0))
            acc = term if acc is None else acc + term
        out[mc] = acc


def prolong_add(fine, coarse, e, v, out):
    m_rows, groups, ty = fine
    cm, _, cty = coarse
    a, b = iota2(LANES, LANES)
    for m in range(0, m_rows, 2):
        acc = None
        for q in range(groups):
            qc, mc = divmod((q * m_rows + m) // 2, cm)
            inside = (b >= q * ty) & (b < (q + 1) * ty) & (a - qc * cty == (b - q * ty) // 2)
            term = lane_dot(e[mc], jnp.where(inside, 1.0, 0.0))
            acc = term if acc is None else acc + term
        out[m] = v[m] + acc
        out[m + 1] = v[m + 1] + acc


class Setter:
    def __init__(self, ref):
        self.ref = ref

    def __call__(self, m, value):
        self.ref[m] = value


def messages(geom, xlo, xhi, ydn, yun, winv):
    raw = [part_of(geom, xlo, 0), part_of(geom, xlo, 1), part_of(geom, xhi, 0), part_of(geom, xhi, 1), ydn[0:Z, :], yun[0:Z, :]]
    d = block_dot(winv, jnp.concatenate(raw, axis=1))
    return Halo(*[d[:, k * LANES : (k + 1) * LANES] for k in range(6)])


def own_data(geom, xlo, xhi, ydn, yun):
    dn, un = ydn[0:Z, :], yun[0:Z, :]
    f_sides = jnp.where(odd_lanes(), dn, un)
    c_sides = roll(f_sides, -64)
    return (
        part_of(geom, xlo, 0),
        part_of(geom, xlo, 2),
        part_of(geom, xhi, 0),
        part_of(geom, xhi, 2),
        f_sides,
        c_sides,
    )


def flags_of(geom, own, xlo, xhi, ydn, yun):
    return Flags(own[...], tail_of(geom, xlo, 3), tail_of(geom, xhi, 3), ydn[Z : Z + 8, :], yun[Z : Z + 8, :])


def load_top(src, dst):
    for x in range(24):
        dst[x, 0:NZ, :] = src[pl.ds(x, NZ, stride=24), :]
        dst[x, NZ:Z, :] = jnp.zeros((Z - NZ, LANES), F32)


STRIPS = {2: (6, 32, 256), 3: (3, 16, 128)}


def in_tile(strip):
    _, ty, width = strip
    return lane_ids((Z, width)) % ty


def group_dot(x, mat):
    parts = [lane_dot(x[:, k : k + LANES], mat) for k in range(0, x.shape[1], LANES)]
    return parts[0] if len(parts) == 1 else jnp.concatenate(parts, axis=1)


def turn_groups(strip, x, flags, k, count):
    _, ty, width = strip
    a, b = iota2(LANES, LANES)
    mat = jnp.where((a // ty == b // ty) & (b % ty < count) & (a % ty == count - 1 - b % ty), 1.0, 0.0)
    flag = jnp.broadcast_to(flags[k : k + 1, :], (Z, width))
    return jnp.where(flag > 0.5, group_dot(x, mat), x)


def strip_ends(strip, v, flags):
    m_rows, ty, _ = strip
    low = turn_groups(strip, roll(v[m_rows - 1], ty), flags, 0, ty)
    high = turn_groups(strip, roll(v[0], -ty), flags, 1, ty)
    return low, high


def strip_column(strip, v, y, offset, out):
    lt = in_tile(strip)
    for m in range(strip[0]):
        out = jnp.where(lt == offset + m, roll(v[m], offset + m - y), out)
    return out


def strip_message(strip, v, c, ends, up, down):
    m_rows, ty, width = strip
    lt = in_tile(strip)
    for ref, edge, second in ((up, ty - 1, ty - 2), (down, 0, 1)):
        out = strip_column(strip, v, edge, 0, jnp.zeros((Z, width), F32))
        out = strip_column(strip, v, second, m_rows, out)
        if c is not None:
            out = strip_column(strip, c, edge, 2 * m_rows, out)
        for k, end in enumerate(ends):
            out = jnp.where(lt == 3 * m_rows + k, roll(end, 3 * m_rows + k - edge), out)
        ref[0:Z, :] = out


def strip_edges(strip, winv, co, v, sides):
    m_rows, _, width = strip
    lt = in_tile(strip)
    r = []
    for x, raw, flags, k, y in sides:
        mine = strip_column(strip, v, y, 0, jnp.zeros((Z, width), F32))
        mine = turn_groups(strip, mine, flags, k, m_rows)
        low = jnp.where(lt == 0, roll(x, -3 * m_rows), roll(x, 1))
        high = jnp.where(lt == m_rows - 1, roll(x, -2 * m_rows - 2), roll(x, -1))
        r.append(residual(co, raw, roll(raw, -2 * m_rows), x, roll(x, -m_rows) + mine + low + high))
    d = block_dot(winv, jnp.concatenate(r, axis=1))
    return [side[0] + d[:, k * width : (k + 1) * width] for k, side in enumerate(sides)]


def strip_frame(strip, flags, low, high):
    return turn_groups(strip, low, flags, 2, strip[0]), turn_groups(strip, high, flags, 3, strip[0])


def strip_residual(strip, co, v, f, c, ends, sides, m):
    m_rows, ty, _ = strip
    lt = in_tile(strip)
    low_x = v[m - 1] if m > 0 else ends[0]
    high_x = v[m + 1] if m < m_rows - 1 else ends[1]
    low = 0.0 if sides is None else roll(sides[0], -m)
    high = 0.0 if sides is None else roll(sides[1], ty - 1 - m)
    low_y = jnp.where(lt == 0, low, roll(v[m], 1))
    high_y = jnp.where(lt == ty - 1, high, roll(v[m], -1))
    return residual(co, f[m], c[m], v[m], low_x + high_x + low_y + high_y)


def strip_relax(strip, winv, co, v, f, c, flags, sides, store):
    ends = strip_ends(strip, v, flags)
    for m in range(strip[0]):
        r = strip_residual(strip, co, v, f, c, ends, sides, m)
        store(m, v[m] + block_dot(winv, r))


def strip_add_sides(strip, winv, part, sides, store):
    m_rows, ty, width = strip
    lt = in_tile(strip)
    d = block_dot(winv, jnp.concatenate(sides, axis=1) * 0.0625)
    for m in range(m_rows):
        low, high = roll(d[:, :width], -m), roll(d[:, width:], ty - 1 - m)
        store(m, part[m] + jnp.where(lt == 0, low, jnp.where(lt == ty - 1, high, 0.0)))


def strip_restrict(v, out):
    a, b = iota2(LANES, LANES)
    for m in range(3):
        both = v[2 * m] + v[2 * m + 1]
        out[m] = lane_dot(both[:, :LANES], jnp.where(a // 2 == b, 0.25, 0.0)) + lane_dot(
            both[:, LANES:], jnp.where(a // 2 == b - 64, 0.25, 0.0)
        )


def open_strip_kernel(chunks, f, c, flags, up, down):
    strip = STRIPS[2]
    group = lane_ids((Z, LANES)) // 32
    for m in range(6):
        for ref, k in ((f, m), (c, 6 + m)):
            part = (k // 4) * Z
            halves = []
            for h in range(2):
                acc = None
                for g in range(4):
                    x = roll(chunks[4 * h + g, part : part + Z, :], (g - k % 4) * 32)
                    acc = x if acc is None else jnp.where(group == g, x, acc)
                halves.append(acc)
            ref[m] = jnp.concatenate(halves, axis=1)
    group = lane_ids((8, LANES)) // 32
    for h in range(2):
        acc = None
        for g in range(4):
            x = chunks[4 * h + g, 3 * Z : 3 * Z + 8, :]
            acc = x if acc is None else jnp.where(group == g, x, acc)
        flags[:, h * LANES : (h + 1) * LANES] = acc
    strip_message(strip, f, c, strip_ends(strip, f, flags), up, down)
    up[Z : Z + 8, :] = flags[...]
    down[Z : Z + 8, :] = flags[...]


def strip_sides(values, raws, dn, un, ty):
    return (
        (values[0], raws[0], dn[Z : Z + 8, :], 3, 0),
        (values[1], raws[1], un[Z : Z + 8, :], 2, ty - 1),
    )


def pre_strip_kernel(f, c, w, vz, flags, dn, un, one, part, v_out, f_next, c_next, fl_next, up, down, res):
    strip = STRIPS[2]
    width = strip[2]
    winv = w[...].astype(BF16)
    co = Coef(vz, width)
    raws = [dn[0:Z, :], un[0:Z, :]]
    values = [block_dot(winv, x) for x in raws]
    edges = strip_edges(strip, winv, co, one, strip_sides(values, raws, dn, un, strip[1]))
    strip_add_sides(strip, winv, part, strip_frame(strip, flags, *values), Setter(v_out))
    ends = strip_ends(strip, v_out, flags)
    sides = strip_frame(strip, flags, *edges)
    for m in range(6):
        res[m] = strip_residual(strip, co, v_out, f, c, ends, sides, m)
    strip_restrict(res, f_next)
    strip_restrict(c, c_next)
    a, b = iota2(LANES, LANES)
    fl_next[...] = lane_dot(flags[:, :LANES], jnp.where((b < 64) & (a == (b // 16) * 32), 1.0, 0.0)) + lane_dot(
        flags[:, LANES:], jnp.where((b >= 64) & (a == (b // 16 - 4) * 32), 1.0, 0.0)
    )
    small = STRIPS[3]
    strip_message(small, f_next, c_next, strip_ends(small, f_next, fl_next), up, down)
    up[Z : Z + 8, :] = fl_next[...]
    down[Z : Z + 8, :] = fl_next[...]


def bottom_strip_kernel(f, c, w, vz, flags, dn, un, first, part, v_out, up, down, one):
    strip = STRIPS[3]
    winv = w[...].astype(BF16)
    co = Coef(vz)
    raws = [dn[0:Z, :], un[0:Z, :]]
    values = [block_dot(winv, x) for x in raws]
    edges = strip_edges(strip, winv, co, first, strip_sides(values, raws, dn, un, strip[1]))
    strip_add_sides(strip, winv, part, strip_frame(strip, flags, *values), Setter(one))
    strip_relax(strip, winv, co, one, f, c, flags, strip_frame(strip, flags, *edges), Setter(v_out))
    strip_message(strip, v_out, None, (), up, down)


def last_strip_kernel(w, flags, dn, un, part, fine_v, fine_flags, _lo, _hi, g, up, down, e):
    strip, fine = STRIPS[3], STRIPS[2]
    winv = w[...].astype(BF16)
    strip_add_sides(strip, winv, part, strip_frame(strip, flags, dn[...], un[...]), Setter(e))
    a, b = iota2(LANES, LANES)
    for m in range(3):
        add = jnp.concatenate([lane_dot(e[m], jnp.where(a == 64 * h + b // 2, 1.0, 0.0)) for h in range(2)], axis=1)
        g[2 * m] = fine_v[2 * m] + add
        g[2 * m + 1] = fine_v[2 * m + 1] + add
    strip_message(fine, g, None, strip_ends(fine, g, fine_flags), up, down)


def alone_kernel(level, first):
    def kernel(f, c, w, vz, *refs):
        winv = w[...].astype(BF16)
        flags = None
        if level >= 2:
            flags, *refs = refs
        v, part = refs
        if level < 2:
            if first:
                start_tile(GEOM[level], winv, f, Setter(v))
            relax_tile(GEOM[level], winv, Coef(vz), v, f, c, ALONE, Setter(part))
        else:
            strip = STRIPS[level]
            if first:
                for m in range(strip[0]):
                    v[m] = block_dot(winv, f[m])
            strip_relax(strip, winv, Coef(vz, strip[2]), v, f, c, flags, None, Setter(part))

    return kernel


def post_strip_kernel(
    f, c, w, vz, flags, dn, un, g, part, gdn, gun, fine_v, xlo, xhi, own, g_out, lo_out, hi_out, up, down, one, e, tile, yup, ydown
):
    strip = STRIPS[2]
    fine, geom = GEOM[1], GEOM[2]
    winv = w[...].astype(BF16)
    co = Coef(vz, strip[2])
    raws = [dn[0:Z, :], un[0:Z, :]]
    values = [gdn[...], gun[...]]
    edges = strip_edges(strip, winv, co, g, strip_sides(values, raws, dn, un, strip[1]))
    strip_add_sides(strip, winv, part, strip_frame(strip, flags, *values), Setter(one))
    strip_relax(strip, winv, co, one, f, c, flags, strip_frame(strip, flags, *edges), Setter(e))

    place = lax.axis_index("gx")

    def tile_row(m, step):
        t = lax.rem(place + (step + 8), 8)
        return pltpu.roll(e[m], lax.rem(8 - t, 8) * 32, axis=1)[:, :LANES]

    for m in range(6):
        tile[m] = tile_row(m, 0)
    prolong_add(fine, geom, tile, fine_v, g_out)
    a, b = iota2(LANES, LANES)
    spread = jnp.where((b < 64) & (a == b // 2), 1.0, 0.0)
    extras = []
    for ref, out, step, near in ((xlo, lo_out, -1, 5), (xhi, hi_out, 1, 0)):
        first, last = tile_row(0, step), tile_row(5, step)
        add = lane_dot(last if near else first, spread)
        adds = (col(first, 0), col(first, 31), col(last, 0), col(last, 31))
        extras.append([x + y for x, y in zip(corner_columns(tail_of(fine, ref, 2)), adds)])
        out[...] = pack(fine, [part_of(fine, ref, 0) + add, part_of(fine, ref, 1) + add])[0]
    put_y(fine, g_out, None, yup, ydown)
    up[...], down[...] = merge_y(*extras, own, yup[...], ydown[...])


def strip_ring(up, down):
    nx, ny = lax.axis_size("gx"), lax.axis_size("gy")

    def pairs(step):
        out = []
        for i in range(nx):
            for j in range(ny):
                to = (j + step) % ny
                other = i ^ 1 if (2 * j // ny) != (2 * to // ny) else i
                out.append((i * ny + j, other * ny + to))
        return out

    both = ("gx", "gy")
    return lax.ppermute(up, both, pairs(1)), lax.ppermute(down, both, pairs(-1))


ANY = pl.BlockSpec(memory_space=pl.ANY)
LIMIT = 14 * 1024 * 1024
VMEM = pl.BlockSpec(memory_space=pltpu.VMEM)


def call(kernel, outs, args, scratch=(), name=None, after=0):
    return pl.pallas_call(
        kernel,
        out_shape=[jax.ShapeDtypeStruct(s, F32) for s in outs],
        in_specs=[VMEM] * (len(args) - after) + [ANY] * after,
        out_specs=[VMEM] * len(outs),
        scratch_shapes=[pltpu.VMEM(s, F32) for s in scratch],
        compiler_params=pltpu.CompilerParams(vmem_limit_bytes=LIMIT),
        name=name,
    )(*args)


def tile_shape(level):
    return (GEOM[level][0], Z, LANES)


def x_shape(level, count):
    return (packed(GEOM[level], count) * Z + 8, LANES)


Y_FULL = (Z + 8, LANES)


def open_kernel(f_in, c_in, vert_in, flip_in, up, down, own, vz, f_low, f_high, c_low, c_high, vert, flip, sems):
    pairs = (
        (vert_in, vert),
        (flip_in, flip),
        (f_in.at[:, 0:2, :], f_low),
        (f_in.at[:, 22:24, :], f_high),
        (c_in.at[:, 0:1, :], c_low),
        (c_in.at[:, 23:24, :], c_high),
    )
    copies = [pltpu.make_async_copy(src, dst, sems.at[k]) for k, (src, dst) in enumerate(pairs)]
    for copy in copies:
        copy.start()
    for copy in copies[:2]:
        copy.wait()
    a, b = iota2(8, 4)
    flags = jnp.broadcast_to(flip[...].astype(F32), (8, 4))
    flags = jnp.broadcast_to(jnp.sum(jnp.where(a == b, flags, 0.0), axis=1, keepdims=True), (8, LANES))
    own[...] = flags
    a, b = iota2(Z, NZ + 1)
    coef = jnp.broadcast_to(vert[...], (Z, NZ + 1))
    high = jnp.sum(jnp.where((b == a + 1) & (a < NZ), coef, 0.0), axis=1, keepdims=True)
    low = jnp.sum(jnp.where((b == a) & (a < NZ), coef, 0.0), axis=1, keepdims=True)
    columns = [jnp.broadcast_to(x * 0.0625, (Z, LANES)) for x in (4.0 + high + low, high, low)]
    lane = zl()
    vz[...] = jnp.where(lane == 0, columns[0], jnp.where(lane == 1, columns[1], columns[2]))
    up[...] = jnp.zeros(up.shape, F32)
    down[...] = jnp.zeros(down.shape, F32)
    for copy in copies[2:]:
        copy.wait()
    up[0:NZ, :] = f_high[:, 1, :]
    up[Z : Z + NZ, :] = f_high[:, 0, :]
    up[2 * Z : 2 * Z + NZ, :] = c_high[:, 0, :]
    down[0:NZ, :] = f_low[:, 0, :]
    down[Z : Z + NZ, :] = f_low[:, 1, :]
    down[2 * Z : 2 * Z + NZ, :] = c_low[:, 0, :]
    first, last = down[0:Z, :], up[0:Z, :]
    tail = flags + corner_rows([col(first, 0), col(first, LANES - 1), col(last, 0), col(last, LANES - 1)])
    up[3 * Z : 3 * Z + 8, :] = tail
    down[3 * Z : 3 * Z + 8, :] = tail


def block_matrix(inv):
    width = 3 * Z
    a, b = iota2(BLK, width)
    b = b % Z
    spread = jnp.where((b % BLK == a) & (b < NZ), 1.0, 0.0).astype(BF16)
    whole = jnp.zeros((NZ, width), F32)
    left = inv
    for _ in range(3):
        part = left.astype(BF16)
        whole = whole + jnp.dot(part, spread, preferred_element_type=F32)
        left = left - part.astype(F32)
    a, b = iota2(NZ, width)
    whole = jnp.where(a // BLK == (b % Z) // BLK, whole, 0.0)
    high = whole.astype(BF16).astype(F32)
    return jnp.where((b >= Z) & (b < 2 * Z), whole - high, high)


def side_kernel(f_in, c_in, inv, vz, own, f, c, w0, w1, w2, w3, one, part, c_next, c_tile, yup, ydown):
    load_top(f_in, f)
    load_top(c_in, c)
    put_y(GEOM[0], f, c, yup, ydown)
    yup[Z : Z + 8, :] = own[...]
    ydown[Z : Z + 8, :] = own[...]
    for level, w in enumerate((w0, w1, w2, w3)):
        w[0:NZ, :] = block_matrix(inv[level])
        w[NZ:Z, :] = jnp.zeros((Z - NZ, 3 * Z), F32)
    winv = w0[...].astype(BF16)
    start_tile(GEOM[0], winv, f, Setter(one))
    relax_tile(GEOM[0], winv, Coef(vz), one, f, c, ALONE, Setter(part))
    restrict(GEOM[0], GEOM[1], c, c_next)
    restrict(GEOM[1], GEOM[2], c_next, c_tile)


def merge_kernel(level, count):
    geom = GEOM[level]

    def kernel(xlo, xhi, flags, yup, ydown, up, down):
        lo, hi = corner_columns(tail_of(geom, xlo, count)), corner_columns(tail_of(geom, xhi, count))
        up[...] = yup[...]
        down[...] = ydown[...]
        a, b = merge_y(lo, hi, flags, yup[0:Z, :], ydown[0:Z, :])
        up[0:Z, :] = a
        down[0:Z, :] = b

    return kernel


def pre_tile(level, f, c, w, vz, own, xlo, xhi, ydn, yun, one, part, v_out, res):
    geom = GEOM[level]
    winv = w[...].astype(BF16)
    co = Coef(vz)
    fl = flags_of(geom, own, xlo, xhi, ydn, yun)
    halo = messages(geom, xlo, xhi, ydn, yun, winv)
    lo2, hi2, sides2 = relax_edges(geom, winv, co, one, halo, fl, *own_data(geom, xlo, xhi, ydn, yun))
    add_edges(geom, winv, part, frame(geom, fl, halo.lo, halo.hi, halo.sides()), Setter(v_out))
    lo, hi, sides = frame(geom, fl, lo2, hi2, sides2)
    for m in range(geom[0]):
        res[m] = tile_residual(geom, co, v_out, f, c, lo, hi, sides, m)


def pre0_kernel(f, c, w, vz, own, xlo, xhi, ydn, yun, one, part, c_next, v_out, f_next, up, down, yup, ydown, res):
    pre_tile(0, f, c, w, vz, own, xlo, xhi, ydn, yun, one, part, v_out, res)
    coarse = GEOM[1]
    restrict(GEOM[0], coarse, res, f_next)
    put_x(coarse, f_next, c_next, up, down, own[...])
    put_y(coarse, f_next, c_next, yup, ydown)
    yup[Z : Z + 8, :] = own[...]
    ydown[Z : Z + 8, :] = own[...]


def pre1_kernel(f, c, w, vz, own, xlo, xhi, ydn, yun, one, part, c_tile, v_out, up, down, chunks, res, f_next):
    pre_tile(1, f, c, w, vz, own, xlo, xhi, ydn, yun, one, part, v_out, res)
    restrict(GEOM[1], GEOM[2], res, f_next)
    put_x(GEOM[1], v_out, None, up, down)
    whole = pack(GEOM[2], [f_next[m] for m in range(6)] + [c_tile[m] for m in range(6)])
    for t in range(8):
        for k, part in enumerate(whole):
            chunks[t, k * Z : (k + 1) * Z, :] = part
        chunks[t, 3 * Z : 3 * Z + 8, :] = own[...]


def post_kernel(level):
    geom = GEOM[level]

    def sweeps(f, c, w, vz, own, xlo, xhi, ydn, yun, g, part, glo, ghi, gdn, gun, one, store):
        winv = w[...].astype(BF16)
        co = Coef(vz)
        fl = flags_of(geom, own, xlo, xhi, ydn, yun)
        halo = Halo(
            part_of(geom, glo, 0), part_of(geom, glo, 1), part_of(geom, ghi, 0), part_of(geom, ghi, 1), gdn[...], gun[...]
        )
        lo2, hi2, sides2 = relax_edges(geom, winv, co, g, halo, fl, *own_data(geom, xlo, xhi, ydn, yun))
        add_edges(geom, winv, part, frame(geom, fl, halo.lo, halo.hi, halo.sides()), Setter(one))
        relax_tile(geom, winv, co, one, f, c, frame(geom, fl, lo2, hi2, sides2), store)

    if level == 0:

        def kernel(f, c, w, vz, own, xlo, xhi, ydn, yun, g, part, glo, ghi, gdn, gun, out, one):
            def store(x, value):
                out[pl.ds(x, NZ, stride=24), :] = value[0:NZ, :]

            sweeps(f, c, w, vz, own, xlo, xhi, ydn, yun, g, part, glo, ghi, gdn, gun, one, store)

        return kernel

    fine = GEOM[level - 1]

    def kernel(f, c, w, vz, own, xlo, xhi, ydn, yun, g, part, glo, ghi, gdn, gun, fine_v, g_out, up, down, yup, ydown, one, e):
        sweeps(f, c, w, vz, own, xlo, xhi, ydn, yun, g, part, glo, ghi, gdn, gun, one, Setter(e))
        prolong_add(fine, geom, e, fine_v, g_out)
        put_x(fine, g_out, None, up, down)
        put_y(fine, g_out, None, yup, ydown)

    return kernel


def both_ways(up, down, axis):
    n = lax.axis_size(axis)
    fwd = [(i, (i + 1) % n) for i in range(n)]
    back = [((i + 1) % n, i) for i in range(n)]
    return lax.ppermute(up, axis, fwd), lax.ppermute(down, axis, back)


def on_device(right_side, helm_coef, vert_coef, block_inverse, edge_flip):
    inv = block_inverse.reshape(4, NZ, BLK)
    f_in = right_side.reshape(NZ * 24, LANES)
    c_in = helm_coef.reshape(NZ * 24, LANES)
    vert = vert_coef.reshape(1, NZ + 1)
    flip = edge_flip.reshape(1, 4)

    ys = (Z, LANES)
    t0, t1, t2 = tile_shape(0), tile_shape(1), tile_shape(2)
    xs = x_shape(0, 3)
    up, down, own, vz = pl.pallas_call(
        open_kernel,
        out_shape=[jax.ShapeDtypeStruct(x, F32) for x in (xs, xs, (8, LANES), ys)],
        in_specs=[ANY] * 4,
        out_specs=[VMEM] * 4,
        scratch_shapes=[pltpu.VMEM((NZ, 2, LANES), F32)] * 2
        + [pltpu.VMEM((NZ, 1, LANES), F32)] * 2
        + [pltpu.VMEM((1, NZ + 1), F32), pltpu.VMEM((1, 4), jnp.int32), pltpu.SemaphoreType.DMA((6,))],
        compiler_params=pltpu.CompilerParams(vmem_limit_bytes=58 * 1024 * 1024),
        name="open",
    )(right_side, helm_coef, vert, flip)
    xlo, xhi = both_ways(up, down, "gx")
    ws = (Z, 3 * Z)
    f, c, *w, one, part, c1, c_tile, yup, ydown = call(
        side_kernel,
        [t0, t0] + [ws] * 4 + [t0, t0, t1, t2, Y_FULL, Y_FULL],
        [f_in, c_in, inv, vz, own],
        name="side",
    )

    def to_sides(level, count, xlo, xhi, yup, ydown):
        shape = yup.shape
        yup, ydown = call(merge_kernel(level, count), [shape, shape], [xlo, xhi, own, yup, ydown], name=f"merge{level}")
        return both_ways(yup, ydown, "gy")

    got0 = (xlo, xhi, *to_sides(0, 3, xlo, xhi, yup, ydown))
    xs = x_shape(1, 3)
    v0, f1, up, down, yup, ydown = call(
        pre0_kernel, [t0, t1, xs, xs, Y_FULL, Y_FULL], [f, c, w[0], vz, own, *got0, one, part, c1], [t0], name="pre0"
    )
    xlo, xhi = both_ways(up, down, "gx")
    one, part = call(alone_kernel(1, True), [t1, t1], [f1, c1, w[1], vz], name="alone1")
    got1 = (xlo, xhi, *to_sides(1, 3, xlo, xhi, yup, ydown))
    xs = x_shape(1, 2)
    v1, up, down, chunks = call(
        pre1_kernel,
        [t1, xs, xs, (8, 3 * Z + 8, LANES)],
        [f1, c1, w[1], vz, own, *got1, one, part, c_tile],
        [t1, t2],
        name="pre1",
    )
    v1_lo, v1_hi = both_ways(up, down, "gx")
    chunks = lax.all_to_all(chunks, "gx", 0, 0)
    s2, s3 = (6, Z, 256), (3, Z, 128)
    m2, m3 = (Z, 256), (Z, 128)
    full2, full3 = (Z + 8, 256), (Z + 8, 128)
    f2, c2, fl2, up, down = call(
        open_strip_kernel, [s2, s2, (8, 256), full2, full2], [chunks], name="open2"
    )
    side2 = strip_ring(up, down)
    one, part = call(alone_kernel(2, True), [s2, s2], [f2, c2, w[2], vz, fl2], name="alone2")
    v2, f3, c3, fl3, up, down = call(
        pre_strip_kernel, [s2, s3, s3, (8, 128), full3, full3], [f2, c2, w[2], vz, fl2, *side2, one, part], [s2], name="pre2"
    )
    side3 = strip_ring(up, down)
    one, part = call(alone_kernel(3, True), [s3, s3], [f3, c3, w[3], vz, fl3], name="alone3")
    v3, up, down = call(
        bottom_strip_kernel, [s3, m3, m3], [f3, c3, w[3], vz, fl3, *side3, one, part], [s3], name="bottom"
    )
    side = strip_ring(up, down)
    (part,) = call(alone_kernel(3, False), [s3], [f3, c3, w[3], vz, fl3, v3], name="again3")
    g2, up, down = call(last_strip_kernel, [s2, m2, m2], [w[3], fl3, *side, part, v2, fl2, v1_lo, v1_hi], [s3], name="last", after=2)
    side = strip_ring(up, down)
    (part,) = call(alone_kernel(2, False), [s2], [f2, c2, w[2], vz, fl2, g2], name="again2")
    g1, lo, hi, up, down = call(
        post_strip_kernel,
        [t1, ys, ys, ys, ys],
        [f2, c2, w[2], vz, fl2, *side2, g2, part, *side, v1, v1_lo, v1_hi, own],
        [s2, s2, t2, ys, ys],
        name="post2",
    )
    side = both_ways(up, down, "gy")
    (part,) = call(alone_kernel(1, False), [t1], [f1, c1, w[1], vz, g1], name="again1")
    xs = x_shape(0, 2)
    g0, up, down, yup, ydown = call(
        post_kernel(1),
        [t0, xs, xs, ys, ys],
        [f1, c1, w[1], vz, own, *got1, g1, part, lo, hi, *side, v0],
        [t1, t1],
        name="post1",
    )
    xlo, xhi = both_ways(up, down, "gx")
    (part,) = call(alone_kernel(0, False), [t0], [f, c, w[0], vz, g0], name="again0")
    got = (xlo, xhi, *to_sides(0, 2, xlo, xhi, yup, ydown))
    (out,) = call(
        post_kernel(0), [(NZ * 24, LANES)], [f, c, w[0], vz, own, *got0, g0, part, *got], [t0], name="post0"
    )
    return out.reshape(NZ, 24, LANES)


def solution(mesh):
    placed = (P(None, "gx", "gy"), P(None, "gx", "gy"), P(), P(), P("gx", "gy", None))
    return jax.shard_map(
        on_device, mesh=mesh, in_specs=placed, out_specs=P(None, "gx", "gy"), check_vma=False
    )
```

```python
import jax
import jax.numpy as jnp
from jax import lax
from jax.experimental import pallas as pl
from jax.experimental.pallas import tpu as pltpu
from jax.sharding import PartitionSpec as P

BLK = 14
NBLK = 5
NZ = 70
Z = 72
LANES = 128
F32 = jnp.float32
BF16 = jnp.bfloat16

GEOM = ((24, 1, 128), (6, 2, 64), (6, 1, 32), (3, 1, 16))


def lane_ids(shape):
    return lax.broadcasted_iota(jnp.int32, shape, len(shape) - 1)


def zl():
    return lane_ids((Z, LANES))


def roll(x, shift):
    shift = shift % x.shape[-1]
    return x if shift == 0 else pltpu.roll(x, shift, axis=1)


def col(x, k):
    return jnp.broadcast_to(x[:, k : k + 1], (Z, LANES))


def iota2(n, m):
    return lax.broadcasted_iota(jnp.int32, (n, m), 0), lax.broadcasted_iota(jnp.int32, (n, m), 1)


def lane_dot(x, mat):
    hi = x.astype(BF16).astype(F32)
    both = jnp.concatenate([hi, x - hi], axis=1).astype(BF16)
    twice = jnp.concatenate([mat, mat], axis=0).astype(BF16)
    return jnp.dot(both, twice, preferred_element_type=F32)


def block_dot(winv, x):
    hi = x.astype(BF16).astype(F32)
    parts = jnp.concatenate([hi, hi, x - hi], axis=0).astype(BF16)
    return jnp.dot(winv, parts, preferred_element_type=F32)


def reverse_matrix(width):
    a, b = iota2(LANES, LANES)
    return jnp.where((b < width) & (a == width - 1 - b), 1.0, 0.0)


def flag_row(flags, k):
    return jnp.broadcast_to(flags[k : k + 1, :], (Z, LANES))


class Coef:
    def __init__(self, ref, width=LANES):
        self.mid = jnp.broadcast_to(ref[:, 0:1], (Z, width))
        self.up = jnp.broadcast_to(ref[:, 1:2], (Z, width))
        self.down = jnp.broadcast_to(ref[:, 2:3], (Z, width))


def residual(co, f, c, v, beside):
    above = pltpu.roll(v, Z - 1, axis=0)
    below = pltpu.roll(v, 1, axis=0)
    return f - (c * 0.0625 + co.mid) * v + beside * 0.0625 + co.up * above + co.down * below


def row_of(geom, v, row):
    m_rows, _, ty = geom
    q, m = divmod(row, m_rows)
    return roll(v[m], -q * ty)


def corners(geom, v):
    m_rows, groups, ty = geom
    last = v[m_rows - 1]
    base = (groups - 1) * ty
    return corner_rows([col(v[0], 0), col(v[0], ty - 1), col(last, base), col(last, base + ty - 1)])


def corner_rows(columns):
    lane = zl()
    out = jnp.zeros((Z, LANES), F32)
    for k, column in enumerate(columns):
        out = jnp.where(lane == 4 + k, column, out)
    return jnp.concatenate([out, jnp.zeros((LANES - Z, LANES), F32)], axis=0).T[0:8, :]


def corner_columns(rows):
    out = jnp.concatenate([rows, jnp.zeros((LANES - 8, LANES), F32)], axis=0).T[0:Z, :]
    return [col(out, 4 + k) for k in range(4)]


def whole_rows(geom):
    return geom[1] == 1 and geom[2] == LANES


def tile_rows(geom):
    m_rows, groups, ty = geom
    return [(q * m_rows + m, m, q * ty) for m in range(m_rows) for q in range(groups)]


def own_columns(geom, v):
    ty = geom[2]
    lane = zl()
    out = jnp.zeros((Z, LANES), F32)
    for r, m, base in tile_rows(geom):
        row = v[m]
        first = roll(row, 2 * r + 1 - base)
        out = jnp.where(lane == 2 * r + 1, first, out)
        last = first if whole_rows(geom) else roll(row, 2 * r - (base + ty - 1))
        out = jnp.where(lane == 2 * r, last, out)
    return out


def pack(geom, parts):
    ty = geom[2]
    per = LANES // ty
    out = []
    for first in range(0, len(parts), per):
        lane = zl()
        acc = parts[first]
        for k, part in enumerate(parts[first + 1 : first + per], 1):
            acc = jnp.where(lane < k * ty, acc, roll(part, k * ty))
        out.append(acc)
    return out


def packed(geom, count):
    per = LANES // geom[2]
    return -(-count // per)


def part_of(geom, ref, k):
    ty = geom[2]
    per = LANES // ty
    return roll(ref[(k // per) * Z : (k // per + 1) * Z, :], -(k % per) * ty)


def put_x(geom, v, c, up, down, flags=None):
    m_rows, groups, _ = geom
    tx = m_rows * groups
    tail = corners(geom, v)
    if flags is not None:
        tail = tail + flags
    for ref, edge, second in ((up, tx - 1, tx - 2), (down, 0, 1)):
        parts = [row_of(geom, v, edge), row_of(geom, v, second)]
        if c is not None:
            parts.append(row_of(geom, c, edge))
        put_parts(geom, parts, tail, ref)


def put_parts(geom, parts, tail, ref):
    whole = pack(geom, parts)
    for k, part in enumerate(whole):
        ref[k * Z : (k + 1) * Z, :] = part
    ref[len(whole) * Z : len(whole) * Z + 8, :] = tail


def tail_of(geom, ref, count):
    n = packed(geom, count) * Z
    return ref[n : n + 8, :]


def put_y(geom, v, c, up, down):
    ty = geom[2]
    lane = zl()
    out_up = jnp.zeros((Z, LANES), F32)
    out_down = out_up
    for r, m, base in tile_rows(geom):
        row = v[m]
        mine = lane // 2 == r
        last = roll(row, 2 * r + 1 - (base + ty - 1))
        first = roll(row, 2 * r - base)
        out_up = jnp.where(mine, last, out_up)
        out_down = jnp.where(mine, first, out_down)
        if c is not None:
            row = c[m]
            out_up = jnp.where(lane == 65 + 2 * r, roll(row, 65 + 2 * r - (base + ty - 1)), out_up)
            out_down = jnp.where(lane == 64 + 2 * r, roll(row, 64 + 2 * r - base), out_down)
    up[0:Z, :] = out_up
    down[0:Z, :] = out_down


def merge_y(lo, hi, flags, up, down):
    lane = zl()
    f0, f1 = flag_row(flags, 0) > 0.5, flag_row(flags, 1) > 0.5

    def fill(part, values):
        for k, value in enumerate(values):
            part = jnp.where(lane == 112 + k, value, part)
        return part

    up_new = fill(up, [lo[3], lo[1], hi[1], hi[3], jnp.where(f0, lo[2], lo[3]), jnp.where(f1, hi[0], hi[1])])
    down_new = fill(down, [lo[2], lo[0], hi[0], hi[2], jnp.where(f0, lo[3], lo[2]), jnp.where(f1, hi[1], hi[0])])
    return up_new, down_new


def odd_lanes():
    return zl() % 2 == 1


class Halo:
    def __init__(self, lo, lo2, hi, hi2, dn, un):
        self.lo, self.lo2, self.hi, self.hi2, self.dn, self.un = lo, lo2, hi, hi2, dn, un

    def sides(self):
        return jnp.where(odd_lanes(), self.dn, self.un)

    def seconds(self):
        return jnp.where(odd_lanes(), roll(self.dn, 1), roll(self.un, -1))


class Flags:
    def __init__(self, own, lo, hi, dn, un):
        self.own, self.lo, self.hi, self.dn, self.un = own, lo, hi, dn, un


def turn_row(geom, row, flag):
    return jnp.where(flag > 0.5, lane_dot(row, reverse_matrix(geom[2])), row)


def turn_sides(geom, sides, flag_dn, flag_un):
    tx = geom[0] * geom[1]
    flag = jnp.where(odd_lanes(), flag_dn, flag_un)
    a, b = iota2(LANES, LANES)
    mat = jnp.where((b < 2 * tx) & (a == 2 * (tx - 1 - b // 2) + b % 2), 1.0, 0.0)
    return jnp.where(flag > 0.5, lane_dot(sides, mat), sides)


def frame(geom, fl, lo, hi, sides):
    return (
        turn_row(geom, lo, flag_row(fl.own, 0)),
        turn_row(geom, hi, flag_row(fl.own, 1)),
        turn_sides(geom, sides, flag_row(fl.own, 2), flag_row(fl.own, 3)),
    )


def relax_edges(geom, winv, co, v, columns, halo, fl, f_lo, c_lo, f_hi, c_hi, f_sides, c_sides):
    m_rows, groups, ty = geom
    tx = m_rows * groups
    lane = zl()
    dn, un = halo.dn, halo.un

    def beside_row(edge, second, mine, low, high):
        left = jnp.where(lane == 0, low, roll(edge, 1))
        right = jnp.where(lane == ty - 1, high, roll(edge, -1))
        return second + mine + left + right

    def choose(flags, k, first, other):
        return jnp.where(flag_row(flags, k) > 0.5, other, first)

    b_lo = beside_row(
        halo.lo,
        halo.lo2,
        turn_row(geom, row_of(geom, v, 0), flag_row(fl.lo, 1)),
        choose(fl.lo, 2, col(dn, 112), col(dn, 113)),
        choose(fl.lo, 3, col(un, 112), col(un, 113)),
    )
    b_hi = beside_row(
        halo.hi,
        halo.hi2,
        turn_row(geom, row_of(geom, v, tx - 1), flag_row(fl.hi, 0)),
        choose(fl.hi, 2, col(dn, 114), col(dn, 115)),
        choose(fl.hi, 3, col(un, 114), col(un, 115)),
    )
    edge = halo.sides()
    mine = turn_sides(geom, columns, flag_row(fl.dn, 3), flag_row(fl.un, 2))
    below = jnp.where(lane == 1, col(dn, 116), jnp.where(lane == 0, col(un, 116), roll(edge, 2)))
    last = 2 * (tx - 1)
    above = jnp.where(lane == last + 1, col(dn, 117), jnp.where(lane == last, col(un, 117), roll(edge, -2)))
    b_sides = halo.seconds() + mine + below + above
    r_lo = residual(co, f_lo, c_lo, halo.lo, b_lo)
    r_hi = residual(co, f_hi, c_hi, halo.hi, b_hi)
    r_sides = residual(co, f_sides, c_sides, edge, b_sides)
    d = block_dot(winv, jnp.concatenate([r_lo, r_hi, r_sides], axis=1))
    return halo.lo + d[:, :LANES], halo.hi + d[:, LANES : 2 * LANES], edge + d[:, 2 * LANES :]


def tile_residual(geom, co, v, f, c, lo, hi, sides, m):
    m_rows, groups, ty = geom
    lane = zl()
    here = v[m]
    if lo is None:
        lo = hi = jnp.zeros((Z, LANES), F32)
    if m > 0:
        low_x = v[m - 1]
    else:
        low_x = lo if groups == 1 else jnp.where(lane < ty, lo, roll(v[m_rows - 1], ty))
    if m < m_rows - 1:
        high_x = v[m + 1]
    elif groups == 1:
        high_x = hi
    else:
        high_x = jnp.where(lane < (groups - 1) * ty, roll(v[0], -ty), roll(hi, (groups - 1) * ty))
    low_y, high_y = roll(here, 1), roll(here, -1)
    if sides is None:
        low_y = jnp.where(lane % ty == 0, 0.0, low_y)
        high_y = jnp.where(lane % ty == ty - 1, 0.0, high_y)
        return residual(co, f[m], c[m], here, low_x + high_x + low_y + high_y)
    for q in range(groups):
        row = q * m_rows + m
        low = roll(sides, q * ty - 2 * row - 1)
        high = low if whole_rows(geom) else roll(sides, q * ty + ty - 1 - 2 * row)
        low_y = jnp.where(lane == q * ty, low, low_y)
        high_y = jnp.where(lane == q * ty + ty - 1, high, high_y)
    return residual(co, f[m], c[m], here, low_x + high_x + low_y + high_y)


def relax_tile(geom, winv, co, v, f, c, edges, store):
    lo, hi, sides = edges
    for m in range(0, geom[0], 2):
        rows = [k for k in (m, m + 1) if k < geom[0]]
        r = [tile_residual(geom, co, v, f, c, lo, hi, sides, k) for k in rows]
        d = block_dot(winv, r[0] if len(r) == 1 else jnp.concatenate(r, axis=1))
        for i, k in enumerate(rows):
            store(k, v[k] + d[:, i * LANES : (i + 1) * LANES])


ALONE = (None, None, None)


def edge_terms(geom, winv, edges):
    ty = geom[2]
    lane = zl()
    d = block_dot(winv, jnp.concatenate(edges, axis=1) * 0.0625)
    low, high, sides = [d[:, k * LANES : (k + 1) * LANES] for k in range(3)]
    if ty < LANES:
        low = jnp.where(lane < ty, low, 0.0)
        high = jnp.where(lane < ty, high, 0.0)
    return low, high, sides


def with_terms(geom, x, terms, m):
    m_rows, groups, ty = geom
    low, high, sides = terms
    lane = zl()
    if m == 0:
        x = x + low
    if m == m_rows - 1:
        x = x + roll(high, (groups - 1) * ty)
    for q in range(groups):
        row = q * m_rows + m
        first = roll(sides, q * ty - 2 * row - 1)
        last = first if whole_rows(geom) else roll(sides, q * ty + ty - 1 - 2 * row)
        x = x + jnp.where(lane == q * ty, first, jnp.where(lane == q * ty + ty - 1, last, 0.0))
    return x


def add_edges(geom, winv, part, edges, store):
    terms = edge_terms(geom, winv, edges)
    for m in range(geom[0]):
        store(m, with_terms(geom, part[m], terms, m))


def start_tile(geom, winv, f, store):
    for m in range(0, geom[0], 2):
        rows = [k for k in (m, m + 1) if k < geom[0]]
        parts = [f[k] for k in rows]
        d = block_dot(winv, parts[0] if len(parts) == 1 else jnp.concatenate(parts, axis=1))
        for i, k in enumerate(rows):
            store(k, d[:, i * LANES : (i + 1) * LANES])


def restrict(fine, coarse, v, out, wanted=None):
    m_rows, _, ty = fine
    cm, cq, cty = coarse
    a, b = iota2(LANES, LANES)
    for mc in range(cm):
        acc = None
        for qc in range(cq):
            if wanted is not None and qc * cm + mc not in wanted:
                continue
            q, m = divmod(2 * (qc * cm + mc), m_rows)
            inside = (b >= qc * cty) & (b < (qc + 1) * cty) & (a // 2 == b - qc * cty + q * (ty // 2))
            term = lane_dot(v[m] + v[m + 1], jnp.where(inside, 0.25, 0.0))
            acc = term if acc is None else acc + term
        if acc is not None:
            out[mc] = acc


def prolong_add(fine, coarse, e, v, out, rows=None):
    m_rows, groups, ty = fine
    cm, _, cty = coarse
    a, b = iota2(LANES, LANES)
    for m in range(0, m_rows, 2) if rows is None else rows:
        acc = None
        for q in range(groups):
            qc, mc = divmod((q * m_rows + m) // 2, cm)
            inside = (b >= q * ty) & (b < (q + 1) * ty) & (a - qc * cty == (b - q * ty) // 2)
            term = lane_dot(e[mc], jnp.where(inside, 1.0, 0.0))
            acc = term if acc is None else acc + term
        out[m] = v[m] + acc
        out[m + 1] = v[m + 1] + acc


class Setter:
    def __init__(self, ref):
        self.ref = ref

    def __call__(self, m, value):
        self.ref[m] = value


def messages(geom, xlo, xhi, ydn, yun, winv):
    raw = [part_of(geom, xlo, 0), part_of(geom, xlo, 1), part_of(geom, xhi, 0), part_of(geom, xhi, 1), ydn[0:Z, :], yun[0:Z, :]]
    d = block_dot(winv, jnp.concatenate(raw, axis=1))
    return Halo(*[d[:, k * LANES : (k + 1) * LANES] for k in range(6)])


def own_data(geom, xlo, xhi, ydn, yun):
    dn, un = ydn[0:Z, :], yun[0:Z, :]
    f_sides = jnp.where(odd_lanes(), dn, un)
    c_sides = roll(f_sides, -64)
    return (
        part_of(geom, xlo, 0),
        part_of(geom, xlo, 2),
        part_of(geom, xhi, 0),
        part_of(geom, xhi, 2),
        f_sides,
        c_sides,
    )


def flags_of(geom, own, xlo, xhi, ydn, yun):
    return Flags(own[...], tail_of(geom, xlo, 3), tail_of(geom, xhi, 3), ydn[Z : Z + 8, :], yun[Z : Z + 8, :])


def load_top(src, dst):
    for x in range(24):
        dst[x, 0:NZ, :] = src[pl.ds(x, NZ, stride=24), :]
        dst[x, NZ:Z, :] = jnp.zeros((Z - NZ, LANES), F32)


STRIPS = {2: (6, 32, 256), 3: (3, 16, 128)}


def in_tile(strip):
    _, ty, width = strip
    return lane_ids((Z, width)) % ty


def group_dot(x, mat):
    parts = [lane_dot(x[:, k : k + LANES], mat) for k in range(0, x.shape[1], LANES)]
    return parts[0] if len(parts) == 1 else jnp.concatenate(parts, axis=1)


def turn_groups(strip, x, flags, k, count):
    _, ty, width = strip
    a, b = iota2(LANES, LANES)
    mat = jnp.where((a // ty == b // ty) & (b % ty < count) & (a % ty == count - 1 - b % ty), 1.0, 0.0)
    flag = jnp.broadcast_to(flags[k : k + 1, :], (Z, width))
    return jnp.where(flag > 0.5, group_dot(x, mat), x)


def strip_ends(strip, v, flags):
    m_rows, ty, _ = strip
    low = turn_groups(strip, roll(v[m_rows - 1], ty), flags, 0, ty)
    high = turn_groups(strip, roll(v[0], -ty), flags, 1, ty)
    return low, high


def strip_column(strip, v, y, offset, out):
    lt = in_tile(strip)
    for m in range(strip[0]):
        out = jnp.where(lt == offset + m, roll(v[m], offset + m - y), out)
    return out


def strip_message(strip, v, c, ends, up, down):
    m_rows, ty, width = strip
    lt = in_tile(strip)
    for ref, edge, second in ((up, ty - 1, ty - 2), (down, 0, 1)):
        out = strip_column(strip, v, edge, 0, jnp.zeros((Z, width), F32))
        out = strip_column(strip, v, second, m_rows, out)
        if c is not None:
            out = strip_column(strip, c, edge, 2 * m_rows, out)
        for k, end in enumerate(ends):
            out = jnp.where(lt == 3 * m_rows + k, roll(end, 3 * m_rows + k - edge), out)
        ref[0:Z, :] = out


def strip_edges(strip, winv, co, sides):
    m_rows, _, width = strip
    lt = in_tile(strip)
    r = []
    for x, raw, flags, k, mine in sides:
        mine = turn_groups(strip, mine, flags, k, m_rows)
        low = jnp.where(lt == 0, roll(x, -3 * m_rows), roll(x, 1))
        high = jnp.where(lt == m_rows - 1, roll(x, -2 * m_rows - 2), roll(x, -1))
        r.append(residual(co, raw, roll(raw, -2 * m_rows), x, roll(x, -m_rows) + mine + low + high))
    d = block_dot(winv, jnp.concatenate(r, axis=1))
    return [side[0] + d[:, k * width : (k + 1) * width] for k, side in enumerate(sides)]


def strip_frame(strip, flags, low, high):
    return turn_groups(strip, low, flags, 2, strip[0]), turn_groups(strip, high, flags, 3, strip[0])


def strip_residual(strip, co, v, f, c, ends, sides, m):
    m_rows, ty, _ = strip
    lt = in_tile(strip)
    low_x = v[m - 1] if m > 0 else ends[0]
    high_x = v[m + 1] if m < m_rows - 1 else ends[1]
    low = 0.0 if sides is None else roll(sides[0], -m)
    high = 0.0 if sides is None else roll(sides[1], ty - 1 - m)
    low_y = jnp.where(lt == 0, low, roll(v[m], 1))
    high_y = jnp.where(lt == ty - 1, high, roll(v[m], -1))
    return residual(co, f[m], c[m], v[m], low_x + high_x + low_y + high_y)


def strip_relax(strip, winv, co, v, f, c, flags, sides, store):
    ends = strip_ends(strip, v, flags)
    for m in range(strip[0]):
        r = strip_residual(strip, co, v, f, c, ends, sides, m)
        store(m, v[m] + block_dot(winv, r))


def strip_add_sides(strip, winv, part, sides, store):
    m_rows, ty, width = strip
    lt = in_tile(strip)
    d = block_dot(winv, jnp.concatenate(sides, axis=1) * 0.0625)
    for m in range(m_rows):
        low, high = roll(d[:, :width], -m), roll(d[:, width:], ty - 1 - m)
        store(m, part[m] + jnp.where(lt == 0, low, jnp.where(lt == ty - 1, high, 0.0)))


def strip_restrict(v, out):
    a, b = iota2(LANES, LANES)
    for m in range(3):
        both = v[2 * m] + v[2 * m + 1]
        out[m] = lane_dot(both[:, :LANES], jnp.where(a // 2 == b, 0.25, 0.0)) + lane_dot(
            both[:, LANES:], jnp.where(a // 2 == b - 64, 0.25, 0.0)
        )


def open_strip_kernel(chunks, f, c, flags, up, down):
    strip = STRIPS[2]
    group = lane_ids((Z, LANES)) // 32
    for m in range(6):
        for ref, k in ((f, m), (c, 6 + m)):
            part = (k // 4) * Z
            halves = []
            for h in range(2):
                acc = None
                for g in range(4):
                    x = chunks[4 * h + g, part : part + Z, :]
                    acc = x if acc is None else jnp.where(group == (g + k) % 4, x, acc)
                halves.append(roll(acc, -(k % 4) * 32))
            ref[m] = jnp.concatenate(halves, axis=1)
    group = lane_ids((8, LANES)) // 32
    for h in range(2):
        acc = None
        for g in range(4):
            x = chunks[4 * h + g, 3 * Z : 3 * Z + 8, :]
            acc = x if acc is None else jnp.where(group == g, x, acc)
        flags[:, h * LANES : (h + 1) * LANES] = acc
    strip_message(strip, f, c, strip_ends(strip, f, flags), up, down)
    up[Z : Z + 8, :] = flags[...]
    down[Z : Z + 8, :] = flags[...]


def strip_sides(values, raws, dn, un, first, last):
    return (
        (values[0], raws[0], dn[Z : Z + 8, :], 3, first[...]),
        (values[1], raws[1], un[Z : Z + 8, :], 2, last[...]),
    )


def pre_strip_kernel(f, c, w, vz, flags, dn, un, part, first, last, fl_next, c_up, c_down, v_out, f_next, up, down, res):
    strip = STRIPS[2]
    width = strip[2]
    winv = w[...].astype(BF16)
    co = Coef(vz, width)
    raws = [dn[0:Z, :], un[0:Z, :]]
    values = [block_dot(winv, x) for x in raws]
    edges = strip_edges(strip, winv, co, strip_sides(values, raws, dn, un, first, last))
    strip_add_sides(strip, winv, part, strip_frame(strip, flags, *values), Setter(v_out))
    ends = strip_ends(strip, v_out, flags)
    sides = strip_frame(strip, flags, *edges)
    for m in range(6):
        res[m] = strip_residual(strip, co, v_out, f, c, ends, sides, m)
    strip_restrict(res, f_next)
    small = STRIPS[3]
    strip_message(small, f_next, None, strip_ends(small, f_next, fl_next), up, down)
    up[0:Z, :] = up[0:Z, :] + c_up[...]
    down[0:Z, :] = down[0:Z, :] + c_down[...]
    up[Z : Z + 8, :] = fl_next[...]
    down[Z : Z + 8, :] = fl_next[...]


def next_coef_kernel(c, flags, c_next, fl_next, up, down):
    strip_restrict(c, c_next)
    a, b = iota2(LANES, LANES)
    fl_next[...] = lane_dot(flags[:, :LANES], jnp.where((b < 64) & (a == (b // 16) * 32), 1.0, 0.0)) + lane_dot(
        flags[:, LANES:], jnp.where((b >= 64) & (a == (b // 16 - 4) * 32), 1.0, 0.0)
    )
    small = STRIPS[3]
    zero = jnp.zeros((Z, LANES), F32)
    up[...] = strip_column(small, c_next, small[1] - 1, 2 * small[0], zero)
    down[...] = strip_column(small, c_next, 0, 2 * small[0], zero)


def bottom_strip_kernel(f, c, w, vz, flags, dn, un, part, first, last, v_out, up, down, one):
    strip = STRIPS[3]
    winv = w[...].astype(BF16)
    co = Coef(vz)
    raws = [dn[0:Z, :], un[0:Z, :]]
    values = [block_dot(winv, x) for x in raws]
    edges = strip_edges(strip, winv, co, strip_sides(values, raws, dn, un, first, last))
    strip_add_sides(strip, winv, part, strip_frame(strip, flags, *values), Setter(one))
    strip_relax(strip, winv, co, one, f, c, flags, strip_frame(strip, flags, *edges), Setter(v_out))
    strip_message(strip, v_out, None, (), up, down)


def last_strip_kernel(w, flags, dn, un, part, base_up, base_down, _lo, _hi, e, up, down, small_up, small_down):
    strip, fine = STRIPS[3], STRIPS[2]
    winv = w[...].astype(BF16)
    strip_add_sides(strip, winv, part, strip_frame(strip, flags, dn[...], un[...]), Setter(e))
    strip_message(strip, e, None, strip_ends(strip, e, flags), small_up, small_down)
    a, b = iota2(LANES, LANES)
    for h in range(2):
        lt = b % 32
        source = jnp.where(lt < 12, (lt % 6) // 2, jnp.where((lt == 18) | (lt == 19), lt - 9, 15))
        spread = jnp.where((lt != 15) & (a == 64 * h + (b // 32) * 16 + source) & (source < 15), 1.0, 0.0)
        half = slice(h * LANES, (h + 1) * LANES)
        up[:, half] = base_up[:, half] + lane_dot(small_up[...], spread)
        down[:, half] = base_down[:, half] + lane_dot(small_down[...], spread)


def base_message_kernel(v, flags, up, down):
    strip_message(STRIPS[2], v, None, strip_ends(STRIPS[2], v, flags), up, down)


def again2_kernel(f, c, w, vz, flags, v, e, tile_v, g, part, low, high, yup, ydown):
    strip = STRIPS[2]
    a, b = iota2(LANES, LANES)
    for m in range(3):
        add = jnp.concatenate([lane_dot(e[m], jnp.where(a == 64 * h + b // 2, 1.0, 0.0)) for h in range(2)], axis=1)
        g[2 * m] = v[2 * m] + add
        g[2 * m + 1] = v[2 * m + 1] + add
    strip_relax(strip, w[...].astype(BF16), Coef(vz, strip[2]), g, f, c, flags, None, Setter(part))
    zero = jnp.zeros((Z, strip[2]), F32)
    low[...] = strip_column(strip, g, 0, 0, zero)
    high[...] = strip_column(strip, g, strip[1] - 1, 0, zero)
    put_y(GEOM[1], tile_v, None, yup, ydown)


def alone_kernel(level):
    strip = STRIPS[level]

    def kernel(f, c, w, vz, flags, part, low, high, v):
        winv = w[...].astype(BF16)
        for m in range(strip[0]):
            v[m] = block_dot(winv, f[m])
        strip_relax(strip, winv, Coef(vz, strip[2]), v, f, c, flags, None, Setter(part))
        zero = jnp.zeros((Z, strip[2]), F32)
        low[...] = strip_column(strip, v, 0, 0, zero)
        high[...] = strip_column(strip, v, strip[1] - 1, 0, zero)

    return kernel


def again3_kernel(f, c, w, vz, flags, v, part):
    strip_relax(STRIPS[3], w[...].astype(BF16), Coef(vz), v, f, c, flags, None, Setter(part))


def tile_row(e, m, step):
    t = lax.rem(lax.axis_index("gx") + (step + 8), 8)
    half = jnp.where(t < 4, e[m, :, :LANES], e[m, :, LANES:])
    return pltpu.roll(half, lax.rem(8 - t, 4) * 32, axis=1)


def post_strip_kernel(
    f, c, w, vz, flags, dn, un, part, first_column, last_column, gdn, gun, xlo, xhi, own, yup, ydown, e, up, down, one
):
    strip = STRIPS[2]
    fine = GEOM[1]
    winv = w[...].astype(BF16)
    co = Coef(vz, strip[2])
    raws = [dn[0:Z, :], un[0:Z, :]]
    values = [gdn[...], gun[...]]
    edges = strip_edges(strip, winv, co, strip_sides(values, raws, dn, un, first_column, last_column))
    strip_add_sides(strip, winv, part, strip_frame(strip, flags, *values), Setter(one))
    strip_relax(strip, winv, co, one, f, c, flags, strip_frame(strip, flags, *edges), Setter(e))
    extras = []
    for ref, step in ((xlo, -1), (xhi, 1)):
        first, last = tile_row(e, 0, step), tile_row(e, 5, step)
        adds = (col(first, 0), col(first, 31), col(last, 0), col(last, 31))
        extras.append([x + y for x, y in zip(corner_columns(tail_of(fine, ref, 2)), adds)])
    group = zl() // 4
    add_up = add_down = jnp.zeros((Z, LANES), F32)
    for m in range(6):
        row = tile_row(e, m, 0)
        add_up = jnp.where(group == m, col(row, 31), add_up)
        add_down = jnp.where(group == m, col(row, 0), add_down)
    up[...], down[...] = merge_y(*extras, own, yup[...] + add_up, ydown[...] + add_down)


def again1_kernel(f, c, w, vz, v, e, xlo, xhi, g, part, columns, lo_out, hi_out, tile):
    fine, geom = GEOM[1], GEOM[2]
    for m in range(6):
        tile[m] = tile_row(e, m, 0)
    prolong_add(fine, geom, tile, v, g)
    a, b = iota2(LANES, LANES)
    spread = jnp.where((b < 64) & (a == b // 2), 1.0, 0.0)
    for ref, out, row in ((xlo, lo_out, tile_row(e, 5, -1)), (xhi, hi_out, tile_row(e, 0, 1))):
        add = lane_dot(row, spread)
        out[...] = pack(fine, [part_of(fine, ref, 0) + add, part_of(fine, ref, 1) + add])[0]
    columns[...] = own_columns(fine, g)
    relax_tile(fine, w[...].astype(BF16), Coef(vz), g, f, c, ALONE, Setter(part))


def swap_pairs(axis, which, nearest=False):
    sizes = lax.axis_size("gx"), lax.axis_size("gy")
    out = []
    for i in range(sizes[0]):
        for j in range(sizes[1]):
            at = [i, j]
            dim = 0 if axis == "gx" else 1
            n = sizes[dim]
            at[dim] = (at[dim] ^ 1) if which == 0 else (at[dim] + (1 if at[dim] % 2 else n - 1)) % n
            if nearest and 2 * j // n != 2 * at[1] // n:
                at[0] = i ^ 1
            out.append((i * sizes[1] + j, at[0] * sizes[1] + at[1]))
    return out


def swap(first, second, axis, nearest=False):
    both = ("gx", "gy")
    return (
        lax.ppermute(first, both, swap_pairs(axis, 0, nearest)),
        lax.ppermute(second, both, swap_pairs(axis, 1, nearest)),
    )


ANY = pl.BlockSpec(memory_space=pl.ANY)
LIMIT = 14 * 1024 * 1024
VMEM = pl.BlockSpec(memory_space=pltpu.VMEM)


class Either:
    def __init__(self, first, a, b):
        self.first, self.a, self.b = first, a, b

    def __getitem__(self, index):
        return jnp.where(self.first, self.a[index], self.b[index])


def is_even(axis):
    return lax.rem(lax.axis_index(axis), 2) == 0


def by_swaps(kernel, n_in, n_out, got, send):
    def wrapped(*refs):
        refs = list(refs)
        for place, axis in got:
            a, b = refs[place], refs[place + 1]
            refs[place], refs[place + 1] = Either(is_even(axis), b, a), Either(is_even(axis), a, b)
        extra = refs[len(refs) - 2 * len(send) :]
        refs = refs[: len(refs) - 2 * len(send)]
        outs = []
        for k, (place, axis) in enumerate(send):
            place += n_in
            outs.append((refs[place], refs[place + 1], extra[2 * k], extra[2 * k + 1], axis))
            refs[place], refs[place + 1] = extra[2 * k], extra[2 * k + 1]
        kernel(*refs)
        for first, second, up, down, axis in outs:
            even = is_even(axis)
            up, down = up[...], down[...]
            first[...] = jnp.where(even, up, down)
            second[...] = jnp.where(even, down, up)

    return wrapped


def call(kernel, outs, args, scratch=(), name=None, after=0, got=(), send=()):
    scratch = [pltpu.VMEM(s, F32) for s in scratch]
    scratch += [pltpu.VMEM(outs[place], F32) for place, _ in send for _ in range(2)]
    return pl.pallas_call(
        by_swaps(kernel, len(args), len(outs), got, send),
        out_shape=[jax.ShapeDtypeStruct(s, F32) for s in outs],
        in_specs=[VMEM] * (len(args) - after) + [ANY] * after,
        out_specs=[VMEM] * len(outs),
        scratch_shapes=scratch,
        compiler_params=pltpu.CompilerParams(vmem_limit_bytes=LIMIT),
        name=name,
    )(*args)


def tile_shape(level):
    return (GEOM[level][0], Z, LANES)


def x_shape(level, count):
    return (packed(GEOM[level], count) * Z + 8, LANES)


Y_FULL = (Z + 8, LANES)


def open_kernel(f_in, c_in, vert_in, flip_in, up, down, own, vz, f_low, f_high, c_low, c_high, vert, flip, sems):
    pairs = (
        (vert_in, vert),
        (flip_in, flip),
        (f_in.at[:, 0:2, :], f_low),
        (f_in.at[:, 22:24, :], f_high),
        (c_in.at[:, 0:1, :], c_low),
        (c_in.at[:, 23:24, :], c_high),
    )
    copies = [pltpu.make_async_copy(src, dst, sems.at[k]) for k, (src, dst) in enumerate(pairs)]
    for copy in copies:
        copy.start()
    for copy in copies[:2]:
        copy.wait()
    a, b = iota2(8, 4)
    flags = jnp.broadcast_to(flip[...].astype(F32), (8, 4))
    flags = jnp.broadcast_to(jnp.sum(jnp.where(a == b, flags, 0.0), axis=1, keepdims=True), (8, LANES))
    own[...] = flags
    a, b = iota2(Z, NZ + 1)
    coef = jnp.broadcast_to(vert[...], (Z, NZ + 1))
    high = jnp.sum(jnp.where((b == a + 1) & (a < NZ), coef, 0.0), axis=1, keepdims=True)
    low = jnp.sum(jnp.where((b == a) & (a < NZ), coef, 0.0), axis=1, keepdims=True)
    columns = [jnp.broadcast_to(x * 0.0625, (Z, LANES)) for x in (4.0 + high + low, high, low)]
    lane = zl()
    vz[...] = jnp.where(lane == 0, columns[0], jnp.where(lane == 1, columns[1], columns[2]))
    up[...] = jnp.zeros(up.shape, F32)
    down[...] = jnp.zeros(down.shape, F32)
    for copy in copies[2:]:
        copy.wait()
    up[0:NZ, :] = f_high[:, 1, :]
    up[Z : Z + NZ, :] = f_high[:, 0, :]
    up[2 * Z : 2 * Z + NZ, :] = c_high[:, 0, :]
    down[0:NZ, :] = f_low[:, 0, :]
    down[Z : Z + NZ, :] = f_low[:, 1, :]
    down[2 * Z : 2 * Z + NZ, :] = c_low[:, 0, :]
    first, last = down[0:Z, :], up[0:Z, :]
    tail = flags + corner_rows([col(first, 0), col(first, LANES - 1), col(last, 0), col(last, LANES - 1)])
    up[3 * Z : 3 * Z + 8, :] = tail
    down[3 * Z : 3 * Z + 8, :] = tail


def block_matrix(inv):
    width = 3 * Z
    a, b = iota2(BLK, width)
    b = b % Z
    spread = jnp.where((b % BLK == a) & (b < NZ), 1.0, 0.0).astype(BF16)
    whole = jnp.zeros((NZ, width), F32)
    left = inv
    for _ in range(3):
        part = left.astype(BF16)
        whole = whole + jnp.dot(part, spread, preferred_element_type=F32)
        left = left - part.astype(F32)
    a, b = iota2(NZ, width)
    whole = jnp.where(a // BLK == (b % Z) // BLK, whole, 0.0)
    high = whole.astype(BF16).astype(F32)
    return jnp.where((b >= Z) & (b < 2 * Z), whole - high, high)


def side_kernel(f_in, c_in, inv, vz, own, f, c, w0, w1, w2, w3, one, part, columns, c_next, c_tile, yup, ydown):
    load_top(f_in, f)
    load_top(c_in, c)
    put_y(GEOM[0], f, c, yup, ydown)
    yup[Z : Z + 8, :] = own[...]
    ydown[Z : Z + 8, :] = own[...]
    for level, w in enumerate((w0, w1, w2, w3)):
        w[0:NZ, :] = block_matrix(inv[level])
        w[NZ:Z, :] = jnp.zeros((Z - NZ, 3 * Z), F32)
    winv = w0[...].astype(BF16)
    start_tile(GEOM[0], winv, f, Setter(one))
    relax_tile(GEOM[0], winv, Coef(vz), one, f, c, ALONE, Setter(part))
    columns[...] = own_columns(GEOM[0], one)
    restrict(GEOM[0], GEOM[1], c, c_next)
    restrict(GEOM[1], GEOM[2], c_next, c_tile)


def merge_kernel(level, count):
    geom = GEOM[level]

    def kernel(xlo, xhi, flags, yup, ydown, up, down):
        lo, hi = corner_columns(tail_of(geom, xlo, count)), corner_columns(tail_of(geom, xhi, count))
        up[...] = yup[...]
        down[...] = ydown[...]
        a, b = merge_y(lo, hi, flags, yup[0:Z, :], ydown[0:Z, :])
        up[0:Z, :] = a
        down[0:Z, :] = b

    return kernel


def pre_edges(geom, f, c, w, vz, own, xlo, xhi, ydn, yun, one, columns):
    winv = w[...].astype(BF16)
    fl = flags_of(geom, own, xlo, xhi, ydn, yun)
    halo = messages(geom, xlo, xhi, ydn, yun, winv)
    relaxed = relax_edges(geom, winv, Coef(vz), one, columns[...], halo, fl, *own_data(geom, xlo, xhi, ydn, yun))
    terms = edge_terms(geom, winv, frame(geom, fl, halo.lo, halo.hi, halo.sides()))
    return terms, frame(geom, fl, *relaxed)


def pre0_kernel(f, c, w, vz, own, xlo, xhi, ydn, yun, one, part, columns, c_next, up, down, terms_out, edges_out, v, res, f_next):
    geom, coarse = GEOM[0], GEOM[1]
    terms, edges = pre_edges(geom, f, c, w, vz, own, xlo, xhi, ydn, yun, one, columns)
    for k in range(3):
        terms_out[k] = terms[k]
        edges_out[k] = edges[k]
    co = Coef(vz)
    for m in (*range(5), *range(19, 24)):
        v[m] = with_terms(geom, part[m], terms, m)
    for m in (*range(4), *range(20, 24)):
        res[m] = tile_residual(geom, co, v, f, c, *edges, m)
    restrict(geom, coarse, res, f_next, (0, 1, 10, 11))
    put_x(coarse, f_next, c_next, up, down, own[...])


def mid1_kernel(f, c, part, terms_in, edges_in, vz, w, c_next, own, v, f_next, one, part_next, columns, yup, ydown, res):
    geom, coarse = GEOM[0], GEOM[1]
    co = Coef(vz)
    terms = [terms_in[k] for k in range(3)]
    edges = [edges_in[k] for k in range(3)]
    for m in range(24):
        v[m] = with_terms(geom, part[m], terms, m)
    for m in range(24):
        res[m] = tile_residual(geom, co, v, f, c, *edges, m)
    restrict(geom, coarse, res, f_next)
    put_y(coarse, f_next, c_next, yup, ydown)
    yup[Z : Z + 8, :] = own[...]
    ydown[Z : Z + 8, :] = own[...]
    winv = w[...].astype(BF16)
    start_tile(coarse, winv, f_next, Setter(one))
    relax_tile(coarse, winv, co, one, f_next, c_next, ALONE, Setter(part_next))
    columns[...] = own_columns(coarse, one)


def pre1_kernel(f, c, w, vz, own, xlo, xhi, ydn, yun, one, part, columns, c_tile, v_out, up, down, chunks, res, f_next):
    geom = GEOM[1]
    terms, edges = pre_edges(geom, f, c, w, vz, own, xlo, xhi, ydn, yun, one, columns)
    for m in range(6):
        v_out[m] = with_terms(geom, part[m], terms, m)
    co = Coef(vz)
    for m in range(6):
        res[m] = tile_residual(geom, co, v_out, f, c, *edges, m)
    restrict(geom, GEOM[2], res, f_next)
    put_x(geom, v_out, None, up, down)
    whole = pack(GEOM[2], [f_next[m] for m in range(6)] + [c_tile[m] for m in range(6)])
    turn = lax.rem(lax.axis_index("gx"), 4) * 32
    whole = [pltpu.roll(x, turn, axis=1) for x in whole]
    for t in range(8):
        for k, x in enumerate(whole):
            chunks[t, k * Z : (k + 1) * Z, :] = x
        chunks[t, 3 * Z : 3 * Z + 8, :] = own[...]


def again0_kernel(f, c, w, vz, e, v, g, part, columns, yup, ydown):
    prolong_add(GEOM[0], GEOM[1], e, v, g)
    put_y(GEOM[0], g, None, yup, ydown)
    columns[...] = own_columns(GEOM[0], g)
    relax_tile(GEOM[0], w[...].astype(BF16), Coef(vz), g, f, c, ALONE, Setter(part))


def post_sweeps(geom, f, c, w, vz, own, xlo, xhi, ydn, yun, g, part, columns, glo, ghi, gdn, gun, one, store):
    winv = w[...].astype(BF16)
    co = Coef(vz)
    fl = flags_of(geom, own, xlo, xhi, ydn, yun)
    halo = Halo(
        part_of(geom, glo, 0), part_of(geom, glo, 1), part_of(geom, ghi, 0), part_of(geom, ghi, 1), gdn[...], gun[...]
    )
    relaxed = relax_edges(geom, winv, co, g, columns[...], halo, fl, *own_data(geom, xlo, xhi, ydn, yun))
    add_edges(geom, winv, part, frame(geom, fl, halo.lo, halo.hi, halo.sides()), Setter(one))
    relax_tile(geom, winv, co, one, f, c, frame(geom, fl, *relaxed), store)


def post0_kernel(f, c, w, vz, own, xlo, xhi, ydn, yun, g, part, columns, glo, ghi, gdn, gun, out, one):
    def store(x, value):
        out[pl.ds(x, NZ, stride=24), :] = value[0:NZ, :]

    post_sweeps(GEOM[0], f, c, w, vz, own, xlo, xhi, ydn, yun, g, part, columns, glo, ghi, gdn, gun, one, store)


def post1_kernel(
    f, c, w, vz, own, xlo, xhi, ydn, yun, g, part, columns, glo, ghi, gdn, gun, fine_v, e, up, down, one, fine_g
):
    post_sweeps(GEOM[1], f, c, w, vz, own, xlo, xhi, ydn, yun, g, part, columns, glo, ghi, gdn, gun, one, Setter(e))
    prolong_add(GEOM[0], GEOM[1], e, fine_v, fine_g, (0, 22))
    put_x(GEOM[0], fine_g, None, up, down)


def on_device(right_side, helm_coef, vert_coef, block_inverse, edge_flip):
    inv = block_inverse.reshape(4, NZ, BLK)
    f_in = right_side.reshape(NZ * 24, LANES)
    c_in = helm_coef.reshape(NZ * 24, LANES)
    vert = vert_coef.reshape(1, NZ + 1)
    flip = edge_flip.reshape(1, 4)

    ys = (Z, LANES)
    t0, t1, t2 = tile_shape(0), tile_shape(1), tile_shape(2)
    xs = x_shape(0, 3)
    up, down, own, vz = pl.pallas_call(
        by_swaps(open_kernel, 4, 4, (), ((0, "gx"),)),
        out_shape=[jax.ShapeDtypeStruct(x, F32) for x in (xs, xs, (8, LANES), ys)],
        in_specs=[ANY] * 4,
        out_specs=[VMEM] * 4,
        scratch_shapes=[pltpu.VMEM((NZ, 2, LANES), F32)] * 2
        + [pltpu.VMEM((NZ, 1, LANES), F32)] * 2
        + [pltpu.VMEM((1, NZ + 1), F32), pltpu.VMEM((1, 4), jnp.int32), pltpu.SemaphoreType.DMA((6,))]
        + [pltpu.VMEM(xs, F32)] * 2,
        compiler_params=pltpu.CompilerParams(vmem_limit_bytes=58 * 1024 * 1024),
        name="open",
    )(right_side, helm_coef, vert, flip)
    xlo, xhi = swap(up, down, "gx")
    ws = (Z, 3 * Z)
    f, c, *w, one, part, columns, c1, c_tile, yup, ydown = call(
        side_kernel,
        [t0, t0] + [ws] * 4 + [t0, t0, ys, t1, t2, Y_FULL, Y_FULL],
        [f_in, c_in, inv, vz, own],
        name="side",
    )

    def to_sides(level, count, xlo, xhi, yup, ydown):
        shape = yup.shape
        yup, ydown = call(merge_kernel(level, count), [shape, shape], [xlo, xhi, own, yup, ydown], name=f"merge{level}", got=((0, "gx"),), send=((0, "gy"),))
        return swap(yup, ydown, "gy")

    got0 = (xlo, xhi, *to_sides(0, 3, xlo, xhi, yup, ydown))
    xs = x_shape(1, 3)
    three = (3, Z, LANES)
    up, down, terms, edges = call(
        pre0_kernel,
        [xs, xs, three, three],
        [f, c, w[0], vz, own, *got0, one, part, columns, c1],
        [t0, t0, t1],
        name="pre0",
        got=((5, "gx"), (7, "gy")),
        send=((0, "gx"),),
    )
    xlo, xhi = swap(up, down, "gx")
    v0, f1, one, part, columns, yup, ydown = call(
        mid1_kernel,
        [t0, t1, t1, t1, ys, Y_FULL, Y_FULL],
        [f, c, part, terms, edges, vz, w[1], c1, own],
        [t0],
        name="mid1",
    )
    got1 = (xlo, xhi, *to_sides(1, 3, xlo, xhi, yup, ydown))
    xs = x_shape(1, 2)
    v1, up, down, chunks = call(
        pre1_kernel,
        [t1, xs, xs, (8, 3 * Z + 8, LANES)],
        [f1, c1, w[1], vz, own, *got1, one, part, columns, c_tile],
        [t1, t2],
        name="pre1",
        got=((5, "gx"), (7, "gy")),
        send=((1, "gx"),),
    )
    v1_lo, v1_hi = swap(up, down, "gx")
    chunks = lax.all_to_all(chunks, "gx", 0, 0)
    s2, s3 = (6, Z, 256), (3, Z, 128)
    m2, m3 = (Z, 256), (Z, 128)
    full2, full3 = (Z + 8, 256), (Z + 8, 128)
    f2, c2, fl2, up, down = call(
        open_strip_kernel, [s2, s2, (8, 256), full2, full2], [chunks], name="open2", send=((3, "gy"),)
    )
    side2 = swap(up, down, "gy", True)
    alone = call(alone_kernel(2), [s2, m2, m2], [f2, c2, w[2], vz, fl2], [s2], name="alone2")
    c3, fl3, c_up, c_down = call(next_coef_kernel, [s3, (8, 128), m3, m3], [c2, fl2], name="coef3")
    v2, f3, up, down = call(
        pre_strip_kernel,
        [s2, s3, full3, full3],
        [f2, c2, w[2], vz, fl2, *side2, *alone, fl3, c_up, c_down],
        [s2],
        name="pre2",
        got=((5, "gy"),),
        send=((2, "gy"),),
    )
    side3 = swap(up, down, "gy", True)
    alone = call(alone_kernel(3), [s3, m3, m3], [f3, c3, w[3], vz, fl3], [s3], name="alone3")
    v3, up, down = call(
        bottom_strip_kernel, [s3, m3, m3], [f3, c3, w[3], vz, fl3, *side3, *alone], [s3], name="bottom", got=((5, "gy"),), send=((1, "gy"),)
    )
    side = swap(up, down, "gy", True)
    (part,) = call(again3_kernel, [s3], [f3, c3, w[3], vz, fl3, v3], name="again3")
    base_up, base_down = call(base_message_kernel, [m2, m2], [v2, fl2], name="base2")
    e3, up, down = call(
        last_strip_kernel,
        [s3, m2, m2],
        [w[3], fl3, *side, part, base_up, base_down, v1_lo, v1_hi],
        [m3, m3],
        name="last",
        after=2,
        got=((2, "gy"),),
        send=((1, "gy"),),
    )
    side = swap(up, down, "gy", True)
    g2, *alone, yup, ydown = call(
        again2_kernel, [s2, s2, m2, m2, ys, ys], [f2, c2, w[2], vz, fl2, v2, e3, v1], name="again2"
    )
    e2, up, down = call(
        post_strip_kernel,
        [s2, ys, ys],
        [f2, c2, w[2], vz, fl2, *side2, *alone, *side, v1_lo, v1_hi, own, yup, ydown],
        [s2],
        name="post2",
        got=((5, "gy"), (10, "gy"), (12, "gx")),
        send=((1, "gy"),),
    )
    side = swap(up, down, "gy")
    g1, part, columns, lo, hi = call(
        again1_kernel, [t1, t1, ys, ys, ys], [f1, c1, w[1], vz, v1, e2, v1_lo, v1_hi], [t2], name="again1", got=((6, "gx"),)
    )
    xs = x_shape(0, 2)
    e1, up, down = call(
        post1_kernel,
        [t1, xs, xs],
        [f1, c1, w[1], vz, own, *got1, g1, part, columns, lo, hi, *side, v0],
        [t1, t0],
        name="post1",
        got=((5, "gx"), (7, "gy"), (14, "gy")),
        send=((1, "gx"),),
    )
    xlo, xhi = swap(up, down, "gx")
    g0, part, columns, yup, ydown = call(
        again0_kernel, [t0, t0, ys, ys, ys], [f, c, w[0], vz, e1, v0], name="again0"
    )
    got = (xlo, xhi, *to_sides(0, 2, xlo, xhi, yup, ydown))
    (out,) = call(
        post0_kernel, [(NZ * 24, LANES)], [f, c, w[0], vz, own, *got0, g0, part, columns, *got], [t0], name="post0",
        got=((5, "gx"), (7, "gy"), (12, "gx"), (14, "gy")),
    )
    return out.reshape(NZ, 24, LANES)


def solution(mesh):
    placed = (P(None, "gx", "gy"), P(None, "gx", "gy"), P(), P(), P("gx", "gy", None))
    return jax.shard_map(
        on_device, mesh=mesh, in_specs=placed, out_specs=P(None, "gx", "gy"), check_vma=False
    )
```

```python
import jax
import jax.numpy as jnp
from jax import lax
from jax.experimental import pallas as pl
from jax.experimental.pallas import tpu as pltpu
from jax.sharding import PartitionSpec as P

BLK = 14
NBLK = 5
NZ = 70
Z = 72
LANES = 128
F32 = jnp.float32
BF16 = jnp.bfloat16

GEOM = ((24, 1, 128), (6, 2, 64), (6, 1, 32), (3, 1, 16))


def lane_ids(shape):
    return lax.broadcasted_iota(jnp.int32, shape, len(shape) - 1)


def zl():
    return lane_ids((Z, LANES))


def roll(x, shift):
    shift = shift % x.shape[-1]
    return x if shift == 0 else pltpu.roll(x, shift, axis=1)


def col(x, k):
    return jnp.broadcast_to(x[:, k : k + 1], (Z, LANES))


def iota2(n, m):
    return lax.broadcasted_iota(jnp.int32, (n, m), 0), lax.broadcasted_iota(jnp.int32, (n, m), 1)


def lane_dot(x, mat):
    hi = x.astype(BF16).astype(F32)
    both = jnp.concatenate([hi, x - hi], axis=1).astype(BF16)
    twice = jnp.concatenate([mat, mat], axis=0).astype(BF16)
    return jnp.dot(both, twice, preferred_element_type=F32)


def block_dot(winv, x):
    hi = x.astype(BF16).astype(F32)
    parts = jnp.concatenate([hi, hi, x - hi], axis=0).astype(BF16)
    return jnp.dot(winv, parts, preferred_element_type=F32)


def reverse_matrix(width):
    a, b = iota2(LANES, LANES)
    return jnp.where((b < width) & (a == width - 1 - b), 1.0, 0.0)


def flag_row(flags, k):
    return jnp.broadcast_to(flags[k : k + 1, :], (Z, LANES))


class Coef:
    def __init__(self, ref, width=LANES):
        self.mid = jnp.broadcast_to(ref[:, 0:1], (Z, width))
        self.up = jnp.broadcast_to(ref[:, 1:2], (Z, width))
        self.down = jnp.broadcast_to(ref[:, 2:3], (Z, width))


def residual(co, f, c, v, beside):
    above = pltpu.roll(v, Z - 1, axis=0)
    below = pltpu.roll(v, 1, axis=0)
    return f - (c * 0.0625 + co.mid) * v + beside * 0.0625 + co.up * above + co.down * below


def row_of(geom, v, row):
    m_rows, _, ty = geom
    q, m = divmod(row, m_rows)
    return roll(v[m], -q * ty)


def corners(geom, v):
    m_rows, groups, ty = geom
    last = v[m_rows - 1]
    base = (groups - 1) * ty
    return corner_rows([col(v[0], 0), col(v[0], ty - 1), col(last, base), col(last, base + ty - 1)])


def corner_rows(columns):
    lane = zl()
    out = jnp.zeros((Z, LANES), F32)
    for k, column in enumerate(columns):
        out = jnp.where(lane == 4 + k, column, out)
    return jnp.concatenate([out, jnp.zeros((LANES - Z, LANES), F32)], axis=0).T[0:8, :]


def corner_columns(rows):
    out = jnp.concatenate([rows, jnp.zeros((LANES - 8, LANES), F32)], axis=0).T[0:Z, :]
    return [col(out, 4 + k) for k in range(4)]


def whole_rows(geom):
    return geom[1] == 1 and geom[2] == LANES


def tile_rows(geom):
    m_rows, groups, ty = geom
    return [(q * m_rows + m, m, q * ty) for m in range(m_rows) for q in range(groups)]


def own_columns(geom, v):
    ty = geom[2]
    lane = zl()
    out = jnp.zeros((Z, LANES), F32)
    for r, m, base in tile_rows(geom):
        row = v[m]
        first = roll(row, 2 * r + 1 - base)
        out = jnp.where(lane == 2 * r + 1, first, out)
        last = first if whole_rows(geom) else roll(row, 2 * r - (base + ty - 1))
        out = jnp.where(lane == 2 * r, last, out)
    return out


def pack(geom, parts):
    ty = geom[2]
    per = LANES // ty
    out = []
    for first in range(0, len(parts), per):
        lane = zl()
        acc = parts[first]
        for k, part in enumerate(parts[first + 1 : first + per], 1):
            acc = jnp.where(lane < k * ty, acc, roll(part, k * ty))
        out.append(acc)
    return out


def packed(geom, count):
    per = LANES // geom[2]
    return -(-count // per)


def part_of(geom, ref, k):
    ty = geom[2]
    per = LANES // ty
    return roll(ref[(k // per) * Z : (k // per + 1) * Z, :], -(k % per) * ty)


def put_x(geom, v, c, up, down, flags=None):
    m_rows, groups, _ = geom
    tx = m_rows * groups
    tail = corners(geom, v)
    if flags is not None:
        tail = tail + flags
    for ref, edge, second in ((up, tx - 1, tx - 2), (down, 0, 1)):
        parts = [row_of(geom, v, edge), row_of(geom, v, second)]
        if c is not None:
            parts.append(row_of(geom, c, edge))
        put_parts(geom, parts, tail, ref)


def put_parts(geom, parts, tail, ref):
    whole = pack(geom, parts)
    for k, part in enumerate(whole):
        ref[k * Z : (k + 1) * Z, :] = part
    ref[len(whole) * Z : len(whole) * Z + 8, :] = tail


def tail_of(geom, ref, count):
    n = packed(geom, count) * Z
    return ref[n : n + 8, :]


def put_y(geom, v, c, up, down):
    ty = geom[2]
    lane = zl()
    out_up = jnp.zeros((Z, LANES), F32)
    out_down = out_up
    for r, m, base in tile_rows(geom):
        row = v[m]
        mine = lane // 2 == r
        last = roll(row, 2 * r + 1 - (base + ty - 1))
        first = roll(row, 2 * r - base)
        out_up = jnp.where(mine, last, out_up)
        out_down = jnp.where(mine, first, out_down)
        if c is not None:
            row = c[m]
            out_up = jnp.where(lane == 65 + 2 * r, roll(row, 65 + 2 * r - (base + ty - 1)), out_up)
            out_down = jnp.where(lane == 64 + 2 * r, roll(row, 64 + 2 * r - base), out_down)
    up[0:Z, :] = out_up
    down[0:Z, :] = out_down


def merge_y(lo, hi, flags, up, down):
    lane = zl()
    f0, f1 = flag_row(flags, 0) > 0.5, flag_row(flags, 1) > 0.5

    def fill(part, values):
        for k, value in enumerate(values):
            part = jnp.where(lane == 112 + k, value, part)
        return part

    up_new = fill(up, [lo[3], lo[1], hi[1], hi[3], jnp.where(f0, lo[2], lo[3]), jnp.where(f1, hi[0], hi[1])])
    down_new = fill(down, [lo[2], lo[0], hi[0], hi[2], jnp.where(f0, lo[3], lo[2]), jnp.where(f1, hi[1], hi[0])])
    return up_new, down_new


def odd_lanes():
    return zl() % 2 == 1


class Halo:
    def __init__(self, lo, lo2, hi, hi2, dn, un):
        self.lo, self.lo2, self.hi, self.hi2, self.dn, self.un = lo, lo2, hi, hi2, dn, un

    def sides(self):
        return jnp.where(odd_lanes(), self.dn, self.un)

    def seconds(self):
        return jnp.where(odd_lanes(), roll(self.dn, 1), roll(self.un, -1))


class Flags:
    def __init__(self, own, lo, hi, dn, un):
        self.own, self.lo, self.hi, self.dn, self.un = own, lo, hi, dn, un


def turn_row(geom, row, flag):
    return jnp.where(flag > 0.5, lane_dot(row, reverse_matrix(geom[2])), row)


def turn_sides(geom, sides, flag_dn, flag_un):
    tx = geom[0] * geom[1]
    flag = jnp.where(odd_lanes(), flag_dn, flag_un)
    a, b = iota2(LANES, LANES)
    mat = jnp.where((b < 2 * tx) & (a == 2 * (tx - 1 - b // 2) + b % 2), 1.0, 0.0)
    return jnp.where(flag > 0.5, lane_dot(sides, mat), sides)


def frame(geom, fl, lo, hi, sides):
    return (
        turn_row(geom, lo, flag_row(fl.own, 0)),
        turn_row(geom, hi, flag_row(fl.own, 1)),
        turn_sides(geom, sides, flag_row(fl.own, 2), flag_row(fl.own, 3)),
    )


def relax_edges(geom, winv, co, v, columns, halo, fl, f_lo, c_lo, f_hi, c_hi, f_sides, c_sides):
    m_rows, groups, ty = geom
    tx = m_rows * groups
    lane = zl()
    dn, un = halo.dn, halo.un

    def beside_row(edge, second, mine, low, high):
        left = jnp.where(lane == 0, low, roll(edge, 1))
        right = jnp.where(lane == ty - 1, high, roll(edge, -1))
        return second + mine + left + right

    def choose(flags, k, first, other):
        return jnp.where(flag_row(flags, k) > 0.5, other, first)

    b_lo = beside_row(
        halo.lo,
        halo.lo2,
        turn_row(geom, row_of(geom, v, 0), flag_row(fl.lo, 1)),
        choose(fl.lo, 2, col(dn, 112), col(dn, 113)),
        choose(fl.lo, 3, col(un, 112), col(un, 113)),
    )
    b_hi = beside_row(
        halo.hi,
        halo.hi2,
        turn_row(geom, row_of(geom, v, tx - 1), flag_row(fl.hi, 0)),
        choose(fl.hi, 2, col(dn, 114), col(dn, 115)),
        choose(fl.hi, 3, col(un, 114), col(un, 115)),
    )
    edge = halo.sides()
    mine = turn_sides(geom, columns, flag_row(fl.dn, 3), flag_row(fl.un, 2))
    below = jnp.where(lane == 1, col(dn, 116), jnp.where(lane == 0, col(un, 116), roll(edge, 2)))
    last = 2 * (tx - 1)
    above = jnp.where(lane == last + 1, col(dn, 117), jnp.where(lane == last, col(un, 117), roll(edge, -2)))
    b_sides = halo.seconds() + mine + below + above
    r_lo = residual(co, f_lo, c_lo, halo.lo, b_lo)
    r_hi = residual(co, f_hi, c_hi, halo.hi, b_hi)
    r_sides = residual(co, f_sides, c_sides, edge, b_sides)
    d = block_dot(winv, jnp.concatenate([r_lo, r_hi, r_sides], axis=1))
    return halo.lo + d[:, :LANES], halo.hi + d[:, LANES : 2 * LANES], edge + d[:, 2 * LANES :]


def tile_residual(geom, co, v, f, c, lo, hi, sides, m):
    m_rows, groups, ty = geom
    lane = zl()
    here = v[m]
    if lo is None:
        lo = hi = jnp.zeros((Z, LANES), F32)
    if m > 0:
        low_x = v[m - 1]
    else:
        low_x = lo if groups == 1 else jnp.where(lane < ty, lo, roll(v[m_rows - 1], ty))
    if m < m_rows - 1:
        high_x = v[m + 1]
    elif groups == 1:
        high_x = hi
    else:
        high_x = jnp.where(lane < (groups - 1) * ty, roll(v[0], -ty), roll(hi, (groups - 1) * ty))
    low_y, high_y = roll(here, 1), roll(here, -1)
    if sides is None:
        low_y = jnp.where(lane % ty == 0, 0.0, low_y)
        high_y = jnp.where(lane % ty == ty - 1, 0.0, high_y)
        return residual(co, f[m], c[m], here, low_x + high_x + low_y + high_y)
    for q in range(groups):
        row = q * m_rows + m
        low = roll(sides, q * ty - 2 * row - 1)
        high = low if whole_rows(geom) else roll(sides, q * ty + ty - 1 - 2 * row)
        low_y = jnp.where(lane == q * ty, low, low_y)
        high_y = jnp.where(lane == q * ty + ty - 1, high, high_y)
    return residual(co, f[m], c[m], here, low_x + high_x + low_y + high_y)


def relax_tile(geom, winv, co, v, f, c, edges, store):
    lo, hi, sides = edges
    for m in range(0, geom[0], 2):
        rows = [k for k in (m, m + 1) if k < geom[0]]
        r = [tile_residual(geom, co, v, f, c, lo, hi, sides, k) for k in rows]
        d = block_dot(winv, r[0] if len(r) == 1 else jnp.concatenate(r, axis=1))
        for i, k in enumerate(rows):
            store(k, v[k] + d[:, i * LANES : (i + 1) * LANES])


ALONE = (None, None, None)


def edge_terms(geom, winv, edges):
    ty = geom[2]
    lane = zl()
    d = block_dot(winv, jnp.concatenate(edges, axis=1) * 0.0625)
    low, high, sides = [d[:, k * LANES : (k + 1) * LANES] for k in range(3)]
    if ty < LANES:
        low = jnp.where(lane < ty, low, 0.0)
        high = jnp.where(lane < ty, high, 0.0)
    return low, high, sides


def with_terms(geom, x, terms, m):
    m_rows, groups, ty = geom
    low, high, sides = terms
    lane = zl()
    if m == 0:
        x = x + low
    if m == m_rows - 1:
        x = x + roll(high, (groups - 1) * ty)
    for q in range(groups):
        row = q * m_rows + m
        first = roll(sides, q * ty - 2 * row - 1)
        last = first if whole_rows(geom) else roll(sides, q * ty + ty - 1 - 2 * row)
        x = x + jnp.where(lane == q * ty, first, jnp.where(lane == q * ty + ty - 1, last, 0.0))
    return x


def add_edges(geom, winv, part, edges, store):
    terms = edge_terms(geom, winv, edges)
    for m in range(geom[0]):
        store(m, with_terms(geom, part[m], terms, m))


def start_tile(geom, winv, f, store):
    for m in range(0, geom[0], 2):
        rows = [k for k in (m, m + 1) if k < geom[0]]
        parts = [f[k] for k in rows]
        d = block_dot(winv, parts[0] if len(parts) == 1 else jnp.concatenate(parts, axis=1))
        for i, k in enumerate(rows):
            store(k, d[:, i * LANES : (i + 1) * LANES])


def restrict(fine, coarse, v, out, wanted=None):
    m_rows, _, ty = fine
    cm, cq, cty = coarse
    a, b = iota2(LANES, LANES)
    for mc in range(cm):
        acc = None
        for qc in range(cq):
            if wanted is not None and qc * cm + mc not in wanted:
                continue
            q, m = divmod(2 * (qc * cm + mc), m_rows)
            inside = (b >= qc * cty) & (b < (qc + 1) * cty) & (a // 2 == b - qc * cty + q * (ty // 2))
            term = lane_dot(v[m] + v[m + 1], jnp.where(inside, 0.25, 0.0))
            acc = term if acc is None else acc + term
        if acc is not None:
            out[mc] = acc


def prolong_add(fine, coarse, e, v, out, rows=None):
    m_rows, groups, ty = fine
    cm, _, cty = coarse
    a, b = iota2(LANES, LANES)
    for m in range(0, m_rows, 2) if rows is None else rows:
        acc = None
        for q in range(groups):
            qc, mc = divmod((q * m_rows + m) // 2, cm)
            inside = (b >= q * ty) & (b < (q + 1) * ty) & (a - qc * cty == (b - q * ty) // 2)
            term = lane_dot(e[mc], jnp.where(inside, 1.0, 0.0))
            acc = term if acc is None else acc + term
        out[m] = v[m] + acc
        out[m + 1] = v[m + 1] + acc


class Setter:
    def __init__(self, ref):
        self.ref = ref

    def __call__(self, m, value):
        self.ref[m] = value


def messages(geom, xlo, xhi, ydn, yun, winv):
    raw = [part_of(geom, xlo, 0), part_of(geom, xlo, 1), part_of(geom, xhi, 0), part_of(geom, xhi, 1), ydn[0:Z, :], yun[0:Z, :]]
    d = block_dot(winv, jnp.concatenate(raw, axis=1))
    return Halo(*[d[:, k * LANES : (k + 1) * LANES] for k in range(6)])


def own_data(geom, xlo, xhi, ydn, yun):
    dn, un = ydn[0:Z, :], yun[0:Z, :]
    f_sides = jnp.where(odd_lanes(), dn, un)
    c_sides = roll(f_sides, -64)
    return (
        part_of(geom, xlo, 0),
        part_of(geom, xlo, 2),
        part_of(geom, xhi, 0),
        part_of(geom, xhi, 2),
        f_sides,
        c_sides,
    )


def flags_of(geom, own, xlo, xhi, ydn, yun):
    return Flags(own[...], tail_of(geom, xlo, 3), tail_of(geom, xhi, 3), ydn[Z : Z + 8, :], yun[Z : Z + 8, :])


def load_top(src, dst):
    for x in range(24):
        dst[x, 0:NZ, :] = src[pl.ds(x, NZ, stride=24), :]
        dst[x, NZ:Z, :] = jnp.zeros((Z - NZ, LANES), F32)


STRIPS = {2: (6, 32, 256), 3: (3, 16, 128)}


def in_tile(strip):
    _, ty, width = strip
    return lane_ids((Z, width)) % ty


def group_dot(x, mat):
    parts = [lane_dot(x[:, k : k + LANES], mat) for k in range(0, x.shape[1], LANES)]
    return parts[0] if len(parts) == 1 else jnp.concatenate(parts, axis=1)


def turn_groups(strip, x, flags, k, count):
    _, ty, width = strip
    a, b = iota2(LANES, LANES)
    mat = jnp.where((a // ty == b // ty) & (b % ty < count) & (a % ty == count - 1 - b % ty), 1.0, 0.0)
    flag = jnp.broadcast_to(flags[k : k + 1, :], (Z, width))
    return jnp.where(flag > 0.5, group_dot(x, mat), x)


def strip_ends(strip, v, flags):
    m_rows, ty, _ = strip
    low = turn_groups(strip, roll(v[m_rows - 1], ty), flags, 0, ty)
    high = turn_groups(strip, roll(v[0], -ty), flags, 1, ty)
    return low, high


def strip_column(strip, v, y, offset, out):
    lt = in_tile(strip)
    for m in range(strip[0]):
        out = jnp.where(lt == offset + m, roll(v[m], offset + m - y), out)
    return out


def strip_message(strip, v, c, ends, up, down):
    m_rows, ty, width = strip
    lt = in_tile(strip)
    for ref, edge, second in ((up, ty - 1, ty - 2), (down, 0, 1)):
        out = strip_column(strip, v, edge, 0, jnp.zeros((Z, width), F32))
        out = strip_column(strip, v, second, m_rows, out)
        if c is not None:
            out = strip_column(strip, c, edge, 2 * m_rows, out)
        for k, end in enumerate(ends):
            out = jnp.where(lt == 3 * m_rows + k, roll(end, 3 * m_rows + k - edge), out)
        ref[0:Z, :] = out


def strip_edges(strip, winv, co, sides):
    m_rows, _, width = strip
    lt = in_tile(strip)
    r = []
    for x, raw, flags, k, mine in sides:
        mine = turn_groups(strip, mine, flags, k, m_rows)
        low = jnp.where(lt == 0, roll(x, -3 * m_rows), roll(x, 1))
        high = jnp.where(lt == m_rows - 1, roll(x, -2 * m_rows - 2), roll(x, -1))
        r.append(residual(co, raw, roll(raw, -2 * m_rows), x, roll(x, -m_rows) + mine + low + high))
    d = block_dot(winv, jnp.concatenate(r, axis=1))
    return [side[0] + d[:, k * width : (k + 1) * width] for k, side in enumerate(sides)]


def strip_frame(strip, flags, low, high):
    return turn_groups(strip, low, flags, 2, strip[0]), turn_groups(strip, high, flags, 3, strip[0])


def strip_residual(strip, co, v, f, c, ends, sides, m):
    m_rows, ty, _ = strip
    lt = in_tile(strip)
    low_x = v[m - 1] if m > 0 else ends[0]
    high_x = v[m + 1] if m < m_rows - 1 else ends[1]
    low = 0.0 if sides is None else roll(sides[0], -m)
    high = 0.0 if sides is None else roll(sides[1], ty - 1 - m)
    low_y = jnp.where(lt == 0, low, roll(v[m], 1))
    high_y = jnp.where(lt == ty - 1, high, roll(v[m], -1))
    return residual(co, f[m], c[m], v[m], low_x + high_x + low_y + high_y)


def strip_relax(strip, winv, co, v, f, c, flags, sides, store):
    ends = strip_ends(strip, v, flags)
    for m in range(strip[0]):
        r = strip_residual(strip, co, v, f, c, ends, sides, m)
        store(m, v[m] + block_dot(winv, r))


def strip_add_sides(strip, winv, part, sides, store):
    m_rows, ty, width = strip
    lt = in_tile(strip)
    d = block_dot(winv, jnp.concatenate(sides, axis=1) * 0.0625)
    for m in range(m_rows):
        low, high = roll(d[:, :width], -m), roll(d[:, width:], ty - 1 - m)
        store(m, part[m] + jnp.where(lt == 0, low, jnp.where(lt == ty - 1, high, 0.0)))


def strip_side_terms(strip, winv, co, flags, c_columns, sides, sides_next):
    m_rows, ty, width = strip
    lt = in_tile(strip)
    d = block_dot(winv, jnp.concatenate(sides, axis=1) * 0.0625)
    first, last = d[:, :width], d[:, width:]
    turned = [jnp.broadcast_to(flags[k : k + 1, :], (Z, width)) > 0.5 for k in range(2)]
    step = ty - m_rows + 1
    r = []
    for mine, other, c, beyond in ((first, last, c_columns[0], sides_next[0]), (last, first, c_columns[1], sides_next[1])):
        low = jnp.where(turned[0], roll(other, step), roll(mine, step))
        high = jnp.where(turned[1], roll(other, -step), roll(mine, -step))
        low = jnp.where(lt == 0, low, roll(mine, 1))
        high = jnp.where(lt == m_rows - 1, high, roll(mine, -1))
        r.append(residual(co, beyond * 0.0625, c, mine, low + high))
    return first, last, r


def strip_restrict(v, out):
    a, b = iota2(LANES, LANES)
    for m in range(3):
        both = v[2 * m] + v[2 * m + 1]
        out[m] = lane_dot(both[:, :LANES], jnp.where(a // 2 == b, 0.25, 0.0)) + lane_dot(
            both[:, LANES:], jnp.where(a // 2 == b - 64, 0.25, 0.0)
        )


def open_strip_kernel(chunks, f, c, flags, up, down):
    strip = STRIPS[2]
    group = lane_ids((Z, LANES)) // 32
    for m in range(6):
        for ref, k in ((f, m), (c, 6 + m)):
            part = (k // 4) * Z
            halves = []
            for h in range(2):
                acc = None
                for g in range(4):
                    x = chunks[4 * h + g, part : part + Z, :]
                    acc = x if acc is None else jnp.where(group == (g + k) % 4, x, acc)
                halves.append(roll(acc, -(k % 4) * 32))
            ref[m] = jnp.concatenate(halves, axis=1)
    group = lane_ids((8, LANES)) // 32
    for h in range(2):
        acc = None
        for g in range(4):
            x = chunks[4 * h + g, 3 * Z : 3 * Z + 8, :]
            acc = x if acc is None else jnp.where(group == g, x, acc)
        flags[:, h * LANES : (h + 1) * LANES] = acc
    strip_message(strip, f, c, strip_ends(strip, f, flags), up, down)
    up[Z : Z + 8, :] = flags[...]
    down[Z : Z + 8, :] = flags[...]


def strip_sides(values, raws, dn, un, first, last):
    return (
        (values[0], raws[0], dn[Z : Z + 8, :], 3, first[...]),
        (values[1], raws[1], un[Z : Z + 8, :], 2, last[...]),
    )


def column_restrict(strip, x):
    a, b = iota2(LANES, LANES)
    out = None
    for h in range(2):
        inside = (b // 16 == 4 * h + a // 32) & ((a % 32) // 2 == b % 16) & (a % 32 < strip[0])
        term = lane_dot(x[:, h * LANES : (h + 1) * LANES], jnp.where(inside, 0.25, 0.0))
        out = term if out is None else out + term
    return out


def pre_strip_kernel(
    w, vz, flags, dn, un, first_column, last_column, c_low, c_high, f_part, fl_next, base_up, base_down, terms, f_next, up, down
):
    strip, small = STRIPS[2], STRIPS[3]
    winv = w[...].astype(BF16)
    co = Coef(vz, strip[2])
    raws = [dn[0:Z, :], un[0:Z, :]]
    values = block_dot(winv, jnp.concatenate(raws, axis=1))
    values = [values[:, : strip[2]], values[:, strip[2] :]]
    edges = strip_edges(strip, winv, co, strip_sides(values, raws, dn, un, first_column, last_column))
    first, last, r = strip_side_terms(
        strip, winv, co, flags, (c_low[...], c_high[...]), strip_frame(strip, flags, *values), strip_frame(strip, flags, *edges)
    )
    terms[0] = first
    terms[1] = last
    low = column_restrict(strip, r[0] + first * 0.0625)
    high = column_restrict(strip, r[1] + last * 0.0625)
    m_rows, ty, width = small
    lt = in_tile(small)
    for m in range(m_rows):
        x = jnp.where(lt == 0, roll(low, -m), 0.0)
        f_next[m] = f_part[m] + jnp.where(lt == ty - 1, roll(high, ty - 1 - m), x)
    turned = [jnp.broadcast_to(fl_next[k : k + 1, :], (Z, width)) > 0.5 for k in range(2)]
    for ref, base, mine, other in ((up, base_up, high, low), (down, base_down, low, high)):
        before, after = 3 * m_rows + ty - m_rows + 1, 3 * m_rows + 1 - ty
        end_low = jnp.where(turned[0], roll(other, before), roll(mine, before))
        end_high = jnp.where(turned[1], roll(other, after), roll(mine, after))
        add = jnp.where(lt < m_rows, mine, 0.0)
        add = jnp.where(lt == 3 * m_rows, end_low, add)
        add = jnp.where(lt == 3 * m_rows + 1, end_high, add)
        ref[0:Z, :] = base[...] + add
        ref[Z : Z + 8, :] = fl_next[...]


def next_coef_kernel(c, flags, c_next, fl_next, low, high, low_next, high_next):
    strip_restrict(c, c_next)
    a, b = iota2(LANES, LANES)
    fl_next[...] = lane_dot(flags[:, :LANES], jnp.where((b < 64) & (a == (b // 16) * 32), 1.0, 0.0)) + lane_dot(
        flags[:, LANES:], jnp.where((b >= 64) & (a == (b // 16 - 4) * 32), 1.0, 0.0)
    )
    for strip, ref, first, last in ((STRIPS[2], c, low, high), (STRIPS[3], c_next, low_next, high_next)):
        zero = jnp.zeros((Z, strip[2]), F32)
        first[...] = strip_column(strip, ref, 0, 0, zero)
        last[...] = strip_column(strip, ref, strip[1] - 1, 0, zero)


def alone2_kernel(f, c, w, vz, flags, c_next, fl_next, part, low, high, f_part, up, down, v, res):
    strip, small = STRIPS[2], STRIPS[3]
    winv = w[...].astype(BF16)
    co = Coef(vz, strip[2])
    for m in range(6):
        v[m] = block_dot(winv, f[m])
    zero = jnp.zeros((Z, strip[2]), F32)
    low[...] = strip_column(strip, v, 0, 0, zero)
    high[...] = strip_column(strip, v, strip[1] - 1, 0, zero)
    strip_relax(strip, winv, co, v, f, c, flags, None, Setter(part))
    ends = strip_ends(strip, part, flags)
    for m in range(6):
        res[m] = strip_residual(strip, co, part, f, c, ends, None, m)
    strip_restrict(res, f_part)
    strip_message(small, f_part, c_next, strip_ends(small, f_part, fl_next), up, down)


def bottom_strip_kernel(
    w, vz, flags, dn, un, first_column, last_column, c_low, c_high, part_low, part_high, terms, up, down
):
    strip = STRIPS[3]
    width = strip[2]
    winv = w[...].astype(BF16)
    co = Coef(vz)
    raws = [dn[0:Z, :], un[0:Z, :]]
    values = block_dot(winv, jnp.concatenate(raws, axis=1))
    values = [values[:, :width], values[:, width:]]
    edges = strip_edges(strip, winv, co, strip_sides(values, raws, dn, un, first_column, last_column))
    first, last, r = strip_side_terms(
        strip, winv, co, flags, (c_low[...], c_high[...]), strip_frame(strip, flags, *values), strip_frame(strip, flags, *edges)
    )
    d = block_dot(winv, jnp.concatenate([r[0], first * 0.0625, last * 0.0625, r[1]], axis=1))
    d = [d[:, k * width : (k + 1) * width] for k in range(4)]
    d[0] = first + d[0]
    d[3] = last + d[3]
    for k in range(4):
        terms[k] = d[k]
    up[...] = part_high[...] + d[3]
    down[...] = part_low[...] + d[0]


def with_columns(strip, x, terms, m):
    ty = strip[1]
    lt = in_tile(strip)
    for k, y in enumerate((0, 1, ty - 2, ty - 1)):
        x = x + jnp.where(lt == y, roll(terms[k], y - m), 0.0)
    return x


def last_strip_kernel(w, flags, dn, un, part, base_up, base_down, _lo, _hi, e, up, down, small_up, small_down):
    strip, fine = STRIPS[3], STRIPS[2]
    winv = w[...].astype(BF16)
    strip_add_sides(strip, winv, part, strip_frame(strip, flags, dn[...], un[...]), Setter(e))
    strip_message(strip, e, None, strip_ends(strip, e, flags), small_up, small_down)
    a, b = iota2(LANES, LANES)
    for h in range(2):
        lt = b % 32
        source = jnp.where(lt < 12, (lt % 6) // 2, jnp.where((lt == 18) | (lt == 19), lt - 9, 15))
        spread = jnp.where((lt != 15) & (a == 64 * h + (b // 32) * 16 + source) & (source < 15), 1.0, 0.0)
        half = slice(h * LANES, (h + 1) * LANES)
        up[:, half] = base_up[:, half] + lane_dot(small_up[...], spread)
        down[:, half] = base_down[:, half] + lane_dot(small_down[...], spread)


def base_message_kernel(part, flags, terms, v, up, down):
    strip = STRIPS[2]
    lt = in_tile(strip)
    for m in range(6):
        x = jnp.where(lt == 0, roll(terms[0], -m), 0.0)
        v[m] = part[m] + jnp.where(lt == strip[1] - 1, roll(terms[1], strip[1] - 1 - m), x)
    strip_message(strip, v, None, strip_ends(strip, v, flags), up, down)


def again2_kernel(f, c, w, vz, flags, v, e, tile_v, low, high, part_low, part_high, yup, ydown, twice, g, part):
    strip = STRIPS[2]
    a, b = iota2(LANES, LANES)
    for m in range(3):
        add = jnp.concatenate([lane_dot(e[m], jnp.where(a == 64 * h + b // 2, 1.0, 0.0)) for h in range(2)], axis=1)
        g[2 * m] = v[2 * m] + add
        g[2 * m + 1] = v[2 * m + 1] + add
    zero = jnp.zeros((Z, strip[2]), F32)
    low[...] = strip_column(strip, g, 0, 0, zero)
    high[...] = strip_column(strip, g, strip[1] - 1, 0, zero)
    winv = w[...].astype(BF16)
    co = Coef(vz, strip[2])
    strip_relax(strip, winv, co, g, f, c, flags, None, Setter(part))
    strip_relax(strip, winv, co, part, f, c, flags, None, Setter(twice))
    part_low[...] = strip_column(strip, twice, 0, 0, zero)
    part_high[...] = strip_column(strip, twice, strip[1] - 1, 0, zero)
    put_y(GEOM[1], tile_v, None, yup, ydown)


def alone3_kernel(f, c, w, vz, flags, low, high, part_low, part_high, twice, v, part):
    strip = STRIPS[3]
    winv = w[...].astype(BF16)
    co = Coef(vz)
    for m in range(3):
        v[m] = block_dot(winv, f[m])
    strip_relax(strip, winv, co, v, f, c, flags, None, Setter(part))
    strip_relax(strip, winv, co, part, f, c, flags, None, Setter(twice))
    zero = jnp.zeros((Z, LANES), F32)
    for ref, first, last in ((v, low, high), (twice, part_low, part_high)):
        first[...] = strip_column(strip, ref, 0, 0, zero)
        last[...] = strip_column(strip, ref, strip[1] - 1, 0, zero)


def again3_kernel(f, c, w, vz, flags, twice, terms, part, v):
    strip = STRIPS[3]
    for m in range(3):
        v[m] = with_columns(strip, twice[m], terms, m)
    strip_relax(strip, w[...].astype(BF16), Coef(vz), v, f, c, flags, None, Setter(part))


def tile_lanes(x, step):
    t = lax.rem(lax.axis_index("gx") + (step + 8), 8)
    half = jnp.where(t < 4, x[:, :LANES], x[:, LANES:])
    return pltpu.roll(half, lax.rem(8 - t, 4) * 32, axis=1)


def post_strip_kernel(
    w, vz, flags, dn, un, first_column, last_column, c_low, c_high, part_low, part_high, gdn, gun, xlo, xhi, own, yup, ydown, terms, up, down
):
    strip = STRIPS[2]
    fine = GEOM[1]
    width = strip[2]
    winv = w[...].astype(BF16)
    co = Coef(vz, width)
    raws = [dn[0:Z, :], un[0:Z, :]]
    values = [gdn[...], gun[...]]
    edges = strip_edges(strip, winv, co, strip_sides(values, raws, dn, un, first_column, last_column))
    first, last, r = strip_side_terms(
        strip, winv, co, flags, (c_low[...], c_high[...]), strip_frame(strip, flags, *values), strip_frame(strip, flags, *edges)
    )
    d = block_dot(winv, jnp.concatenate([r[0], first * 0.0625, last * 0.0625, r[1]], axis=1))
    d = [d[:, k * width : (k + 1) * width] for k in range(4)]
    d[0] = first + d[0]
    d[3] = last + d[3]
    for k in range(4):
        terms[k] = d[k]
    low, high = part_low[...] + d[0], part_high[...] + d[3]
    extras = []
    for ref, step in ((xlo, -1), (xhi, 1)):
        near, far = tile_lanes(low, step), tile_lanes(high, step)
        adds = (col(near, 0), col(far, 0), col(near, 5), col(far, 5))
        extras.append([x + y for x, y in zip(corner_columns(tail_of(fine, ref, 2)), adds)])
    group = zl() // 4
    near, far = tile_lanes(low, 0), tile_lanes(high, 0)
    add_up = add_down = jnp.zeros((Z, LANES), F32)
    for m in range(6):
        add_up = jnp.where(group == m, col(far, m), add_up)
        add_down = jnp.where(group == m, col(near, m), add_down)
    up[...], down[...] = merge_y(*extras, own, yup[...] + add_up, ydown[...] + add_down)


def again1_kernel(f, c, w, vz, v, twice, terms, xlo, xhi, g, part, columns, lo_out, hi_out, tile):
    fine, geom = GEOM[1], GEOM[2]
    rows = []
    for m in range(6):
        rows.append(with_columns(STRIPS[2], twice[m], terms, m))
        tile[m] = tile_lanes(rows[m], 0)
    prolong_add(fine, geom, tile, v, g)
    a, b = iota2(LANES, LANES)
    spread = jnp.where((b < 64) & (a == b // 2), 1.0, 0.0)
    for ref, out, row in ((xlo, lo_out, tile_lanes(rows[5], -1)), (xhi, hi_out, tile_lanes(rows[0], 1))):
        add = lane_dot(row, spread)
        out[...] = pack(fine, [part_of(fine, ref, 0) + add, part_of(fine, ref, 1) + add])[0]
    columns[...] = own_columns(fine, g)
    relax_tile(fine, w[...].astype(BF16), Coef(vz), g, f, c, ALONE, Setter(part))


def swap_pairs(axis, which, nearest=False):
    sizes = lax.axis_size("gx"), lax.axis_size("gy")
    out = []
    for i in range(sizes[0]):
        for j in range(sizes[1]):
            at = [i, j]
            dim = 0 if axis == "gx" else 1
            n = sizes[dim]
            at[dim] = (at[dim] ^ 1) if which == 0 else (at[dim] + (1 if at[dim] % 2 else n - 1)) % n
            if nearest and 2 * j // n != 2 * at[1] // n:
                at[0] = i ^ 1
            out.append((i * sizes[1] + j, at[0] * sizes[1] + at[1]))
    return out


def swap(first, second, axis, nearest=False):
    both = ("gx", "gy")
    return (
        lax.ppermute(first, both, swap_pairs(axis, 0, nearest)),
        lax.ppermute(second, both, swap_pairs(axis, 1, nearest)),
    )


ANY = pl.BlockSpec(memory_space=pl.ANY)
LIMIT = 14 * 1024 * 1024
VMEM = pl.BlockSpec(memory_space=pltpu.VMEM)


class Either:
    def __init__(self, first, a, b):
        self.first, self.a, self.b = first, a, b

    def __getitem__(self, index):
        return jnp.where(self.first, self.a[index], self.b[index])


def is_even(axis):
    return lax.rem(lax.axis_index(axis), 2) == 0


def by_swaps(kernel, n_in, n_out, got, send):
    def wrapped(*refs):
        refs = list(refs)
        for place, axis in got:
            a, b = refs[place], refs[place + 1]
            refs[place], refs[place + 1] = Either(is_even(axis), b, a), Either(is_even(axis), a, b)
        extra = refs[len(refs) - 2 * len(send) :]
        refs = refs[: len(refs) - 2 * len(send)]
        outs = []
        for k, (place, axis) in enumerate(send):
            place += n_in
            outs.append((refs[place], refs[place + 1], extra[2 * k], extra[2 * k + 1], axis))
            refs[place], refs[place + 1] = extra[2 * k], extra[2 * k + 1]
        kernel(*refs)
        for first, second, up, down, axis in outs:
            even = is_even(axis)
            up, down = up[...], down[...]
            first[...] = jnp.where(even, up, down)
            second[...] = jnp.where(even, down, up)

    return wrapped


def call(kernel, outs, args, scratch=(), name=None, after=0, got=(), send=()):
    scratch = [pltpu.VMEM(s, F32) for s in scratch]
    scratch += [pltpu.VMEM(outs[place], F32) for place, _ in send for _ in range(2)]
    return pl.pallas_call(
        by_swaps(kernel, len(args), len(outs), got, send),
        out_shape=[jax.ShapeDtypeStruct(s, F32) for s in outs],
        in_specs=[VMEM] * (len(args) - after) + [ANY] * after,
        out_specs=[VMEM] * len(outs),
        scratch_shapes=scratch,
        compiler_params=pltpu.CompilerParams(vmem_limit_bytes=LIMIT),
        name=name,
    )(*args)


def tile_shape(level):
    return (GEOM[level][0], Z, LANES)


def x_shape(level, count):
    return (packed(GEOM[level], count) * Z + 8, LANES)


Y_FULL = (Z + 8, LANES)


def open_kernel(f_in, c_in, vert_in, flip_in, up, down, own, vz, f_low, f_high, c_low, c_high, vert, flip, sems):
    pairs = (
        (vert_in, vert),
        (flip_in, flip),
        (f_in.at[:, 0:2, :], f_low),
        (f_in.at[:, 22:24, :], f_high),
        (c_in.at[:, 0:1, :], c_low),
        (c_in.at[:, 23:24, :], c_high),
    )
    copies = [pltpu.make_async_copy(src, dst, sems.at[k]) for k, (src, dst) in enumerate(pairs)]
    for copy in copies:
        copy.start()
    for copy in copies[:2]:
        copy.wait()
    a, b = iota2(8, 4)
    flags = jnp.broadcast_to(flip[...].astype(F32), (8, 4))
    flags = jnp.broadcast_to(jnp.sum(jnp.where(a == b, flags, 0.0), axis=1, keepdims=True), (8, LANES))
    own[...] = flags
    a, b = iota2(Z, NZ + 1)
    coef = jnp.broadcast_to(vert[...], (Z, NZ + 1))
    high = jnp.sum(jnp.where((b == a + 1) & (a < NZ), coef, 0.0), axis=1, keepdims=True)
    low = jnp.sum(jnp.where((b == a) & (a < NZ), coef, 0.0), axis=1, keepdims=True)
    columns = [jnp.broadcast_to(x * 0.0625, (Z, LANES)) for x in (4.0 + high + low, high, low)]
    lane = zl()
    vz[...] = jnp.where(lane == 0, columns[0], jnp.where(lane == 1, columns[1], columns[2]))
    up[...] = jnp.zeros(up.shape, F32)
    down[...] = jnp.zeros(down.shape, F32)
    for copy in copies[2:]:
        copy.wait()
    up[0:NZ, :] = f_high[:, 1, :]
    up[Z : Z + NZ, :] = f_high[:, 0, :]
    up[2 * Z : 2 * Z + NZ, :] = c_high[:, 0, :]
    down[0:NZ, :] = f_low[:, 0, :]
    down[Z : Z + NZ, :] = f_low[:, 1, :]
    down[2 * Z : 2 * Z + NZ, :] = c_low[:, 0, :]
    first, last = down[0:Z, :], up[0:Z, :]
    tail = flags + corner_rows([col(first, 0), col(first, LANES - 1), col(last, 0), col(last, LANES - 1)])
    up[3 * Z : 3 * Z + 8, :] = tail
    down[3 * Z : 3 * Z + 8, :] = tail


def block_matrix(inv):
    width = 3 * Z
    a, b = iota2(BLK, width)
    b = b % Z
    spread = jnp.where((b % BLK == a) & (b < NZ), 1.0, 0.0).astype(BF16)
    whole = jnp.zeros((NZ, width), F32)
    left = inv
    for _ in range(3):
        part = left.astype(BF16)
        whole = whole + jnp.dot(part, spread, preferred_element_type=F32)
        left = left - part.astype(F32)
    a, b = iota2(NZ, width)
    whole = jnp.where(a // BLK == (b % Z) // BLK, whole, 0.0)
    high = whole.astype(BF16).astype(F32)
    return jnp.where((b >= Z) & (b < 2 * Z), whole - high, high)


def side_kernel(f_in, c_in, inv, vz, own, f, c, w0, w1, w2, w3, one, part, columns, c_next, c_tile, yup, ydown):
    load_top(f_in, f)
    load_top(c_in, c)
    put_y(GEOM[0], f, c, yup, ydown)
    yup[Z : Z + 8, :] = own[...]
    ydown[Z : Z + 8, :] = own[...]
    for level, w in enumerate((w0, w1, w2, w3)):
        w[0:NZ, :] = block_matrix(inv[level])
        w[NZ:Z, :] = jnp.zeros((Z - NZ, 3 * Z), F32)
    winv = w0[...].astype(BF16)
    start_tile(GEOM[0], winv, f, Setter(one))
    relax_tile(GEOM[0], winv, Coef(vz), one, f, c, ALONE, Setter(part))
    columns[...] = own_columns(GEOM[0], one)
    restrict(GEOM[0], GEOM[1], c, c_next)
    restrict(GEOM[1], GEOM[2], c_next, c_tile)


def merge_kernel(level, count):
    geom = GEOM[level]

    def kernel(xlo, xhi, flags, yup, ydown, up, down):
        lo, hi = corner_columns(tail_of(geom, xlo, count)), corner_columns(tail_of(geom, xhi, count))
        up[...] = yup[...]
        down[...] = ydown[...]
        a, b = merge_y(lo, hi, flags, yup[0:Z, :], ydown[0:Z, :])
        up[0:Z, :] = a
        down[0:Z, :] = b

    return kernel


def pre_edges(geom, f, c, w, vz, own, xlo, xhi, ydn, yun, one, columns):
    winv = w[...].astype(BF16)
    fl = flags_of(geom, own, xlo, xhi, ydn, yun)
    halo = messages(geom, xlo, xhi, ydn, yun, winv)
    relaxed = relax_edges(geom, winv, Coef(vz), one, columns[...], halo, fl, *own_data(geom, xlo, xhi, ydn, yun))
    terms = edge_terms(geom, winv, frame(geom, fl, halo.lo, halo.hi, halo.sides()))
    return terms, frame(geom, fl, *relaxed)


def pre0_kernel(f, c, w, vz, own, xlo, xhi, ydn, yun, one, part, columns, c_next, up, down, terms_out, edges_out, v, res, f_next):
    geom, coarse = GEOM[0], GEOM[1]
    terms, edges = pre_edges(geom, f, c, w, vz, own, xlo, xhi, ydn, yun, one, columns)
    for k in range(3):
        terms_out[k] = terms[k]
        edges_out[k] = edges[k]
    co = Coef(vz)
    for m in (*range(5), *range(19, 24)):
        v[m] = with_terms(geom, part[m], terms, m)
    for m in (*range(4), *range(20, 24)):
        res[m] = tile_residual(geom, co, v, f, c, *edges, m)
    restrict(geom, coarse, res, f_next, (0, 1, 10, 11))
    put_x(coarse, f_next, c_next, up, down, own[...])


def mid1_kernel(f, c, part, terms_in, edges_in, vz, w, c_next, own, v, f_next, one, part_next, columns, yup, ydown, res):
    geom, coarse = GEOM[0], GEOM[1]
    co = Coef(vz)
    terms = [terms_in[k] for k in range(3)]
    edges = [edges_in[k] for k in range(3)]
    for m in range(24):
        v[m] = with_terms(geom, part[m], terms, m)
    for m in range(24):
        res[m] = tile_residual(geom, co, v, f, c, *edges, m)
    restrict(geom, coarse, res, f_next)
    put_y(coarse, f_next, c_next, yup, ydown)
    yup[Z : Z + 8, :] = own[...]
    ydown[Z : Z + 8, :] = own[...]
    winv = w[...].astype(BF16)
    start_tile(coarse, winv, f_next, Setter(one))
    relax_tile(coarse, winv, co, one, f_next, c_next, ALONE, Setter(part_next))
    columns[...] = own_columns(coarse, one)


def pre1_kernel(f, c, w, vz, own, xlo, xhi, ydn, yun, one, part, columns, c_tile, v_out, up, down, chunks, res, f_next):
    geom = GEOM[1]
    terms, edges = pre_edges(geom, f, c, w, vz, own, xlo, xhi, ydn, yun, one, columns)
    for m in range(6):
        v_out[m] = with_terms(geom, part[m], terms, m)
    co = Coef(vz)
    for m in range(6):
        res[m] = tile_residual(geom, co, v_out, f, c, *edges, m)
    restrict(geom, GEOM[2], res, f_next)
    put_x(geom, v_out, None, up, down)
    whole = pack(GEOM[2], [f_next[m] for m in range(6)] + [c_tile[m] for m in range(6)])
    turn = lax.rem(lax.axis_index("gx"), 4) * 32
    whole = [pltpu.roll(x, turn, axis=1) for x in whole]
    for t in range(8):
        for k, x in enumerate(whole):
            chunks[t, k * Z : (k + 1) * Z, :] = x
        chunks[t, 3 * Z : 3 * Z + 8, :] = own[...]


def again0_kernel(f, c, w, vz, e, v, g, part, columns, c_columns, yup, ydown):
    prolong_add(GEOM[0], GEOM[1], e, v, g)
    put_y(GEOM[0], g, None, yup, ydown)
    columns[...] = own_columns(GEOM[0], g)
    c_columns[...] = own_columns(GEOM[0], c)
    relax_tile(GEOM[0], w[...].astype(BF16), Coef(vz), g, f, c, ALONE, Setter(part))


def twice0_kernel(f, c, w, vz, part, _after, twice):
    relax_tile(GEOM[0], w[...].astype(BF16), Coef(vz), part, f, c, ALONE, Setter(twice))


def post_edges(geom, f, c, w, vz, own, xlo, xhi, ydn, yun, g, columns, glo, ghi, gdn, gun):
    fl = flags_of(geom, own, xlo, xhi, ydn, yun)
    halo = Halo(
        part_of(geom, glo, 0), part_of(geom, glo, 1), part_of(geom, ghi, 0), part_of(geom, ghi, 1), gdn[...], gun[...]
    )
    winv = w[...].astype(BF16)
    relaxed = relax_edges(geom, winv, Coef(vz), g, columns[...], halo, fl, *own_data(geom, xlo, xhi, ydn, yun))
    return frame(geom, fl, halo.lo, halo.hi, halo.sides()), frame(geom, fl, *relaxed)


def post0_kernel(f, c, w, vz, own, xlo, xhi, ydn, yun, g, columns, c_columns, twice, glo, ghi, gdn, gun, out):
    geom = GEOM[0]
    rows = geom[0]
    winv = w[...].astype(BF16)
    co = Coef(vz)
    lane = zl()
    edges, edges_next = post_edges(geom, f, c, w, vz, own, xlo, xhi, ydn, yun, g, columns, glo, ghi, gdn, gun)
    low, high, sides = edge_terms(geom, winv, edges)

    def row_residual(v, c_row, beyond):
        beside = jnp.where(lane == 0, 0.0, roll(v, 1)) + jnp.where(lane == LANES - 1, 0.0, roll(v, -1))
        return residual(co, beyond * 0.0625, c_row, v, beside)

    beside = jnp.where(lane < 2, 0.0, roll(sides, 2)) + jnp.where(lane >= 2 * rows - 2, 0.0, roll(sides, -2))
    r = [
        row_residual(low, c[0], edges_next[0]),
        low * 0.0625,
        high * 0.0625,
        row_residual(high, c[rows - 1], edges_next[1]),
        residual(co, edges_next[2] * 0.0625, c_columns[...], sides, beside),
        sides * 0.0625,
    ]
    d = block_dot(winv, jnp.concatenate(r, axis=1))
    d = [d[:, k * LANES : (k + 1) * LANES] for k in range(6)]
    a, b = iota2(LANES, LANES)
    outer = jnp.where((b % 4 == 1) | (b % 4 == 2), 1.0, 0.0) * jnp.where(a == 2 * (b // 4) + b % 4 - 1, 1.0, 0.0)
    inner = jnp.where((b % 4 == 0) | (b % 4 == 3), 1.0, 0.0) * jnp.where(a == 2 * (b // 4) + b % 4 // 3, 1.0, 0.0)
    four = lane_dot(sides + d[4], outer) + lane_dot(d[5], inner)
    inside = (lane < 2) | (lane >= LANES - 2)
    row_terms = {0: low + d[0], 1: d[1], rows - 2: d[2], rows - 1: high + d[3]}
    for m in range(rows):
        x = twice[m] + jnp.where(inside, roll(four, -4 * m - 2), 0.0)
        if m in row_terms:
            x = x + row_terms[m]
        out[pl.ds(m, NZ, stride=24), :] = x[0:NZ, :]


def post1_kernel(
    f, c, w, vz, own, xlo, xhi, ydn, yun, g, part, columns, glo, ghi, gdn, gun, fine_v, e, up, down, one, fine_g
):
    geom = GEOM[1]
    edges, edges_next = post_edges(geom, f, c, w, vz, own, xlo, xhi, ydn, yun, g, columns, glo, ghi, gdn, gun)
    winv = w[...].astype(BF16)
    add_edges(geom, winv, part, edges, Setter(one))
    relax_tile(geom, winv, Coef(vz), one, f, c, edges_next, Setter(e))
    prolong_add(GEOM[0], GEOM[1], e, fine_v, fine_g, (0, 22))
    put_x(GEOM[0], fine_g, None, up, down)


def on_device(right_side, helm_coef, vert_coef, block_inverse, edge_flip):
    inv = block_inverse.reshape(4, NZ, BLK)
    f_in = right_side.reshape(NZ * 24, LANES)
    c_in = helm_coef.reshape(NZ * 24, LANES)
    vert = vert_coef.reshape(1, NZ + 1)
    flip = edge_flip.reshape(1, 4)

    ys = (Z, LANES)
    t0, t1, t2 = tile_shape(0), tile_shape(1), tile_shape(2)
    xs = x_shape(0, 3)
    up, down, own, vz = pl.pallas_call(
        by_swaps(open_kernel, 4, 4, (), ((0, "gx"),)),
        out_shape=[jax.ShapeDtypeStruct(x, F32) for x in (xs, xs, (8, LANES), ys)],
        in_specs=[ANY] * 4,
        out_specs=[VMEM] * 4,
        scratch_shapes=[pltpu.VMEM((NZ, 2, LANES), F32)] * 2
        + [pltpu.VMEM((NZ, 1, LANES), F32)] * 2
        + [pltpu.VMEM((1, NZ + 1), F32), pltpu.VMEM((1, 4), jnp.int32), pltpu.SemaphoreType.DMA((6,))]
        + [pltpu.VMEM(xs, F32)] * 2,
        compiler_params=pltpu.CompilerParams(vmem_limit_bytes=58 * 1024 * 1024),
        name="open",
    )(right_side, helm_coef, vert, flip)
    xlo, xhi = swap(up, down, "gx")
    ws = (Z, 3 * Z)
    f, c, *w, one, part, columns, c1, c_tile, yup, ydown = call(
        side_kernel,
        [t0, t0] + [ws] * 4 + [t0, t0, ys, t1, t2, Y_FULL, Y_FULL],
        [f_in, c_in, inv, vz, own],
        name="side",
    )

    def to_sides(level, count, xlo, xhi, yup, ydown):
        shape = yup.shape
        yup, ydown = call(merge_kernel(level, count), [shape, shape], [xlo, xhi, own, yup, ydown], name=f"merge{level}", got=((0, "gx"),), send=((0, "gy"),))
        return swap(yup, ydown, "gy")

    got0 = (xlo, xhi, *to_sides(0, 3, xlo, xhi, yup, ydown))
    xs = x_shape(1, 3)
    three = (3, Z, LANES)
    up, down, terms, edges = call(
        pre0_kernel,
        [xs, xs, three, three],
        [f, c, w[0], vz, own, *got0, one, part, columns, c1],
        [t0, t0, t1],
        name="pre0",
        got=((5, "gx"), (7, "gy")),
        send=((0, "gx"),),
    )
    xlo, xhi = swap(up, down, "gx")
    v0, f1, one, part, columns, yup, ydown = call(
        mid1_kernel,
        [t0, t1, t1, t1, ys, Y_FULL, Y_FULL],
        [f, c, part, terms, edges, vz, w[1], c1, own],
        [t0],
        name="mid1",
    )
    got1 = (xlo, xhi, *to_sides(1, 3, xlo, xhi, yup, ydown))
    xs = x_shape(1, 2)
    v1, up, down, chunks = call(
        pre1_kernel,
        [t1, xs, xs, (8, 3 * Z + 8, LANES)],
        [f1, c1, w[1], vz, own, *got1, one, part, columns, c_tile],
        [t1, t2],
        name="pre1",
        got=((5, "gx"), (7, "gy")),
        send=((1, "gx"),),
    )
    v1_lo, v1_hi = swap(up, down, "gx")
    chunks = lax.all_to_all(chunks, "gx", 0, 0)
    s2, s3 = (6, Z, 256), (3, Z, 128)
    m2, m3 = (Z, 256), (Z, 128)
    full2, full3 = (Z + 8, 256), (Z + 8, 128)
    f2, c2, fl2, up, down = call(
        open_strip_kernel, [s2, s2, (8, 256), full2, full2], [chunks], name="open2", send=((3, "gy"),)
    )
    side2 = swap(up, down, "gy", True)
    c3, fl3, *c_sides = call(next_coef_kernel, [s3, (8, 128), m2, m2, m3, m3], [c2, fl2], name="coef3")
    part2, first, last, f_part, base_up, base_down = call(
        alone2_kernel, [s2, m2, m2, s3, m3, m3], [f2, c2, w[2], vz, fl2, c3, fl3], [s2, s2], name="alone2"
    )
    terms2, f3, up, down = call(
        pre_strip_kernel,
        [(2, *m2), s3, full3, full3],
        [w[2], vz, fl2, *side2, first, last, *c_sides[:2], f_part, fl3, base_up, base_down],
        name="pre2",
        got=((3, "gy"),),
        send=((2, "gy"),),
    )
    side3 = swap(up, down, "gy", True)
    *alone, twice = call(alone3_kernel, [m3] * 4 + [s3], [f3, c3, w[3], vz, fl3], [s3, s3], name="alone3")
    terms, up, down = call(
        bottom_strip_kernel,
        [(4, *m3), m3, m3],
        [w[3], vz, fl3, *side3, *alone[:2], *c_sides[2:], *alone[2:]],
        name="bottom",
        got=((3, "gy"),),
        send=((1, "gy"),),
    )
    side = swap(up, down, "gy", True)
    (part,) = call(again3_kernel, [s3], [f3, c3, w[3], vz, fl3, twice, terms], [s3], name="again3")
    v2, base_up, base_down = call(base_message_kernel, [s2, m2, m2], [part2, fl2, terms2], name="base2")
    e3, up, down = call(
        last_strip_kernel,
        [s3, m2, m2],
        [w[3], fl3, *side, part, base_up, base_down, v1_lo, v1_hi],
        [m3, m3],
        name="last",
        after=2,
        got=((2, "gy"),),
        send=((1, "gy"),),
    )
    side = swap(up, down, "gy", True)
    first, last, part_low, part_high, yup, ydown, twice = call(
        again2_kernel, [m2] * 4 + [ys, ys, s2], [f2, c2, w[2], vz, fl2, v2, e3, v1], [s2, s2], name="again2"
    )
    terms, up, down = call(
        post_strip_kernel,
        [(4, *m2), ys, ys],
        [w[2], vz, fl2, *side2, first, last, *c_sides[:2], part_low, part_high, *side, v1_lo, v1_hi, own, yup, ydown],
        name="post2",
        got=((3, "gy"), (11, "gy"), (13, "gx")),
        send=((1, "gy"),),
    )
    side = swap(up, down, "gy")
    g1, part, columns, lo, hi = call(
        again1_kernel, [t1, t1, ys, ys, ys], [f1, c1, w[1], vz, v1, twice, terms, v1_lo, v1_hi], [t2], name="again1", got=((7, "gx"),)
    )
    xs = x_shape(0, 2)
    e1, up, down = call(
        post1_kernel,
        [t1, xs, xs],
        [f1, c1, w[1], vz, own, *got1, g1, part, columns, lo, hi, *side, v0],
        [t1, t0],
        name="post1",
        got=((5, "gx"), (7, "gy"), (14, "gy")),
        send=((1, "gx"),),
    )
    xlo, xhi = swap(up, down, "gx")
    g0, part, columns, c_columns, yup, ydown = call(
        again0_kernel, [t0, t0, ys, ys, ys, ys], [f, c, w[0], vz, e1, v0], name="again0"
    )
    up, down = call(
        merge_kernel(0, 2), [ys, ys], [xlo, xhi, own, yup, ydown], name="merge0", got=((0, "gx"),), send=((0, "gy"),)
    )
    side = swap(up, down, "gy")
    (twice,) = call(twice0_kernel, [t0], [f, c, w[0], vz, part, up], name="twice0", after=1)
    (out,) = call(
        post0_kernel,
        [(NZ * 24, LANES)],
        [f, c, w[0], vz, own, *got0, g0, columns, c_columns, twice, xlo, xhi, *side],
        name="post0",
        got=((5, "gx"), (7, "gy"), (13, "gx"), (15, "gy")),
    )
    return out.reshape(NZ, 24, LANES)


def solution(mesh):
    placed = (P(None, "gx", "gy"), P(None, "gx", "gy"), P(), P(), P("gx", "gy", None))
    return jax.shard_map(
        on_device, mesh=mesh, in_specs=placed, out_specs=P(None, "gx", "gy"), check_vma=False
    )
```

```python
import jax
import jax.numpy as jnp
from jax import lax
from jax.experimental import pallas as pl
from jax.experimental.pallas import tpu as pltpu
from jax.sharding import PartitionSpec as P

BLK = 14
NBLK = 5
NZ = 70
Z = 72
LANES = 128
F32 = jnp.float32
BF16 = jnp.bfloat16

GEOM = ((24, 1, 128), (6, 2, 64), (6, 1, 32), (3, 1, 16))


def lane_ids(shape):
    return lax.broadcasted_iota(jnp.int32, shape, len(shape) - 1)


def zl():
    return lane_ids((Z, LANES))


def roll(x, shift):
    shift = shift % x.shape[-1]
    return x if shift == 0 else pltpu.roll(x, shift, axis=1)


def col(x, k):
    return jnp.broadcast_to(x[:, k : k + 1], (Z, LANES))


def iota2(n, m):
    return lax.broadcasted_iota(jnp.int32, (n, m), 0), lax.broadcasted_iota(jnp.int32, (n, m), 1)


def lane_dot(x, mat):
    hi = x.astype(BF16).astype(F32)
    both = jnp.concatenate([hi, x - hi], axis=1).astype(BF16)
    twice = jnp.concatenate([mat, mat], axis=0).astype(BF16)
    return jnp.dot(both, twice, preferred_element_type=F32)


def block_dot(winv, x):
    hi = x.astype(BF16).astype(F32)
    parts = jnp.concatenate([hi, hi, x - hi], axis=0).astype(BF16)
    return jnp.dot(winv, parts, preferred_element_type=F32)


def reverse_matrix(width):
    a, b = iota2(LANES, LANES)
    return jnp.where((b < width) & (a == width - 1 - b), 1.0, 0.0)


def flag_row(flags, k):
    return jnp.broadcast_to(flags[k : k + 1, :], (Z, LANES))


class Coef:
    def __init__(self, ref, width=LANES):
        self.mid = jnp.broadcast_to(ref[:, 0:1], (Z, width))
        self.up = jnp.broadcast_to(ref[:, 1:2], (Z, width))
        self.down = jnp.broadcast_to(ref[:, 2:3], (Z, width))


def residual(co, f, c, v, beside):
    above = pltpu.roll(v, Z - 1, axis=0)
    below = pltpu.roll(v, 1, axis=0)
    return f - (c * 0.0625 + co.mid) * v + beside * 0.0625 + co.up * above + co.down * below


def row_of(geom, v, row):
    m_rows, _, ty = geom
    q, m = divmod(row, m_rows)
    return roll(v[m], -q * ty)


def corners(geom, v):
    m_rows, groups, ty = geom
    last = v[m_rows - 1]
    base = (groups - 1) * ty
    return corner_rows([col(v[0], 0), col(v[0], ty - 1), col(last, base), col(last, base + ty - 1)])


def corner_rows(columns):
    lane = zl()
    out = jnp.zeros((Z, LANES), F32)
    for k, column in enumerate(columns):
        out = jnp.where(lane == 4 + k, column, out)
    return jnp.concatenate([out, jnp.zeros((LANES - Z, LANES), F32)], axis=0).T[0:8, :]


def corner_columns(rows):
    out = jnp.concatenate([rows, jnp.zeros((LANES - 8, LANES), F32)], axis=0).T[0:Z, :]
    return [col(out, 4 + k) for k in range(4)]


def whole_rows(geom):
    return geom[1] == 1 and geom[2] == LANES


def tile_rows(geom):
    m_rows, groups, ty = geom
    return [(q * m_rows + m, m, q * ty) for m in range(m_rows) for q in range(groups)]


def own_columns(geom, v):
    ty = geom[2]
    lane = zl()
    out = jnp.zeros((Z, LANES), F32)
    for r, m, base in tile_rows(geom):
        row = v[m]
        first = roll(row, 2 * r + 1 - base)
        out = jnp.where(lane == 2 * r + 1, first, out)
        last = first if whole_rows(geom) else roll(row, 2 * r - (base + ty - 1))
        out = jnp.where(lane == 2 * r, last, out)
    return out


def pack(geom, parts):
    ty = geom[2]
    per = LANES // ty
    out = []
    for first in range(0, len(parts), per):
        lane = zl()
        acc = parts[first]
        for k, part in enumerate(parts[first + 1 : first + per], 1):
            acc = jnp.where(lane < k * ty, acc, roll(part, k * ty))
        out.append(acc)
    return out


def packed(geom, count):
    per = LANES // geom[2]
    return -(-count // per)


def part_of(geom, ref, k):
    ty = geom[2]
    per = LANES // ty
    return roll(ref[(k // per) * Z : (k // per + 1) * Z, :], -(k % per) * ty)


def put_x(geom, v, c, up, down, flags=None):
    m_rows, groups, _ = geom
    tx = m_rows * groups
    tail = corners(geom, v)
    if flags is not None:
        tail = tail + flags
    for ref, edge, second in ((up, tx - 1, tx - 2), (down, 0, 1)):
        parts = [row_of(geom, v, edge), row_of(geom, v, second)]
        if c is not None:
            parts.append(row_of(geom, c, edge))
        put_parts(geom, parts, tail, ref)


SPLIT = 40


def halved(geom, count):
    return geom[2] == 64 and count == 3


def put_parts(geom, parts, tail, ref):
    if halved(geom, len(parts)):
        lane = lane_ids((SPLIT, LANES))
        rest = jnp.concatenate([parts[2][SPLIT:Z, :], jnp.zeros((2 * SPLIT - Z, LANES), F32)], axis=0)
        ref[0:Z, :] = pack(geom, parts[:2])[0]
        ref[Z : Z + SPLIT, :] = jnp.where(lane < 64, parts[2][0:SPLIT, :], roll(rest, 64))
        ref[Z + SPLIT : Z + SPLIT + 8, :] = tail
        return
    whole = pack(geom, parts)
    for k, part in enumerate(whole):
        ref[k * Z : (k + 1) * Z, :] = part
    ref[len(whole) * Z : len(whole) * Z + 8, :] = tail


def tail_of(geom, ref, count):
    n = message_rows(geom, count)
    return ref[n : n + 8, :]


def message_rows(geom, count):
    return Z + SPLIT if halved(geom, count) else packed(geom, count) * Z


def put_y(geom, v, c, up, down):
    ty = geom[2]
    lane = zl()
    out_up = jnp.zeros((Z, LANES), F32)
    out_down = out_up
    for r, m, base in tile_rows(geom):
        row = v[m]
        mine = lane // 2 == r
        last = roll(row, 2 * r + 1 - (base + ty - 1))
        first = roll(row, 2 * r - base)
        out_up = jnp.where(mine, last, out_up)
        out_down = jnp.where(mine, first, out_down)
        if c is not None:
            row = c[m]
            out_up = jnp.where(lane == 65 + 2 * r, roll(row, 65 + 2 * r - (base + ty - 1)), out_up)
            out_down = jnp.where(lane == 64 + 2 * r, roll(row, 64 + 2 * r - base), out_down)
    up[0:Z, :] = out_up
    down[0:Z, :] = out_down


def merge_y(lo, hi, flags, up, down):
    lane = zl()
    f0, f1 = flag_row(flags, 0) > 0.5, flag_row(flags, 1) > 0.5

    def fill(part, values):
        for k, value in enumerate(values):
            part = jnp.where(lane == 112 + k, value, part)
        return part

    up_new = fill(up, [lo[3], lo[1], hi[1], hi[3], jnp.where(f0, lo[2], lo[3]), jnp.where(f1, hi[0], hi[1])])
    down_new = fill(down, [lo[2], lo[0], hi[0], hi[2], jnp.where(f0, lo[3], lo[2]), jnp.where(f1, hi[1], hi[0])])
    return up_new, down_new


def odd_lanes():
    return zl() % 2 == 1


class Halo:
    def __init__(self, lo, lo2, hi, hi2, dn, un):
        self.lo, self.lo2, self.hi, self.hi2, self.dn, self.un = lo, lo2, hi, hi2, dn, un

    def sides(self):
        return jnp.where(odd_lanes(), self.dn, self.un)

    def seconds(self):
        return jnp.where(odd_lanes(), roll(self.dn, 1), roll(self.un, -1))


class Flags:
    def __init__(self, own, lo, hi, dn, un):
        self.own, self.lo, self.hi, self.dn, self.un = own, lo, hi, dn, un


def turn_row(geom, row, flag):
    return jnp.where(flag > 0.5, lane_dot(row, reverse_matrix(geom[2])), row)


def turn_sides(geom, sides, flag_dn, flag_un):
    tx = geom[0] * geom[1]
    flag = jnp.where(odd_lanes(), flag_dn, flag_un)
    a, b = iota2(LANES, LANES)
    mat = jnp.where((b < 2 * tx) & (a == 2 * (tx - 1 - b // 2) + b % 2), 1.0, 0.0)
    return jnp.where(flag > 0.5, lane_dot(sides, mat), sides)


def frame(geom, fl, lo, hi, sides):
    return (
        turn_row(geom, lo, flag_row(fl.own, 0)),
        turn_row(geom, hi, flag_row(fl.own, 1)),
        turn_sides(geom, sides, flag_row(fl.own, 2), flag_row(fl.own, 3)),
    )


def relax_edges(geom, winv, co, v, columns, halo, fl, f_lo, c_lo, f_hi, c_hi, f_sides, c_sides):
    m_rows, groups, ty = geom
    tx = m_rows * groups
    lane = zl()
    dn, un = halo.dn, halo.un

    def beside_row(edge, second, mine, low, high):
        left = jnp.where(lane == 0, low, roll(edge, 1))
        right = jnp.where(lane == ty - 1, high, roll(edge, -1))
        return second + mine + left + right

    def choose(flags, k, first, other):
        return jnp.where(flag_row(flags, k) > 0.5, other, first)

    b_lo = beside_row(
        halo.lo,
        halo.lo2,
        turn_row(geom, row_of(geom, v, 0), flag_row(fl.lo, 1)),
        choose(fl.lo, 2, col(dn, 112), col(dn, 113)),
        choose(fl.lo, 3, col(un, 112), col(un, 113)),
    )
    b_hi = beside_row(
        halo.hi,
        halo.hi2,
        turn_row(geom, row_of(geom, v, tx - 1), flag_row(fl.hi, 0)),
        choose(fl.hi, 2, col(dn, 114), col(dn, 115)),
        choose(fl.hi, 3, col(un, 114), col(un, 115)),
    )
    edge = halo.sides()
    mine = turn_sides(geom, columns, flag_row(fl.dn, 3), flag_row(fl.un, 2))
    below = jnp.where(lane == 1, col(dn, 116), jnp.where(lane == 0, col(un, 116), roll(edge, 2)))
    last = 2 * (tx - 1)
    above = jnp.where(lane == last + 1, col(dn, 117), jnp.where(lane == last, col(un, 117), roll(edge, -2)))
    b_sides = halo.seconds() + mine + below + above
    r_lo = residual(co, f_lo, c_lo, halo.lo, b_lo)
    r_hi = residual(co, f_hi, c_hi, halo.hi, b_hi)
    r_sides = residual(co, f_sides, c_sides, edge, b_sides)
    d = block_dot(winv, jnp.concatenate([r_lo, r_hi, r_sides], axis=1))
    return halo.lo + d[:, :LANES], halo.hi + d[:, LANES : 2 * LANES], edge + d[:, 2 * LANES :]


def tile_residual(geom, co, v, f, c, lo, hi, sides, m):
    m_rows, groups, ty = geom
    lane = zl()
    here = v[m]
    if lo is None:
        lo = hi = jnp.zeros((Z, LANES), F32)
    if m > 0:
        low_x = v[m - 1]
    else:
        low_x = lo if groups == 1 else jnp.where(lane < ty, lo, roll(v[m_rows - 1], ty))
    if m < m_rows - 1:
        high_x = v[m + 1]
    elif groups == 1:
        high_x = hi
    else:
        high_x = jnp.where(lane < (groups - 1) * ty, roll(v[0], -ty), roll(hi, (groups - 1) * ty))
    low_y, high_y = roll(here, 1), roll(here, -1)
    if sides is None:
        low_y = jnp.where(lane % ty == 0, 0.0, low_y)
        high_y = jnp.where(lane % ty == ty - 1, 0.0, high_y)
        return residual(co, f[m], c[m], here, low_x + high_x + low_y + high_y)
    for q in range(groups):
        row = q * m_rows + m
        low = roll(sides, q * ty - 2 * row - 1)
        high = low if whole_rows(geom) else roll(sides, q * ty + ty - 1 - 2 * row)
        low_y = jnp.where(lane == q * ty, low, low_y)
        high_y = jnp.where(lane == q * ty + ty - 1, high, high_y)
    return residual(co, f[m], c[m], here, low_x + high_x + low_y + high_y)


def relax_tile(geom, winv, co, v, f, c, edges, store):
    lo, hi, sides = edges
    for m in range(0, geom[0], 2):
        rows = [k for k in (m, m + 1) if k < geom[0]]
        r = [tile_residual(geom, co, v, f, c, lo, hi, sides, k) for k in rows]
        d = block_dot(winv, r[0] if len(r) == 1 else jnp.concatenate(r, axis=1))
        for i, k in enumerate(rows):
            store(k, v[k] + d[:, i * LANES : (i + 1) * LANES])


ALONE = (None, None, None)


def edge_terms(geom, winv, edges):
    ty = geom[2]
    lane = zl()
    d = block_dot(winv, jnp.concatenate(edges, axis=1) * 0.0625)
    low, high, sides = [d[:, k * LANES : (k + 1) * LANES] for k in range(3)]
    if ty < LANES:
        low = jnp.where(lane < ty, low, 0.0)
        high = jnp.where(lane < ty, high, 0.0)
    return low, high, sides


def with_terms(geom, x, terms, m):
    m_rows, groups, ty = geom
    low, high, sides = terms
    lane = zl()
    if m == 0:
        x = x + low
    if m == m_rows - 1:
        x = x + roll(high, (groups - 1) * ty)
    for q in range(groups):
        row = q * m_rows + m
        first = roll(sides, q * ty - 2 * row - 1)
        last = first if whole_rows(geom) else roll(sides, q * ty + ty - 1 - 2 * row)
        x = x + jnp.where(lane == q * ty, first, jnp.where(lane == q * ty + ty - 1, last, 0.0))
    return x


def add_edges(geom, winv, part, edges, store):
    terms = edge_terms(geom, winv, edges)
    for m in range(geom[0]):
        store(m, with_terms(geom, part[m], terms, m))


def start_tile(geom, winv, f, store):
    for m in range(0, geom[0], 2):
        rows = [k for k in (m, m + 1) if k < geom[0]]
        parts = [f[k] for k in rows]
        d = block_dot(winv, parts[0] if len(parts) == 1 else jnp.concatenate(parts, axis=1))
        for i, k in enumerate(rows):
            store(k, d[:, i * LANES : (i + 1) * LANES])


def restrict(fine, coarse, v, out, wanted=None):
    m_rows, _, ty = fine
    cm, cq, cty = coarse
    a, b = iota2(LANES, LANES)
    for mc in range(cm):
        acc = None
        for qc in range(cq):
            if wanted is not None and qc * cm + mc not in wanted:
                continue
            q, m = divmod(2 * (qc * cm + mc), m_rows)
            inside = (b >= qc * cty) & (b < (qc + 1) * cty) & (a // 2 == b - qc * cty + q * (ty // 2))
            term = lane_dot(v[m] + v[m + 1], jnp.where(inside, 0.25, 0.0))
            acc = term if acc is None else acc + term
        if acc is not None:
            out[mc] = acc


def prolong_add(fine, coarse, e, v, out, rows=None):
    m_rows, groups, ty = fine
    cm, _, cty = coarse
    a, b = iota2(LANES, LANES)
    for m in range(0, m_rows, 2) if rows is None else rows:
        acc = None
        for q in range(groups):
            qc, mc = divmod((q * m_rows + m) // 2, cm)
            inside = (b >= q * ty) & (b < (q + 1) * ty) & (a - qc * cty == (b - q * ty) // 2)
            term = lane_dot(e[mc], jnp.where(inside, 1.0, 0.0))
            acc = term if acc is None else acc + term
        out[m] = v[m] + acc
        out[m + 1] = v[m + 1] + acc


class Setter:
    def __init__(self, ref):
        self.ref = ref

    def __call__(self, m, value):
        self.ref[m] = value


def messages(geom, xlo, xhi, ydn, yun, winv):
    raw = [part_of(geom, xlo, 0), part_of(geom, xlo, 1), part_of(geom, xhi, 0), part_of(geom, xhi, 1), ydn[0:Z, :], yun[0:Z, :]]
    d = block_dot(winv, jnp.concatenate(raw, axis=1))
    return Halo(*[d[:, k * LANES : (k + 1) * LANES] for k in range(6)])


def third_of(geom, ref):
    if not halved(geom, 3):
        return part_of(geom, ref, 2)
    both = ref[Z : Z + SPLIT, :]
    return jnp.concatenate([both, roll(both[0 : Z - SPLIT, :], 64)], axis=0)


def own_data(geom, xlo, xhi, ydn, yun):
    dn, un = ydn[0:Z, :], yun[0:Z, :]
    f_sides = jnp.where(odd_lanes(), dn, un)
    c_sides = roll(f_sides, -64)
    return (
        part_of(geom, xlo, 0),
        third_of(geom, xlo),
        part_of(geom, xhi, 0),
        third_of(geom, xhi),
        f_sides,
        c_sides,
    )


def flags_of(geom, own, xlo, xhi, ydn, yun):
    return Flags(own[...], tail_of(geom, xlo, 3), tail_of(geom, xhi, 3), ydn[Z : Z + 8, :], yun[Z : Z + 8, :])


def load_top(src, dst):
    for x in range(24):
        dst[x, 0:NZ, :] = src[pl.ds(x, NZ, stride=24), :]
        dst[x, NZ:Z, :] = jnp.zeros((Z - NZ, LANES), F32)


STRIPS = {2: (6, 32, 256), 3: (3, 16, 128)}


def in_tile(strip):
    _, ty, width = strip
    return lane_ids((Z, width)) % ty


def group_dot(x, mat):
    parts = [lane_dot(x[:, k : k + LANES], mat) for k in range(0, x.shape[1], LANES)]
    return parts[0] if len(parts) == 1 else jnp.concatenate(parts, axis=1)


def turn_groups(strip, x, flags, k, count):
    _, ty, width = strip
    a, b = iota2(LANES, LANES)
    mat = jnp.where((a // ty == b // ty) & (b % ty < count) & (a % ty == count - 1 - b % ty), 1.0, 0.0)
    flag = jnp.broadcast_to(flags[k : k + 1, :], (Z, width))
    return jnp.where(flag > 0.5, group_dot(x, mat), x)


def strip_ends(strip, v, flags):
    m_rows, ty, _ = strip
    low = turn_groups(strip, roll(v[m_rows - 1], ty), flags, 0, ty)
    high = turn_groups(strip, roll(v[0], -ty), flags, 1, ty)
    return low, high


def strip_column(strip, v, y, offset, out):
    lt = in_tile(strip)
    for m in range(strip[0]):
        out = jnp.where(lt == offset + m, roll(v[m], offset + m - y), out)
    return out


def strip_message(strip, v, c, ends, up, down):
    m_rows, ty, width = strip
    lt = in_tile(strip)
    for ref, edge, second in ((up, ty - 1, ty - 2), (down, 0, 1)):
        out = strip_column(strip, v, edge, 0, jnp.zeros((Z, width), F32))
        out = strip_column(strip, v, second, m_rows, out)
        if c is not None:
            out = strip_column(strip, c, edge, 2 * m_rows, out)
        for k, end in enumerate(ends):
            out = jnp.where(lt == 3 * m_rows + k, roll(end, 3 * m_rows + k - edge), out)
        ref[0:Z, :] = out


def strip_edges(strip, winv, co, sides):
    m_rows, _, width = strip
    lt = in_tile(strip)
    r = []
    for x, raw, flags, k, mine in sides:
        mine = turn_groups(strip, mine, flags, k, m_rows)
        low = jnp.where(lt == 0, roll(x, -3 * m_rows), roll(x, 1))
        high = jnp.where(lt == m_rows - 1, roll(x, -2 * m_rows - 2), roll(x, -1))
        r.append(residual(co, raw, roll(raw, -2 * m_rows), x, roll(x, -m_rows) + mine + low + high))
    d = block_dot(winv, jnp.concatenate(r, axis=1))
    return [side[0] + d[:, k * width : (k + 1) * width] for k, side in enumerate(sides)]


def strip_frame(strip, flags, low, high):
    return turn_groups(strip, low, flags, 2, strip[0]), turn_groups(strip, high, flags, 3, strip[0])


def strip_residual(strip, co, v, f, c, ends, sides, m):
    m_rows, ty, _ = strip
    lt = in_tile(strip)
    low_x = v[m - 1] if m > 0 else ends[0]
    high_x = v[m + 1] if m < m_rows - 1 else ends[1]
    low = 0.0 if sides is None else roll(sides[0], -m)
    high = 0.0 if sides is None else roll(sides[1], ty - 1 - m)
    low_y = jnp.where(lt == 0, low, roll(v[m], 1))
    high_y = jnp.where(lt == ty - 1, high, roll(v[m], -1))
    return residual(co, f[m], c[m], v[m], low_x + high_x + low_y + high_y)


def strip_relax(strip, winv, co, v, f, c, flags, sides, store):
    ends = strip_ends(strip, v, flags)
    for m in range(strip[0]):
        r = strip_residual(strip, co, v, f, c, ends, sides, m)
        store(m, v[m] + block_dot(winv, r))


def strip_add_sides(strip, winv, part, sides, store):
    m_rows, ty, width = strip
    lt = in_tile(strip)
    d = block_dot(winv, jnp.concatenate(sides, axis=1) * 0.0625)
    for m in range(m_rows):
        low, high = roll(d[:, :width], -m), roll(d[:, width:], ty - 1 - m)
        store(m, part[m] + jnp.where(lt == 0, low, jnp.where(lt == ty - 1, high, 0.0)))


def strip_side_terms(strip, winv, co, flags, c_columns, sides, sides_next):
    m_rows, ty, width = strip
    lt = in_tile(strip)
    d = block_dot(winv, jnp.concatenate(sides, axis=1) * 0.0625)
    first, last = d[:, :width], d[:, width:]
    turned = [jnp.broadcast_to(flags[k : k + 1, :], (Z, width)) > 0.5 for k in range(2)]
    step = ty - m_rows + 1
    r = []
    for mine, other, c, beyond in ((first, last, c_columns[0], sides_next[0]), (last, first, c_columns[1], sides_next[1])):
        low = jnp.where(turned[0], roll(other, step), roll(mine, step))
        high = jnp.where(turned[1], roll(other, -step), roll(mine, -step))
        low = jnp.where(lt == 0, low, roll(mine, 1))
        high = jnp.where(lt == m_rows - 1, high, roll(mine, -1))
        r.append(residual(co, beyond * 0.0625, c, mine, low + high))
    return first, last, r


def strip_restrict(v, out):
    a, b = iota2(LANES, LANES)
    for m in range(3):
        both = v[2 * m] + v[2 * m + 1]
        out[m] = lane_dot(both[:, :LANES], jnp.where(a // 2 == b, 0.25, 0.0)) + lane_dot(
            both[:, LANES:], jnp.where(a // 2 == b - 64, 0.25, 0.0)
        )


def open_strip_kernel(chunks, f, c, flags, up, down):
    strip = STRIPS[2]
    group = lane_ids((Z, LANES)) // 32
    for m in range(6):
        for ref, k in ((f, m), (c, 6 + m)):
            part = (k // 4) * Z
            halves = []
            for h in range(2):
                acc = None
                for g in range(4):
                    x = chunks[4 * h + g, part : part + Z, :]
                    acc = x if acc is None else jnp.where(group == (g + k) % 4, x, acc)
                halves.append(roll(acc, -(k % 4) * 32))
            ref[m] = jnp.concatenate(halves, axis=1)
    group = lane_ids((8, LANES)) // 32
    for h in range(2):
        acc = None
        for g in range(4):
            x = chunks[4 * h + g, 3 * Z : 3 * Z + 8, :]
            acc = x if acc is None else jnp.where(group == g, x, acc)
        flags[:, h * LANES : (h + 1) * LANES] = acc
    strip_message(strip, f, c, strip_ends(strip, f, flags), up, down)
    up[Z : Z + 8, :] = flags[...]
    down[Z : Z + 8, :] = flags[...]


def strip_sides(values, raws, dn, un, first, last):
    return (
        (values[0], raws[0], dn[Z : Z + 8, :], 3, first[...]),
        (values[1], raws[1], un[Z : Z + 8, :], 2, last[...]),
    )


def column_restrict(strip, x):
    a, b = iota2(LANES, LANES)
    out = None
    for h in range(2):
        inside = (b // 16 == 4 * h + a // 32) & ((a % 32) // 2 == b % 16) & (a % 32 < strip[0])
        term = lane_dot(x[:, h * LANES : (h + 1) * LANES], jnp.where(inside, 0.25, 0.0))
        out = term if out is None else out + term
    return out


def pre_strip_kernel(
    w, vz, flags, dn, un, first_column, last_column, c_low, c_high, f_part, fl_next, base_up, base_down, terms, f_next, up, down
):
    strip, small = STRIPS[2], STRIPS[3]
    winv = w[...].astype(BF16)
    co = Coef(vz, strip[2])
    raws = [dn[0:Z, :], un[0:Z, :]]
    values = block_dot(winv, jnp.concatenate(raws, axis=1))
    values = [values[:, : strip[2]], values[:, strip[2] :]]
    edges = strip_edges(strip, winv, co, strip_sides(values, raws, dn, un, first_column, last_column))
    first, last, r = strip_side_terms(
        strip, winv, co, flags, (c_low[...], c_high[...]), strip_frame(strip, flags, *values), strip_frame(strip, flags, *edges)
    )
    terms[0] = first
    terms[1] = last
    low = column_restrict(strip, r[0] + first * 0.0625)
    high = column_restrict(strip, r[1] + last * 0.0625)
    m_rows, ty, width = small
    lt = in_tile(small)
    for m in range(m_rows):
        x = jnp.where(lt == 0, roll(low, -m), 0.0)
        f_next[m] = f_part[m] + jnp.where(lt == ty - 1, roll(high, ty - 1 - m), x)
    turned = [jnp.broadcast_to(fl_next[k : k + 1, :], (Z, width)) > 0.5 for k in range(2)]
    for ref, base, mine, other in ((up, base_up, high, low), (down, base_down, low, high)):
        before, after = 3 * m_rows + ty - m_rows + 1, 3 * m_rows + 1 - ty
        end_low = jnp.where(turned[0], roll(other, before), roll(mine, before))
        end_high = jnp.where(turned[1], roll(other, after), roll(mine, after))
        add = jnp.where(lt < m_rows, mine, 0.0)
        add = jnp.where(lt == 3 * m_rows, end_low, add)
        add = jnp.where(lt == 3 * m_rows + 1, end_high, add)
        ref[0:Z, :] = base[...] + add
        ref[Z : Z + 8, :] = fl_next[...]


def next_coef_kernel(c, flags, c_next, fl_next, low, high, low_next, high_next):
    strip_restrict(c, c_next)
    a, b = iota2(LANES, LANES)
    fl_next[...] = lane_dot(flags[:, :LANES], jnp.where((b < 64) & (a == (b // 16) * 32), 1.0, 0.0)) + lane_dot(
        flags[:, LANES:], jnp.where((b >= 64) & (a == (b // 16 - 4) * 32), 1.0, 0.0)
    )
    for strip, ref, first, last in ((STRIPS[2], c, low, high), (STRIPS[3], c_next, low_next, high_next)):
        zero = jnp.zeros((Z, strip[2]), F32)
        first[...] = strip_column(strip, ref, 0, 0, zero)
        last[...] = strip_column(strip, ref, strip[1] - 1, 0, zero)


def alone2_kernel(f, c, w, vz, flags, c_next, fl_next, part, low, high, f_part, up, down, v, res):
    strip, small = STRIPS[2], STRIPS[3]
    winv = w[...].astype(BF16)
    co = Coef(vz, strip[2])
    for m in range(6):
        v[m] = block_dot(winv, f[m])
    zero = jnp.zeros((Z, strip[2]), F32)
    low[...] = strip_column(strip, v, 0, 0, zero)
    high[...] = strip_column(strip, v, strip[1] - 1, 0, zero)
    strip_relax(strip, winv, co, v, f, c, flags, None, Setter(part))
    ends = strip_ends(strip, part, flags)
    for m in range(6):
        res[m] = strip_residual(strip, co, part, f, c, ends, None, m)
    strip_restrict(res, f_part)
    strip_message(small, f_part, c_next, strip_ends(small, f_part, fl_next), up, down)


def bottom_strip_kernel(
    w, vz, flags, dn, un, first_column, last_column, c_low, c_high, part_low, part_high, terms, up, down
):
    strip = STRIPS[3]
    width = strip[2]
    winv = w[...].astype(BF16)
    co = Coef(vz)
    raws = [dn[0:Z, :], un[0:Z, :]]
    values = block_dot(winv, jnp.concatenate(raws, axis=1))
    values = [values[:, :width], values[:, width:]]
    edges = strip_edges(strip, winv, co, strip_sides(values, raws, dn, un, first_column, last_column))
    first, last, r = strip_side_terms(
        strip, winv, co, flags, (c_low[...], c_high[...]), strip_frame(strip, flags, *values), strip_frame(strip, flags, *edges)
    )
    d = block_dot(winv, jnp.concatenate([r[0], first * 0.0625, last * 0.0625, r[1]], axis=1))
    d = [d[:, k * width : (k + 1) * width] for k in range(4)]
    d[0] = first + d[0]
    d[3] = last + d[3]
    for k in range(4):
        terms[k] = d[k]
    up[...] = part_high[...] + d[3]
    down[...] = part_low[...] + d[0]


def with_columns(strip, x, terms, m):
    ty = strip[1]
    lt = in_tile(strip)
    for k, y in enumerate((0, 1, ty - 2, ty - 1)):
        x = x + jnp.where(lt == y, roll(terms[k], y - m), 0.0)
    return x


def last_strip_kernel(w, flags, dn, un, part, base_up, base_down, _lo, _hi, e, up, down, small_up, small_down):
    strip, fine = STRIPS[3], STRIPS[2]
    winv = w[...].astype(BF16)
    strip_add_sides(strip, winv, part, strip_frame(strip, flags, dn[...], un[...]), Setter(e))
    strip_message(strip, e, None, strip_ends(strip, e, flags), small_up, small_down)
    a, b = iota2(LANES, LANES)
    for h in range(2):
        lt = b % 32
        source = jnp.where(lt < 12, (lt % 6) // 2, jnp.where((lt == 18) | (lt == 19), lt - 9, 15))
        spread = jnp.where((lt != 15) & (a == 64 * h + (b // 32) * 16 + source) & (source < 15), 1.0, 0.0)
        half = slice(h * LANES, (h + 1) * LANES)
        up[:, half] = base_up[:, half] + lane_dot(small_up[...], spread)
        down[:, half] = base_down[:, half] + lane_dot(small_down[...], spread)


def base_message_kernel(part, flags, terms, v, up, down):
    strip = STRIPS[2]
    lt = in_tile(strip)
    for m in range(6):
        x = jnp.where(lt == 0, roll(terms[0], -m), 0.0)
        v[m] = part[m] + jnp.where(lt == strip[1] - 1, roll(terms[1], strip[1] - 1 - m), x)
    strip_message(strip, v, None, strip_ends(strip, v, flags), up, down)


def again2_kernel(f, c, w, vz, flags, v, e, tile_v, low, high, part_low, part_high, yup, ydown, twice, g, part):
    strip = STRIPS[2]
    a, b = iota2(LANES, LANES)
    for m in range(3):
        add = jnp.concatenate([lane_dot(e[m], jnp.where(a == 64 * h + b // 2, 1.0, 0.0)) for h in range(2)], axis=1)
        g[2 * m] = v[2 * m] + add
        g[2 * m + 1] = v[2 * m + 1] + add
    zero = jnp.zeros((Z, strip[2]), F32)
    low[...] = strip_column(strip, g, 0, 0, zero)
    high[...] = strip_column(strip, g, strip[1] - 1, 0, zero)
    winv = w[...].astype(BF16)
    co = Coef(vz, strip[2])
    strip_relax(strip, winv, co, g, f, c, flags, None, Setter(part))
    strip_relax(strip, winv, co, part, f, c, flags, None, Setter(twice))
    part_low[...] = strip_column(strip, twice, 0, 0, zero)
    part_high[...] = strip_column(strip, twice, strip[1] - 1, 0, zero)
    put_y(GEOM[1], tile_v, None, yup, ydown)


def alone3_kernel(f, c, w, vz, flags, low, high, part_low, part_high, twice, v, part):
    strip = STRIPS[3]
    winv = w[...].astype(BF16)
    co = Coef(vz)
    for m in range(3):
        v[m] = block_dot(winv, f[m])
    strip_relax(strip, winv, co, v, f, c, flags, None, Setter(part))
    strip_relax(strip, winv, co, part, f, c, flags, None, Setter(twice))
    zero = jnp.zeros((Z, LANES), F32)
    for ref, first, last in ((v, low, high), (twice, part_low, part_high)):
        first[...] = strip_column(strip, ref, 0, 0, zero)
        last[...] = strip_column(strip, ref, strip[1] - 1, 0, zero)


def again3_kernel(f, c, w, vz, flags, twice, terms, part, v):
    strip = STRIPS[3]
    for m in range(3):
        v[m] = with_columns(strip, twice[m], terms, m)
    strip_relax(strip, w[...].astype(BF16), Coef(vz), v, f, c, flags, None, Setter(part))


def tile_lanes(x, step):
    t = lax.rem(lax.axis_index("gx") + (step + 8), 8)
    half = jnp.where(t < 4, x[:, :LANES], x[:, LANES:])
    return pltpu.roll(half, lax.rem(8 - t, 4) * 32, axis=1)


def post_strip_kernel(
    w, vz, flags, dn, un, first_column, last_column, c_low, c_high, part_low, part_high, gdn, gun, xlo, xhi, own, yup, ydown, terms, up, down
):
    strip = STRIPS[2]
    fine = GEOM[1]
    width = strip[2]
    winv = w[...].astype(BF16)
    co = Coef(vz, width)
    raws = [dn[0:Z, :], un[0:Z, :]]
    values = [gdn[...], gun[...]]
    edges = strip_edges(strip, winv, co, strip_sides(values, raws, dn, un, first_column, last_column))
    first, last, r = strip_side_terms(
        strip, winv, co, flags, (c_low[...], c_high[...]), strip_frame(strip, flags, *values), strip_frame(strip, flags, *edges)
    )
    d = block_dot(winv, jnp.concatenate([r[0], first * 0.0625, last * 0.0625, r[1]], axis=1))
    d = [d[:, k * width : (k + 1) * width] for k in range(4)]
    d[0] = first + d[0]
    d[3] = last + d[3]
    for k in range(4):
        terms[k] = d[k]
    low, high = part_low[...] + d[0], part_high[...] + d[3]
    extras = []
    for ref, step in ((xlo, -1), (xhi, 1)):
        near, far = tile_lanes(low, step), tile_lanes(high, step)
        adds = (col(near, 0), col(far, 0), col(near, 5), col(far, 5))
        extras.append([x + y for x, y in zip(corner_columns(tail_of(fine, ref, 2)), adds)])
    group = zl() // 4
    near, far = tile_lanes(low, 0), tile_lanes(high, 0)
    add_up = add_down = jnp.zeros((Z, LANES), F32)
    for m in range(6):
        add_up = jnp.where(group == m, col(far, m), add_up)
        add_down = jnp.where(group == m, col(near, m), add_down)
    up[...], down[...] = merge_y(*extras, own, yup[...] + add_up, ydown[...] + add_down)


def again1_kernel(f, c, w, vz, v, twice, terms, xlo, xhi, g, part, columns, lo_out, hi_out, tile):
    fine, geom = GEOM[1], GEOM[2]
    rows = []
    for m in range(6):
        rows.append(with_columns(STRIPS[2], twice[m], terms, m))
        tile[m] = tile_lanes(rows[m], 0)
    prolong_add(fine, geom, tile, v, g)
    a, b = iota2(LANES, LANES)
    spread = jnp.where((b < 64) & (a == b // 2), 1.0, 0.0)
    for ref, out, row in ((xlo, lo_out, tile_lanes(rows[5], -1)), (xhi, hi_out, tile_lanes(rows[0], 1))):
        add = lane_dot(row, spread)
        out[...] = pack(fine, [part_of(fine, ref, 0) + add, part_of(fine, ref, 1) + add])[0]
    columns[...] = own_columns(fine, g)
    relax_tile(fine, w[...].astype(BF16), Coef(vz), g, f, c, ALONE, Setter(part))


def swap_pairs(axis, which, nearest=False):
    sizes = lax.axis_size("gx"), lax.axis_size("gy")
    out = []
    for i in range(sizes[0]):
        for j in range(sizes[1]):
            at = [i, j]
            dim = 0 if axis == "gx" else 1
            n = sizes[dim]
            at[dim] = (at[dim] ^ 1) if which == 0 else (at[dim] + (1 if at[dim] % 2 else n - 1)) % n
            if nearest and 2 * j // n != 2 * at[1] // n:
                at[0] = i ^ 1
            out.append((i * sizes[1] + j, at[0] * sizes[1] + at[1]))
    return out


def swap(first, second, axis, nearest=False):
    both = ("gx", "gy")
    return (
        lax.ppermute(first, both, swap_pairs(axis, 0, nearest)),
        lax.ppermute(second, both, swap_pairs(axis, 1, nearest)),
    )


ANY = pl.BlockSpec(memory_space=pl.ANY)
LIMIT = 14 * 1024 * 1024
VMEM = pl.BlockSpec(memory_space=pltpu.VMEM)


class Either:
    def __init__(self, first, a, b):
        self.first, self.a, self.b = first, a, b

    def __getitem__(self, index):
        return jnp.where(self.first, self.a[index], self.b[index])


def is_even(axis):
    return lax.rem(lax.axis_index(axis), 2) == 0


def by_swaps(kernel, n_in, n_out, got, send):
    def wrapped(*refs):
        refs = list(refs)
        for place, axis in got:
            a, b = refs[place], refs[place + 1]
            refs[place], refs[place + 1] = Either(is_even(axis), b, a), Either(is_even(axis), a, b)
        extra = refs[len(refs) - 2 * len(send) :]
        refs = refs[: len(refs) - 2 * len(send)]
        outs = []
        for k, (place, axis) in enumerate(send):
            place += n_in
            outs.append((refs[place], refs[place + 1], extra[2 * k], extra[2 * k + 1], axis))
            refs[place], refs[place + 1] = extra[2 * k], extra[2 * k + 1]
        kernel(*refs)
        for first, second, up, down, axis in outs:
            even = is_even(axis)
            up, down = up[...], down[...]
            first[...] = jnp.where(even, up, down)
            second[...] = jnp.where(even, down, up)

    return wrapped


def call(kernel, outs, args, scratch=(), name=None, after=0, got=(), send=()):
    scratch = [pltpu.VMEM(s, F32) for s in scratch]
    scratch += [pltpu.VMEM(outs[place], F32) for place, _ in send for _ in range(2)]
    return pl.pallas_call(
        by_swaps(kernel, len(args), len(outs), got, send),
        out_shape=[jax.ShapeDtypeStruct(s, F32) for s in outs],
        in_specs=[VMEM] * (len(args) - after) + [ANY] * after,
        out_specs=[VMEM] * len(outs),
        scratch_shapes=scratch,
        compiler_params=pltpu.CompilerParams(vmem_limit_bytes=LIMIT),
        name=name,
    )(*args)


def tile_shape(level):
    return (GEOM[level][0], Z, LANES)


def x_shape(level, count):
    return (message_rows(GEOM[level], count) + 8, LANES)


Y_FULL = (Z + 8, LANES)


def open_kernel(f_in, c_in, vert_in, flip_in, up, down, own, vz, f_low, f_high, c_low, c_high, vert, flip, sems):
    pairs = (
        (vert_in, vert),
        (flip_in, flip),
        (f_in.at[:, 0:2, :], f_low),
        (f_in.at[:, 22:24, :], f_high),
        (c_in.at[:, 0:1, :], c_low),
        (c_in.at[:, 23:24, :], c_high),
    )
    copies = [pltpu.make_async_copy(src, dst, sems.at[k]) for k, (src, dst) in enumerate(pairs)]
    for copy in copies:
        copy.start()
    for copy in copies[:2]:
        copy.wait()
    a, b = iota2(8, 4)
    flags = jnp.broadcast_to(flip[...].astype(F32), (8, 4))
    flags = jnp.broadcast_to(jnp.sum(jnp.where(a == b, flags, 0.0), axis=1, keepdims=True), (8, LANES))
    own[...] = flags
    a, b = iota2(Z, NZ + 1)
    coef = jnp.broadcast_to(vert[...], (Z, NZ + 1))
    high = jnp.sum(jnp.where((b == a + 1) & (a < NZ), coef, 0.0), axis=1, keepdims=True)
    low = jnp.sum(jnp.where((b == a) & (a < NZ), coef, 0.0), axis=1, keepdims=True)
    columns = [jnp.broadcast_to(x * 0.0625, (Z, LANES)) for x in (4.0 + high + low, high, low)]
    lane = zl()
    vz[...] = jnp.where(lane == 0, columns[0], jnp.where(lane == 1, columns[1], columns[2]))
    up[...] = jnp.zeros(up.shape, F32)
    down[...] = jnp.zeros(down.shape, F32)
    for copy in copies[2:]:
        copy.wait()
    up[0:NZ, :] = f_high[:, 1, :]
    up[Z : Z + NZ, :] = f_high[:, 0, :]
    up[2 * Z : 2 * Z + NZ, :] = c_high[:, 0, :]
    down[0:NZ, :] = f_low[:, 0, :]
    down[Z : Z + NZ, :] = f_low[:, 1, :]
    down[2 * Z : 2 * Z + NZ, :] = c_low[:, 0, :]
    first, last = down[0:Z, :], up[0:Z, :]
    tail = flags + corner_rows([col(first, 0), col(first, LANES - 1), col(last, 0), col(last, LANES - 1)])
    up[3 * Z : 3 * Z + 8, :] = tail
    down[3 * Z : 3 * Z + 8, :] = tail


def block_matrix(inv):
    width = 3 * Z
    a, b = iota2(BLK, width)
    b = b % Z
    spread = jnp.where((b % BLK == a) & (b < NZ), 1.0, 0.0).astype(BF16)
    whole = jnp.zeros((NZ, width), F32)
    left = inv
    for _ in range(3):
        part = left.astype(BF16)
        whole = whole + jnp.dot(part, spread, preferred_element_type=F32)
        left = left - part.astype(F32)
    a, b = iota2(NZ, width)
    whole = jnp.where(a // BLK == (b % Z) // BLK, whole, 0.0)
    high = whole.astype(BF16).astype(F32)
    return jnp.where((b >= Z) & (b < 2 * Z), whole - high, high)


def side_kernel(f_in, c_in, inv, vz, own, f, c, w0, w1, w2, w3, one, part, columns, c_next, c_tile, yup, ydown):
    load_top(f_in, f)
    load_top(c_in, c)
    put_y(GEOM[0], f, c, yup, ydown)
    yup[Z : Z + 8, :] = own[...]
    ydown[Z : Z + 8, :] = own[...]
    for level, w in enumerate((w0, w1, w2, w3)):
        w[0:NZ, :] = block_matrix(inv[level])
        w[NZ:Z, :] = jnp.zeros((Z - NZ, 3 * Z), F32)
    winv = w0[...].astype(BF16)
    start_tile(GEOM[0], winv, f, Setter(one))
    relax_tile(GEOM[0], winv, Coef(vz), one, f, c, ALONE, Setter(part))
    columns[...] = own_columns(GEOM[0], one)
    restrict(GEOM[0], GEOM[1], c, c_next)
    restrict(GEOM[1], GEOM[2], c_next, c_tile)


def merge_kernel(level, count):
    geom = GEOM[level]

    def kernel(xlo, xhi, flags, yup, ydown, up, down):
        lo, hi = tail_of(geom, xlo, count), tail_of(geom, xhi, count)
        lo = [lo[4 + k : 5 + k, :] for k in range(4)]
        hi = [hi[4 + k : 5 + k, :] for k in range(4)]
        f0, f1 = flags[0:1, :] > 0.5, flags[1:2, :] > 0.5
        to_up = [lo[3], lo[1], hi[1], hi[3], jnp.where(f0, lo[2], lo[3]), jnp.where(f1, hi[0], hi[1])]
        to_down = [lo[2], lo[0], hi[0], hi[2], jnp.where(f0, lo[3], lo[2]), jnp.where(f1, hi[1], hi[0])]
        two = jnp.zeros((2, LANES), F32)
        rows = [*to_down, two, jnp.zeros((104, LANES), F32), *to_up, two, jnp.zeros((8, LANES), F32)]
        turned = jnp.concatenate(rows, axis=0).T[0:Z, :]
        lane = zl()
        inside = (lane >= 112) & (lane < 118)
        up[...] = yup[...]
        down[...] = ydown[...]
        up[0:Z, :] = jnp.where(inside, turned, yup[0:Z, :])
        down[0:Z, :] = jnp.where(inside, roll(turned, 112), ydown[0:Z, :])

    return kernel


def pre_edges(geom, f, c, w, vz, own, xlo, xhi, ydn, yun, one, columns):
    winv = w[...].astype(BF16)
    fl = flags_of(geom, own, xlo, xhi, ydn, yun)
    halo = messages(geom, xlo, xhi, ydn, yun, winv)
    relaxed = relax_edges(geom, winv, Coef(vz), one, columns[...], halo, fl, *own_data(geom, xlo, xhi, ydn, yun))
    terms = edge_terms(geom, winv, frame(geom, fl, halo.lo, halo.hi, halo.sides()))
    return terms, frame(geom, fl, *relaxed)


def pre0_kernel(f, c, w, vz, own, xlo, xhi, ydn, yun, one, part, columns, c_next, up, down, terms_out, edges_out, v, res, f_next):
    geom, coarse = GEOM[0], GEOM[1]
    terms, edges = pre_edges(geom, f, c, w, vz, own, xlo, xhi, ydn, yun, one, columns)
    for k in range(3):
        terms_out[k] = terms[k]
        edges_out[k] = edges[k]
    co = Coef(vz)
    for m in (*range(5), *range(19, 24)):
        v[m] = with_terms(geom, part[m], terms, m)
    for m in (*range(4), *range(20, 24)):
        res[m] = tile_residual(geom, co, v, f, c, *edges, m)
    restrict(geom, coarse, res, f_next, (0, 1, 10, 11))
    put_x(coarse, f_next, c_next, up, down, own[...])


def mid1_kernel(f, c, part, terms_in, edges_in, vz, w, c_next, own, v, f_next, one, part_next, columns, yup, ydown, res):
    geom, coarse = GEOM[0], GEOM[1]
    co = Coef(vz)
    terms = [terms_in[k] for k in range(3)]
    edges = [edges_in[k] for k in range(3)]
    for m in range(24):
        v[m] = with_terms(geom, part[m], terms, m)
    for m in range(24):
        res[m] = tile_residual(geom, co, v, f, c, *edges, m)
    restrict(geom, coarse, res, f_next)
    put_y(coarse, f_next, c_next, yup, ydown)
    yup[Z : Z + 8, :] = own[...]
    ydown[Z : Z + 8, :] = own[...]
    winv = w[...].astype(BF16)
    start_tile(coarse, winv, f_next, Setter(one))
    relax_tile(coarse, winv, co, one, f_next, c_next, ALONE, Setter(part_next))
    columns[...] = own_columns(coarse, one)


def pre1_kernel(f, c, w, vz, own, xlo, xhi, ydn, yun, one, part, columns, c_tile, v_out, up, down, chunks, res, f_next):
    geom = GEOM[1]
    terms, edges = pre_edges(geom, f, c, w, vz, own, xlo, xhi, ydn, yun, one, columns)
    for m in range(6):
        v_out[m] = with_terms(geom, part[m], terms, m)
    co = Coef(vz)
    for m in range(6):
        res[m] = tile_residual(geom, co, v_out, f, c, *edges, m)
    restrict(geom, GEOM[2], res, f_next)
    put_x(geom, v_out, None, up, down)
    whole = pack(GEOM[2], [f_next[m] for m in range(6)] + [c_tile[m] for m in range(6)])
    turn = lax.rem(lax.axis_index("gx"), 4) * 32
    whole = [pltpu.roll(x, turn, axis=1) for x in whole]
    for t in range(8):
        for k, x in enumerate(whole):
            chunks[t, k * Z : (k + 1) * Z, :] = x
        chunks[t, 3 * Z : 3 * Z + 8, :] = own[...]


def again0_kernel(f, c, w, vz, e, v, g, part, columns, c_columns, yup, ydown):
    prolong_add(GEOM[0], GEOM[1], e, v, g)
    put_y(GEOM[0], g, None, yup, ydown)
    columns[...] = own_columns(GEOM[0], g)
    c_columns[...] = own_columns(GEOM[0], c)
    relax_tile(GEOM[0], w[...].astype(BF16), Coef(vz), g, f, c, ALONE, Setter(part))


def twice0_kernel(f, c, w, vz, part, _after, twice):
    relax_tile(GEOM[0], w[...].astype(BF16), Coef(vz), part, f, c, ALONE, Setter(twice))


def post_edges(geom, f, c, w, vz, own, xlo, xhi, ydn, yun, g, columns, glo, ghi, gdn, gun):
    fl = flags_of(geom, own, xlo, xhi, ydn, yun)
    halo = Halo(
        part_of(geom, glo, 0), part_of(geom, glo, 1), part_of(geom, ghi, 0), part_of(geom, ghi, 1), gdn[...], gun[...]
    )
    winv = w[...].astype(BF16)
    relaxed = relax_edges(geom, winv, Coef(vz), g, columns[...], halo, fl, *own_data(geom, xlo, xhi, ydn, yun))
    return frame(geom, fl, halo.lo, halo.hi, halo.sides()), frame(geom, fl, *relaxed)


def post0_kernel(f, c, w, vz, own, xlo, xhi, ydn, yun, g, columns, c_columns, twice, glo, ghi, gdn, gun, out):
    geom = GEOM[0]
    rows = geom[0]
    winv = w[...].astype(BF16)
    co = Coef(vz)
    lane = zl()
    edges, edges_next = post_edges(geom, f, c, w, vz, own, xlo, xhi, ydn, yun, g, columns, glo, ghi, gdn, gun)
    low, high, sides = edge_terms(geom, winv, edges)

    def row_residual(v, c_row, beyond):
        beside = jnp.where(lane == 0, 0.0, roll(v, 1)) + jnp.where(lane == LANES - 1, 0.0, roll(v, -1))
        return residual(co, beyond * 0.0625, c_row, v, beside)

    beside = jnp.where(lane < 2, 0.0, roll(sides, 2)) + jnp.where(lane >= 2 * rows - 2, 0.0, roll(sides, -2))
    r = [
        row_residual(low, c[0], edges_next[0]),
        low * 0.0625,
        high * 0.0625,
        row_residual(high, c[rows - 1], edges_next[1]),
        residual(co, edges_next[2] * 0.0625, c_columns[...], sides, beside),
        sides * 0.0625,
    ]
    d = block_dot(winv, jnp.concatenate(r, axis=1))
    d = [d[:, k * LANES : (k + 1) * LANES] for k in range(6)]
    a, b = iota2(LANES, LANES)
    outer = jnp.where((b % 4 == 1) | (b % 4 == 2), 1.0, 0.0) * jnp.where(a == 2 * (b // 4) + b % 4 - 1, 1.0, 0.0)
    inner = jnp.where((b % 4 == 0) | (b % 4 == 3), 1.0, 0.0) * jnp.where(a == 2 * (b // 4) + b % 4 // 3, 1.0, 0.0)
    four = lane_dot(sides + d[4], outer) + lane_dot(d[5], inner)
    inside = (lane < 2) | (lane >= LANES - 2)
    row_terms = {0: low + d[0], 1: d[1], rows - 2: d[2], rows - 1: high + d[3]}
    for m in range(rows):
        x = twice[m] + jnp.where(inside, roll(four, -4 * m - 2), 0.0)
        if m in row_terms:
            x = x + row_terms[m]
        out[pl.ds(m, NZ, stride=24), :] = x[0:NZ, :]


def post1_kernel(
    f, c, w, vz, own, xlo, xhi, ydn, yun, g, part, columns, glo, ghi, gdn, gun, fine_v, e, up, down, one, fine_g
):
    geom = GEOM[1]
    edges, edges_next = post_edges(geom, f, c, w, vz, own, xlo, xhi, ydn, yun, g, columns, glo, ghi, gdn, gun)
    winv = w[...].astype(BF16)
    add_edges(geom, winv, part, edges, Setter(one))
    relax_tile(geom, winv, Coef(vz), one, f, c, edges_next, Setter(e))
    prolong_add(GEOM[0], GEOM[1], e, fine_v, fine_g, (0, 22))
    put_x(GEOM[0], fine_g, None, up, down)


def on_device(right_side, helm_coef, vert_coef, block_inverse, edge_flip):
    inv = block_inverse.reshape(4, NZ, BLK)
    f_in = right_side.reshape(NZ * 24, LANES)
    c_in = helm_coef.reshape(NZ * 24, LANES)
    vert = vert_coef.reshape(1, NZ + 1)
    flip = edge_flip.reshape(1, 4)

    ys = (Z, LANES)
    t0, t1, t2 = tile_shape(0), tile_shape(1), tile_shape(2)
    xs = x_shape(0, 3)
    up, down, own, vz = pl.pallas_call(
        by_swaps(open_kernel, 4, 4, (), ((0, "gx"),)),
        out_shape=[jax.ShapeDtypeStruct(x, F32) for x in (xs, xs, (8, LANES), ys)],
        in_specs=[ANY] * 4,
        out_specs=[VMEM] * 4,
        scratch_shapes=[pltpu.VMEM((NZ, 2, LANES), F32)] * 2
        + [pltpu.VMEM((NZ, 1, LANES), F32)] * 2
        + [pltpu.VMEM((1, NZ + 1), F32), pltpu.VMEM((1, 4), jnp.int32), pltpu.SemaphoreType.DMA((6,))]
        + [pltpu.VMEM(xs, F32)] * 2,
        compiler_params=pltpu.CompilerParams(vmem_limit_bytes=58 * 1024 * 1024),
        name="open",
    )(right_side, helm_coef, vert, flip)
    xlo, xhi = swap(up, down, "gx")
    ws = (Z, 3 * Z)
    f, c, *w, one, part, columns, c1, c_tile, yup, ydown = call(
        side_kernel,
        [t0, t0] + [ws] * 4 + [t0, t0, ys, t1, t2, Y_FULL, Y_FULL],
        [f_in, c_in, inv, vz, own],
        name="side",
    )

    def to_sides(level, count, xlo, xhi, yup, ydown):
        shape = yup.shape
        yup, ydown = call(merge_kernel(level, count), [shape, shape], [xlo, xhi, own, yup, ydown], name=f"merge{level}", got=((0, "gx"),), send=((0, "gy"),))
        return swap(yup, ydown, "gy")

    got0 = (xlo, xhi, *to_sides(0, 3, xlo, xhi, yup, ydown))
    xs = x_shape(1, 3)
    three = (3, Z, LANES)
    up, down, terms, edges = call(
        pre0_kernel,
        [xs, xs, three, three],
        [f, c, w[0], vz, own, *got0, one, part, columns, c1],
        [t0, t0, t1],
        name="pre0",
        got=((5, "gx"), (7, "gy")),
        send=((0, "gx"),),
    )
    xlo, xhi = swap(up, down, "gx")
    v0, f1, one, part, columns, yup, ydown = call(
        mid1_kernel,
        [t0, t1, t1, t1, ys, Y_FULL, Y_FULL],
        [f, c, part, terms, edges, vz, w[1], c1, own],
        [t0],
        name="mid1",
    )
    got1 = (xlo, xhi, *to_sides(1, 3, xlo, xhi, yup, ydown))
    xs = x_shape(1, 2)
    v1, up, down, chunks = call(
        pre1_kernel,
        [t1, xs, xs, (8, 3 * Z + 8, LANES)],
        [f1, c1, w[1], vz, own, *got1, one, part, columns, c_tile],
        [t1, t2],
        name="pre1",
        got=((5, "gx"), (7, "gy")),
        send=((1, "gx"),),
    )
    v1_lo, v1_hi = swap(up, down, "gx")
    chunks = lax.all_to_all(chunks, "gx", 0, 0)
    s2, s3 = (6, Z, 256), (3, Z, 128)
    m2, m3 = (Z, 256), (Z, 128)
    full2, full3 = (Z + 8, 256), (Z + 8, 128)
    f2, c2, fl2, up, down = call(
        open_strip_kernel, [s2, s2, (8, 256), full2, full2], [chunks], name="open2", send=((3, "gy"),)
    )
    side2 = swap(up, down, "gy", True)
    c3, fl3, *c_sides = call(next_coef_kernel, [s3, (8, 128), m2, m2, m3, m3], [c2, fl2], name="coef3")
    part2, first, last, f_part, base_up, base_down = call(
        alone2_kernel, [s2, m2, m2, s3, m3, m3], [f2, c2, w[2], vz, fl2, c3, fl3], [s2, s2], name="alone2"
    )
    terms2, f3, up, down = call(
        pre_strip_kernel,
        [(2, *m2), s3, full3, full3],
        [w[2], vz, fl2, *side2, first, last, *c_sides[:2], f_part, fl3, base_up, base_down],
        name="pre2",
        got=((3, "gy"),),
        send=((2, "gy"),),
    )
    side3 = swap(up, down, "gy", True)
    *alone, twice = call(alone3_kernel, [m3] * 4 + [s3], [f3, c3, w[3], vz, fl3], [s3, s3], name="alone3")
    terms, up, down = call(
        bottom_strip_kernel,
        [(4, *m3), m3, m3],
        [w[3], vz, fl3, *side3, *alone[:2], *c_sides[2:], *alone[2:]],
        name="bottom",
        got=((3, "gy"),),
        send=((1, "gy"),),
    )
    side = swap(up, down, "gy", True)
    (part,) = call(again3_kernel, [s3], [f3, c3, w[3], vz, fl3, twice, terms], [s3], name="again3")
    v2, base_up, base_down = call(base_message_kernel, [s2, m2, m2], [part2, fl2, terms2], name="base2")
    e3, up, down = call(
        last_strip_kernel,
        [s3, m2, m2],
        [w[3], fl3, *side, part, base_up, base_down, v1_lo, v1_hi],
        [m3, m3],
        name="last",
        after=2,
        got=((2, "gy"),),
        send=((1, "gy"),),
    )
    side = swap(up, down, "gy", True)
    first, last, part_low, part_high, yup, ydown, twice = call(
        again2_kernel, [m2] * 4 + [ys, ys, s2], [f2, c2, w[2], vz, fl2, v2, e3, v1], [s2, s2], name="again2"
    )
    terms, up, down = call(
        post_strip_kernel,
        [(4, *m2), ys, ys],
        [w[2], vz, fl2, *side2, first, last, *c_sides[:2], part_low, part_high, *side, v1_lo, v1_hi, own, yup, ydown],
        name="post2",
        got=((3, "gy"), (11, "gy"), (13, "gx")),
        send=((1, "gy"),),
    )
    side = swap(up, down, "gy")
    g1, part, columns, lo, hi = call(
        again1_kernel, [t1, t1, ys, ys, ys], [f1, c1, w[1], vz, v1, twice, terms, v1_lo, v1_hi], [t2], name="again1", got=((7, "gx"),)
    )
    xs = x_shape(0, 2)
    e1, up, down = call(
        post1_kernel,
        [t1, xs, xs],
        [f1, c1, w[1], vz, own, *got1, g1, part, columns, lo, hi, *side, v0],
        [t1, t0],
        name="post1",
        got=((5, "gx"), (7, "gy"), (14, "gy")),
        send=((1, "gx"),),
    )
    xlo, xhi = swap(up, down, "gx")
    g0, part, columns, c_columns, yup, ydown = call(
        again0_kernel, [t0, t0, ys, ys, ys, ys], [f, c, w[0], vz, e1, v0], name="again0"
    )
    up, down = call(
        merge_kernel(0, 2), [ys, ys], [xlo, xhi, own, yup, ydown], name="merge0", got=((0, "gx"),), send=((0, "gy"),)
    )
    side = swap(up, down, "gy")
    (twice,) = call(twice0_kernel, [t0], [f, c, w[0], vz, part, up], name="twice0", after=1)
    (out,) = call(
        post0_kernel,
        [(NZ * 24, LANES)],
        [f, c, w[0], vz, own, *got0, g0, columns, c_columns, twice, xlo, xhi, *side],
        name="post0",
        got=((5, "gx"), (7, "gy"), (13, "gx"), (15, "gy")),
    )
    return out.reshape(NZ, 24, LANES)


def solution(mesh):
    placed = (P(None, "gx", "gy"), P(None, "gx", "gy"), P(), P(), P("gx", "gy", None))
    return jax.shard_map(
        on_device, mesh=mesh, in_specs=placed, out_specs=P(None, "gx", "gy"), check_vma=False
    )
```

```python
import jax
import jax.numpy as jnp
from jax import lax
from jax.experimental import pallas as pl
from jax.experimental.pallas import tpu as pltpu
from jax.sharding import PartitionSpec as P

BLK = 14
NBLK = 5
NZ = 70
Z = 72
LANES = 128
F32 = jnp.float32
BF16 = jnp.bfloat16

GEOM = ((24, 1, 128), (6, 2, 64), (6, 1, 32), (3, 1, 16))


def lane_ids(shape):
    return lax.broadcasted_iota(jnp.int32, shape, len(shape) - 1)


def zl():
    return lane_ids((Z, LANES))


def roll(x, shift):
    shift = shift % x.shape[-1]
    return x if shift == 0 else pltpu.roll(x, shift, axis=1)


def col(x, k):
    return jnp.broadcast_to(x[:, k : k + 1], (Z, LANES))


def iota2(n, m):
    return lax.broadcasted_iota(jnp.int32, (n, m), 0), lax.broadcasted_iota(jnp.int32, (n, m), 1)


def lane_dot(x, mat):
    hi = x.astype(BF16).astype(F32)
    both = jnp.concatenate([hi, x - hi], axis=1).astype(BF16)
    twice = jnp.concatenate([mat, mat], axis=0).astype(BF16)
    return jnp.dot(both, twice, preferred_element_type=F32)


def block_dot(winv, x):
    hi = x.astype(BF16).astype(F32)
    parts = jnp.concatenate([hi, hi, x - hi], axis=0).astype(BF16)
    return jnp.dot(winv, parts, preferred_element_type=F32)


def reverse_matrix(width):
    a, b = iota2(LANES, LANES)
    return jnp.where((b < width) & (a == width - 1 - b), 1.0, 0.0)


def flag_row(flags, k):
    return jnp.broadcast_to(flags[k : k + 1, :], (Z, LANES))


class Coef:
    def __init__(self, ref, width=LANES):
        self.mid, self.up, self.down = [jnp.concatenate([ref[k]] * (width // LANES), axis=1) for k in range(3)]


def residual(co, f, c, v, beside):
    above = pltpu.roll(v, Z - 1, axis=0)
    below = pltpu.roll(v, 1, axis=0)
    return f - (c * 0.0625 + co.mid) * v + beside * 0.0625 + co.up * above + co.down * below


def row_of(geom, v, row):
    m_rows, _, ty = geom
    q, m = divmod(row, m_rows)
    return roll(v[m], -q * ty)


def corners(geom, v):
    m_rows, groups, ty = geom
    last = v[m_rows - 1]
    base = (groups - 1) * ty
    return corner_rows([col(v[0], 0), col(v[0], ty - 1), col(last, base), col(last, base + ty - 1)])


def corner_rows(columns):
    lane = zl()
    out = jnp.zeros((Z, LANES), F32)
    for k, column in enumerate(columns):
        out = jnp.where(lane == 4 + k, column, out)
    return jnp.concatenate([out, jnp.zeros((LANES - Z, LANES), F32)], axis=0).T[0:8, :]


def corner_columns(rows):
    out = jnp.concatenate([rows, jnp.zeros((LANES - 8, LANES), F32)], axis=0).T[0:Z, :]
    return [col(out, 4 + k) for k in range(4)]


def whole_rows(geom):
    return geom[1] == 1 and geom[2] == LANES


def tile_rows(geom):
    m_rows, groups, ty = geom
    return [(q * m_rows + m, m, q * ty) for m in range(m_rows) for q in range(groups)]


def own_columns(geom, v):
    ty = geom[2]
    lane = zl()
    out = jnp.zeros((Z, LANES), F32)
    for r, m, base in tile_rows(geom):
        row = v[m]
        first = roll(row, 2 * r + 1 - base)
        out = jnp.where(lane == 2 * r + 1, first, out)
        last = first if whole_rows(geom) else roll(row, 2 * r - (base + ty - 1))
        out = jnp.where(lane == 2 * r, last, out)
    return out


def pack(geom, parts):
    ty = geom[2]
    per = LANES // ty
    out = []
    for first in range(0, len(parts), per):
        lane = zl()
        acc = parts[first]
        for k, part in enumerate(parts[first + 1 : first + per], 1):
            acc = jnp.where(lane < k * ty, acc, roll(part, k * ty))
        out.append(acc)
    return out


def packed(geom, count):
    per = LANES // geom[2]
    return -(-count // per)


def part_of(geom, ref, k):
    ty = geom[2]
    per = LANES // ty
    return roll(ref[(k // per) * Z : (k // per + 1) * Z, :], -(k % per) * ty)


def put_x(geom, v, c, up, down, flags=None):
    m_rows, groups, _ = geom
    tx = m_rows * groups
    tail = corners(geom, v)
    if flags is not None:
        tail = tail + flags
    for ref, edge, second in ((up, tx - 1, tx - 2), (down, 0, 1)):
        parts = [row_of(geom, v, edge), row_of(geom, v, second)]
        if c is not None:
            parts.append(row_of(geom, c, edge))
        put_parts(geom, parts, tail, ref)


SPLIT = 40


def halved(geom, count):
    return geom[2] == 64 and count == 3


def put_parts(geom, parts, tail, ref):
    if halved(geom, len(parts)):
        lane = lane_ids((SPLIT, LANES))
        rest = jnp.concatenate([parts[2][SPLIT:Z, :], jnp.zeros((2 * SPLIT - Z, LANES), F32)], axis=0)
        ref[0:Z, :] = pack(geom, parts[:2])[0]
        ref[Z : Z + SPLIT, :] = jnp.where(lane < 64, parts[2][0:SPLIT, :], roll(rest, 64))
        ref[Z + SPLIT : Z + SPLIT + 8, :] = tail
        return
    whole = pack(geom, parts)
    for k, part in enumerate(whole):
        ref[k * Z : (k + 1) * Z, :] = part
    ref[len(whole) * Z : len(whole) * Z + 8, :] = tail


def tail_of(geom, ref, count):
    n = message_rows(geom, count)
    return ref[n : n + 8, :]


def message_rows(geom, count):
    return Z + SPLIT if halved(geom, count) else packed(geom, count) * Z


def put_y(geom, v, c, up, down):
    ty = geom[2]
    lane = zl()
    out_up = jnp.zeros((Z, LANES), F32)
    out_down = out_up
    for r, m, base in tile_rows(geom):
        row = v[m]
        mine = lane // 2 == r
        last = roll(row, 2 * r + 1 - (base + ty - 1))
        first = roll(row, 2 * r - base)
        out_up = jnp.where(mine, last, out_up)
        out_down = jnp.where(mine, first, out_down)
        if c is not None:
            row = c[m]
            out_up = jnp.where(lane == 65 + 2 * r, roll(row, 65 + 2 * r - (base + ty - 1)), out_up)
            out_down = jnp.where(lane == 64 + 2 * r, roll(row, 64 + 2 * r - base), out_down)
    up[0:Z, :] = out_up
    down[0:Z, :] = out_down


def relay_order(lo, hi, f0, f1):
    up = [lo[3], lo[1], hi[1], hi[3], jnp.where(f0, lo[2], lo[3]), jnp.where(f1, hi[0], hi[1])]
    down = [lo[2], lo[0], hi[0], hi[2], jnp.where(f0, lo[3], lo[2]), jnp.where(f1, hi[1], hi[0])]
    return up, down


def relayed(lo, hi, flags):
    lo = [lo[4 + k : 5 + k, :] for k in range(4)]
    hi = [hi[4 + k : 5 + k, :] for k in range(4)]
    up, down = relay_order(lo, hi, flags[0:1, :] > 0.5, flags[1:2, :] > 0.5)
    two = jnp.zeros((2, LANES), F32)
    rows = [*down, two, jnp.zeros((104, LANES), F32), *up, two, jnp.zeros((8, LANES), F32)]
    turned = jnp.concatenate(rows, axis=0).T[0:Z, :]
    lane = zl()
    inside = (lane >= 112) & (lane < 118)
    return jnp.where(inside, turned, 0.0), jnp.where(inside, roll(turned, 112), 0.0)


def odd_lanes():
    return zl() % 2 == 1


class Halo:
    def __init__(self, lo, lo2, hi, hi2, dn, un):
        self.lo, self.lo2, self.hi, self.hi2, self.dn, self.un = lo, lo2, hi, hi2, dn, un

    def sides(self):
        return jnp.where(odd_lanes(), self.dn, self.un)

    def seconds(self):
        return jnp.where(odd_lanes(), roll(self.dn, 1), roll(self.un, -1))


class Flags:
    def __init__(self, own, lo, hi, dn, un):
        self.own, self.lo, self.hi, self.dn, self.un = own, lo, hi, dn, un


def turn_row(geom, row, flag):
    return jnp.where(flag > 0.5, lane_dot(row, reverse_matrix(geom[2])), row)


def turn_sides(geom, sides, flag_dn, flag_un):
    tx = geom[0] * geom[1]
    flag = jnp.where(odd_lanes(), flag_dn, flag_un)
    a, b = iota2(LANES, LANES)
    mat = jnp.where((b < 2 * tx) & (a == 2 * (tx - 1 - b // 2) + b % 2), 1.0, 0.0)
    return jnp.where(flag > 0.5, lane_dot(sides, mat), sides)


def frame(geom, fl, lo, hi, sides):
    return (
        turn_row(geom, lo, flag_row(fl.own, 0)),
        turn_row(geom, hi, flag_row(fl.own, 1)),
        turn_sides(geom, sides, flag_row(fl.own, 2), flag_row(fl.own, 3)),
    )


def relax_edges(geom, winv, co, v, columns, halo, fl, f_lo, c_lo, f_hi, c_hi, f_sides, c_sides):
    m_rows, groups, ty = geom
    tx = m_rows * groups
    lane = zl()
    dn, un = halo.dn, halo.un

    def beside_row(edge, second, mine, low, high):
        left = jnp.where(lane == 0, roll(low, -112), roll(edge, 1))
        right = jnp.where(lane == ty - 1, roll(high, ty - 113), roll(edge, -1))
        return second + mine + left + right

    def choose(flags, k, x, place):
        x = roll(x, 112 - place)
        return jnp.where(flag_row(flags, k) > 0.5, roll(x, -1), x)

    b_lo = beside_row(
        halo.lo,
        halo.lo2,
        turn_row(geom, row_of(geom, v, 0), flag_row(fl.lo, 1)),
        choose(fl.lo, 2, dn, 112),
        choose(fl.lo, 3, un, 112),
    )
    b_hi = beside_row(
        halo.hi,
        halo.hi2,
        turn_row(geom, row_of(geom, v, tx - 1), flag_row(fl.hi, 0)),
        choose(fl.hi, 2, dn, 114),
        choose(fl.hi, 3, un, 114),
    )
    edge = halo.sides()
    mine = turn_sides(geom, columns, flag_row(fl.dn, 3), flag_row(fl.un, 2))
    below = jnp.where(lane == 1, roll(dn, -115), jnp.where(lane == 0, roll(un, -116), roll(edge, 2)))
    last = 2 * (tx - 1)
    above = jnp.where(lane == last + 1, roll(dn, last - 116), jnp.where(lane == last, roll(un, last - 117), roll(edge, -2)))
    b_sides = halo.seconds() + mine + below + above
    r_lo = residual(co, f_lo, c_lo, halo.lo, b_lo)
    r_hi = residual(co, f_hi, c_hi, halo.hi, b_hi)
    r_sides = residual(co, f_sides, c_sides, edge, b_sides)
    d = block_dot(winv, jnp.concatenate([r_lo, r_hi, r_sides], axis=1))
    return halo.lo + d[:, :LANES], halo.hi + d[:, LANES : 2 * LANES], edge + d[:, 2 * LANES :]


def tile_residual(geom, co, v, f, c, lo, hi, sides, m):
    m_rows, groups, ty = geom
    lane = zl()
    here = v[m]
    if lo is None:
        lo = hi = jnp.zeros((Z, LANES), F32)
    if m > 0:
        low_x = v[m - 1]
    else:
        low_x = lo if groups == 1 else jnp.where(lane < ty, lo, roll(v[m_rows - 1], ty))
    if m < m_rows - 1:
        high_x = v[m + 1]
    elif groups == 1:
        high_x = hi
    else:
        high_x = jnp.where(lane < (groups - 1) * ty, roll(v[0], -ty), roll(hi, (groups - 1) * ty))
    low_y, high_y = roll(here, 1), roll(here, -1)
    if sides is None:
        low_y = jnp.where(lane % ty == 0, 0.0, low_y)
        high_y = jnp.where(lane % ty == ty - 1, 0.0, high_y)
        return residual(co, f[m], c[m], here, low_x + high_x + low_y + high_y)
    for q in range(groups):
        row = q * m_rows + m
        low = roll(sides, q * ty - 2 * row - 1)
        high = low if whole_rows(geom) else roll(sides, q * ty + ty - 1 - 2 * row)
        low_y = jnp.where(lane == q * ty, low, low_y)
        high_y = jnp.where(lane == q * ty + ty - 1, high, high_y)
    return residual(co, f[m], c[m], here, low_x + high_x + low_y + high_y)


def relax_tile(geom, winv, co, v, f, c, edges, store):
    lo, hi, sides = edges
    for m in range(0, geom[0], 2):
        rows = [k for k in (m, m + 1) if k < geom[0]]
        r = [tile_residual(geom, co, v, f, c, lo, hi, sides, k) for k in rows]
        d = block_dot(winv, r[0] if len(r) == 1 else jnp.concatenate(r, axis=1))
        for i, k in enumerate(rows):
            store(k, v[k] + d[:, i * LANES : (i + 1) * LANES])


ALONE = (None, None, None)


def edge_terms(geom, winv, edges):
    ty = geom[2]
    lane = zl()
    d = block_dot(winv, jnp.concatenate(edges, axis=1) * 0.0625)
    low, high, sides = [d[:, k * LANES : (k + 1) * LANES] for k in range(3)]
    if ty < LANES:
        low = jnp.where(lane < ty, low, 0.0)
        high = jnp.where(lane < ty, high, 0.0)
    return low, high, sides


def with_terms(geom, x, terms, m):
    m_rows, groups, ty = geom
    low, high, sides = terms
    lane = zl()
    if m == 0:
        x = x + low
    if m == m_rows - 1:
        x = x + roll(high, (groups - 1) * ty)
    for q in range(groups):
        row = q * m_rows + m
        first = roll(sides, q * ty - 2 * row - 1)
        last = first if whole_rows(geom) else roll(sides, q * ty + ty - 1 - 2 * row)
        x = x + jnp.where(lane == q * ty, first, jnp.where(lane == q * ty + ty - 1, last, 0.0))
    return x


def add_edges(geom, winv, part, edges, store):
    terms = edge_terms(geom, winv, edges)
    for m in range(geom[0]):
        store(m, with_terms(geom, part[m], terms, m))


def start_tile(geom, winv, f, store):
    for m in range(0, geom[0], 2):
        rows = [k for k in (m, m + 1) if k < geom[0]]
        parts = [f[k] for k in rows]
        d = block_dot(winv, parts[0] if len(parts) == 1 else jnp.concatenate(parts, axis=1))
        for i, k in enumerate(rows):
            store(k, d[:, i * LANES : (i + 1) * LANES])


def restrict(fine, coarse, v, out, wanted=None):
    m_rows, _, ty = fine
    cm, cq, cty = coarse
    a, b = iota2(LANES, LANES)
    for mc in range(cm):
        acc = None
        for qc in range(cq):
            if wanted is not None and qc * cm + mc not in wanted:
                continue
            q, m = divmod(2 * (qc * cm + mc), m_rows)
            inside = (b >= qc * cty) & (b < (qc + 1) * cty) & (a // 2 == b - qc * cty + q * (ty // 2))
            term = lane_dot(v[m] + v[m + 1], jnp.where(inside, 0.25, 0.0))
            acc = term if acc is None else acc + term
        if acc is not None:
            out[mc] = acc


def prolong_add(fine, coarse, e, v, out, rows=None):
    m_rows, groups, ty = fine
    cm, _, cty = coarse
    a, b = iota2(LANES, LANES)
    for m in range(0, m_rows, 2) if rows is None else rows:
        acc = None
        for q in range(groups):
            qc, mc = divmod((q * m_rows + m) // 2, cm)
            inside = (b >= q * ty) & (b < (q + 1) * ty) & (a - qc * cty == (b - q * ty) // 2)
            term = lane_dot(e[mc], jnp.where(inside, 1.0, 0.0))
            acc = term if acc is None else acc + term
        out[m] = v[m] + acc
        out[m + 1] = v[m + 1] + acc


class Setter:
    def __init__(self, ref):
        self.ref = ref

    def __call__(self, m, value):
        self.ref[m] = value


def messages(geom, xlo, xhi, ydn, yun, winv):
    raw = [part_of(geom, xlo, 0), part_of(geom, xlo, 1), part_of(geom, xhi, 0), part_of(geom, xhi, 1), ydn[0:Z, :], yun[0:Z, :]]
    d = block_dot(winv, jnp.concatenate(raw, axis=1))
    return Halo(*[d[:, k * LANES : (k + 1) * LANES] for k in range(6)])


def third_of(geom, ref):
    if not halved(geom, 3):
        return part_of(geom, ref, 2)
    both = ref[Z : Z + SPLIT, :]
    return jnp.concatenate([both, roll(both[0 : Z - SPLIT, :], 64)], axis=0)


def own_data(geom, xlo, xhi, ydn, yun):
    dn, un = ydn[0:Z, :], yun[0:Z, :]
    f_sides = jnp.where(odd_lanes(), dn, un)
    c_sides = roll(f_sides, -64)
    return (
        part_of(geom, xlo, 0),
        third_of(geom, xlo),
        part_of(geom, xhi, 0),
        third_of(geom, xhi),
        f_sides,
        c_sides,
    )


def flags_of(geom, own, xlo, xhi, ydn, yun):
    return Flags(own[...], tail_of(geom, xlo, 3), tail_of(geom, xhi, 3), ydn[Z : Z + 8, :], yun[Z : Z + 8, :])


def load_top(src, dst):
    for x in range(24):
        dst[x, 0:NZ, :] = src[pl.ds(x, NZ, stride=24), :]
        dst[x, NZ:Z, :] = jnp.zeros((Z - NZ, LANES), F32)


STRIPS = {2: (6, 32, 256), 3: (3, 16, 128)}


def in_tile(strip):
    _, ty, width = strip
    return lane_ids((Z, width)) % ty


def group_dot(x, mat):
    parts = [lane_dot(x[:, k : k + LANES], mat) for k in range(0, x.shape[1], LANES)]
    return parts[0] if len(parts) == 1 else jnp.concatenate(parts, axis=1)


def turn_groups(strip, x, flags, k, count):
    _, ty, width = strip
    a, b = iota2(LANES, LANES)
    mat = jnp.where((a // ty == b // ty) & (b % ty < count) & (a % ty == count - 1 - b % ty), 1.0, 0.0)
    flag = jnp.broadcast_to(flags[k : k + 1, :], (Z, width))
    return jnp.where(flag > 0.5, group_dot(x, mat), x)


def strip_ends(strip, v, flags):
    m_rows, ty, _ = strip
    low = turn_groups(strip, roll(v[m_rows - 1], ty), flags, 0, ty)
    high = turn_groups(strip, roll(v[0], -ty), flags, 1, ty)
    return low, high


def strip_column(strip, v, y, offset, out):
    lt = in_tile(strip)
    for m in range(strip[0]):
        out = jnp.where(lt == offset + m, roll(v[m], offset + m - y), out)
    return out


def strip_message(strip, v, c, ends, up, down):
    m_rows, ty, width = strip
    lt = in_tile(strip)
    for ref, edge, second in ((up, ty - 1, ty - 2), (down, 0, 1)):
        out = strip_column(strip, v, edge, 0, jnp.zeros((Z, width), F32))
        out = strip_column(strip, v, second, m_rows, out)
        if c is not None:
            out = strip_column(strip, c, edge, 2 * m_rows, out)
        for k, end in enumerate(ends):
            out = jnp.where(lt == 3 * m_rows + k, roll(end, 3 * m_rows + k - edge), out)
        ref[0:Z, :] = out


def strip_edges(strip, winv, co, sides):
    m_rows, _, width = strip
    lt = in_tile(strip)
    r = []
    for x, raw, flags, k, mine in sides:
        mine = turn_groups(strip, mine, flags, k, m_rows)
        low = jnp.where(lt == 0, roll(x, -3 * m_rows), roll(x, 1))
        high = jnp.where(lt == m_rows - 1, roll(x, -2 * m_rows - 2), roll(x, -1))
        r.append(residual(co, raw, roll(raw, -2 * m_rows), x, roll(x, -m_rows) + mine + low + high))
    d = block_dot(winv, jnp.concatenate(r, axis=1))
    return [side[0] + d[:, k * width : (k + 1) * width] for k, side in enumerate(sides)]


def strip_frame(strip, flags, low, high):
    return turn_groups(strip, low, flags, 2, strip[0]), turn_groups(strip, high, flags, 3, strip[0])


def strip_residual(strip, co, v, f, c, ends, sides, m):
    m_rows, ty, _ = strip
    lt = in_tile(strip)
    low_x = v[m - 1] if m > 0 else ends[0]
    high_x = v[m + 1] if m < m_rows - 1 else ends[1]
    low = 0.0 if sides is None else roll(sides[0], -m)
    high = 0.0 if sides is None else roll(sides[1], ty - 1 - m)
    low_y = jnp.where(lt == 0, low, roll(v[m], 1))
    high_y = jnp.where(lt == ty - 1, high, roll(v[m], -1))
    return residual(co, f[m], c[m], v[m], low_x + high_x + low_y + high_y)


def strip_relax(strip, winv, co, v, f, c, flags, sides, store):
    ends = strip_ends(strip, v, flags)
    for m in range(strip[0]):
        r = strip_residual(strip, co, v, f, c, ends, sides, m)
        store(m, v[m] + block_dot(winv, r))


def strip_add_sides(strip, winv, part, sides, store):
    m_rows, ty, width = strip
    lt = in_tile(strip)
    d = block_dot(winv, jnp.concatenate(sides, axis=1) * 0.0625)
    for m in range(m_rows):
        low, high = roll(d[:, :width], -m), roll(d[:, width:], ty - 1 - m)
        store(m, part[m] + jnp.where(lt == 0, low, jnp.where(lt == ty - 1, high, 0.0)))


def strip_side_terms(strip, winv, co, flags, c_columns, sides, sides_next):
    m_rows, ty, width = strip
    lt = in_tile(strip)
    d = block_dot(winv, jnp.concatenate(sides, axis=1) * 0.0625)
    first, last = d[:, :width], d[:, width:]
    turned = [jnp.broadcast_to(flags[k : k + 1, :], (Z, width)) > 0.5 for k in range(2)]
    step = ty - m_rows + 1
    r = []
    for mine, other, c, beyond in ((first, last, c_columns[0], sides_next[0]), (last, first, c_columns[1], sides_next[1])):
        low = jnp.where(turned[0], roll(other, step), roll(mine, step))
        high = jnp.where(turned[1], roll(other, -step), roll(mine, -step))
        low = jnp.where(lt == 0, low, roll(mine, 1))
        high = jnp.where(lt == m_rows - 1, high, roll(mine, -1))
        r.append(residual(co, beyond * 0.0625, c, mine, low + high))
    return first, last, r


def strip_restrict(v, out):
    a, b = iota2(LANES, LANES)
    for m in range(3):
        both = v[2 * m] + v[2 * m + 1]
        out[m] = lane_dot(both[:, :LANES], jnp.where(a // 2 == b, 0.25, 0.0)) + lane_dot(
            both[:, LANES:], jnp.where(a // 2 == b - 64, 0.25, 0.0)
        )


def open_strip_kernel(chunks, f, c, flags, up, down):
    strip = STRIPS[2]
    group = lane_ids((Z, LANES)) // 32
    for m in range(6):
        for ref, k in ((f, m), (c, 6 + m)):
            part = (k // 4) * Z
            halves = []
            for h in range(2):
                acc = None
                for g in range(4):
                    x = chunks[4 * h + g, part : part + Z, :]
                    acc = x if acc is None else jnp.where(group == (g + k) % 4, x, acc)
                halves.append(roll(acc, -(k % 4) * 32))
            ref[m] = jnp.concatenate(halves, axis=1)
    group = lane_ids((8, LANES)) // 32
    for h in range(2):
        acc = None
        for g in range(4):
            x = chunks[4 * h + g, 3 * Z : 3 * Z + 8, :]
            acc = x if acc is None else jnp.where(group == g, x, acc)
        flags[:, h * LANES : (h + 1) * LANES] = acc
    strip_message(strip, f, c, strip_ends(strip, f, flags), up, down)
    up[Z : Z + 8, :] = flags[...]
    down[Z : Z + 8, :] = flags[...]


def strip_sides(values, raws, dn, un, first, last):
    return (
        (values[0], raws[0], dn[Z : Z + 8, :], 3, first[...]),
        (values[1], raws[1], un[Z : Z + 8, :], 2, last[...]),
    )


def column_restrict(strip, x):
    a, b = iota2(LANES, LANES)
    out = None
    for h in range(2):
        inside = (b // 16 == 4 * h + a // 32) & ((a % 32) // 2 == b % 16) & (a % 32 < strip[0])
        term = lane_dot(x[:, h * LANES : (h + 1) * LANES], jnp.where(inside, 0.25, 0.0))
        out = term if out is None else out + term
    return out


def pre_strip_kernel(
    w, vz, flags, dn, un, first_column, last_column, c_low, c_high, f_part, fl_next, base_up, base_down, terms, f_next, up, down
):
    strip, small = STRIPS[2], STRIPS[3]
    winv = w[...].astype(BF16)
    co = Coef(vz, strip[2])
    raws = [dn[0:Z, :], un[0:Z, :]]
    values = block_dot(winv, jnp.concatenate(raws, axis=1))
    values = [values[:, : strip[2]], values[:, strip[2] :]]
    edges = strip_edges(strip, winv, co, strip_sides(values, raws, dn, un, first_column, last_column))
    first, last, r = strip_side_terms(
        strip, winv, co, flags, (c_low[...], c_high[...]), strip_frame(strip, flags, *values), strip_frame(strip, flags, *edges)
    )
    terms[0] = first
    terms[1] = last
    low = column_restrict(strip, r[0] + first * 0.0625)
    high = column_restrict(strip, r[1] + last * 0.0625)
    m_rows, ty, width = small
    lt = in_tile(small)
    for m in range(m_rows):
        x = jnp.where(lt == 0, roll(low, -m), 0.0)
        f_next[m] = f_part[m] + jnp.where(lt == ty - 1, roll(high, ty - 1 - m), x)
    turned = [jnp.broadcast_to(fl_next[k : k + 1, :], (Z, width)) > 0.5 for k in range(2)]
    for ref, base, mine, other in ((up, base_up, high, low), (down, base_down, low, high)):
        before, after = 3 * m_rows + ty - m_rows + 1, 3 * m_rows + 1 - ty
        end_low = jnp.where(turned[0], roll(other, before), roll(mine, before))
        end_high = jnp.where(turned[1], roll(other, after), roll(mine, after))
        add = jnp.where(lt < m_rows, mine, 0.0)
        add = jnp.where(lt == 3 * m_rows, end_low, add)
        add = jnp.where(lt == 3 * m_rows + 1, end_high, add)
        ref[0:Z, :] = base[...] + add
        ref[Z : Z + 8, :] = fl_next[...]


def next_coef_kernel(c, flags, c_next, fl_next, low, high, low_next, high_next):
    strip_restrict(c, c_next)
    a, b = iota2(LANES, LANES)
    fl_next[...] = lane_dot(flags[:, :LANES], jnp.where((b < 64) & (a == (b // 16) * 32), 1.0, 0.0)) + lane_dot(
        flags[:, LANES:], jnp.where((b >= 64) & (a == (b // 16 - 4) * 32), 1.0, 0.0)
    )
    for strip, ref, first, last in ((STRIPS[2], c, low, high), (STRIPS[3], c_next, low_next, high_next)):
        zero = jnp.zeros((Z, strip[2]), F32)
        first[...] = strip_column(strip, ref, 0, 0, zero)
        last[...] = strip_column(strip, ref, strip[1] - 1, 0, zero)


def alone2_kernel(f, c, w, vz, flags, c_next, fl_next, part, low, high, f_part, up, down, v, res):
    strip, small = STRIPS[2], STRIPS[3]
    winv = w[...].astype(BF16)
    co = Coef(vz, strip[2])
    for m in range(6):
        v[m] = block_dot(winv, f[m])
    zero = jnp.zeros((Z, strip[2]), F32)
    low[...] = strip_column(strip, v, 0, 0, zero)
    high[...] = strip_column(strip, v, strip[1] - 1, 0, zero)
    strip_relax(strip, winv, co, v, f, c, flags, None, Setter(part))
    ends = strip_ends(strip, part, flags)
    for m in range(6):
        res[m] = strip_residual(strip, co, part, f, c, ends, None, m)
    strip_restrict(res, f_part)
    strip_message(small, f_part, c_next, strip_ends(small, f_part, fl_next), up, down)


def bottom_strip_kernel(
    w, vz, flags, dn, un, first_column, last_column, c_low, c_high, part_low, part_high, terms, up, down
):
    strip = STRIPS[3]
    width = strip[2]
    winv = w[...].astype(BF16)
    co = Coef(vz)
    raws = [dn[0:Z, :], un[0:Z, :]]
    values = block_dot(winv, jnp.concatenate(raws, axis=1))
    values = [values[:, :width], values[:, width:]]
    edges = strip_edges(strip, winv, co, strip_sides(values, raws, dn, un, first_column, last_column))
    first, last, r = strip_side_terms(
        strip, winv, co, flags, (c_low[...], c_high[...]), strip_frame(strip, flags, *values), strip_frame(strip, flags, *edges)
    )
    d = block_dot(winv, jnp.concatenate([r[0], first * 0.0625, last * 0.0625, r[1]], axis=1))
    d = [d[:, k * width : (k + 1) * width] for k in range(4)]
    d[0] = first + d[0]
    d[3] = last + d[3]
    for k in range(4):
        terms[k] = d[k]
    up[...] = part_high[...] + d[3]
    down[...] = part_low[...] + d[0]


def with_columns(strip, x, terms, m):
    ty = strip[1]
    lt = in_tile(strip)
    for k, y in enumerate((0, 1, ty - 2, ty - 1)):
        x = x + jnp.where(lt == y, roll(terms[k], y - m), 0.0)
    return x


def last_strip_kernel(w, flags, dn, un, part, base_up, base_down, _lo, _hi, e, up, down, small_up, small_down):
    strip, fine = STRIPS[3], STRIPS[2]
    winv = w[...].astype(BF16)
    strip_add_sides(strip, winv, part, strip_frame(strip, flags, dn[...], un[...]), Setter(e))
    strip_message(strip, e, None, strip_ends(strip, e, flags), small_up, small_down)
    a, b = iota2(LANES, LANES)
    for h in range(2):
        lt = b % 32
        source = jnp.where(lt < 12, (lt % 6) // 2, jnp.where((lt == 18) | (lt == 19), lt - 9, 15))
        spread = jnp.where((lt != 15) & (a == 64 * h + (b // 32) * 16 + source) & (source < 15), 1.0, 0.0)
        half = slice(h * LANES, (h + 1) * LANES)
        up[:, half] = base_up[:, half] + lane_dot(small_up[...], spread)
        down[:, half] = base_down[:, half] + lane_dot(small_down[...], spread)


def base_message_kernel(part, flags, terms, v, up, down):
    strip = STRIPS[2]
    lt = in_tile(strip)
    for m in range(6):
        x = jnp.where(lt == 0, roll(terms[0], -m), 0.0)
        v[m] = part[m] + jnp.where(lt == strip[1] - 1, roll(terms[1], strip[1] - 1 - m), x)
    strip_message(strip, v, None, strip_ends(strip, v, flags), up, down)


def again2_kernel(f, c, w, vz, flags, v, e, tile_v, xlo, xhi, own, low, high, part_low, part_high, yup, ydown, twice, g, part):
    strip = STRIPS[2]
    a, b = iota2(LANES, LANES)
    for m in range(3):
        add = jnp.concatenate([lane_dot(e[m], jnp.where(a == 64 * h + b // 2, 1.0, 0.0)) for h in range(2)], axis=1)
        g[2 * m] = v[2 * m] + add
        g[2 * m + 1] = v[2 * m + 1] + add
    zero = jnp.zeros((Z, strip[2]), F32)
    low[...] = strip_column(strip, g, 0, 0, zero)
    high[...] = strip_column(strip, g, strip[1] - 1, 0, zero)
    winv = w[...].astype(BF16)
    co = Coef(vz, strip[2])
    strip_relax(strip, winv, co, g, f, c, flags, None, Setter(part))
    strip_relax(strip, winv, co, part, f, c, flags, None, Setter(twice))
    part_low[...] = strip_column(strip, twice, 0, 0, zero)
    part_high[...] = strip_column(strip, twice, strip[1] - 1, 0, zero)
    put_y(GEOM[1], tile_v, None, yup, ydown)
    add_up, add_down = relayed(tail_of(GEOM[1], xlo, 2), tail_of(GEOM[1], xhi, 2), own)
    yup[...] = yup[...] + add_up
    ydown[...] = ydown[...] + add_down


def alone3_kernel(f, c, w, vz, flags, low, high, part_low, part_high, twice, v, part):
    strip = STRIPS[3]
    winv = w[...].astype(BF16)
    co = Coef(vz)
    for m in range(3):
        v[m] = block_dot(winv, f[m])
    strip_relax(strip, winv, co, v, f, c, flags, None, Setter(part))
    strip_relax(strip, winv, co, part, f, c, flags, None, Setter(twice))
    zero = jnp.zeros((Z, LANES), F32)
    for ref, first, last in ((v, low, high), (twice, part_low, part_high)):
        first[...] = strip_column(strip, ref, 0, 0, zero)
        last[...] = strip_column(strip, ref, strip[1] - 1, 0, zero)


def again3_kernel(f, c, w, vz, flags, twice, terms, part, v):
    strip = STRIPS[3]
    for m in range(3):
        v[m] = with_columns(strip, twice[m], terms, m)
    strip_relax(strip, w[...].astype(BF16), Coef(vz), v, f, c, flags, None, Setter(part))


def tile_lanes(x, step):
    t = lax.rem(lax.axis_index("gx") + (step + 8), 8)
    half = jnp.where(t < 4, x[:, :LANES], x[:, LANES:])
    return pltpu.roll(half, lax.rem(8 - t, 4) * 32, axis=1)


def post_strip_kernel(
    w, vz, flags, dn, un, first_column, last_column, c_low, c_high, part_low, part_high, gdn, gun, own, yup, ydown, terms, up, down
):
    strip = STRIPS[2]
    width = strip[2]
    winv = w[...].astype(BF16)
    co = Coef(vz, width)
    raws = [dn[0:Z, :], un[0:Z, :]]
    values = [gdn[...], gun[...]]
    edges = strip_edges(strip, winv, co, strip_sides(values, raws, dn, un, first_column, last_column))
    first, last, r = strip_side_terms(
        strip, winv, co, flags, (c_low[...], c_high[...]), strip_frame(strip, flags, *values), strip_frame(strip, flags, *edges)
    )
    d = block_dot(winv, jnp.concatenate([r[0], first * 0.0625, last * 0.0625, r[1]], axis=1))
    d = [d[:, k * width : (k + 1) * width] for k in range(4)]
    d[0] = first + d[0]
    d[3] = last + d[3]
    for k in range(4):
        terms[k] = d[k]
    low, high = part_low[...] + d[0], part_high[...] + d[3]
    lane = zl()

    def tile_corners(step):
        first_lanes, last_lanes = tile_lanes(low, step), tile_lanes(high, step)
        return [roll(x, 112 - place) for x, place in ((first_lanes, 0), (last_lanes, 0), (first_lanes, 5), (last_lanes, 5))]

    f0, f1 = flag_row(own, 0) > 0.5, flag_row(own, 1) > 0.5
    a, b = iota2(LANES, LANES)
    spread = jnp.where((b < 24) & (a == b // 4), 1.0, 0.0)
    add_up = lane_dot(tile_lanes(high, 0), spread)
    add_down = lane_dot(tile_lanes(low, 0), spread)
    to_up, to_down = relay_order(tile_corners(-1), tile_corners(1), f0, f1)
    for k in range(6):
        add_up = jnp.where(lane == 112 + k, roll(to_up[k], k), add_up)
        add_down = jnp.where(lane == 112 + k, roll(to_down[k], k), add_down)
    up[...] = yup[...] + add_up
    down[...] = ydown[...] + add_down


def again1_kernel(f, c, w, vz, v, twice, terms, xlo, xhi, g, part, columns, lo_out, hi_out, tile):
    fine, geom = GEOM[1], GEOM[2]
    rows = []
    for m in range(6):
        rows.append(with_columns(STRIPS[2], twice[m], terms, m))
        tile[m] = tile_lanes(rows[m], 0)
    prolong_add(fine, geom, tile, v, g)
    a, b = iota2(LANES, LANES)
    spread = jnp.where((b < 64) & (a == b // 2), 1.0, 0.0)
    for ref, out, row in ((xlo, lo_out, tile_lanes(rows[5], -1)), (xhi, hi_out, tile_lanes(rows[0], 1))):
        add = lane_dot(row, spread)
        out[...] = pack(fine, [part_of(fine, ref, 0) + add, part_of(fine, ref, 1) + add])[0]
    columns[...] = own_columns(fine, g)
    relax_tile(fine, w[...].astype(BF16), Coef(vz), g, f, c, ALONE, Setter(part))


def swap_pairs(axis, which, nearest=False):
    sizes = lax.axis_size("gx"), lax.axis_size("gy")
    out = []
    for i in range(sizes[0]):
        for j in range(sizes[1]):
            at = [i, j]
            dim = 0 if axis == "gx" else 1
            n = sizes[dim]
            at[dim] = (at[dim] ^ 1) if which == 0 else (at[dim] + (1 if at[dim] % 2 else n - 1)) % n
            if nearest and 2 * j // n != 2 * at[1] // n:
                at[0] = i ^ 1
            out.append((i * sizes[1] + j, at[0] * sizes[1] + at[1]))
    return out


def swap(first, second, axis, nearest=False):
    both = ("gx", "gy")
    return (
        lax.ppermute(first, both, swap_pairs(axis, 0, nearest)),
        lax.ppermute(second, both, swap_pairs(axis, 1, nearest)),
    )


ANY = pl.BlockSpec(memory_space=pl.ANY)
LIMIT = 14 * 1024 * 1024
VMEM = pl.BlockSpec(memory_space=pltpu.VMEM)


class Either:
    def __init__(self, first, a, b):
        self.first, self.a, self.b = first, a, b

    def __getitem__(self, index):
        return jnp.where(self.first, self.a[index], self.b[index])


def is_even(axis):
    return lax.rem(lax.axis_index(axis), 2) == 0


def by_swaps(kernel, n_in, n_out, got, send):
    def wrapped(*refs):
        refs = list(refs)
        for place, axis in got:
            a, b = refs[place], refs[place + 1]
            refs[place], refs[place + 1] = Either(is_even(axis), b, a), Either(is_even(axis), a, b)
        extra = refs[len(refs) - 2 * len(send) :]
        refs = refs[: len(refs) - 2 * len(send)]
        outs = []
        for k, (place, axis) in enumerate(send):
            place += n_in
            outs.append((refs[place], refs[place + 1], extra[2 * k], extra[2 * k + 1], axis))
            refs[place], refs[place + 1] = extra[2 * k], extra[2 * k + 1]
        kernel(*refs)
        for first, second, up, down, axis in outs:
            even = is_even(axis)
            up, down = up[...], down[...]
            first[...] = jnp.where(even, up, down)
            second[...] = jnp.where(even, down, up)

    return wrapped


def call(kernel, outs, args, scratch=(), name=None, after=0, got=(), send=()):
    scratch = [pltpu.VMEM(s, F32) for s in scratch]
    scratch += [pltpu.VMEM(outs[place], F32) for place, _ in send for _ in range(2)]
    return pl.pallas_call(
        by_swaps(kernel, len(args), len(outs), got, send),
        out_shape=[jax.ShapeDtypeStruct(s, F32) for s in outs],
        in_specs=[VMEM] * (len(args) - after) + [ANY] * after,
        out_specs=[VMEM] * len(outs),
        scratch_shapes=scratch,
        compiler_params=pltpu.CompilerParams(vmem_limit_bytes=LIMIT),
        name=name,
    )(*args)


def tile_shape(level):
    return (GEOM[level][0], Z, LANES)


def x_shape(level, count):
    return (message_rows(GEOM[level], count) + 8, LANES)


Y_FULL = (Z + 8, LANES)


def open_kernel(f_in, c_in, vert_in, flip_in, up, down, own, vz, f_low, f_high, c_low, c_high, vert, flip, sems):
    pairs = (
        (vert_in, vert),
        (flip_in, flip),
        (f_in.at[:, 0:2, :], f_low),
        (f_in.at[:, 22:24, :], f_high),
        (c_in.at[:, 0:1, :], c_low),
        (c_in.at[:, 23:24, :], c_high),
    )
    copies = [pltpu.make_async_copy(src, dst, sems.at[k]) for k, (src, dst) in enumerate(pairs)]
    for copy in copies:
        copy.start()
    for copy in copies[:2]:
        copy.wait()
    a, b = iota2(8, 4)
    flags = jnp.broadcast_to(flip[...].astype(F32), (8, 4))
    flags = jnp.broadcast_to(jnp.sum(jnp.where(a == b, flags, 0.0), axis=1, keepdims=True), (8, LANES))
    own[...] = flags
    a, b = iota2(Z, NZ + 1)
    coef = jnp.broadcast_to(vert[...], (Z, NZ + 1))
    high = jnp.sum(jnp.where((b == a + 1) & (a < NZ), coef, 0.0), axis=1, keepdims=True)
    low = jnp.sum(jnp.where((b == a) & (a < NZ), coef, 0.0), axis=1, keepdims=True)
    columns = [jnp.broadcast_to(x * 0.0625, (Z, LANES)) for x in (4.0 + high + low, high, low)]
    for k in range(3):
        vz[k] = columns[k]
    up[...] = jnp.zeros(up.shape, F32)
    down[...] = jnp.zeros(down.shape, F32)
    for copy in copies[2:]:
        copy.wait()
    up[0:NZ, :] = f_high[:, 1, :]
    up[Z : Z + NZ, :] = f_high[:, 0, :]
    up[2 * Z : 2 * Z + NZ, :] = c_high[:, 0, :]
    down[0:NZ, :] = f_low[:, 0, :]
    down[Z : Z + NZ, :] = f_low[:, 1, :]
    down[2 * Z : 2 * Z + NZ, :] = c_low[:, 0, :]
    first, last = down[0:Z, :], up[0:Z, :]
    tail = flags + corner_rows([col(first, 0), col(first, LANES - 1), col(last, 0), col(last, LANES - 1)])
    up[3 * Z : 3 * Z + 8, :] = tail
    down[3 * Z : 3 * Z + 8, :] = tail


def block_matrix(inv):
    width = 3 * Z
    a, b = iota2(BLK, width)
    b = b % Z
    spread = jnp.where((b % BLK == a) & (b < NZ), 1.0, 0.0).astype(BF16)
    whole = jnp.zeros((NZ, width), F32)
    left = inv
    for _ in range(3):
        part = left.astype(BF16)
        whole = whole + jnp.dot(part, spread, preferred_element_type=F32)
        left = left - part.astype(F32)
    a, b = iota2(NZ, width)
    whole = jnp.where(a // BLK == (b % Z) // BLK, whole, 0.0)
    high = whole.astype(BF16).astype(F32)
    return jnp.where((b >= Z) & (b < 2 * Z), whole - high, high)


def side_kernel(f_in, c_in, inv, vz, own, f, c, w0, w1, w2, w3, one, part, columns, c_next, c_tile, yup, ydown):
    load_top(f_in, f)
    load_top(c_in, c)
    put_y(GEOM[0], f, c, yup, ydown)
    yup[Z : Z + 8, :] = own[...]
    ydown[Z : Z + 8, :] = own[...]
    for level, w in enumerate((w0, w1, w2, w3)):
        w[0:NZ, :] = block_matrix(inv[level])
        w[NZ:Z, :] = jnp.zeros((Z - NZ, 3 * Z), F32)
    winv = w0[...].astype(BF16)
    start_tile(GEOM[0], winv, f, Setter(one))
    relax_tile(GEOM[0], winv, Coef(vz), one, f, c, ALONE, Setter(part))
    columns[...] = own_columns(GEOM[0], one)
    restrict(GEOM[0], GEOM[1], c, c_next)
    restrict(GEOM[1], GEOM[2], c_next, c_tile)


def merge_kernel(level, count):
    geom = GEOM[level]

    def kernel(xlo, xhi, flags, yup, ydown, up, down):
        add_up, add_down = relayed(tail_of(geom, xlo, count), tail_of(geom, xhi, count), flags)
        up[...] = yup[...]
        down[...] = ydown[...]
        up[0:Z, :] = yup[0:Z, :] + add_up
        down[0:Z, :] = ydown[0:Z, :] + add_down

    return kernel


def pre_edges(geom, f, c, w, vz, own, xlo, xhi, ydn, yun, one, columns):
    winv = w[...].astype(BF16)
    fl = flags_of(geom, own, xlo, xhi, ydn, yun)
    halo = messages(geom, xlo, xhi, ydn, yun, winv)
    relaxed = relax_edges(geom, winv, Coef(vz), one, columns[...], halo, fl, *own_data(geom, xlo, xhi, ydn, yun))
    terms = edge_terms(geom, winv, frame(geom, fl, halo.lo, halo.hi, halo.sides()))
    return terms, frame(geom, fl, *relaxed)


def pre0_kernel(f, c, w, vz, own, xlo, xhi, ydn, yun, one, part, columns, c_next, up, down, terms_out, edges_out, v, res, f_next):
    geom, coarse = GEOM[0], GEOM[1]
    terms, edges = pre_edges(geom, f, c, w, vz, own, xlo, xhi, ydn, yun, one, columns)
    for k in range(3):
        terms_out[k] = terms[k]
        edges_out[k] = edges[k]
    co = Coef(vz)
    for m in (*range(5), *range(19, 24)):
        v[m] = with_terms(geom, part[m], terms, m)
    for m in (*range(4), *range(20, 24)):
        res[m] = tile_residual(geom, co, v, f, c, *edges, m)
    restrict(geom, coarse, res, f_next, (0, 1, 10, 11))
    put_x(coarse, f_next, c_next, up, down, own[...])


def mid1_kernel(f, c, part, terms_in, edges_in, vz, w, c_next, own, v, f_next, one, part_next, columns, yup, ydown, res):
    geom, coarse = GEOM[0], GEOM[1]
    co = Coef(vz)
    terms = [terms_in[k] for k in range(3)]
    edges = [edges_in[k] for k in range(3)]
    for m in range(24):
        v[m] = with_terms(geom, part[m], terms, m)
    for m in range(24):
        res[m] = tile_residual(geom, co, v, f, c, *edges, m)
    restrict(geom, coarse, res, f_next)
    put_y(coarse, f_next, c_next, yup, ydown)
    yup[Z : Z + 8, :] = own[...]
    ydown[Z : Z + 8, :] = own[...]
    winv = w[...].astype(BF16)
    start_tile(coarse, winv, f_next, Setter(one))
    relax_tile(coarse, winv, co, one, f_next, c_next, ALONE, Setter(part_next))
    columns[...] = own_columns(coarse, one)


def pre1_kernel(f, c, w, vz, own, xlo, xhi, ydn, yun, one, part, columns, c_tile, v_out, up, down, chunks, res, f_next):
    geom = GEOM[1]
    terms, edges = pre_edges(geom, f, c, w, vz, own, xlo, xhi, ydn, yun, one, columns)
    for m in range(6):
        v_out[m] = with_terms(geom, part[m], terms, m)
    co = Coef(vz)
    for m in range(6):
        res[m] = tile_residual(geom, co, v_out, f, c, *edges, m)
    restrict(geom, GEOM[2], res, f_next)
    put_x(geom, v_out, None, up, down)
    whole = pack(GEOM[2], [f_next[m] for m in range(6)] + [c_tile[m] for m in range(6)])
    turn = lax.rem(lax.axis_index("gx"), 4) * 32
    whole = [pltpu.roll(x, turn, axis=1) for x in whole]
    for t in range(8):
        for k, x in enumerate(whole):
            chunks[t, k * Z : (k + 1) * Z, :] = x
        chunks[t, 3 * Z : 3 * Z + 8, :] = own[...]


def again0_kernel(f, c, w, vz, e, v, g, part, columns, c_columns, yup, ydown):
    prolong_add(GEOM[0], GEOM[1], e, v, g)
    put_y(GEOM[0], g, None, yup, ydown)
    columns[...] = own_columns(GEOM[0], g)
    c_columns[...] = own_columns(GEOM[0], c)
    relax_tile(GEOM[0], w[...].astype(BF16), Coef(vz), g, f, c, ALONE, Setter(part))


def twice0_kernel(f, c, w, vz, part, _after, twice):
    relax_tile(GEOM[0], w[...].astype(BF16), Coef(vz), part, f, c, ALONE, Setter(twice))


def post_edges(geom, f, c, w, vz, own, xlo, xhi, ydn, yun, g, columns, glo, ghi, gdn, gun):
    fl = flags_of(geom, own, xlo, xhi, ydn, yun)
    halo = Halo(
        part_of(geom, glo, 0), part_of(geom, glo, 1), part_of(geom, ghi, 0), part_of(geom, ghi, 1), gdn[...], gun[...]
    )
    winv = w[...].astype(BF16)
    relaxed = relax_edges(geom, winv, Coef(vz), g, columns[...], halo, fl, *own_data(geom, xlo, xhi, ydn, yun))
    return frame(geom, fl, halo.lo, halo.hi, halo.sides()), frame(geom, fl, *relaxed)


def post0_kernel(f, c, w, vz, own, xlo, xhi, ydn, yun, g, columns, c_columns, twice, glo, ghi, gdn, gun, out):
    geom = GEOM[0]
    rows = geom[0]
    winv = w[...].astype(BF16)
    co = Coef(vz)
    lane = zl()
    edges, edges_next = post_edges(geom, f, c, w, vz, own, xlo, xhi, ydn, yun, g, columns, glo, ghi, gdn, gun)
    low, high, sides = edge_terms(geom, winv, edges)

    def row_residual(v, c_row, beyond):
        beside = jnp.where(lane == 0, 0.0, roll(v, 1)) + jnp.where(lane == LANES - 1, 0.0, roll(v, -1))
        return residual(co, beyond * 0.0625, c_row, v, beside)

    beside = jnp.where(lane < 2, 0.0, roll(sides, 2)) + jnp.where(lane >= 2 * rows - 2, 0.0, roll(sides, -2))
    r = [
        row_residual(low, c[0], edges_next[0]),
        low * 0.0625,
        high * 0.0625,
        row_residual(high, c[rows - 1], edges_next[1]),
        residual(co, edges_next[2] * 0.0625, c_columns[...], sides, beside),
        sides * 0.0625,
    ]
    d = block_dot(winv, jnp.concatenate(r, axis=1))
    d = [d[:, k * LANES : (k + 1) * LANES] for k in range(6)]
    a, b = iota2(LANES, LANES)
    outer = jnp.where((b % 4 == 1) | (b % 4 == 2), 1.0, 0.0) * jnp.where(a == 2 * (b // 4) + b % 4 - 1, 1.0, 0.0)
    inner = jnp.where((b % 4 == 0) | (b % 4 == 3), 1.0, 0.0) * jnp.where(a == 2 * (b // 4) + b % 4 // 3, 1.0, 0.0)
    four = lane_dot(sides + d[4], outer) + lane_dot(d[5], inner)
    inside = (lane < 2) | (lane >= LANES - 2)
    row_terms = {0: low + d[0], 1: d[1], rows - 2: d[2], rows - 1: high + d[3]}
    for m in range(rows):
        x = twice[m] + jnp.where(inside, roll(four, -4 * m - 2), 0.0)
        if m in row_terms:
            x = x + row_terms[m]
        out[pl.ds(m, NZ, stride=24), :] = x[0:NZ, :]


def post1_kernel(
    f, c, w, vz, own, xlo, xhi, ydn, yun, g, part, columns, glo, ghi, gdn, gun, fine_v, e, up, down, one, fine_g
):
    geom = GEOM[1]
    edges, edges_next = post_edges(geom, f, c, w, vz, own, xlo, xhi, ydn, yun, g, columns, glo, ghi, gdn, gun)
    winv = w[...].astype(BF16)
    add_edges(geom, winv, part, edges, Setter(one))
    relax_tile(geom, winv, Coef(vz), one, f, c, edges_next, Setter(e))
    prolong_add(GEOM[0], GEOM[1], e, fine_v, fine_g, (0, 22))
    put_x(GEOM[0], fine_g, None, up, down)


def on_device(right_side, helm_coef, vert_coef, block_inverse, edge_flip):
    inv = block_inverse.reshape(4, NZ, BLK)
    f_in = right_side.reshape(NZ * 24, LANES)
    c_in = helm_coef.reshape(NZ * 24, LANES)
    vert = vert_coef.reshape(1, NZ + 1)
    flip = edge_flip.reshape(1, 4)

    ys = (Z, LANES)
    t0, t1, t2 = tile_shape(0), tile_shape(1), tile_shape(2)
    xs = x_shape(0, 3)
    up, down, own, vz = pl.pallas_call(
        by_swaps(open_kernel, 4, 4, (), ((0, "gx"),)),
        out_shape=[jax.ShapeDtypeStruct(x, F32) for x in (xs, xs, (8, LANES), (3, Z, LANES))],
        in_specs=[ANY] * 4,
        out_specs=[VMEM] * 4,
        scratch_shapes=[pltpu.VMEM((NZ, 2, LANES), F32)] * 2
        + [pltpu.VMEM((NZ, 1, LANES), F32)] * 2
        + [pltpu.VMEM((1, NZ + 1), F32), pltpu.VMEM((1, 4), jnp.int32), pltpu.SemaphoreType.DMA((6,))]
        + [pltpu.VMEM(xs, F32)] * 2,
        compiler_params=pltpu.CompilerParams(vmem_limit_bytes=58 * 1024 * 1024),
        name="open",
    )(right_side, helm_coef, vert, flip)
    xlo, xhi = swap(up, down, "gx")
    ws = (Z, 3 * Z)
    f, c, *w, one, part, columns, c1, c_tile, yup, ydown = call(
        side_kernel,
        [t0, t0] + [ws] * 4 + [t0, t0, ys, t1, t2, Y_FULL, Y_FULL],
        [f_in, c_in, inv, vz, own],
        name="side",
    )

    def to_sides(level, count, xlo, xhi, yup, ydown):
        shape = yup.shape
        yup, ydown = call(merge_kernel(level, count), [shape, shape], [xlo, xhi, own, yup, ydown], name=f"merge{level}", got=((0, "gx"),), send=((0, "gy"),))
        return swap(yup, ydown, "gy")

    got0 = (xlo, xhi, *to_sides(0, 3, xlo, xhi, yup, ydown))
    xs = x_shape(1, 3)
    three = (3, Z, LANES)
    up, down, terms, edges = call(
        pre0_kernel,
        [xs, xs, three, three],
        [f, c, w[0], vz, own, *got0, one, part, columns, c1],
        [t0, t0, t1],
        name="pre0",
        got=((5, "gx"), (7, "gy")),
        send=((0, "gx"),),
    )
    xlo, xhi = swap(up, down, "gx")
    v0, f1, one, part, columns, yup, ydown = call(
        mid1_kernel,
        [t0, t1, t1, t1, ys, Y_FULL, Y_FULL],
        [f, c, part, terms, edges, vz, w[1], c1, own],
        [t0],
        name="mid1",
    )
    got1 = (xlo, xhi, *to_sides(1, 3, xlo, xhi, yup, ydown))
    xs = x_shape(1, 2)
    v1, up, down, chunks = call(
        pre1_kernel,
        [t1, xs, xs, (8, 3 * Z + 8, LANES)],
        [f1, c1, w[1], vz, own, *got1, one, part, columns, c_tile],
        [t1, t2],
        name="pre1",
        got=((5, "gx"), (7, "gy")),
        send=((1, "gx"),),
    )
    v1_lo, v1_hi = swap(up, down, "gx")
    chunks = lax.all_to_all(chunks, "gx", 0, 0)
    s2, s3 = (6, Z, 256), (3, Z, 128)
    m2, m3 = (Z, 256), (Z, 128)
    full2, full3 = (Z + 8, 256), (Z + 8, 128)
    f2, c2, fl2, up, down = call(
        open_strip_kernel, [s2, s2, (8, 256), full2, full2], [chunks], name="open2", send=((3, "gy"),)
    )
    side2 = swap(up, down, "gy", True)
    c3, fl3, *c_sides = call(next_coef_kernel, [s3, (8, 128), m2, m2, m3, m3], [c2, fl2], name="coef3")
    part2, first, last, f_part, base_up, base_down = call(
        alone2_kernel, [s2, m2, m2, s3, m3, m3], [f2, c2, w[2], vz, fl2, c3, fl3], [s2, s2], name="alone2"
    )
    terms2, f3, up, down = call(
        pre_strip_kernel,
        [(2, *m2), s3, full3, full3],
        [w[2], vz, fl2, *side2, first, last, *c_sides[:2], f_part, fl3, base_up, base_down],
        name="pre2",
        got=((3, "gy"),),
        send=((2, "gy"),),
    )
    side3 = swap(up, down, "gy", True)
    *alone, twice = call(alone3_kernel, [m3] * 4 + [s3], [f3, c3, w[3], vz, fl3], [s3, s3], name="alone3")
    terms, up, down = call(
        bottom_strip_kernel,
        [(4, *m3), m3, m3],
        [w[3], vz, fl3, *side3, *alone[:2], *c_sides[2:], *alone[2:]],
        name="bottom",
        got=((3, "gy"),),
        send=((1, "gy"),),
    )
    side = swap(up, down, "gy", True)
    (part,) = call(again3_kernel, [s3], [f3, c3, w[3], vz, fl3, twice, terms], [s3], name="again3")
    v2, base_up, base_down = call(base_message_kernel, [s2, m2, m2], [part2, fl2, terms2], name="base2")
    e3, up, down = call(
        last_strip_kernel,
        [s3, m2, m2],
        [w[3], fl3, *side, part, base_up, base_down, v1_lo, v1_hi],
        [m3, m3],
        name="last",
        after=2,
        got=((2, "gy"),),
        send=((1, "gy"),),
    )
    side = swap(up, down, "gy", True)
    first, last, part_low, part_high, yup, ydown, twice = call(
        again2_kernel, [m2] * 4 + [ys, ys, s2], [f2, c2, w[2], vz, fl2, v2, e3, v1, v1_lo, v1_hi, own], [s2, s2], name="again2", got=((8, "gx"),)
    )
    terms, up, down = call(
        post_strip_kernel,
        [(4, *m2), ys, ys],
        [w[2], vz, fl2, *side2, first, last, *c_sides[:2], part_low, part_high, *side, own, yup, ydown],
        name="post2",
        got=((3, "gy"), (11, "gy")),
        send=((1, "gy"),),
    )
    side = swap(up, down, "gy")
    g1, part, columns, lo, hi = call(
        again1_kernel, [t1, t1, ys, ys, ys], [f1, c1, w[1], vz, v1, twice, terms, v1_lo, v1_hi], [t2], name="again1", got=((7, "gx"),)
    )
    xs = x_shape(0, 2)
    e1, up, down = call(
        post1_kernel,
        [t1, xs, xs],
        [f1, c1, w[1], vz, own, *got1, g1, part, columns, lo, hi, *side, v0],
        [t1, t0],
        name="post1",
        got=((5, "gx"), (7, "gy"), (14, "gy")),
        send=((1, "gx"),),
    )
    xlo, xhi = swap(up, down, "gx")
    g0, part, columns, c_columns, yup, ydown = call(
        again0_kernel, [t0, t0, ys, ys, ys, ys], [f, c, w[0], vz, e1, v0], name="again0"
    )
    up, down = call(
        merge_kernel(0, 2), [ys, ys], [xlo, xhi, own, yup, ydown], name="merge0", got=((0, "gx"),), send=((0, "gy"),)
    )
    side = swap(up, down, "gy")
    (twice,) = call(twice0_kernel, [t0], [f, c, w[0], vz, part, up], name="twice0", after=1)
    (out,) = call(
        post0_kernel,
        [(NZ * 24, LANES)],
        [f, c, w[0], vz, own, *got0, g0, columns, c_columns, twice, xlo, xhi, *side],
        name="post0",
        got=((5, "gx"), (7, "gy"), (13, "gx"), (15, "gy")),
    )
    return out.reshape(NZ, 24, LANES)


def solution(mesh):
    placed = (P(None, "gx", "gy"), P(None, "gx", "gy"), P(), P(), P("gx", "gy", None))
    return jax.shard_map(
        on_device, mesh=mesh, in_specs=placed, out_specs=P(None, "gx", "gy"), check_vma=False
    )
```

```python
import jax
import jax.numpy as jnp
from jax import lax
from jax.experimental import pallas as pl
from jax.experimental.pallas import tpu as pltpu
from jax.sharding import PartitionSpec as P

BLK = 14
NBLK = 5
NZ = 70
Z = 72
LANES = 128
F32 = jnp.float32
BF16 = jnp.bfloat16

GEOM = ((24, 1, 128), (6, 2, 64), (6, 1, 32), (3, 1, 16))


def lane_ids(shape):
    return lax.broadcasted_iota(jnp.int32, shape, len(shape) - 1)


def zl():
    return lane_ids((Z, LANES))


def roll(x, shift):
    shift = shift % x.shape[-1]
    return x if shift == 0 else pltpu.roll(x, shift, axis=1)


def col(x, k):
    return jnp.broadcast_to(x[:, k : k + 1], (Z, LANES))


def iota2(n, m):
    return lax.broadcasted_iota(jnp.int32, (n, m), 0), lax.broadcasted_iota(jnp.int32, (n, m), 1)


def lane_dot(x, mat):
    hi = x.astype(BF16).astype(F32)
    both = jnp.concatenate([hi, x - hi], axis=1).astype(BF16)
    twice = jnp.concatenate([mat, mat], axis=0).astype(BF16)
    return jnp.dot(both, twice, preferred_element_type=F32)


def block_dot(winv, x):
    hi = x.astype(BF16).astype(F32)
    parts = jnp.concatenate([hi, hi, x - hi], axis=0).astype(BF16)
    return jnp.dot(winv, parts, preferred_element_type=F32)


def reverse_matrix(width):
    a, b = iota2(LANES, LANES)
    return jnp.where((b < width) & (a == width - 1 - b), 1.0, 0.0)


def flag_row(flags, k):
    return jnp.broadcast_to(flags[k : k + 1, :], (Z, LANES))


class Coef:
    def __init__(self, ref, width=LANES):
        self.mid, self.up, self.down = [jnp.concatenate([ref[k]] * (width // LANES), axis=1) for k in range(3)]


def residual(co, f, c, v, beside):
    above = pltpu.roll(v, Z - 1, axis=0)
    below = pltpu.roll(v, 1, axis=0)
    return f - (c * 0.0625 + co.mid) * v + beside * 0.0625 + co.up * above + co.down * below


def row_of(geom, v, row):
    m_rows, _, ty = geom
    q, m = divmod(row, m_rows)
    return roll(v[m], -q * ty)


def corners(geom, v):
    m_rows, groups, ty = geom
    last = v[m_rows - 1]
    base = (groups - 1) * ty
    return corner_rows([col(v[0], 0), col(v[0], ty - 1), col(last, base), col(last, base + ty - 1)])


def corner_rows(columns):
    lane = zl()
    out = jnp.zeros((Z, LANES), F32)
    for k, column in enumerate(columns):
        out = jnp.where(lane == 4 + k, column, out)
    return jnp.concatenate([out, jnp.zeros((LANES - Z, LANES), F32)], axis=0).T[0:8, :]


def corner_columns(rows):
    out = jnp.concatenate([rows, jnp.zeros((LANES - 8, LANES), F32)], axis=0).T[0:Z, :]
    return [col(out, 4 + k) for k in range(4)]


def whole_rows(geom):
    return geom[1] == 1 and geom[2] == LANES


def tile_rows(geom):
    m_rows, groups, ty = geom
    return [(q * m_rows + m, m, q * ty) for m in range(m_rows) for q in range(groups)]


def own_columns(geom, v):
    ty = geom[2]
    lane = zl()
    out = jnp.zeros((Z, LANES), F32)
    for r, m, base in tile_rows(geom):
        row = v[m]
        first = roll(row, 2 * r + 1 - base)
        out = jnp.where(lane == 2 * r + 1, first, out)
        last = first if whole_rows(geom) else roll(row, 2 * r - (base + ty - 1))
        out = jnp.where(lane == 2 * r, last, out)
    return out


def pack(geom, parts):
    ty = geom[2]
    per = LANES // ty
    out = []
    for first in range(0, len(parts), per):
        lane = zl()
        acc = parts[first]
        for k, part in enumerate(parts[first + 1 : first + per], 1):
            acc = jnp.where(lane < k * ty, acc, roll(part, k * ty))
        out.append(acc)
    return out


def packed(geom, count):
    per = LANES // geom[2]
    return -(-count // per)


def part_of(geom, ref, k):
    ty = geom[2]
    per = LANES // ty
    return roll(ref[(k // per) * Z : (k // per + 1) * Z, :], -(k % per) * ty)


def put_x(geom, v, c, up, down, flags=None):
    m_rows, groups, _ = geom
    tx = m_rows * groups
    tail = corners(geom, v)
    if flags is not None:
        tail = tail + flags
    for ref, edge, second in ((up, tx - 1, tx - 2), (down, 0, 1)):
        parts = [row_of(geom, v, edge), row_of(geom, v, second)]
        if c is not None:
            parts.append(row_of(geom, c, edge))
        put_parts(geom, parts, tail, ref)


SPLIT = 40


def halved(geom, count):
    return geom[2] == 64 and count == 3


def put_parts(geom, parts, tail, ref):
    if halved(geom, len(parts)):
        lane = lane_ids((SPLIT, LANES))
        rest = jnp.concatenate([parts[2][SPLIT:Z, :], jnp.zeros((2 * SPLIT - Z, LANES), F32)], axis=0)
        ref[0:Z, :] = pack(geom, parts[:2])[0]
        ref[Z : Z + SPLIT, :] = jnp.where(lane < 64, parts[2][0:SPLIT, :], roll(rest, 64))
        ref[Z + SPLIT : Z + SPLIT + 8, :] = tail
        return
    whole = pack(geom, parts)
    for k, part in enumerate(whole):
        ref[k * Z : (k + 1) * Z, :] = part
    ref[len(whole) * Z : len(whole) * Z + 8, :] = tail


def tail_of(geom, ref, count):
    n = message_rows(geom, count)
    return ref[n : n + 8, :]


def message_rows(geom, count):
    return Z + SPLIT if halved(geom, count) else packed(geom, count) * Z


def put_y(geom, v, c, up, down):
    ty = geom[2]
    lane = zl()
    out_up = jnp.zeros((Z, LANES), F32)
    out_down = out_up
    for r, m, base in tile_rows(geom):
        row = v[m]
        mine = lane // 2 == r
        last = roll(row, 2 * r + 1 - (base + ty - 1))
        first = roll(row, 2 * r - base)
        out_up = jnp.where(mine, last, out_up)
        out_down = jnp.where(mine, first, out_down)
        if c is not None:
            row = c[m]
            out_up = jnp.where(lane == 65 + 2 * r, roll(row, 65 + 2 * r - (base + ty - 1)), out_up)
            out_down = jnp.where(lane == 64 + 2 * r, roll(row, 64 + 2 * r - base), out_down)
    up[0:Z, :] = out_up
    down[0:Z, :] = out_down


def relay_order(lo, hi, f0, f1):
    up = [lo[3], lo[1], hi[1], hi[3], jnp.where(f0, lo[2], lo[3]), jnp.where(f1, hi[0], hi[1])]
    down = [lo[2], lo[0], hi[0], hi[2], jnp.where(f0, lo[3], lo[2]), jnp.where(f1, hi[1], hi[0])]
    return up, down


def relayed(lo, hi, flags):
    lo = [lo[4 + k : 5 + k, :] for k in range(4)]
    hi = [hi[4 + k : 5 + k, :] for k in range(4)]
    up, down = relay_order(lo, hi, flags[0:1, :] > 0.5, flags[1:2, :] > 0.5)
    two = jnp.zeros((2, LANES), F32)
    rows = [*down, two, jnp.zeros((104, LANES), F32), *up, two, jnp.zeros((8, LANES), F32)]
    turned = jnp.concatenate(rows, axis=0).T[0:Z, :]
    lane = zl()
    inside = (lane >= 112) & (lane < 118)
    return jnp.where(inside, turned, 0.0), jnp.where(inside, roll(turned, 112), 0.0)


def odd_lanes():
    return zl() % 2 == 1


class Halo:
    def __init__(self, lo, lo2, hi, hi2, dn, un):
        self.lo, self.lo2, self.hi, self.hi2, self.dn, self.un = lo, lo2, hi, hi2, dn, un

    def sides(self):
        return jnp.where(odd_lanes(), self.dn, self.un)

    def seconds(self):
        return jnp.where(odd_lanes(), roll(self.dn, 1), roll(self.un, -1))


class Flags:
    def __init__(self, own, lo, hi, dn, un):
        self.own, self.lo, self.hi, self.dn, self.un = own, lo, hi, dn, un


def turn_row(geom, row, flag):
    return jnp.where(flag > 0.5, lane_dot(row, reverse_matrix(geom[2])), row)


def turn_sides(geom, sides, flag_dn, flag_un):
    tx = geom[0] * geom[1]
    flag = jnp.where(odd_lanes(), flag_dn, flag_un)
    a, b = iota2(LANES, LANES)
    mat = jnp.where((b < 2 * tx) & (a == 2 * (tx - 1 - b // 2) + b % 2), 1.0, 0.0)
    return jnp.where(flag > 0.5, lane_dot(sides, mat), sides)


def frame(geom, fl, lo, hi, sides):
    return (
        turn_row(geom, lo, flag_row(fl.own, 0)),
        turn_row(geom, hi, flag_row(fl.own, 1)),
        turn_sides(geom, sides, flag_row(fl.own, 2), flag_row(fl.own, 3)),
    )


def relax_edges(geom, winv, co, v, columns, halo, fl, f_lo, c_lo, f_hi, c_hi, f_sides, c_sides):
    m_rows, groups, ty = geom
    tx = m_rows * groups
    lane = zl()
    dn, un = halo.dn, halo.un

    def beside_row(edge, second, mine, low, high):
        left = jnp.where(lane == 0, roll(low, -112), roll(edge, 1))
        right = jnp.where(lane == ty - 1, roll(high, ty - 113), roll(edge, -1))
        return second + mine + left + right

    def choose(flags, k, x, place):
        x = roll(x, 112 - place)
        return jnp.where(flag_row(flags, k) > 0.5, roll(x, -1), x)

    b_lo = beside_row(
        halo.lo,
        halo.lo2,
        turn_row(geom, row_of(geom, v, 0), flag_row(fl.lo, 1)),
        choose(fl.lo, 2, dn, 112),
        choose(fl.lo, 3, un, 112),
    )
    b_hi = beside_row(
        halo.hi,
        halo.hi2,
        turn_row(geom, row_of(geom, v, tx - 1), flag_row(fl.hi, 0)),
        choose(fl.hi, 2, dn, 114),
        choose(fl.hi, 3, un, 114),
    )
    edge = halo.sides()
    mine = turn_sides(geom, columns, flag_row(fl.dn, 3), flag_row(fl.un, 2))
    below = jnp.where(lane == 1, roll(dn, -115), jnp.where(lane == 0, roll(un, -116), roll(edge, 2)))
    last = 2 * (tx - 1)
    above = jnp.where(lane == last + 1, roll(dn, last - 116), jnp.where(lane == last, roll(un, last - 117), roll(edge, -2)))
    b_sides = halo.seconds() + mine + below + above
    r_lo = residual(co, f_lo, c_lo, halo.lo, b_lo)
    r_hi = residual(co, f_hi, c_hi, halo.hi, b_hi)
    r_sides = residual(co, f_sides, c_sides, edge, b_sides)
    d = block_dot(winv, jnp.concatenate([r_lo, r_hi, r_sides], axis=1))
    return halo.lo + d[:, :LANES], halo.hi + d[:, LANES : 2 * LANES], edge + d[:, 2 * LANES :]


def tile_residual(geom, co, v, f, c, lo, hi, sides, m):
    m_rows, groups, ty = geom
    lane = zl()
    here = v[m]
    if lo is None:
        lo = hi = jnp.zeros((Z, LANES), F32)
    if m > 0:
        low_x = v[m - 1]
    else:
        low_x = lo if groups == 1 else jnp.where(lane < ty, lo, roll(v[m_rows - 1], ty))
    if m < m_rows - 1:
        high_x = v[m + 1]
    elif groups == 1:
        high_x = hi
    else:
        high_x = jnp.where(lane < (groups - 1) * ty, roll(v[0], -ty), roll(hi, (groups - 1) * ty))
    low_y, high_y = roll(here, 1), roll(here, -1)
    if sides is None:
        low_y = jnp.where(lane % ty == 0, 0.0, low_y)
        high_y = jnp.where(lane % ty == ty - 1, 0.0, high_y)
        return residual(co, f[m], c[m], here, low_x + high_x + low_y + high_y)
    for q in range(groups):
        row = q * m_rows + m
        low = roll(sides, q * ty - 2 * row - 1)
        high = low if whole_rows(geom) else roll(sides, q * ty + ty - 1 - 2 * row)
        low_y = jnp.where(lane == q * ty, low, low_y)
        high_y = jnp.where(lane == q * ty + ty - 1, high, high_y)
    return residual(co, f[m], c[m], here, low_x + high_x + low_y + high_y)


def relax_tile(geom, winv, co, v, f, c, edges, store):
    lo, hi, sides = edges
    for m in range(0, geom[0], 2):
        rows = [k for k in (m, m + 1) if k < geom[0]]
        r = [tile_residual(geom, co, v, f, c, lo, hi, sides, k) for k in rows]
        d = block_dot(winv, r[0] if len(r) == 1 else jnp.concatenate(r, axis=1))
        for i, k in enumerate(rows):
            store(k, v[k] + d[:, i * LANES : (i + 1) * LANES])


ALONE = (None, None, None)


def edge_terms(geom, winv, edges):
    ty = geom[2]
    lane = zl()
    d = block_dot(winv, jnp.concatenate(edges, axis=1) * 0.0625)
    low, high, sides = [d[:, k * LANES : (k + 1) * LANES] for k in range(3)]
    if ty < LANES:
        low = jnp.where(lane < ty, low, 0.0)
        high = jnp.where(lane < ty, high, 0.0)
    return low, high, sides


def with_terms(geom, x, terms, m):
    m_rows, groups, ty = geom
    low, high, sides = terms
    lane = zl()
    if m == 0:
        x = x + low
    if m == m_rows - 1:
        x = x + roll(high, (groups - 1) * ty)
    for q in range(groups):
        row = q * m_rows + m
        first = roll(sides, q * ty - 2 * row - 1)
        last = first if whole_rows(geom) else roll(sides, q * ty + ty - 1 - 2 * row)
        x = x + jnp.where(lane == q * ty, first, jnp.where(lane == q * ty + ty - 1, last, 0.0))
    return x


def add_edges(geom, winv, part, edges, store):
    terms = edge_terms(geom, winv, edges)
    for m in range(geom[0]):
        store(m, with_terms(geom, part[m], terms, m))


def start_tile(geom, winv, f, store):
    for m in range(0, geom[0], 2):
        rows = [k for k in (m, m + 1) if k < geom[0]]
        parts = [f[k] for k in rows]
        d = block_dot(winv, parts[0] if len(parts) == 1 else jnp.concatenate(parts, axis=1))
        for i, k in enumerate(rows):
            store(k, d[:, i * LANES : (i + 1) * LANES])


def restrict(fine, coarse, v, out, wanted=None):
    m_rows, _, ty = fine
    cm, cq, cty = coarse
    a, b = iota2(LANES, LANES)
    for mc in range(cm):
        acc = None
        for qc in range(cq):
            if wanted is not None and qc * cm + mc not in wanted:
                continue
            q, m = divmod(2 * (qc * cm + mc), m_rows)
            inside = (b >= qc * cty) & (b < (qc + 1) * cty) & (a // 2 == b - qc * cty + q * (ty // 2))
            term = lane_dot(v[m] + v[m + 1], jnp.where(inside, 0.25, 0.0))
            acc = term if acc is None else acc + term
        if acc is not None:
            out[mc] = acc


def prolong_add(fine, coarse, e, v, out, rows=None):
    m_rows, groups, ty = fine
    cm, _, cty = coarse
    a, b = iota2(LANES, LANES)
    for m in range(0, m_rows, 2) if rows is None else rows:
        acc = None
        for q in range(groups):
            qc, mc = divmod((q * m_rows + m) // 2, cm)
            inside = (b >= q * ty) & (b < (q + 1) * ty) & (a - qc * cty == (b - q * ty) // 2)
            term = lane_dot(e[mc], jnp.where(inside, 1.0, 0.0))
            acc = term if acc is None else acc + term
        out[m] = v[m] + acc
        out[m + 1] = v[m + 1] + acc


class Setter:
    def __init__(self, ref):
        self.ref = ref

    def __call__(self, m, value):
        self.ref[m] = value


def messages(geom, xlo, xhi, ydn, yun, winv):
    raw = [part_of(geom, xlo, 0), part_of(geom, xlo, 1), part_of(geom, xhi, 0), part_of(geom, xhi, 1), ydn[0:Z, :], yun[0:Z, :]]
    d = block_dot(winv, jnp.concatenate(raw, axis=1))
    return Halo(*[d[:, k * LANES : (k + 1) * LANES] for k in range(6)])


def third_of(geom, ref):
    if not halved(geom, 3):
        return part_of(geom, ref, 2)
    both = ref[Z : Z + SPLIT, :]
    return jnp.concatenate([both, roll(both[0 : Z - SPLIT, :], 64)], axis=0)


def own_data(geom, xlo, xhi, ydn, yun):
    dn, un = ydn[0:Z, :], yun[0:Z, :]
    f_sides = jnp.where(odd_lanes(), dn, un)
    c_sides = roll(f_sides, -64)
    return (
        part_of(geom, xlo, 0),
        third_of(geom, xlo),
        part_of(geom, xhi, 0),
        third_of(geom, xhi),
        f_sides,
        c_sides,
    )


def flags_of(geom, own, xlo, xhi, ydn, yun):
    return Flags(own[...], tail_of(geom, xlo, 3), tail_of(geom, xhi, 3), ydn[Z : Z + 8, :], yun[Z : Z + 8, :])


def load_top(src, dst):
    for x in range(24):
        dst[x, 0:NZ, :] = src[pl.ds(x, NZ, stride=24), :]
        dst[x, NZ:Z, :] = jnp.zeros((Z - NZ, LANES), F32)


STRIPS = {2: (6, 32, 256), 3: (3, 16, 128)}


def in_tile(strip):
    _, ty, width = strip
    return lane_ids((Z, width)) % ty


def group_dot(x, mat):
    parts = [lane_dot(x[:, k : k + LANES], mat) for k in range(0, x.shape[1], LANES)]
    return parts[0] if len(parts) == 1 else jnp.concatenate(parts, axis=1)


def turn_groups(strip, x, flags, k, count):
    _, ty, width = strip
    a, b = iota2(LANES, LANES)
    mat = jnp.where((a // ty == b // ty) & (b % ty < count) & (a % ty == count - 1 - b % ty), 1.0, 0.0)
    flag = jnp.broadcast_to(flags[k : k + 1, :], (Z, width))
    return jnp.where(flag > 0.5, group_dot(x, mat), x)


def strip_ends(strip, v, flags):
    m_rows, ty, _ = strip
    low = turn_groups(strip, roll(v[m_rows - 1], ty), flags, 0, ty)
    high = turn_groups(strip, roll(v[0], -ty), flags, 1, ty)
    return low, high


def strip_column(strip, v, y, offset, out):
    lt = in_tile(strip)
    for m in range(strip[0]):
        out = jnp.where(lt == offset + m, roll(v[m], offset + m - y), out)
    return out


def strip_message(strip, v, c, ends, up, down):
    m_rows, ty, width = strip
    lt = in_tile(strip)
    for ref, edge, second in ((up, ty - 1, ty - 2), (down, 0, 1)):
        out = strip_column(strip, v, edge, 0, jnp.zeros((Z, width), F32))
        out = strip_column(strip, v, second, m_rows, out)
        if c is not None:
            out = strip_column(strip, c, edge, 2 * m_rows, out)
        for k, end in enumerate(ends):
            out = jnp.where(lt == 3 * m_rows + k, roll(end, 3 * m_rows + k - edge), out)
        ref[0:Z, :] = out


def strip_edges(strip, winv, co, sides):
    m_rows, _, width = strip
    lt = in_tile(strip)
    r = []
    for x, raw, flags, k, mine in sides:
        mine = turn_groups(strip, mine, flags, k, m_rows)
        low = jnp.where(lt == 0, roll(x, -3 * m_rows), roll(x, 1))
        high = jnp.where(lt == m_rows - 1, roll(x, -2 * m_rows - 2), roll(x, -1))
        r.append(residual(co, raw, roll(raw, -2 * m_rows), x, roll(x, -m_rows) + mine + low + high))
    d = block_dot(winv, jnp.concatenate(r, axis=1))
    return [side[0] + d[:, k * width : (k + 1) * width] for k, side in enumerate(sides)]


def strip_frame(strip, flags, low, high):
    return turn_groups(strip, low, flags, 2, strip[0]), turn_groups(strip, high, flags, 3, strip[0])


def strip_residual(strip, co, v, f, c, ends, sides, m):
    m_rows, ty, _ = strip
    lt = in_tile(strip)
    low_x = v[m - 1] if m > 0 else ends[0]
    high_x = v[m + 1] if m < m_rows - 1 else ends[1]
    low = 0.0 if sides is None else roll(sides[0], -m)
    high = 0.0 if sides is None else roll(sides[1], ty - 1 - m)
    low_y = jnp.where(lt == 0, low, roll(v[m], 1))
    high_y = jnp.where(lt == ty - 1, high, roll(v[m], -1))
    return residual(co, f[m], c[m], v[m], low_x + high_x + low_y + high_y)


def strip_relax(strip, winv, co, v, f, c, flags, sides, store):
    ends = strip_ends(strip, v, flags)
    for m in range(strip[0]):
        r = strip_residual(strip, co, v, f, c, ends, sides, m)
        store(m, v[m] + block_dot(winv, r))


def strip_add_sides(strip, winv, part, sides, store):
    m_rows, ty, width = strip
    lt = in_tile(strip)
    d = block_dot(winv, jnp.concatenate(sides, axis=1) * 0.0625)
    for m in range(m_rows):
        low, high = roll(d[:, :width], -m), roll(d[:, width:], ty - 1 - m)
        store(m, part[m] + jnp.where(lt == 0, low, jnp.where(lt == ty - 1, high, 0.0)))


def strip_side_terms(strip, winv, co, flags, c_columns, sides, sides_next):
    m_rows, ty, width = strip
    lt = in_tile(strip)
    d = block_dot(winv, jnp.concatenate(sides, axis=1) * 0.0625)
    first, last = d[:, :width], d[:, width:]
    turned = [jnp.broadcast_to(flags[k : k + 1, :], (Z, width)) > 0.5 for k in range(2)]
    step = ty - m_rows + 1
    r = []
    for mine, other, c, beyond in ((first, last, c_columns[0], sides_next[0]), (last, first, c_columns[1], sides_next[1])):
        low = jnp.where(turned[0], roll(other, step), roll(mine, step))
        high = jnp.where(turned[1], roll(other, -step), roll(mine, -step))
        low = jnp.where(lt == 0, low, roll(mine, 1))
        high = jnp.where(lt == m_rows - 1, high, roll(mine, -1))
        r.append(residual(co, beyond * 0.0625, c, mine, low + high))
    return first, last, r


def strip_restrict(v, out):
    a, b = iota2(LANES, LANES)
    for m in range(3):
        both = v[2 * m] + v[2 * m + 1]
        out[m] = lane_dot(both[:, :LANES], jnp.where(a // 2 == b, 0.25, 0.0)) + lane_dot(
            both[:, LANES:], jnp.where(a // 2 == b - 64, 0.25, 0.0)
        )


def open_strip_kernel(chunks, f, c, flags, up, down):
    strip = STRIPS[2]
    group = lane_ids((Z, LANES)) // 32
    for m in range(6):
        for ref, k in ((f, m), (c, 6 + m)):
            part = (k // 4) * Z
            halves = []
            for h in range(2):
                acc = None
                for g in range(4):
                    x = chunks[4 * h + g, part : part + Z, :]
                    acc = x if acc is None else jnp.where(group == (g + k) % 4, x, acc)
                halves.append(roll(acc, -(k % 4) * 32))
            ref[m] = jnp.concatenate(halves, axis=1)
    group = lane_ids((8, LANES)) // 32
    for h in range(2):
        acc = None
        for g in range(4):
            x = chunks[4 * h + g, 3 * Z : 3 * Z + 8, :]
            acc = x if acc is None else jnp.where(group == g, x, acc)
        flags[:, h * LANES : (h + 1) * LANES] = acc
    strip_message(strip, f, c, strip_ends(strip, f, flags), up, down)
    up[Z : Z + 8, :] = flags[...]
    down[Z : Z + 8, :] = flags[...]


def strip_sides(values, raws, dn, un, first, last):
    return (
        (values[0], raws[0], dn[Z : Z + 8, :], 3, first[...]),
        (values[1], raws[1], un[Z : Z + 8, :], 2, last[...]),
    )


def column_restrict(strip, x):
    a, b = iota2(LANES, LANES)
    out = None
    for h in range(2):
        inside = (b // 16 == 4 * h + a // 32) & ((a % 32) // 2 == b % 16) & (a % 32 < strip[0])
        term = lane_dot(x[:, h * LANES : (h + 1) * LANES], jnp.where(inside, 0.25, 0.0))
        out = term if out is None else out + term
    return out


def pre_strip_kernel(
    w, vz, flags, dn, un, first_column, last_column, c_low, c_high, f_part, fl_next, base_up, base_down, terms, f_next, up, down
):
    strip, small = STRIPS[2], STRIPS[3]
    winv = w[...].astype(BF16)
    co = Coef(vz, strip[2])
    raws = [dn[0:Z, :], un[0:Z, :]]
    values = block_dot(winv, jnp.concatenate(raws, axis=1))
    values = [values[:, : strip[2]], values[:, strip[2] :]]
    edges = strip_edges(strip, winv, co, strip_sides(values, raws, dn, un, first_column, last_column))
    first, last, r = strip_side_terms(
        strip, winv, co, flags, (c_low[...], c_high[...]), strip_frame(strip, flags, *values), strip_frame(strip, flags, *edges)
    )
    terms[0] = first
    terms[1] = last
    low = column_restrict(strip, r[0] + first * 0.0625)
    high = column_restrict(strip, r[1] + last * 0.0625)
    m_rows, ty, width = small
    lt = in_tile(small)
    for m in range(m_rows):
        x = jnp.where(lt == 0, roll(low, -m), 0.0)
        f_next[m] = f_part[m] + jnp.where(lt == ty - 1, roll(high, ty - 1 - m), x)
    turned = [jnp.broadcast_to(fl_next[k : k + 1, :], (Z, width)) > 0.5 for k in range(2)]
    for ref, base, mine, other in ((up, base_up, high, low), (down, base_down, low, high)):
        before, after = 3 * m_rows + ty - m_rows + 1, 3 * m_rows + 1 - ty
        end_low = jnp.where(turned[0], roll(other, before), roll(mine, before))
        end_high = jnp.where(turned[1], roll(other, after), roll(mine, after))
        add = jnp.where(lt < m_rows, mine, 0.0)
        add = jnp.where(lt == 3 * m_rows, end_low, add)
        add = jnp.where(lt == 3 * m_rows + 1, end_high, add)
        ref[0:Z, :] = base[...] + add
        ref[Z : Z + 8, :] = fl_next[...]


def next_coef_kernel(c, flags, c_next, fl_next, low, high, low_next, high_next):
    strip_restrict(c, c_next)
    a, b = iota2(LANES, LANES)
    fl_next[...] = lane_dot(flags[:, :LANES], jnp.where((b < 64) & (a == (b // 16) * 32), 1.0, 0.0)) + lane_dot(
        flags[:, LANES:], jnp.where((b >= 64) & (a == (b // 16 - 4) * 32), 1.0, 0.0)
    )
    for strip, ref, first, last in ((STRIPS[2], c, low, high), (STRIPS[3], c_next, low_next, high_next)):
        zero = jnp.zeros((Z, strip[2]), F32)
        first[...] = strip_column(strip, ref, 0, 0, zero)
        last[...] = strip_column(strip, ref, strip[1] - 1, 0, zero)


def alone2_kernel(f, c, w, vz, flags, c_next, fl_next, part, low, high, f_part, up, down, v, res):
    strip, small = STRIPS[2], STRIPS[3]
    winv = w[...].astype(BF16)
    co = Coef(vz, strip[2])
    for m in range(6):
        v[m] = block_dot(winv, f[m])
    zero = jnp.zeros((Z, strip[2]), F32)
    low[...] = strip_column(strip, v, 0, 0, zero)
    high[...] = strip_column(strip, v, strip[1] - 1, 0, zero)
    strip_relax(strip, winv, co, v, f, c, flags, None, Setter(part))
    ends = strip_ends(strip, part, flags)
    for m in range(6):
        res[m] = strip_residual(strip, co, part, f, c, ends, None, m)
    strip_restrict(res, f_part)
    strip_message(small, f_part, c_next, strip_ends(small, f_part, fl_next), up, down)


def bottom_strip_kernel(
    w, vz, flags, dn, un, first_column, last_column, c_low, c_high, part_low, part_high, terms, up, down
):
    strip = STRIPS[3]
    width = strip[2]
    winv = w[...].astype(BF16)
    co = Coef(vz)
    raws = [dn[0:Z, :], un[0:Z, :]]
    values = block_dot(winv, jnp.concatenate(raws, axis=1))
    values = [values[:, :width], values[:, width:]]
    edges = strip_edges(strip, winv, co, strip_sides(values, raws, dn, un, first_column, last_column))
    first, last, r = strip_side_terms(
        strip, winv, co, flags, (c_low[...], c_high[...]), strip_frame(strip, flags, *values), strip_frame(strip, flags, *edges)
    )
    d = block_dot(winv, jnp.concatenate([r[0], first * 0.0625, last * 0.0625, r[1]], axis=1))
    d = [d[:, k * width : (k + 1) * width] for k in range(4)]
    d[0] = first + d[0]
    d[3] = last + d[3]
    for k in range(4):
        terms[k] = d[k]
    up[...] = part_high[...] + d[3]
    down[...] = part_low[...] + d[0]


def with_columns(strip, x, terms, m):
    ty = strip[1]
    lt = in_tile(strip)
    for k, y in enumerate((0, 1, ty - 2, ty - 1)):
        x = x + jnp.where(lt == y, roll(terms[k], y - m), 0.0)
    return x


def last_strip_kernel(w, flags, dn, un, part, base_up, base_down, _lo, _hi, e, up, down, small_up, small_down):
    strip, fine = STRIPS[3], STRIPS[2]
    winv = w[...].astype(BF16)
    strip_add_sides(strip, winv, part, strip_frame(strip, flags, dn[...], un[...]), Setter(e))
    strip_message(strip, e, None, strip_ends(strip, e, flags), small_up, small_down)
    a, b = iota2(LANES, LANES)
    for h in range(2):
        lt = b % 32
        source = jnp.where(lt < 12, (lt % 6) // 2, jnp.where((lt == 18) | (lt == 19), lt - 9, 15))
        spread = jnp.where((lt != 15) & (a == 64 * h + (b // 32) * 16 + source) & (source < 15), 1.0, 0.0)
        half = slice(h * LANES, (h + 1) * LANES)
        up[:, half] = base_up[:, half] + lane_dot(small_up[...], spread)
        down[:, half] = base_down[:, half] + lane_dot(small_down[...], spread)


def base_message_kernel(part, flags, terms, v, up, down):
    strip = STRIPS[2]
    lt = in_tile(strip)
    for m in range(6):
        x = jnp.where(lt == 0, roll(terms[0], -m), 0.0)
        v[m] = part[m] + jnp.where(lt == strip[1] - 1, roll(terms[1], strip[1] - 1 - m), x)
    strip_message(strip, v, None, strip_ends(strip, v, flags), up, down)


def again2_kernel(f, c, w, vz, flags, v, e, tile_v, xlo, xhi, own, low, high, part_low, part_high, yup, ydown, twice, g, part):
    strip = STRIPS[2]
    a, b = iota2(LANES, LANES)
    for m in range(3):
        add = jnp.concatenate([lane_dot(e[m], jnp.where(a == 64 * h + b // 2, 1.0, 0.0)) for h in range(2)], axis=1)
        g[2 * m] = v[2 * m] + add
        g[2 * m + 1] = v[2 * m + 1] + add
    zero = jnp.zeros((Z, strip[2]), F32)
    low[...] = strip_column(strip, g, 0, 0, zero)
    high[...] = strip_column(strip, g, strip[1] - 1, 0, zero)
    winv = w[...].astype(BF16)
    co = Coef(vz, strip[2])
    strip_relax(strip, winv, co, g, f, c, flags, None, Setter(part))
    strip_relax(strip, winv, co, part, f, c, flags, None, Setter(twice))
    part_low[...] = strip_column(strip, twice, 0, 0, zero)
    part_high[...] = strip_column(strip, twice, strip[1] - 1, 0, zero)
    put_y(GEOM[1], tile_v, None, yup, ydown)
    add_up, add_down = relayed(tail_of(GEOM[1], xlo, 2), tail_of(GEOM[1], xhi, 2), own)
    yup[...] = yup[...] + add_up
    ydown[...] = ydown[...] + add_down


def alone3_kernel(f, c, w, vz, flags, low, high, part_low, part_high, twice, v, part):
    strip = STRIPS[3]
    winv = w[...].astype(BF16)
    co = Coef(vz)
    for m in range(3):
        v[m] = block_dot(winv, f[m])
    strip_relax(strip, winv, co, v, f, c, flags, None, Setter(part))
    strip_relax(strip, winv, co, part, f, c, flags, None, Setter(twice))
    zero = jnp.zeros((Z, LANES), F32)
    for ref, first, last in ((v, low, high), (twice, part_low, part_high)):
        first[...] = strip_column(strip, ref, 0, 0, zero)
        last[...] = strip_column(strip, ref, strip[1] - 1, 0, zero)


def again3_kernel(f, c, w, vz, flags, twice, terms, part, v):
    strip = STRIPS[3]
    for m in range(3):
        v[m] = with_columns(strip, twice[m], terms, m)
    strip_relax(strip, w[...].astype(BF16), Coef(vz), v, f, c, flags, None, Setter(part))


def tile_lanes(x, step):
    t = lax.rem(lax.axis_index("gx") + (step + 8), 8)
    half = jnp.where(t < 4, x[:, :LANES], x[:, LANES:])
    return pltpu.roll(half, lax.rem(8 - t, 4) * 32, axis=1)


def post_strip_kernel(
    w, vz, flags, dn, un, first_column, last_column, c_low, c_high, part_low, part_high, gdn, gun, own, yup, ydown, terms, up, down
):
    strip = STRIPS[2]
    width = strip[2]
    winv = w[...].astype(BF16)
    co = Coef(vz, width)
    raws = [dn[0:Z, :], un[0:Z, :]]
    values = [gdn[...], gun[...]]
    edges = strip_edges(strip, winv, co, strip_sides(values, raws, dn, un, first_column, last_column))
    first, last, r = strip_side_terms(
        strip, winv, co, flags, (c_low[...], c_high[...]), strip_frame(strip, flags, *values), strip_frame(strip, flags, *edges)
    )
    d = block_dot(winv, jnp.concatenate([r[0], first * 0.0625, last * 0.0625, r[1]], axis=1))
    d = [d[:, k * width : (k + 1) * width] for k in range(4)]
    d[0] = first + d[0]
    d[3] = last + d[3]
    for k in range(4):
        terms[k] = d[k]
    low, high = part_low[...] + d[0], part_high[...] + d[3]
    lane = zl()

    def tile_corners(step):
        first_lanes, last_lanes = tile_lanes(low, step), tile_lanes(high, step)
        return [roll(x, 112 - place) for x, place in ((first_lanes, 0), (last_lanes, 0), (first_lanes, 5), (last_lanes, 5))]

    f0, f1 = flag_row(own, 0) > 0.5, flag_row(own, 1) > 0.5
    a, b = iota2(LANES, LANES)
    spread = jnp.where((b < 24) & (a == b // 4), 1.0, 0.0)
    add_up = lane_dot(tile_lanes(high, 0), spread)
    add_down = lane_dot(tile_lanes(low, 0), spread)
    to_up, to_down = relay_order(tile_corners(-1), tile_corners(1), f0, f1)
    for k in range(6):
        add_up = jnp.where(lane == 112 + k, roll(to_up[k], k), add_up)
        add_down = jnp.where(lane == 112 + k, roll(to_down[k], k), add_down)
    up[...] = yup[...] + add_up
    down[...] = ydown[...] + add_down


def again1_kernel(f, c, w, vz, v, twice, terms, xlo, xhi, g, part, columns, lo_out, hi_out, tile):
    fine, geom = GEOM[1], GEOM[2]
    rows = []
    for m in range(6):
        rows.append(with_columns(STRIPS[2], twice[m], terms, m))
        tile[m] = tile_lanes(rows[m], 0)
    prolong_add(fine, geom, tile, v, g)
    a, b = iota2(LANES, LANES)
    spread = jnp.where((b < 64) & (a == b // 2), 1.0, 0.0)
    for ref, out, row in ((xlo, lo_out, tile_lanes(rows[5], -1)), (xhi, hi_out, tile_lanes(rows[0], 1))):
        add = lane_dot(row, spread)
        out[...] = pack(fine, [part_of(fine, ref, 0) + add, part_of(fine, ref, 1) + add])[0]
    columns[...] = own_columns(fine, g)
    relax_tile(fine, w[...].astype(BF16), Coef(vz), g, f, c, ALONE, Setter(part))


def swap_pairs(axis, which, nearest=False):
    sizes = lax.axis_size("gx"), lax.axis_size("gy")
    out = []
    for i in range(sizes[0]):
        for j in range(sizes[1]):
            at = [i, j]
            dim = 0 if axis == "gx" else 1
            n = sizes[dim]
            at[dim] = (at[dim] ^ 1) if which == 0 else (at[dim] + (1 if at[dim] % 2 else n - 1)) % n
            if nearest and 2 * j // n != 2 * at[1] // n:
                at[0] = i ^ 1
            out.append((i * sizes[1] + j, at[0] * sizes[1] + at[1]))
    return out


def swap(first, second, axis, nearest=False):
    both = ("gx", "gy")
    return (
        lax.ppermute(first, both, swap_pairs(axis, 0, nearest)),
        lax.ppermute(second, both, swap_pairs(axis, 1, nearest)),
    )


ANY = pl.BlockSpec(memory_space=pl.ANY)
LIMIT = 14 * 1024 * 1024
VMEM = pl.BlockSpec(memory_space=pltpu.VMEM)


class Either:
    def __init__(self, first, a, b):
        self.first, self.a, self.b = first, a, b

    def __getitem__(self, index):
        return jnp.where(self.first, self.a[index], self.b[index])


def is_even(axis):
    return lax.rem(lax.axis_index(axis), 2) == 0


def by_swaps(kernel, n_in, n_out, got, send):
    def wrapped(*refs):
        refs = list(refs)
        for place, axis in got:
            a, b = refs[place], refs[place + 1]
            refs[place], refs[place + 1] = Either(is_even(axis), b, a), Either(is_even(axis), a, b)
        extra = refs[len(refs) - 2 * len(send) :]
        refs = refs[: len(refs) - 2 * len(send)]
        outs = []
        for k, (place, axis) in enumerate(send):
            place += n_in
            outs.append((refs[place], refs[place + 1], extra[2 * k], extra[2 * k + 1], axis))
            refs[place], refs[place + 1] = extra[2 * k], extra[2 * k + 1]
        kernel(*refs)
        for first, second, up, down, axis in outs:
            even = is_even(axis)
            up, down = up[...], down[...]
            first[...] = jnp.where(even, up, down)
            second[...] = jnp.where(even, down, up)

    return wrapped


def call(kernel, outs, args, scratch=(), name=None, after=0, got=(), send=()):
    scratch = [pltpu.VMEM(s, F32) for s in scratch]
    scratch += [pltpu.VMEM(outs[place], F32) for place, _ in send for _ in range(2)]
    return pl.pallas_call(
        by_swaps(kernel, len(args), len(outs), got, send),
        out_shape=[jax.ShapeDtypeStruct(s, F32) for s in outs],
        in_specs=[VMEM] * (len(args) - after) + [ANY] * after,
        out_specs=[VMEM] * len(outs),
        scratch_shapes=scratch,
        compiler_params=pltpu.CompilerParams(vmem_limit_bytes=LIMIT),
        name=name,
    )(*args)


def tile_shape(level):
    return (GEOM[level][0], Z, LANES)


def x_shape(level, count):
    return (message_rows(GEOM[level], count) + 8, LANES)


Y_FULL = (Z + 8, LANES)


def open_kernel(f_in, c_in, vert_in, flip_in, up, down, own, vz, f_low, f_high, c_low, c_high, vert, flip, sems):
    pairs = (
        (vert_in, vert),
        (flip_in, flip),
        (f_in.at[:, 0:2, :], f_low),
        (f_in.at[:, 22:24, :], f_high),
        (c_in.at[:, 0:1, :], c_low),
        (c_in.at[:, 23:24, :], c_high),
    )
    copies = [pltpu.make_async_copy(src, dst, sems.at[k]) for k, (src, dst) in enumerate(pairs)]
    for copy in copies:
        copy.start()
    for copy in copies[:2]:
        copy.wait()
    a, b = iota2(8, 4)
    flags = jnp.broadcast_to(flip[...].astype(F32), (8, 4))
    flags = jnp.broadcast_to(jnp.sum(jnp.where(a == b, flags, 0.0), axis=1, keepdims=True), (8, LANES))
    own[...] = flags
    a, b = iota2(Z, NZ + 1)
    coef = jnp.broadcast_to(vert[...], (Z, NZ + 1))
    high = jnp.sum(jnp.where((b == a + 1) & (a < NZ), coef, 0.0), axis=1, keepdims=True)
    low = jnp.sum(jnp.where((b == a) & (a < NZ), coef, 0.0), axis=1, keepdims=True)
    columns = [jnp.broadcast_to(x * 0.0625, (Z, LANES)) for x in (4.0 + high + low, high, low)]
    for k in range(3):
        vz[k] = columns[k]
    up[...] = jnp.zeros(up.shape, F32)
    down[...] = jnp.zeros(down.shape, F32)
    for copy in copies[2:]:
        copy.wait()
    up[0:NZ, :] = f_high[:, 1, :]
    up[Z : Z + NZ, :] = f_high[:, 0, :]
    up[2 * Z : 2 * Z + NZ, :] = c_high[:, 0, :]
    down[0:NZ, :] = f_low[:, 0, :]
    down[Z : Z + NZ, :] = f_low[:, 1, :]
    down[2 * Z : 2 * Z + NZ, :] = c_low[:, 0, :]
    first, last = down[0:Z, :], up[0:Z, :]
    tail = flags + corner_rows([col(first, 0), col(first, LANES - 1), col(last, 0), col(last, LANES - 1)])
    up[3 * Z : 3 * Z + 8, :] = tail
    down[3 * Z : 3 * Z + 8, :] = tail


def block_matrix(inv):
    width = 3 * Z
    a, b = iota2(BLK, width)
    b = b % Z
    spread = jnp.where((b % BLK == a) & (b < NZ), 1.0, 0.0).astype(BF16)
    whole = jnp.zeros((NZ, width), F32)
    left = inv
    for _ in range(3):
        part = left.astype(BF16)
        whole = whole + jnp.dot(part, spread, preferred_element_type=F32)
        left = left - part.astype(F32)
    a, b = iota2(NZ, width)
    whole = jnp.where(a // BLK == (b % Z) // BLK, whole, 0.0)
    high = whole.astype(BF16).astype(F32)
    return jnp.where((b >= Z) & (b < 2 * Z), whole - high, high)


def side_kernel(f_in, c_in, inv, vz, own, f, c, w0, w1, w2, w3, one, part, columns, c_next, c_tile, yup, ydown):
    load_top(f_in, f)
    load_top(c_in, c)
    put_y(GEOM[0], f, c, yup, ydown)
    yup[Z : Z + 8, :] = own[...]
    ydown[Z : Z + 8, :] = own[...]
    for level, w in enumerate((w0, w1, w2, w3)):
        w[0:NZ, :] = block_matrix(inv[level])
        w[NZ:Z, :] = jnp.zeros((Z - NZ, 3 * Z), F32)
    winv = w0[...].astype(BF16)
    start_tile(GEOM[0], winv, f, Setter(one))
    relax_tile(GEOM[0], winv, Coef(vz), one, f, c, ALONE, Setter(part))
    columns[...] = own_columns(GEOM[0], one)
    restrict(GEOM[0], GEOM[1], c, c_next)
    restrict(GEOM[1], GEOM[2], c_next, c_tile)


def merge_kernel(level, count):
    geom = GEOM[level]

    def kernel(xlo, xhi, flags, yup, ydown, up, down):
        add_up, add_down = relayed(tail_of(geom, xlo, count), tail_of(geom, xhi, count), flags)
        up[...] = yup[...]
        down[...] = ydown[...]
        up[0:Z, :] = yup[0:Z, :] + add_up
        down[0:Z, :] = ydown[0:Z, :] + add_down

    return kernel


def pre_edges(geom, f, c, w, vz, own, xlo, xhi, ydn, yun, one, columns):
    winv = w[...].astype(BF16)
    fl = flags_of(geom, own, xlo, xhi, ydn, yun)
    halo = messages(geom, xlo, xhi, ydn, yun, winv)
    relaxed = relax_edges(geom, winv, Coef(vz), one, columns[...], halo, fl, *own_data(geom, xlo, xhi, ydn, yun))
    terms = edge_terms(geom, winv, frame(geom, fl, halo.lo, halo.hi, halo.sides()))
    return terms, frame(geom, fl, *relaxed)


def pre0_kernel(f, c, w, vz, own, xlo, xhi, ydn, yun, one, part, columns, c_next, up, down, terms_out, edges_out, v, res, f_next):
    geom, coarse = GEOM[0], GEOM[1]
    terms, edges = pre_edges(geom, f, c, w, vz, own, xlo, xhi, ydn, yun, one, columns)
    for k in range(3):
        terms_out[k] = terms[k]
        edges_out[k] = edges[k]
    co = Coef(vz)
    for m in (*range(5), *range(19, 24)):
        v[m] = with_terms(geom, part[m], terms, m)
    for m in (*range(4), *range(20, 24)):
        res[m] = tile_residual(geom, co, v, f, c, *edges, m)
    restrict(geom, coarse, res, f_next, (0, 1, 10, 11))
    put_x(coarse, f_next, c_next, up, down, own[...])


def mid1_kernel(f, c, part, terms_in, edges_in, vz, w, c_next, own, v, f_next, one, part_next, columns, yup, ydown, res):
    geom, coarse = GEOM[0], GEOM[1]
    co = Coef(vz)
    terms = [terms_in[k] for k in range(3)]
    edges = [edges_in[k] for k in range(3)]
    for m in range(24):
        v[m] = with_terms(geom, part[m], terms, m)
    for m in range(24):
        res[m] = tile_residual(geom, co, v, f, c, *edges, m)
    restrict(geom, coarse, res, f_next)
    put_y(coarse, f_next, c_next, yup, ydown)
    yup[Z : Z + 8, :] = own[...]
    ydown[Z : Z + 8, :] = own[...]
    winv = w[...].astype(BF16)
    start_tile(coarse, winv, f_next, Setter(one))
    relax_tile(coarse, winv, co, one, f_next, c_next, ALONE, Setter(part_next))
    columns[...] = own_columns(coarse, one)


def pre1_kernel(f, c, w, vz, own, xlo, xhi, ydn, yun, one, part, columns, c_tile, v_out, up, down, chunks, res, f_next):
    geom = GEOM[1]
    terms, edges = pre_edges(geom, f, c, w, vz, own, xlo, xhi, ydn, yun, one, columns)
    for m in range(6):
        v_out[m] = with_terms(geom, part[m], terms, m)
    co = Coef(vz)
    for m in range(6):
        res[m] = tile_residual(geom, co, v_out, f, c, *edges, m)
    restrict(geom, GEOM[2], res, f_next)
    put_x(geom, v_out, None, up, down)
    whole = pack(GEOM[2], [f_next[m] for m in range(6)] + [c_tile[m] for m in range(6)])
    turn = lax.rem(lax.axis_index("gx"), 4) * 32
    whole = [pltpu.roll(x, turn, axis=1) for x in whole]
    for t in range(8):
        for k, x in enumerate(whole):
            chunks[t, k * Z : (k + 1) * Z, :] = x
        chunks[t, 3 * Z : 3 * Z + 8, :] = own[...]


def again0_kernel(f, c, w, vz, e, v, g, part, columns, yup, ydown):
    prolong_add(GEOM[0], GEOM[1], e, v, g)
    put_y(GEOM[0], g, None, yup, ydown)
    columns[...] = own_columns(GEOM[0], g)
    relax_tile(GEOM[0], w[...].astype(BF16), Coef(vz), g, f, c, ALONE, Setter(part))


def twice0_kernel(f, c, w, vz, part, _after, twice, c_columns):
    c_columns[...] = own_columns(GEOM[0], c)
    relax_tile(GEOM[0], w[...].astype(BF16), Coef(vz), part, f, c, ALONE, Setter(twice))


def post_edges(geom, f, c, w, vz, own, xlo, xhi, ydn, yun, g, columns, glo, ghi, gdn, gun):
    fl = flags_of(geom, own, xlo, xhi, ydn, yun)
    halo = Halo(
        part_of(geom, glo, 0), part_of(geom, glo, 1), part_of(geom, ghi, 0), part_of(geom, ghi, 1), gdn[...], gun[...]
    )
    winv = w[...].astype(BF16)
    relaxed = relax_edges(geom, winv, Coef(vz), g, columns[...], halo, fl, *own_data(geom, xlo, xhi, ydn, yun))
    return frame(geom, fl, halo.lo, halo.hi, halo.sides()), frame(geom, fl, *relaxed)


def post0_kernel(f, c, w, vz, own, xlo, xhi, ydn, yun, g, columns, c_columns, twice, glo, ghi, gdn, gun, out):
    geom = GEOM[0]
    rows = geom[0]
    winv = w[...].astype(BF16)
    co = Coef(vz)
    lane = zl()
    edges, edges_next = post_edges(geom, f, c, w, vz, own, xlo, xhi, ydn, yun, g, columns, glo, ghi, gdn, gun)
    low, high, sides = edge_terms(geom, winv, edges)

    def row_residual(v, c_row, beyond):
        beside = jnp.where(lane == 0, 0.0, roll(v, 1)) + jnp.where(lane == LANES - 1, 0.0, roll(v, -1))
        return residual(co, beyond * 0.0625, c_row, v, beside)

    beside = jnp.where(lane < 2, 0.0, roll(sides, 2)) + jnp.where(lane >= 2 * rows - 2, 0.0, roll(sides, -2))
    r = [
        row_residual(low, c[0], edges_next[0]),
        low * 0.0625,
        high * 0.0625,
        row_residual(high, c[rows - 1], edges_next[1]),
        residual(co, edges_next[2] * 0.0625, c_columns[...], sides, beside),
        sides * 0.0625,
    ]
    d = block_dot(winv, jnp.concatenate(r, axis=1))
    d = [d[:, k * LANES : (k + 1) * LANES] for k in range(6)]
    a, b = iota2(LANES, LANES)
    outer = jnp.where((b % 4 == 1) | (b % 4 == 2), 1.0, 0.0) * jnp.where(a == 2 * (b // 4) + b % 4 - 1, 1.0, 0.0)
    inner = jnp.where((b % 4 == 0) | (b % 4 == 3), 1.0, 0.0) * jnp.where(a == 2 * (b // 4) + b % 4 // 3, 1.0, 0.0)
    four = lane_dot(sides + d[4], outer) + lane_dot(d[5], inner)
    inside = (lane < 2) | (lane >= LANES - 2)
    row_terms = {0: low + d[0], 1: d[1], rows - 2: d[2], rows - 1: high + d[3]}
    for m in range(rows):
        x = twice[m] + jnp.where(inside, roll(four, -4 * m - 2), 0.0)
        if m in row_terms:
            x = x + row_terms[m]
        out[pl.ds(m, NZ, stride=24), :] = x[0:NZ, :]


def post1_kernel(
    f, c, w, vz, own, xlo, xhi, ydn, yun, g, part, columns, glo, ghi, gdn, gun, fine_v, e, up, down, one, fine_g
):
    geom = GEOM[1]
    edges, edges_next = post_edges(geom, f, c, w, vz, own, xlo, xhi, ydn, yun, g, columns, glo, ghi, gdn, gun)
    winv = w[...].astype(BF16)
    add_edges(geom, winv, part, edges, Setter(one))
    relax_tile(geom, winv, Coef(vz), one, f, c, edges_next, Setter(e))
    prolong_add(GEOM[0], GEOM[1], e, fine_v, fine_g, (0, 22))
    put_x(GEOM[0], fine_g, None, up, down)


def on_device(right_side, helm_coef, vert_coef, block_inverse, edge_flip):
    inv = block_inverse.reshape(4, NZ, BLK)
    f_in = right_side.reshape(NZ * 24, LANES)
    c_in = helm_coef.reshape(NZ * 24, LANES)
    vert = vert_coef.reshape(1, NZ + 1)
    flip = edge_flip.reshape(1, 4)

    ys = (Z, LANES)
    t0, t1, t2 = tile_shape(0), tile_shape(1), tile_shape(2)
    xs = x_shape(0, 3)
    up, down, own, vz = pl.pallas_call(
        by_swaps(open_kernel, 4, 4, (), ((0, "gx"),)),
        out_shape=[jax.ShapeDtypeStruct(x, F32) for x in (xs, xs, (8, LANES), (3, Z, LANES))],
        in_specs=[ANY] * 4,
        out_specs=[VMEM] * 4,
        scratch_shapes=[pltpu.VMEM((NZ, 2, LANES), F32)] * 2
        + [pltpu.VMEM((NZ, 1, LANES), F32)] * 2
        + [pltpu.VMEM((1, NZ + 1), F32), pltpu.VMEM((1, 4), jnp.int32), pltpu.SemaphoreType.DMA((6,))]
        + [pltpu.VMEM(xs, F32)] * 2,
        compiler_params=pltpu.CompilerParams(vmem_limit_bytes=58 * 1024 * 1024),
        name="open",
    )(right_side, helm_coef, vert, flip)
    xlo, xhi = swap(up, down, "gx")
    ws = (Z, 3 * Z)
    f, c, *w, one, part, columns, c1, c_tile, yup, ydown = call(
        side_kernel,
        [t0, t0] + [ws] * 4 + [t0, t0, ys, t1, t2, Y_FULL, Y_FULL],
        [f_in, c_in, inv, vz, own],
        name="side",
    )

    def to_sides(level, count, xlo, xhi, yup, ydown):
        shape = yup.shape
        yup, ydown = call(merge_kernel(level, count), [shape, shape], [xlo, xhi, own, yup, ydown], name=f"merge{level}", got=((0, "gx"),), send=((0, "gy"),))
        return swap(yup, ydown, "gy")

    got0 = (xlo, xhi, *to_sides(0, 3, xlo, xhi, yup, ydown))
    xs = x_shape(1, 3)
    three = (3, Z, LANES)
    up, down, terms, edges = call(
        pre0_kernel,
        [xs, xs, three, three],
        [f, c, w[0], vz, own, *got0, one, part, columns, c1],
        [t0, t0, t1],
        name="pre0",
        got=((5, "gx"), (7, "gy")),
        send=((0, "gx"),),
    )
    xlo, xhi = swap(up, down, "gx")
    v0, f1, one, part, columns, yup, ydown = call(
        mid1_kernel,
        [t0, t1, t1, t1, ys, Y_FULL, Y_FULL],
        [f, c, part, terms, edges, vz, w[1], c1, own],
        [t0],
        name="mid1",
    )
    got1 = (xlo, xhi, *to_sides(1, 3, xlo, xhi, yup, ydown))
    xs = x_shape(1, 2)
    v1, up, down, chunks = call(
        pre1_kernel,
        [t1, xs, xs, (8, 3 * Z + 8, LANES)],
        [f1, c1, w[1], vz, own, *got1, one, part, columns, c_tile],
        [t1, t2],
        name="pre1",
        got=((5, "gx"), (7, "gy")),
        send=((1, "gx"),),
    )
    v1_lo, v1_hi = swap(up, down, "gx")
    chunks = lax.all_to_all(chunks, "gx", 0, 0)
    s2, s3 = (6, Z, 256), (3, Z, 128)
    m2, m3 = (Z, 256), (Z, 128)
    full2, full3 = (Z + 8, 256), (Z + 8, 128)
    f2, c2, fl2, up, down = call(
        open_strip_kernel, [s2, s2, (8, 256), full2, full2], [chunks], name="open2", send=((3, "gy"),)
    )
    side2 = swap(up, down, "gy", True)
    c3, fl3, *c_sides = call(next_coef_kernel, [s3, (8, 128), m2, m2, m3, m3], [c2, fl2], name="coef3")
    part2, first, last, f_part, base_up, base_down = call(
        alone2_kernel, [s2, m2, m2, s3, m3, m3], [f2, c2, w[2], vz, fl2, c3, fl3], [s2, s2], name="alone2"
    )
    terms2, f3, up, down = call(
        pre_strip_kernel,
        [(2, *m2), s3, full3, full3],
        [w[2], vz, fl2, *side2, first, last, *c_sides[:2], f_part, fl3, base_up, base_down],
        name="pre2",
        got=((3, "gy"),),
        send=((2, "gy"),),
    )
    side3 = swap(up, down, "gy", True)
    *alone, twice = call(alone3_kernel, [m3] * 4 + [s3], [f3, c3, w[3], vz, fl3], [s3, s3], name="alone3")
    terms, up, down = call(
        bottom_strip_kernel,
        [(4, *m3), m3, m3],
        [w[3], vz, fl3, *side3, *alone[:2], *c_sides[2:], *alone[2:]],
        name="bottom",
        got=((3, "gy"),),
        send=((1, "gy"),),
    )
    side = swap(up, down, "gy", True)
    (part,) = call(again3_kernel, [s3], [f3, c3, w[3], vz, fl3, twice, terms], [s3], name="again3")
    v2, base_up, base_down = call(base_message_kernel, [s2, m2, m2], [part2, fl2, terms2], name="base2")
    e3, up, down = call(
        last_strip_kernel,
        [s3, m2, m2],
        [w[3], fl3, *side, part, base_up, base_down, v1_lo, v1_hi],
        [m3, m3],
        name="last",
        after=2,
        got=((2, "gy"),),
        send=((1, "gy"),),
    )
    side = swap(up, down, "gy", True)
    first, last, part_low, part_high, yup, ydown, twice = call(
        again2_kernel, [m2] * 4 + [ys, ys, s2], [f2, c2, w[2], vz, fl2, v2, e3, v1, v1_lo, v1_hi, own], [s2, s2], name="again2", got=((8, "gx"),)
    )
    terms, up, down = call(
        post_strip_kernel,
        [(4, *m2), ys, ys],
        [w[2], vz, fl2, *side2, first, last, *c_sides[:2], part_low, part_high, *side, own, yup, ydown],
        name="post2",
        got=((3, "gy"), (11, "gy")),
        send=((1, "gy"),),
    )
    side = swap(up, down, "gy")
    g1, part, columns, lo, hi = call(
        again1_kernel, [t1, t1, ys, ys, ys], [f1, c1, w[1], vz, v1, twice, terms, v1_lo, v1_hi], [t2], name="again1", got=((7, "gx"),)
    )
    xs = x_shape(0, 2)
    e1, up, down = call(
        post1_kernel,
        [t1, xs, xs],
        [f1, c1, w[1], vz, own, *got1, g1, part, columns, lo, hi, *side, v0],
        [t1, t0],
        name="post1",
        got=((5, "gx"), (7, "gy"), (14, "gy")),
        send=((1, "gx"),),
    )
    xlo, xhi = swap(up, down, "gx")
    g0, part, columns, yup, ydown = call(
        again0_kernel, [t0, t0, ys, ys, ys], [f, c, w[0], vz, e1, v0], name="again0"
    )
    up, down = call(
        merge_kernel(0, 2), [ys, ys], [xlo, xhi, own, yup, ydown], name="merge0", got=((0, "gx"),), send=((0, "gy"),)
    )
    side = swap(up, down, "gy")
    twice, c_columns = call(twice0_kernel, [t0, ys], [f, c, w[0], vz, part, up], name="twice0", after=1)
    (out,) = call(
        post0_kernel,
        [(NZ * 24, LANES)],
        [f, c, w[0], vz, own, *got0, g0, columns, c_columns, twice, xlo, xhi, *side],
        name="post0",
        got=((5, "gx"), (7, "gy"), (13, "gx"), (15, "gy")),
    )
    return out.reshape(NZ, 24, LANES)


def solution(mesh):
    placed = (P(None, "gx", "gy"), P(None, "gx", "gy"), P(), P(), P("gx", "gy", None))
    return jax.shard_map(
        on_device, mesh=mesh, in_specs=placed, out_specs=P(None, "gx", "gy"), check_vma=False
    )
```

```python
import jax
import jax.numpy as jnp
from jax import lax
from jax.experimental import pallas as pl
from jax.experimental.pallas import tpu as pltpu
from jax.sharding import PartitionSpec as P

BLK = 14
NBLK = 5
NZ = 70
Z = 72
LANES = 128
F32 = jnp.float32
BF16 = jnp.bfloat16

GEOM = ((24, 1, 128), (6, 2, 64), (6, 1, 32), (3, 1, 16))


def lane_ids(shape):
    return lax.broadcasted_iota(jnp.int32, shape, len(shape) - 1)


def zl():
    return lane_ids((Z, LANES))


def roll(x, shift):
    shift = shift % x.shape[-1]
    return x if shift == 0 else pltpu.roll(x, shift, axis=1)


def col(x, k):
    return jnp.broadcast_to(x[:, k : k + 1], (Z, LANES))


def iota2(n, m):
    return lax.broadcasted_iota(jnp.int32, (n, m), 0), lax.broadcasted_iota(jnp.int32, (n, m), 1)


def lane_dot(x, mat):
    hi = x.astype(BF16).astype(F32)
    both = jnp.concatenate([hi, x - hi], axis=1).astype(BF16)
    twice = jnp.concatenate([mat, mat], axis=0).astype(BF16)
    return jnp.dot(both, twice, preferred_element_type=F32)


def block_dot(winv, x):
    hi = x.astype(BF16).astype(F32)
    parts = jnp.concatenate([hi, hi, x - hi], axis=0).astype(BF16)
    return jnp.dot(winv, parts, preferred_element_type=F32)


def reverse_matrix(width):
    a, b = iota2(LANES, LANES)
    return jnp.where((b < width) & (a == width - 1 - b), 1.0, 0.0)


def flag_row(flags, k):
    return jnp.broadcast_to(flags[k : k + 1, :], (Z, LANES))


class Coef:
    def __init__(self, ref, width=LANES):
        self.mid, self.up, self.down = [jnp.concatenate([ref[k]] * (width // LANES), axis=1) for k in range(3)]


def residual(co, f, c, v, beside):
    above = pltpu.roll(v, Z - 1, axis=0)
    below = pltpu.roll(v, 1, axis=0)
    return f - (c * 0.0625 + co.mid) * v + beside * 0.0625 + co.up * above + co.down * below


def row_of(geom, v, row):
    m_rows, _, ty = geom
    q, m = divmod(row, m_rows)
    return roll(v[m], -q * ty)


def corners(geom, v):
    m_rows, groups, ty = geom
    last = v[m_rows - 1]
    base = (groups - 1) * ty
    return corner_rows([col(v[0], 0), col(v[0], ty - 1), col(last, base), col(last, base + ty - 1)])


def corner_rows(columns):
    lane = zl()
    out = jnp.zeros((Z, LANES), F32)
    for k, column in enumerate(columns):
        out = jnp.where(lane == 4 + k, column, out)
    return jnp.concatenate([out, jnp.zeros((LANES - Z, LANES), F32)], axis=0).T[0:8, :]


def corner_columns(rows):
    out = jnp.concatenate([rows, jnp.zeros((LANES - 8, LANES), F32)], axis=0).T[0:Z, :]
    return [col(out, 4 + k) for k in range(4)]


def whole_rows(geom):
    return geom[1] == 1 and geom[2] == LANES


def tile_rows(geom):
    m_rows, groups, ty = geom
    return [(q * m_rows + m, m, q * ty) for m in range(m_rows) for q in range(groups)]


def own_columns(geom, v):
    ty = geom[2]
    lane = zl()
    out = jnp.zeros((Z, LANES), F32)
    for r, m, base in tile_rows(geom):
        row = v[m]
        first = roll(row, 2 * r + 1 - base)
        out = jnp.where(lane == 2 * r + 1, first, out)
        last = first if whole_rows(geom) else roll(row, 2 * r - (base + ty - 1))
        out = jnp.where(lane == 2 * r, last, out)
    return out


def pack(geom, parts):
    ty = geom[2]
    per = LANES // ty
    out = []
    for first in range(0, len(parts), per):
        lane = zl()
        acc = parts[first]
        for k, part in enumerate(parts[first + 1 : first + per], 1):
            acc = jnp.where(lane < k * ty, acc, roll(part, k * ty))
        out.append(acc)
    return out


def packed(geom, count):
    per = LANES // geom[2]
    return -(-count // per)


def part_of(geom, ref, k):
    ty = geom[2]
    per = LANES // ty
    return roll(ref[(k // per) * Z : (k // per + 1) * Z, :], -(k % per) * ty)


def put_x(geom, v, c, up, down, flags=None):
    m_rows, groups, _ = geom
    tx = m_rows * groups
    tail = corners(geom, v)
    if flags is not None:
        tail = tail + flags
    for ref, edge, second in ((up, tx - 1, tx - 2), (down, 0, 1)):
        parts = [row_of(geom, v, edge), row_of(geom, v, second)]
        if c is not None:
            parts.append(row_of(geom, c, edge))
        put_parts(geom, parts, tail, ref)


SPLIT = 40


def halved(geom, count):
    return geom[2] == 64 and count == 3


def put_parts(geom, parts, tail, ref):
    if halved(geom, len(parts)):
        lane = lane_ids((SPLIT, LANES))
        rest = jnp.concatenate([parts[2][SPLIT:Z, :], jnp.zeros((2 * SPLIT - Z, LANES), F32)], axis=0)
        ref[0:Z, :] = pack(geom, parts[:2])[0]
        ref[Z : Z + SPLIT, :] = jnp.where(lane < 64, parts[2][0:SPLIT, :], roll(rest, 64))
        ref[Z + SPLIT : Z + SPLIT + 8, :] = tail
        return
    whole = pack(geom, parts)
    for k, part in enumerate(whole):
        ref[k * Z : (k + 1) * Z, :] = part
    ref[len(whole) * Z : len(whole) * Z + 8, :] = tail


def tail_of(geom, ref, count):
    n = message_rows(geom, count)
    return ref[n : n + 8, :]


def message_rows(geom, count):
    return Z + SPLIT if halved(geom, count) else packed(geom, count) * Z


def put_y(geom, v, c, up, down):
    ty = geom[2]
    lane = zl()
    out_up = jnp.zeros((Z, LANES), F32)
    out_down = out_up
    for r, m, base in tile_rows(geom):
        row = v[m]
        mine = lane // 2 == r
        last = roll(row, 2 * r + 1 - (base + ty - 1))
        first = roll(row, 2 * r - base)
        out_up = jnp.where(mine, last, out_up)
        out_down = jnp.where(mine, first, out_down)
        if c is not None:
            row = c[m]
            out_up = jnp.where(lane == 65 + 2 * r, roll(row, 65 + 2 * r - (base + ty - 1)), out_up)
            out_down = jnp.where(lane == 64 + 2 * r, roll(row, 64 + 2 * r - base), out_down)
    up[0:Z, :] = out_up
    down[0:Z, :] = out_down


def relay_order(lo, hi, f0, f1):
    up = [lo[3], lo[1], hi[1], hi[3], jnp.where(f0, lo[2], lo[3]), jnp.where(f1, hi[0], hi[1])]
    down = [lo[2], lo[0], hi[0], hi[2], jnp.where(f0, lo[3], lo[2]), jnp.where(f1, hi[1], hi[0])]
    return up, down


def relayed(lo, hi, flags):
    lo = [lo[4 + k : 5 + k, :] for k in range(4)]
    hi = [hi[4 + k : 5 + k, :] for k in range(4)]
    up, down = relay_order(lo, hi, flags[0:1, :] > 0.5, flags[1:2, :] > 0.5)
    two = jnp.zeros((2, LANES), F32)
    rows = [*down, two, jnp.zeros((104, LANES), F32), *up, two, jnp.zeros((8, LANES), F32)]
    turned = jnp.concatenate(rows, axis=0).T[0:Z, :]
    lane = zl()
    inside = (lane >= 112) & (lane < 118)
    return jnp.where(inside, turned, 0.0), jnp.where(inside, roll(turned, 112), 0.0)


def odd_lanes():
    return zl() % 2 == 1


class Halo:
    def __init__(self, lo, lo2, hi, hi2, dn, un):
        self.lo, self.lo2, self.hi, self.hi2, self.dn, self.un = lo, lo2, hi, hi2, dn, un

    def sides(self):
        return jnp.where(odd_lanes(), self.dn, self.un)

    def seconds(self):
        return jnp.where(odd_lanes(), roll(self.dn, 1), roll(self.un, -1))


class Flags:
    def __init__(self, own, lo, hi, dn, un):
        self.own, self.lo, self.hi, self.dn, self.un = own, lo, hi, dn, un


def turn_row(geom, row, flag):
    return jnp.where(flag > 0.5, lane_dot(row, reverse_matrix(geom[2])), row)


def turn_sides(geom, sides, flag_dn, flag_un):
    tx = geom[0] * geom[1]
    flag = jnp.where(odd_lanes(), flag_dn, flag_un)
    a, b = iota2(LANES, LANES)
    mat = jnp.where((b < 2 * tx) & (a == 2 * (tx - 1 - b // 2) + b % 2), 1.0, 0.0)
    return jnp.where(flag > 0.5, lane_dot(sides, mat), sides)


def frame(geom, fl, lo, hi, sides):
    return (
        turn_row(geom, lo, flag_row(fl.own, 0)),
        turn_row(geom, hi, flag_row(fl.own, 1)),
        turn_sides(geom, sides, flag_row(fl.own, 2), flag_row(fl.own, 3)),
    )


def relax_edges(geom, winv, co, v, columns, halo, fl, f_lo, c_lo, f_hi, c_hi, f_sides, c_sides):
    m_rows, groups, ty = geom
    tx = m_rows * groups
    lane = zl()
    dn, un = halo.dn, halo.un

    def beside_row(edge, second, mine, low, high):
        left = jnp.where(lane == 0, roll(low, -112), roll(edge, 1))
        right = jnp.where(lane == ty - 1, roll(high, ty - 113), roll(edge, -1))
        return second + mine + left + right

    def choose(flags, k, x, place):
        x = roll(x, 112 - place)
        return jnp.where(flag_row(flags, k) > 0.5, roll(x, -1), x)

    b_lo = beside_row(
        halo.lo,
        halo.lo2,
        turn_row(geom, row_of(geom, v, 0), flag_row(fl.lo, 1)),
        choose(fl.lo, 2, dn, 112),
        choose(fl.lo, 3, un, 112),
    )
    b_hi = beside_row(
        halo.hi,
        halo.hi2,
        turn_row(geom, row_of(geom, v, tx - 1), flag_row(fl.hi, 0)),
        choose(fl.hi, 2, dn, 114),
        choose(fl.hi, 3, un, 114),
    )
    edge = halo.sides()
    mine = turn_sides(geom, columns, flag_row(fl.dn, 3), flag_row(fl.un, 2))
    below = jnp.where(lane == 1, roll(dn, -115), jnp.where(lane == 0, roll(un, -116), roll(edge, 2)))
    last = 2 * (tx - 1)
    above = jnp.where(lane == last + 1, roll(dn, last - 116), jnp.where(lane == last, roll(un, last - 117), roll(edge, -2)))
    b_sides = halo.seconds() + mine + below + above
    r_lo = residual(co, f_lo, c_lo, halo.lo, b_lo)
    r_hi = residual(co, f_hi, c_hi, halo.hi, b_hi)
    r_sides = residual(co, f_sides, c_sides, edge, b_sides)
    d = block_dot(winv, jnp.concatenate([r_lo, r_hi, r_sides], axis=1))
    return halo.lo + d[:, :LANES], halo.hi + d[:, LANES : 2 * LANES], edge + d[:, 2 * LANES :]


def tile_residual(geom, co, v, f, c, lo, hi, sides, m):
    m_rows, groups, ty = geom
    lane = zl()
    here = v[m]
    if lo is None:
        lo = hi = jnp.zeros((Z, LANES), F32)
    if m > 0:
        low_x = v[m - 1]
    else:
        low_x = lo if groups == 1 else jnp.where(lane < ty, lo, roll(v[m_rows - 1], ty))
    if m < m_rows - 1:
        high_x = v[m + 1]
    elif groups == 1:
        high_x = hi
    else:
        high_x = jnp.where(lane < (groups - 1) * ty, roll(v[0], -ty), roll(hi, (groups - 1) * ty))
    low_y, high_y = roll(here, 1), roll(here, -1)
    if sides is None:
        low_y = jnp.where(lane % ty == 0, 0.0, low_y)
        high_y = jnp.where(lane % ty == ty - 1, 0.0, high_y)
        return residual(co, f[m], c[m], here, low_x + high_x + low_y + high_y)
    for q in range(groups):
        row = q * m_rows + m
        low = roll(sides, q * ty - 2 * row - 1)
        high = low if whole_rows(geom) else roll(sides, q * ty + ty - 1 - 2 * row)
        low_y = jnp.where(lane == q * ty, low, low_y)
        high_y = jnp.where(lane == q * ty + ty - 1, high, high_y)
    return residual(co, f[m], c[m], here, low_x + high_x + low_y + high_y)


def relax_tile(geom, winv, co, v, f, c, edges, store):
    lo, hi, sides = edges
    for m in range(0, geom[0], 2):
        rows = [k for k in (m, m + 1) if k < geom[0]]
        r = [tile_residual(geom, co, v, f, c, lo, hi, sides, k) for k in rows]
        d = block_dot(winv, r[0] if len(r) == 1 else jnp.concatenate(r, axis=1))
        for i, k in enumerate(rows):
            store(k, v[k] + d[:, i * LANES : (i + 1) * LANES])


ALONE = (None, None, None)


def edge_terms(geom, winv, edges):
    ty = geom[2]
    lane = zl()
    d = block_dot(winv, jnp.concatenate(edges, axis=1) * 0.0625)
    low, high, sides = [d[:, k * LANES : (k + 1) * LANES] for k in range(3)]
    if ty < LANES:
        low = jnp.where(lane < ty, low, 0.0)
        high = jnp.where(lane < ty, high, 0.0)
    return low, high, sides


def with_terms(geom, x, terms, m):
    m_rows, groups, ty = geom
    low, high, sides = terms
    lane = zl()
    if m == 0:
        x = x + low
    if m == m_rows - 1:
        x = x + roll(high, (groups - 1) * ty)
    for q in range(groups):
        row = q * m_rows + m
        first = roll(sides, q * ty - 2 * row - 1)
        last = first if whole_rows(geom) else roll(sides, q * ty + ty - 1 - 2 * row)
        x = x + jnp.where(lane == q * ty, first, jnp.where(lane == q * ty + ty - 1, last, 0.0))
    return x


def add_edges(geom, winv, part, edges, store):
    terms = edge_terms(geom, winv, edges)
    for m in range(geom[0]):
        store(m, with_terms(geom, part[m], terms, m))


def start_tile(geom, winv, f, store):
    for m in range(0, geom[0], 2):
        rows = [k for k in (m, m + 1) if k < geom[0]]
        parts = [f[k] for k in rows]
        d = block_dot(winv, parts[0] if len(parts) == 1 else jnp.concatenate(parts, axis=1))
        for i, k in enumerate(rows):
            store(k, d[:, i * LANES : (i + 1) * LANES])


def restrict(fine, coarse, v, out, wanted=None):
    m_rows, _, ty = fine
    cm, cq, cty = coarse
    a, b = iota2(LANES, LANES)
    for mc in range(cm):
        acc = None
        for qc in range(cq):
            if wanted is not None and qc * cm + mc not in wanted:
                continue
            q, m = divmod(2 * (qc * cm + mc), m_rows)
            inside = (b >= qc * cty) & (b < (qc + 1) * cty) & (a // 2 == b - qc * cty + q * (ty // 2))
            term = lane_dot(v[m] + v[m + 1], jnp.where(inside, 0.25, 0.0))
            acc = term if acc is None else acc + term
        if acc is not None:
            out[mc] = acc


def prolong_add(fine, coarse, e, v, out, rows=None):
    m_rows, groups, ty = fine
    cm, _, cty = coarse
    a, b = iota2(LANES, LANES)
    for m in range(0, m_rows, 2) if rows is None else rows:
        acc = None
        for q in range(groups):
            qc, mc = divmod((q * m_rows + m) // 2, cm)
            inside = (b >= q * ty) & (b < (q + 1) * ty) & (a - qc * cty == (b - q * ty) // 2)
            term = lane_dot(e[mc], jnp.where(inside, 1.0, 0.0))
            acc = term if acc is None else acc + term
        out[m] = v[m] + acc
        out[m + 1] = v[m + 1] + acc


class Setter:
    def __init__(self, ref):
        self.ref = ref

    def __call__(self, m, value):
        self.ref[m] = value


def messages(geom, xlo, xhi, ydn, yun, winv):
    raw = [part_of(geom, xlo, 0), part_of(geom, xlo, 1), part_of(geom, xhi, 0), part_of(geom, xhi, 1), ydn[0:Z, :], yun[0:Z, :]]
    d = block_dot(winv, jnp.concatenate(raw, axis=1))
    return Halo(*[d[:, k * LANES : (k + 1) * LANES] for k in range(6)])


def third_of(geom, ref):
    if not halved(geom, 3):
        return part_of(geom, ref, 2)
    both = ref[Z : Z + SPLIT, :]
    return jnp.concatenate([both, roll(both[0 : Z - SPLIT, :], 64)], axis=0)


def own_data(geom, xlo, xhi, ydn, yun):
    dn, un = ydn[0:Z, :], yun[0:Z, :]
    f_sides = jnp.where(odd_lanes(), dn, un)
    c_sides = roll(f_sides, -64)
    return (
        part_of(geom, xlo, 0),
        third_of(geom, xlo),
        part_of(geom, xhi, 0),
        third_of(geom, xhi),
        f_sides,
        c_sides,
    )


def flags_of(geom, own, xlo, xhi, ydn, yun):
    return Flags(own[...], tail_of(geom, xlo, 3), tail_of(geom, xhi, 3), ydn[Z : Z + 8, :], yun[Z : Z + 8, :])


def load_top(src, dst):
    for x in range(24):
        dst[x, 0:NZ, :] = src[pl.ds(x, NZ, stride=24), :]
        dst[x, NZ:Z, :] = jnp.zeros((Z - NZ, LANES), F32)


STRIPS = {2: (6, 32, 256), 3: (3, 16, 128)}


def in_tile(strip):
    _, ty, width = strip
    return lane_ids((Z, width)) % ty


def group_dot(x, mat):
    parts = [lane_dot(x[:, k : k + LANES], mat) for k in range(0, x.shape[1], LANES)]
    return parts[0] if len(parts) == 1 else jnp.concatenate(parts, axis=1)


def turn_groups(strip, x, flags, k, count):
    _, ty, width = strip
    a, b = iota2(LANES, LANES)
    mat = jnp.where((a // ty == b // ty) & (b % ty < count) & (a % ty == count - 1 - b % ty), 1.0, 0.0)
    flag = jnp.broadcast_to(flags[k : k + 1, :], (Z, width))
    return jnp.where(flag > 0.5, group_dot(x, mat), x)


def strip_ends(strip, v, flags):
    m_rows, ty, _ = strip
    low = turn_groups(strip, roll(v[m_rows - 1], ty), flags, 0, ty)
    high = turn_groups(strip, roll(v[0], -ty), flags, 1, ty)
    return low, high


def strip_column(strip, v, y, offset, out):
    lt = in_tile(strip)
    for m in range(strip[0]):
        out = jnp.where(lt == offset + m, roll(v[m], offset + m - y), out)
    return out


def strip_message(strip, v, c, ends, up, down):
    m_rows, ty, width = strip
    lt = in_tile(strip)
    for ref, edge, second in ((up, ty - 1, ty - 2), (down, 0, 1)):
        out = strip_column(strip, v, edge, 0, jnp.zeros((Z, width), F32))
        out = strip_column(strip, v, second, m_rows, out)
        if c is not None:
            out = strip_column(strip, c, edge, 2 * m_rows, out)
        for k, end in enumerate(ends):
            out = jnp.where(lt == 3 * m_rows + k, roll(end, 3 * m_rows + k - edge), out)
        ref[0:Z, :] = out


def strip_edges(strip, winv, co, sides):
    m_rows, _, width = strip
    lt = in_tile(strip)
    r = []
    for x, raw, flags, k, mine in sides:
        mine = turn_groups(strip, mine, flags, k, m_rows)
        low = jnp.where(lt == 0, roll(x, -3 * m_rows), roll(x, 1))
        high = jnp.where(lt == m_rows - 1, roll(x, -2 * m_rows - 2), roll(x, -1))
        r.append(residual(co, raw, roll(raw, -2 * m_rows), x, roll(x, -m_rows) + mine + low + high))
    d = block_dot(winv, jnp.concatenate(r, axis=1))
    return [side[0] + d[:, k * width : (k + 1) * width] for k, side in enumerate(sides)]


def strip_frame(strip, flags, low, high):
    return turn_groups(strip, low, flags, 2, strip[0]), turn_groups(strip, high, flags, 3, strip[0])


def strip_residual(strip, co, v, f, c, ends, sides, m):
    m_rows, ty, _ = strip
    lt = in_tile(strip)
    low_x = v[m - 1] if m > 0 else ends[0]
    high_x = v[m + 1] if m < m_rows - 1 else ends[1]
    low = 0.0 if sides is None else roll(sides[0], -m)
    high = 0.0 if sides is None else roll(sides[1], ty - 1 - m)
    low_y = jnp.where(lt == 0, low, roll(v[m], 1))
    high_y = jnp.where(lt == ty - 1, high, roll(v[m], -1))
    return residual(co, f[m], c[m], v[m], low_x + high_x + low_y + high_y)


def strip_relax(strip, winv, co, v, f, c, flags, sides, store):
    ends = strip_ends(strip, v, flags)
    for m in range(strip[0]):
        r = strip_residual(strip, co, v, f, c, ends, sides, m)
        store(m, v[m] + block_dot(winv, r))


def strip_add_sides(strip, winv, part, sides, store):
    m_rows, ty, width = strip
    lt = in_tile(strip)
    d = block_dot(winv, jnp.concatenate(sides, axis=1) * 0.0625)
    for m in range(m_rows):
        low, high = roll(d[:, :width], -m), roll(d[:, width:], ty - 1 - m)
        store(m, part[m] + jnp.where(lt == 0, low, jnp.where(lt == ty - 1, high, 0.0)))


def strip_side_terms(strip, winv, co, flags, c_columns, sides, sides_next):
    m_rows, ty, width = strip
    lt = in_tile(strip)
    d = block_dot(winv, jnp.concatenate(sides, axis=1) * 0.0625)
    first, last = d[:, :width], d[:, width:]
    turned = [jnp.broadcast_to(flags[k : k + 1, :], (Z, width)) > 0.5 for k in range(2)]
    step = ty - m_rows + 1
    r = []
    for mine, other, c, beyond in ((first, last, c_columns[0], sides_next[0]), (last, first, c_columns[1], sides_next[1])):
        low = jnp.where(turned[0], roll(other, step), roll(mine, step))
        high = jnp.where(turned[1], roll(other, -step), roll(mine, -step))
        low = jnp.where(lt == 0, low, roll(mine, 1))
        high = jnp.where(lt == m_rows - 1, high, roll(mine, -1))
        r.append(residual(co, beyond * 0.0625, c, mine, low + high))
    return first, last, r


def strip_restrict(v, out):
    a, b = iota2(LANES, LANES)
    for m in range(3):
        both = v[2 * m] + v[2 * m + 1]
        out[m] = lane_dot(both[:, :LANES], jnp.where(a // 2 == b, 0.25, 0.0)) + lane_dot(
            both[:, LANES:], jnp.where(a // 2 == b - 64, 0.25, 0.0)
        )


def open_strip_kernel(chunks, f, c, flags, up, down):
    strip = STRIPS[2]
    group = lane_ids((Z, LANES)) // 32
    for m in range(6):
        for ref, k in ((f, m), (c, 6 + m)):
            part = (k // 4) * Z
            halves = []
            for h in range(2):
                acc = None
                for g in range(4):
                    x = chunks[4 * h + g, part : part + Z, :]
                    acc = x if acc is None else jnp.where(group == (g + k) % 4, x, acc)
                halves.append(roll(acc, -(k % 4) * 32))
            ref[m] = jnp.concatenate(halves, axis=1)
    group = lane_ids((8, LANES)) // 32
    for h in range(2):
        acc = None
        for g in range(4):
            x = chunks[4 * h + g, 3 * Z : 3 * Z + 8, :]
            acc = x if acc is None else jnp.where(group == g, x, acc)
        flags[:, h * LANES : (h + 1) * LANES] = acc
    strip_message(strip, f, c, strip_ends(strip, f, flags), up, down)
    up[Z : Z + 8, :] = flags[...]
    down[Z : Z + 8, :] = flags[...]


def strip_sides(values, raws, dn, un, first, last):
    return (
        (values[0], raws[0], dn[Z : Z + 8, :], 3, first[...]),
        (values[1], raws[1], un[Z : Z + 8, :], 2, last[...]),
    )


def column_restrict(strip, x):
    a, b = iota2(LANES, LANES)
    out = None
    for h in range(2):
        inside = (b // 16 == 4 * h + a // 32) & ((a % 32) // 2 == b % 16) & (a % 32 < strip[0])
        term = lane_dot(x[:, h * LANES : (h + 1) * LANES], jnp.where(inside, 0.25, 0.0))
        out = term if out is None else out + term
    return out


def pre_strip_kernel(
    w, vz, flags, dn, un, first_column, last_column, c_low, c_high, f_part, fl_next, base_up, base_down, terms, f_next, up, down
):
    strip, small = STRIPS[2], STRIPS[3]
    winv = w[...].astype(BF16)
    co = Coef(vz, strip[2])
    raws = [dn[0:Z, :], un[0:Z, :]]
    values = block_dot(winv, jnp.concatenate(raws, axis=1))
    values = [values[:, : strip[2]], values[:, strip[2] :]]
    edges = strip_edges(strip, winv, co, strip_sides(values, raws, dn, un, first_column, last_column))
    first, last, r = strip_side_terms(
        strip, winv, co, flags, (c_low[...], c_high[...]), strip_frame(strip, flags, *values), strip_frame(strip, flags, *edges)
    )
    terms[0] = first
    terms[1] = last
    low = column_restrict(strip, r[0] + first * 0.0625)
    high = column_restrict(strip, r[1] + last * 0.0625)
    m_rows, ty, width = small
    lt = in_tile(small)
    for m in range(m_rows):
        x = jnp.where(lt == 0, roll(low, -m), 0.0)
        f_next[m] = f_part[m] + jnp.where(lt == ty - 1, roll(high, ty - 1 - m), x)
    turned = [jnp.broadcast_to(fl_next[k : k + 1, :], (Z, width)) > 0.5 for k in range(2)]
    for ref, base, mine, other in ((up, base_up, high, low), (down, base_down, low, high)):
        before, after = 3 * m_rows + ty - m_rows + 1, 3 * m_rows + 1 - ty
        end_low = jnp.where(turned[0], roll(other, before), roll(mine, before))
        end_high = jnp.where(turned[1], roll(other, after), roll(mine, after))
        add = jnp.where(lt < m_rows, mine, 0.0)
        add = jnp.where(lt == 3 * m_rows, end_low, add)
        add = jnp.where(lt == 3 * m_rows + 1, end_high, add)
        ref[0:Z, :] = base[...] + add
        ref[Z : Z + 8, :] = fl_next[...]


def next_coef_kernel(c, flags, c_next, fl_next, low, high, low_next, high_next):
    strip_restrict(c, c_next)
    a, b = iota2(LANES, LANES)
    fl_next[...] = lane_dot(flags[:, :LANES], jnp.where((b < 64) & (a == (b // 16) * 32), 1.0, 0.0)) + lane_dot(
        flags[:, LANES:], jnp.where((b >= 64) & (a == (b // 16 - 4) * 32), 1.0, 0.0)
    )
    for strip, ref, first, last in ((STRIPS[2], c, low, high), (STRIPS[3], c_next, low_next, high_next)):
        zero = jnp.zeros((Z, strip[2]), F32)
        first[...] = strip_column(strip, ref, 0, 0, zero)
        last[...] = strip_column(strip, ref, strip[1] - 1, 0, zero)


def alone2_kernel(f, c, w, vz, flags, c_next, fl_next, part, low, high, f_part, up, down, v, res):
    strip, small = STRIPS[2], STRIPS[3]
    winv = w[...].astype(BF16)
    co = Coef(vz, strip[2])
    for m in range(6):
        v[m] = block_dot(winv, f[m])
    zero = jnp.zeros((Z, strip[2]), F32)
    low[...] = strip_column(strip, v, 0, 0, zero)
    high[...] = strip_column(strip, v, strip[1] - 1, 0, zero)
    strip_relax(strip, winv, co, v, f, c, flags, None, Setter(part))
    ends = strip_ends(strip, part, flags)
    for m in range(6):
        res[m] = strip_residual(strip, co, part, f, c, ends, None, m)
    strip_restrict(res, f_part)
    strip_message(small, f_part, c_next, strip_ends(small, f_part, fl_next), up, down)


def bottom_strip_kernel(
    w, vz, flags, dn, un, first_column, last_column, c_low, c_high, part_low, part_high, terms, up, down
):
    strip = STRIPS[3]
    width = strip[2]
    winv = w[...].astype(BF16)
    co = Coef(vz)
    raws = [dn[0:Z, :], un[0:Z, :]]
    values = block_dot(winv, jnp.concatenate(raws, axis=1))
    values = [values[:, :width], values[:, width:]]
    edges = strip_edges(strip, winv, co, strip_sides(values, raws, dn, un, first_column, last_column))
    first, last, r = strip_side_terms(
        strip, winv, co, flags, (c_low[...], c_high[...]), strip_frame(strip, flags, *values), strip_frame(strip, flags, *edges)
    )
    d = block_dot(winv, jnp.concatenate([r[0], first * 0.0625, last * 0.0625, r[1]], axis=1))
    d = [d[:, k * width : (k + 1) * width] for k in range(4)]
    d[0] = first + d[0]
    d[3] = last + d[3]
    for k in range(4):
        terms[k] = d[k]
    up[...] = part_high[...] + d[3]
    down[...] = part_low[...] + d[0]


def with_columns(strip, x, terms, m):
    ty = strip[1]
    lt = in_tile(strip)
    for k, y in enumerate((0, 1, ty - 2, ty - 1)):
        x = x + jnp.where(lt == y, roll(terms[k], y - m), 0.0)
    return x


def last_strip_kernel(w, flags, dn, un, part, base_up, base_down, _lo, _hi, e, up, down, small_up, small_down):
    strip, fine = STRIPS[3], STRIPS[2]
    winv = w[...].astype(BF16)
    strip_add_sides(strip, winv, part, strip_frame(strip, flags, dn[...], un[...]), Setter(e))
    strip_message(strip, e, None, strip_ends(strip, e, flags), small_up, small_down)
    a, b = iota2(LANES, LANES)
    for h in range(2):
        lt = b % 32
        source = jnp.where(lt < 12, (lt % 6) // 2, jnp.where((lt == 18) | (lt == 19), lt - 9, 15))
        spread = jnp.where((lt != 15) & (a == 64 * h + (b // 32) * 16 + source) & (source < 15), 1.0, 0.0)
        half = slice(h * LANES, (h + 1) * LANES)
        up[:, half] = base_up[:, half] + lane_dot(small_up[...], spread)
        down[:, half] = base_down[:, half] + lane_dot(small_down[...], spread)


def base_message_kernel(part, flags, terms, tile_v, xlo, xhi, own, v, up, down, yup, ydown):
    strip = STRIPS[2]
    lt = in_tile(strip)
    for m in range(6):
        x = jnp.where(lt == 0, roll(terms[0], -m), 0.0)
        v[m] = part[m] + jnp.where(lt == strip[1] - 1, roll(terms[1], strip[1] - 1 - m), x)
    strip_message(strip, v, None, strip_ends(strip, v, flags), up, down)
    put_y(GEOM[1], tile_v, None, yup, ydown)
    add_up, add_down = relayed(tail_of(GEOM[1], xlo, 2), tail_of(GEOM[1], xhi, 2), own)
    yup[...] = yup[...] + add_up
    ydown[...] = ydown[...] + add_down


def again2_kernel(f, c, w, vz, flags, v, e, low, high, part_low, part_high, twice, g, part):
    strip = STRIPS[2]
    a, b = iota2(LANES, LANES)
    for m in range(3):
        add = jnp.concatenate([lane_dot(e[m], jnp.where(a == 64 * h + b // 2, 1.0, 0.0)) for h in range(2)], axis=1)
        g[2 * m] = v[2 * m] + add
        g[2 * m + 1] = v[2 * m + 1] + add
    zero = jnp.zeros((Z, strip[2]), F32)
    low[...] = strip_column(strip, g, 0, 0, zero)
    high[...] = strip_column(strip, g, strip[1] - 1, 0, zero)
    winv = w[...].astype(BF16)
    co = Coef(vz, strip[2])
    strip_relax(strip, winv, co, g, f, c, flags, None, Setter(part))
    strip_relax(strip, winv, co, part, f, c, flags, None, Setter(twice))
    part_low[...] = strip_column(strip, twice, 0, 0, zero)
    part_high[...] = strip_column(strip, twice, strip[1] - 1, 0, zero)


def alone3_kernel(f, c, w, vz, flags, low, high, part_low, part_high, twice, v, part):
    strip = STRIPS[3]
    winv = w[...].astype(BF16)
    co = Coef(vz)
    for m in range(3):
        v[m] = block_dot(winv, f[m])
    strip_relax(strip, winv, co, v, f, c, flags, None, Setter(part))
    strip_relax(strip, winv, co, part, f, c, flags, None, Setter(twice))
    zero = jnp.zeros((Z, LANES), F32)
    for ref, first, last in ((v, low, high), (twice, part_low, part_high)):
        first[...] = strip_column(strip, ref, 0, 0, zero)
        last[...] = strip_column(strip, ref, strip[1] - 1, 0, zero)


def again3_kernel(f, c, w, vz, flags, twice, terms, part, v):
    strip = STRIPS[3]
    for m in range(3):
        v[m] = with_columns(strip, twice[m], terms, m)
    strip_relax(strip, w[...].astype(BF16), Coef(vz), v, f, c, flags, None, Setter(part))


def tile_lanes(x, step):
    t = lax.rem(lax.axis_index("gx") + (step + 8), 8)
    half = jnp.where(t < 4, x[:, :LANES], x[:, LANES:])
    return pltpu.roll(half, lax.rem(8 - t, 4) * 32, axis=1)


def post_strip_kernel(
    w, vz, flags, dn, un, first_column, last_column, c_low, c_high, part_low, part_high, gdn, gun, own, yup, ydown, terms, up, down
):
    strip = STRIPS[2]
    width = strip[2]
    winv = w[...].astype(BF16)
    co = Coef(vz, width)
    raws = [dn[0:Z, :], un[0:Z, :]]
    values = [gdn[...], gun[...]]
    edges = strip_edges(strip, winv, co, strip_sides(values, raws, dn, un, first_column, last_column))
    first, last, r = strip_side_terms(
        strip, winv, co, flags, (c_low[...], c_high[...]), strip_frame(strip, flags, *values), strip_frame(strip, flags, *edges)
    )
    d = block_dot(winv, jnp.concatenate([r[0], first * 0.0625, last * 0.0625, r[1]], axis=1))
    d = [d[:, k * width : (k + 1) * width] for k in range(4)]
    d[0] = first + d[0]
    d[3] = last + d[3]
    for k in range(4):
        terms[k] = d[k]
    low, high = part_low[...] + d[0], part_high[...] + d[3]
    lane = zl()

    def tile_corners(step):
        first_lanes, last_lanes = tile_lanes(low, step), tile_lanes(high, step)
        return [roll(x, 112 - place) for x, place in ((first_lanes, 0), (last_lanes, 0), (first_lanes, 5), (last_lanes, 5))]

    f0, f1 = flag_row(own, 0) > 0.5, flag_row(own, 1) > 0.5
    a, b = iota2(LANES, LANES)
    spread = jnp.where((b < 24) & (a == b // 4), 1.0, 0.0)
    add_up = lane_dot(tile_lanes(high, 0), spread)
    add_down = lane_dot(tile_lanes(low, 0), spread)
    to_up, to_down = relay_order(tile_corners(-1), tile_corners(1), f0, f1)
    for k in range(6):
        add_up = jnp.where(lane == 112 + k, roll(to_up[k], k), add_up)
        add_down = jnp.where(lane == 112 + k, roll(to_down[k], k), add_down)
    up[...] = yup[...] + add_up
    down[...] = ydown[...] + add_down


def again1_kernel(f, c, w, vz, v, twice, terms, xlo, xhi, g, part, columns, lo_out, hi_out, tile):
    fine, geom = GEOM[1], GEOM[2]
    rows = []
    for m in range(6):
        rows.append(with_columns(STRIPS[2], twice[m], terms, m))
        tile[m] = tile_lanes(rows[m], 0)
    prolong_add(fine, geom, tile, v, g)
    a, b = iota2(LANES, LANES)
    spread = jnp.where((b < 64) & (a == b // 2), 1.0, 0.0)
    for ref, out, row in ((xlo, lo_out, tile_lanes(rows[5], -1)), (xhi, hi_out, tile_lanes(rows[0], 1))):
        add = lane_dot(row, spread)
        out[...] = pack(fine, [part_of(fine, ref, 0) + add, part_of(fine, ref, 1) + add])[0]
    columns[...] = own_columns(fine, g)
    relax_tile(fine, w[...].astype(BF16), Coef(vz), g, f, c, ALONE, Setter(part))


def swap_pairs(axis, which, nearest=False):
    sizes = lax.axis_size("gx"), lax.axis_size("gy")
    out = []
    for i in range(sizes[0]):
        for j in range(sizes[1]):
            at = [i, j]
            dim = 0 if axis == "gx" else 1
            n = sizes[dim]
            at[dim] = (at[dim] ^ 1) if which == 0 else (at[dim] + (1 if at[dim] % 2 else n - 1)) % n
            if nearest and 2 * j // n != 2 * at[1] // n:
                at[0] = i ^ 1
            out.append((i * sizes[1] + j, at[0] * sizes[1] + at[1]))
    return out


def swap(first, second, axis, nearest=False):
    both = ("gx", "gy")
    return (
        lax.ppermute(first, both, swap_pairs(axis, 0, nearest)),
        lax.ppermute(second, both, swap_pairs(axis, 1, nearest)),
    )


ANY = pl.BlockSpec(memory_space=pl.ANY)
LIMIT = 14 * 1024 * 1024
VMEM = pl.BlockSpec(memory_space=pltpu.VMEM)


class Either:
    def __init__(self, first, a, b):
        self.first, self.a, self.b = first, a, b

    def __getitem__(self, index):
        return jnp.where(self.first, self.a[index], self.b[index])


def is_even(axis):
    return lax.rem(lax.axis_index(axis), 2) == 0


def by_swaps(kernel, n_in, n_out, got, send):
    def wrapped(*refs):
        refs = list(refs)
        for place, axis in got:
            a, b = refs[place], refs[place + 1]
            refs[place], refs[place + 1] = Either(is_even(axis), b, a), Either(is_even(axis), a, b)
        extra = refs[len(refs) - 2 * len(send) :]
        refs = refs[: len(refs) - 2 * len(send)]
        outs = []
        for k, (place, axis) in enumerate(send):
            place += n_in
            outs.append((refs[place], refs[place + 1], extra[2 * k], extra[2 * k + 1], axis))
            refs[place], refs[place + 1] = extra[2 * k], extra[2 * k + 1]
        kernel(*refs)
        for first, second, up, down, axis in outs:
            even = is_even(axis)
            up, down = up[...], down[...]
            first[...] = jnp.where(even, up, down)
            second[...] = jnp.where(even, down, up)

    return wrapped


def call(kernel, outs, args, scratch=(), name=None, after=0, got=(), send=()):
    scratch = [pltpu.VMEM(s, F32) for s in scratch]
    scratch += [pltpu.VMEM(outs[place], F32) for place, _ in send for _ in range(2)]
    return pl.pallas_call(
        by_swaps(kernel, len(args), len(outs), got, send),
        out_shape=[jax.ShapeDtypeStruct(s, F32) for s in outs],
        in_specs=[VMEM] * (len(args) - after) + [ANY] * after,
        out_specs=[VMEM] * len(outs),
        scratch_shapes=scratch,
        compiler_params=pltpu.CompilerParams(vmem_limit_bytes=LIMIT),
        name=name,
    )(*args)


def tile_shape(level):
    return (GEOM[level][0], Z, LANES)


def x_shape(level, count):
    return (message_rows(GEOM[level], count) + 8, LANES)


Y_FULL = (Z + 8, LANES)


def open_kernel(f_in, c_in, vert_in, flip_in, up, down, own, vz, f_low, f_high, c_low, c_high, vert, flip, sems):
    pairs = (
        (vert_in, vert),
        (flip_in, flip),
        (f_in.at[:, 0:2, :], f_low),
        (f_in.at[:, 22:24, :], f_high),
        (c_in.at[:, 0:1, :], c_low),
        (c_in.at[:, 23:24, :], c_high),
    )
    copies = [pltpu.make_async_copy(src, dst, sems.at[k]) for k, (src, dst) in enumerate(pairs)]
    for copy in copies:
        copy.start()
    for copy in copies[:2]:
        copy.wait()
    a, b = iota2(8, 4)
    flags = jnp.broadcast_to(flip[...].astype(F32), (8, 4))
    flags = jnp.broadcast_to(jnp.sum(jnp.where(a == b, flags, 0.0), axis=1, keepdims=True), (8, LANES))
    own[...] = flags
    a, b = iota2(Z, NZ + 1)
    coef = jnp.broadcast_to(vert[...], (Z, NZ + 1))
    high = jnp.sum(jnp.where((b == a + 1) & (a < NZ), coef, 0.0), axis=1, keepdims=True)
    low = jnp.sum(jnp.where((b == a) & (a < NZ), coef, 0.0), axis=1, keepdims=True)
    columns = [jnp.broadcast_to(x * 0.0625, (Z, LANES)) for x in (4.0 + high + low, high, low)]
    for k in range(3):
        vz[k] = columns[k]
    up[...] = jnp.zeros(up.shape, F32)
    down[...] = jnp.zeros(down.shape, F32)
    for copy in copies[2:]:
        copy.wait()
    up[0:NZ, :] = f_high[:, 1, :]
    up[Z : Z + NZ, :] = f_high[:, 0, :]
    up[2 * Z : 2 * Z + NZ, :] = c_high[:, 0, :]
    down[0:NZ, :] = f_low[:, 0, :]
    down[Z : Z + NZ, :] = f_low[:, 1, :]
    down[2 * Z : 2 * Z + NZ, :] = c_low[:, 0, :]
    first, last = down[0:Z, :], up[0:Z, :]
    tail = flags + corner_rows([col(first, 0), col(first, LANES - 1), col(last, 0), col(last, LANES - 1)])
    up[3 * Z : 3 * Z + 8, :] = tail
    down[3 * Z : 3 * Z + 8, :] = tail


def block_matrix(inv):
    width = 3 * Z
    a, b = iota2(BLK, width)
    b = b % Z
    spread = jnp.where((b % BLK == a) & (b < NZ), 1.0, 0.0).astype(BF16)
    whole = jnp.zeros((NZ, width), F32)
    left = inv
    for _ in range(3):
        part = left.astype(BF16)
        whole = whole + jnp.dot(part, spread, preferred_element_type=F32)
        left = left - part.astype(F32)
    a, b = iota2(NZ, width)
    whole = jnp.where(a // BLK == (b % Z) // BLK, whole, 0.0)
    high = whole.astype(BF16).astype(F32)
    return jnp.where((b >= Z) & (b < 2 * Z), whole - high, high)


def side_kernel(f_in, c_in, inv, vz, own, f, c, w0, w1, w2, w3, one, part, columns, c_next, c_tile, yup, ydown):
    load_top(f_in, f)
    load_top(c_in, c)
    put_y(GEOM[0], f, c, yup, ydown)
    yup[Z : Z + 8, :] = own[...]
    ydown[Z : Z + 8, :] = own[...]
    for level, w in enumerate((w0, w1, w2, w3)):
        w[0:NZ, :] = block_matrix(inv[level])
        w[NZ:Z, :] = jnp.zeros((Z - NZ, 3 * Z), F32)
    winv = w0[...].astype(BF16)
    start_tile(GEOM[0], winv, f, Setter(one))
    relax_tile(GEOM[0], winv, Coef(vz), one, f, c, ALONE, Setter(part))
    columns[...] = own_columns(GEOM[0], one)
    restrict(GEOM[0], GEOM[1], c, c_next)
    restrict(GEOM[1], GEOM[2], c_next, c_tile)


def merge_kernel(level, count):
    geom = GEOM[level]

    def kernel(xlo, xhi, flags, yup, ydown, up, down):
        add_up, add_down = relayed(tail_of(geom, xlo, count), tail_of(geom, xhi, count), flags)
        up[...] = yup[...]
        down[...] = ydown[...]
        up[0:Z, :] = yup[0:Z, :] + add_up
        down[0:Z, :] = ydown[0:Z, :] + add_down

    return kernel


def pre_edges(geom, f, c, w, vz, own, xlo, xhi, ydn, yun, one, columns):
    winv = w[...].astype(BF16)
    fl = flags_of(geom, own, xlo, xhi, ydn, yun)
    halo = messages(geom, xlo, xhi, ydn, yun, winv)
    relaxed = relax_edges(geom, winv, Coef(vz), one, columns[...], halo, fl, *own_data(geom, xlo, xhi, ydn, yun))
    terms = edge_terms(geom, winv, frame(geom, fl, halo.lo, halo.hi, halo.sides()))
    return terms, frame(geom, fl, *relaxed)


def pre0_kernel(f, c, w, vz, own, xlo, xhi, ydn, yun, one, part, columns, c_next, up, down, terms_out, edges_out, v, res, f_next):
    geom, coarse = GEOM[0], GEOM[1]
    terms, edges = pre_edges(geom, f, c, w, vz, own, xlo, xhi, ydn, yun, one, columns)
    for k in range(3):
        terms_out[k] = terms[k]
        edges_out[k] = edges[k]
    co = Coef(vz)
    for m in (*range(5), *range(19, 24)):
        v[m] = with_terms(geom, part[m], terms, m)
    for m in (*range(4), *range(20, 24)):
        res[m] = tile_residual(geom, co, v, f, c, *edges, m)
    restrict(geom, coarse, res, f_next, (0, 1, 10, 11))
    put_x(coarse, f_next, c_next, up, down, own[...])


def mid1_kernel(f, c, part, terms_in, edges_in, vz, w, c_next, own, v, f_next, one, part_next, columns, yup, ydown, res):
    geom, coarse = GEOM[0], GEOM[1]
    co = Coef(vz)
    terms = [terms_in[k] for k in range(3)]
    edges = [edges_in[k] for k in range(3)]
    for m in range(24):
        v[m] = with_terms(geom, part[m], terms, m)
    for m in range(24):
        res[m] = tile_residual(geom, co, v, f, c, *edges, m)
    restrict(geom, coarse, res, f_next)
    put_y(coarse, f_next, c_next, yup, ydown)
    yup[Z : Z + 8, :] = own[...]
    ydown[Z : Z + 8, :] = own[...]
    winv = w[...].astype(BF16)
    start_tile(coarse, winv, f_next, Setter(one))
    relax_tile(coarse, winv, co, one, f_next, c_next, ALONE, Setter(part_next))
    columns[...] = own_columns(coarse, one)


def pre1_kernel(f, c, w, vz, own, xlo, xhi, ydn, yun, one, part, columns, c_tile, v_out, up, down, chunks, res, f_next):
    geom = GEOM[1]
    terms, edges = pre_edges(geom, f, c, w, vz, own, xlo, xhi, ydn, yun, one, columns)
    for m in range(6):
        v_out[m] = with_terms(geom, part[m], terms, m)
    co = Coef(vz)
    for m in range(6):
        res[m] = tile_residual(geom, co, v_out, f, c, *edges, m)
    restrict(geom, GEOM[2], res, f_next)
    put_x(geom, v_out, None, up, down)
    whole = pack(GEOM[2], [f_next[m] for m in range(6)] + [c_tile[m] for m in range(6)])
    turn = lax.rem(lax.axis_index("gx"), 4) * 32
    whole = [pltpu.roll(x, turn, axis=1) for x in whole]
    for t in range(8):
        for k, x in enumerate(whole):
            chunks[t, k * Z : (k + 1) * Z, :] = x
        chunks[t, 3 * Z : 3 * Z + 8, :] = own[...]


def again0_kernel(f, c, w, vz, e, v, g, part, columns, yup, ydown):
    prolong_add(GEOM[0], GEOM[1], e, v, g)
    put_y(GEOM[0], g, None, yup, ydown)
    columns[...] = own_columns(GEOM[0], g)
    relax_tile(GEOM[0], w[...].astype(BF16), Coef(vz), g, f, c, ALONE, Setter(part))


def twice0_kernel(f, c, w, vz, part, _after, twice, c_columns):
    c_columns[...] = own_columns(GEOM[0], c)
    relax_tile(GEOM[0], w[...].astype(BF16), Coef(vz), part, f, c, ALONE, Setter(twice))


def post_edges(geom, f, c, w, vz, own, xlo, xhi, ydn, yun, g, columns, glo, ghi, gdn, gun):
    fl = flags_of(geom, own, xlo, xhi, ydn, yun)
    halo = Halo(
        part_of(geom, glo, 0), part_of(geom, glo, 1), part_of(geom, ghi, 0), part_of(geom, ghi, 1), gdn[...], gun[...]
    )
    winv = w[...].astype(BF16)
    relaxed = relax_edges(geom, winv, Coef(vz), g, columns[...], halo, fl, *own_data(geom, xlo, xhi, ydn, yun))
    return frame(geom, fl, halo.lo, halo.hi, halo.sides()), frame(geom, fl, *relaxed)


def post0_kernel(f, c, w, vz, own, xlo, xhi, ydn, yun, g, columns, c_columns, twice, glo, ghi, gdn, gun, out):
    geom = GEOM[0]
    rows = geom[0]
    winv = w[...].astype(BF16)
    co = Coef(vz)
    lane = zl()
    edges, edges_next = post_edges(geom, f, c, w, vz, own, xlo, xhi, ydn, yun, g, columns, glo, ghi, gdn, gun)
    low, high, sides = edge_terms(geom, winv, edges)

    def row_residual(v, c_row, beyond):
        beside = jnp.where(lane == 0, 0.0, roll(v, 1)) + jnp.where(lane == LANES - 1, 0.0, roll(v, -1))
        return residual(co, beyond * 0.0625, c_row, v, beside)

    beside = jnp.where(lane < 2, 0.0, roll(sides, 2)) + jnp.where(lane >= 2 * rows - 2, 0.0, roll(sides, -2))
    r = [
        row_residual(low, c[0], edges_next[0]),
        low * 0.0625,
        high * 0.0625,
        row_residual(high, c[rows - 1], edges_next[1]),
        residual(co, edges_next[2] * 0.0625, c_columns[...], sides, beside),
        sides * 0.0625,
    ]
    d = block_dot(winv, jnp.concatenate(r, axis=1))
    d = [d[:, k * LANES : (k + 1) * LANES] for k in range(6)]
    a, b = iota2(LANES, LANES)
    outer = jnp.where((b % 4 == 1) | (b % 4 == 2), 1.0, 0.0) * jnp.where(a == 2 * (b // 4) + b % 4 - 1, 1.0, 0.0)
    inner = jnp.where((b % 4 == 0) | (b % 4 == 3), 1.0, 0.0) * jnp.where(a == 2 * (b // 4) + b % 4 // 3, 1.0, 0.0)
    four = lane_dot(sides + d[4], outer) + lane_dot(d[5], inner)
    inside = (lane < 2) | (lane >= LANES - 2)
    row_terms = {0: low + d[0], 1: d[1], rows - 2: d[2], rows - 1: high + d[3]}
    for m in range(rows):
        x = twice[m] + jnp.where(inside, roll(four, -4 * m - 2), 0.0)
        if m in row_terms:
            x = x + row_terms[m]
        out[pl.ds(m, NZ, stride=24), :] = x[0:NZ, :]


def post1_kernel(
    f, c, w, vz, own, xlo, xhi, ydn, yun, g, part, columns, glo, ghi, gdn, gun, fine_v, e, up, down, one, fine_g
):
    geom = GEOM[1]
    edges, edges_next = post_edges(geom, f, c, w, vz, own, xlo, xhi, ydn, yun, g, columns, glo, ghi, gdn, gun)
    winv = w[...].astype(BF16)
    add_edges(geom, winv, part, edges, Setter(one))
    relax_tile(geom, winv, Coef(vz), one, f, c, edges_next, Setter(e))
    prolong_add(GEOM[0], GEOM[1], e, fine_v, fine_g, (0, 22))
    put_x(GEOM[0], fine_g, None, up, down)


def on_device(right_side, helm_coef, vert_coef, block_inverse, edge_flip):
    inv = block_inverse.reshape(4, NZ, BLK)
    f_in = right_side.reshape(NZ * 24, LANES)
    c_in = helm_coef.reshape(NZ * 24, LANES)
    vert = vert_coef.reshape(1, NZ + 1)
    flip = edge_flip.reshape(1, 4)

    ys = (Z, LANES)
    t0, t1, t2 = tile_shape(0), tile_shape(1), tile_shape(2)
    xs = x_shape(0, 3)
    up, down, own, vz = pl.pallas_call(
        by_swaps(open_kernel, 4, 4, (), ((0, "gx"),)),
        out_shape=[jax.ShapeDtypeStruct(x, F32) for x in (xs, xs, (8, LANES), (3, Z, LANES))],
        in_specs=[ANY] * 4,
        out_specs=[VMEM] * 4,
        scratch_shapes=[pltpu.VMEM((NZ, 2, LANES), F32)] * 2
        + [pltpu.VMEM((NZ, 1, LANES), F32)] * 2
        + [pltpu.VMEM((1, NZ + 1), F32), pltpu.VMEM((1, 4), jnp.int32), pltpu.SemaphoreType.DMA((6,))]
        + [pltpu.VMEM(xs, F32)] * 2,
        compiler_params=pltpu.CompilerParams(vmem_limit_bytes=58 * 1024 * 1024),
        name="open",
    )(right_side, helm_coef, vert, flip)
    xlo, xhi = swap(up, down, "gx")
    ws = (Z, 3 * Z)
    f, c, *w, one, part, columns, c1, c_tile, yup, ydown = call(
        side_kernel,
        [t0, t0] + [ws] * 4 + [t0, t0, ys, t1, t2, Y_FULL, Y_FULL],
        [f_in, c_in, inv, vz, own],
        name="side",
    )

    def to_sides(level, count, xlo, xhi, yup, ydown):
        shape = yup.shape
        yup, ydown = call(merge_kernel(level, count), [shape, shape], [xlo, xhi, own, yup, ydown], name=f"merge{level}", got=((0, "gx"),), send=((0, "gy"),))
        return swap(yup, ydown, "gy")

    got0 = (xlo, xhi, *to_sides(0, 3, xlo, xhi, yup, ydown))
    xs = x_shape(1, 3)
    three = (3, Z, LANES)
    up, down, terms, edges = call(
        pre0_kernel,
        [xs, xs, three, three],
        [f, c, w[0], vz, own, *got0, one, part, columns, c1],
        [t0, t0, t1],
        name="pre0",
        got=((5, "gx"), (7, "gy")),
        send=((0, "gx"),),
    )
    xlo, xhi = swap(up, down, "gx")
    v0, f1, one, part, columns, yup, ydown = call(
        mid1_kernel,
        [t0, t1, t1, t1, ys, Y_FULL, Y_FULL],
        [f, c, part, terms, edges, vz, w[1], c1, own],
        [t0],
        name="mid1",
    )
    got1 = (xlo, xhi, *to_sides(1, 3, xlo, xhi, yup, ydown))
    xs = x_shape(1, 2)
    v1, up, down, chunks = call(
        pre1_kernel,
        [t1, xs, xs, (8, 3 * Z + 8, LANES)],
        [f1, c1, w[1], vz, own, *got1, one, part, columns, c_tile],
        [t1, t2],
        name="pre1",
        got=((5, "gx"), (7, "gy")),
        send=((1, "gx"),),
    )
    v1_lo, v1_hi = swap(up, down, "gx")
    chunks = lax.all_to_all(chunks, "gx", 0, 0)
    s2, s3 = (6, Z, 256), (3, Z, 128)
    m2, m3 = (Z, 256), (Z, 128)
    full2, full3 = (Z + 8, 256), (Z + 8, 128)
    f2, c2, fl2, up, down = call(
        open_strip_kernel, [s2, s2, (8, 256), full2, full2], [chunks], name="open2", send=((3, "gy"),)
    )
    side2 = swap(up, down, "gy", True)
    c3, fl3, *c_sides = call(next_coef_kernel, [s3, (8, 128), m2, m2, m3, m3], [c2, fl2], name="coef3")
    part2, first, last, f_part, base_up, base_down = call(
        alone2_kernel, [s2, m2, m2, s3, m3, m3], [f2, c2, w[2], vz, fl2, c3, fl3], [s2, s2], name="alone2"
    )
    terms2, f3, up, down = call(
        pre_strip_kernel,
        [(2, *m2), s3, full3, full3],
        [w[2], vz, fl2, *side2, first, last, *c_sides[:2], f_part, fl3, base_up, base_down],
        name="pre2",
        got=((3, "gy"),),
        send=((2, "gy"),),
    )
    side3 = swap(up, down, "gy", True)
    *alone, twice = call(alone3_kernel, [m3] * 4 + [s3], [f3, c3, w[3], vz, fl3], [s3, s3], name="alone3")
    terms, up, down = call(
        bottom_strip_kernel,
        [(4, *m3), m3, m3],
        [w[3], vz, fl3, *side3, *alone[:2], *c_sides[2:], *alone[2:]],
        name="bottom",
        got=((3, "gy"),),
        send=((1, "gy"),),
    )
    side = swap(up, down, "gy", True)
    (part,) = call(again3_kernel, [s3], [f3, c3, w[3], vz, fl3, twice, terms], [s3], name="again3")
    v2, base_up, base_down, yup, ydown = call(
        base_message_kernel,
        [s2, m2, m2, ys, ys],
        [part2, fl2, terms2, v1, v1_lo, v1_hi, own],
        name="base2",
        got=((4, "gx"),),
    )
    e3, up, down = call(
        last_strip_kernel,
        [s3, m2, m2],
        [w[3], fl3, *side, part, base_up, base_down, v1_lo, v1_hi],
        [m3, m3],
        name="last",
        after=2,
        got=((2, "gy"),),
        send=((1, "gy"),),
    )
    side = swap(up, down, "gy", True)
    first, last, part_low, part_high, twice = call(
        again2_kernel, [m2] * 4 + [s2], [f2, c2, w[2], vz, fl2, v2, e3], [s2, s2], name="again2"
    )
    terms, up, down = call(
        post_strip_kernel,
        [(4, *m2), ys, ys],
        [w[2], vz, fl2, *side2, first, last, *c_sides[:2], part_low, part_high, *side, own, yup, ydown],
        name="post2",
        got=((3, "gy"), (11, "gy")),
        send=((1, "gy"),),
    )
    side = swap(up, down, "gy")
    g1, part, columns, lo, hi = call(
        again1_kernel, [t1, t1, ys, ys, ys], [f1, c1, w[1], vz, v1, twice, terms, v1_lo, v1_hi], [t2], name="again1", got=((7, "gx"),)
    )
    xs = x_shape(0, 2)
    e1, up, down = call(
        post1_kernel,
        [t1, xs, xs],
        [f1, c1, w[1], vz, own, *got1, g1, part, columns, lo, hi, *side, v0],
        [t1, t0],
        name="post1",
        got=((5, "gx"), (7, "gy"), (14, "gy")),
        send=((1, "gx"),),
    )
    xlo, xhi = swap(up, down, "gx")
    g0, part, columns, yup, ydown = call(
        again0_kernel, [t0, t0, ys, ys, ys], [f, c, w[0], vz, e1, v0], name="again0"
    )
    up, down = call(
        merge_kernel(0, 2), [ys, ys], [xlo, xhi, own, yup, ydown], name="merge0", got=((0, "gx"),), send=((0, "gy"),)
    )
    side = swap(up, down, "gy")
    twice, c_columns = call(twice0_kernel, [t0, ys], [f, c, w[0], vz, part, up], name="twice0", after=1)
    (out,) = call(
        post0_kernel,
        [(NZ * 24, LANES)],
        [f, c, w[0], vz, own, *got0, g0, columns, c_columns, twice, xlo, xhi, *side],
        name="post0",
        got=((5, "gx"), (7, "gy"), (13, "gx"), (15, "gy")),
    )
    return out.reshape(NZ, 24, LANES)


def solution(mesh):
    placed = (P(None, "gx", "gy"), P(None, "gx", "gy"), P(), P(), P("gx", "gy", None))
    return jax.shard_map(
        on_device, mesh=mesh, in_specs=placed, out_specs=P(None, "gx", "gy"), check_vma=False
    )
```
